32 devices in a mesh: groups: 2 (over x), store: 16 (over z, y, core).
Axes of the slice: x: 2, y: 2, z: 4, core: 2. Of those that a mesh axis runs over, the one named last changes fastest.
Arguments:
- sources: bfloat16 [16384, 512], P(('groups', 'store')), parts along dimension 0, may hold values from -1800 to 1800
- self_terms: float32 [2, 8192], P(None, 'store'), may hold values from 0.5 to 2
- near_tiles: bfloat16 [2, 32, 5, 256, 256], P(None, 'store'), may hold values from -1 to 1
- near_cols: int32 [32, 5], P('store'), may hold values from 0 to 31, as said below
- near_count: int32 [32], P('store'), may hold values from 1 to 5, as said below
- far_cols: int32 [32, 6], P('store'), may hold values from 0 to 31, as said below
- basis_left: bfloat16 [32, 256, 32], P('store'), may hold values from -2 to 2
- basis_right: bfloat16 [32, 256, 32], P('store'), may hold values from -2 to 2
- couplings: bfloat16 [2, 32, 6, 32, 32], P(None, 'store'), may hold values from -1 to 1
Outputs:
- images: float32 [2, 16384, 512], P(None, ('groups', 'store')), parts along dimension 1
- heights: float32 [4, 512], P('groups'), parts along dimension 0
- norms: float32 [4, 512], P('groups'), parts along dimension 0
The draws below stay inside these ranges and needn't reach their ends.
There are 2 independent parts, one for each index of `groups`. The reference program is written for one: setup_inputs(seed, part) draws one part's arguments, and reference() takes and returns one part's arrays. A program takes and returns all parts, laid end to end along the dimension named above; an argument that names none is the same for every part. Nothing has to cross between parts.
Inputs may be any that keep to these rules, and one draw needn't show every extreme that they name: `near_cols`: the slots of row block i name the blocks i - 2 to i + 2, cyclically, each once, in a drawn order. Slots 0 to near_count - 1 of a row block are live; block 0 has all 5. `far_cols`: a far-field block lies more than 2 blocks from its row block, cyclically.
All inputs are finite; a program needn't handle non-finite values.
Results may differ from the reference program's by a relative error of at most 0.011.
Values may be sent and summed in bfloat16 or wider, within the bound.
No kernel may reach another device: no remote copies, remote signals or barrier semaphores. Data moves between devices by JAX's collectives and lax.ppermute only.
A program may use at most 128 MiB of HBM per device.

```python
import math
import jax
import jax.numpy as jnp
from jax import lax

BLOCK = 256
SOURCES = 512
RANK = 32
REACH = 2
FAR = 6
NEAR = 5
BLOCKS = 32
PANELS = 8192


def draw_sources(key, part):
    key_rows = jax.random.fold_in(key, 0)
    key_cols = jax.random.fold_in(key, 1)
    key_base = jax.random.fold_in(key, 2)
    key_level = jax.random.fold_in(key, 4)
    key_sign = jax.random.fold_in(key, 5)
    key_block = jax.random.fold_in(key, 6)
    position = jnp.arange(PANELS, dtype=jnp.float32) / PANELS
    row_scale = jnp.exp(position * math.log(3.0)) * jnp.exp(jax.random.uniform(key_rows, (PANELS,)) * math.log(10.0))
    col_scale = jnp.exp(jax.random.uniform(key_cols, (SOURCES,)) * math.log(10.0))
    level = 0.7 + 0.6 * jax.random.uniform(key_level, (SOURCES,))
    signs = jnp.where(jax.random.bernoulli(key_sign, 0.5, (SOURCES,)), 1.0, -1.0)
    shared = (signs * level)[None, :]
    block_part = 0.5 * jax.random.normal(key_block, (BLOCKS, 1, SOURCES))
    block_part = jnp.broadcast_to(block_part, (BLOCKS, BLOCK, SOURCES)).reshape(PANELS, SOURCES)
    noise = jax.random.normal(key_base, (PANELS, SOURCES))
    draws_base = 0.6 * noise + shared + block_part
    values = jnp.clip(draws_base, -6.0, 6.0) * row_scale[:, None] * col_scale[None, :]
    return values.astype(jnp.bfloat16)


def draw_near_tiles(key, part):
    key_noise, key_level = jax.random.split(jax.random.fold_in(key, 21), 2)
    spread = 1.0 / math.sqrt(NEAR * BLOCK)
    level = 0.5 / BLOCK * (0.5 + jax.random.uniform(key_level, (2, BLOCKS, NEAR, 1, 1)))
    noise = jnp.clip(jax.random.normal(key_noise, (2, BLOCKS, NEAR, BLOCK, BLOCK)), -4.0, 4.0)
    return (level + spread * noise).astype(jnp.bfloat16)


def basis_draw(key, width):
    key_noise, key_mono = jax.random.split(key, 2)
    spread = 1.0 / math.sqrt(width)
    noise = jnp.clip(jax.random.normal(key_noise, (BLOCKS, BLOCK, RANK)), -4.0, 4.0) * spread
    mono = spread * (0.75 + 0.5 * jax.random.uniform(key_mono, (BLOCKS, BLOCK, RANK)))
    first_col = (jnp.arange(RANK, dtype=jnp.int32) == 0)[None, None, :]
    return jnp.where(first_col, mono, noise).astype(jnp.bfloat16)


def draw_basis_left(key, part):
    return basis_draw(jax.random.fold_in(key, 31), RANK)


def draw_basis_right(key, part):
    return basis_draw(jax.random.fold_in(key, 41), BLOCK)


def draw_couplings(key, part):
    key_noise, key_mono = jax.random.split(jax.random.fold_in(key, 51), 2)
    spread = 1.0 / math.sqrt(FAR * RANK)
    shape_all = (2, BLOCKS, FAR, RANK, RANK)
    noise = jnp.clip(jax.random.normal(key_noise, shape_all), -4.0, 4.0) * spread
    rows_at = jnp.arange(RANK, dtype=jnp.int32)[:, None]
    cols_at = jnp.arange(RANK, dtype=jnp.int32)[None, :]
    column_zero = cols_at == 0
    noise = jnp.where(column_zero, noise / math.sqrt(BLOCK), noise)
    mono_level = 0.6 * math.sqrt(RANK) / (FAR * math.sqrt(BLOCK))
    mono = mono_level * (0.5 + jax.random.uniform(key_mono, shape_all))
    corner = (rows_at == 0) & column_zero
    return jnp.where(corner, mono, noise).astype(jnp.bfloat16)


def draw_near_cols(key, part):
    scores = jax.random.randint(key, (BLOCKS, NEAR), 0, 1 << 20) * NEAR + jnp.arange(NEAR, dtype=jnp.int32)[None, :]
    orders = jnp.argsort(scores, axis=1).astype(jnp.int32)
    rows_at = jnp.arange(BLOCKS, dtype=jnp.int32)[:, None]
    return ((rows_at + orders - REACH) % BLOCKS).astype(jnp.int32)


def draw_near_count(key, part):
    key_first, key_second = jax.random.split(jax.random.fold_in(key, 7), 2)
    first_draw = jax.random.randint(key_first, (BLOCKS,), 1, NEAR + 1)
    second_draw = jax.random.randint(key_second, (BLOCKS,), 1, NEAR + 1)
    counts = jnp.minimum(first_draw, second_draw).at[0].set(NEAR)
    return counts.astype(jnp.int32)


def draw_far_cols(key, part):
    offsets = jax.random.randint(jax.random.fold_in(key, 11), (BLOCKS, FAR), REACH + 1, BLOCKS - REACH)
    rows_at = jnp.arange(BLOCKS, dtype=jnp.int32)[:, None]
    return ((rows_at + offsets) % BLOCKS).astype(jnp.int32)


def level_of(key, dims, shards, low, high):
    loudness = 1.0
    for axis_at, parts in shards:
        draws = jax.random.uniform(jax.random.fold_in(jax.random.fold_in(key, 6), axis_at), (parts,), jnp.float32, low / len(shards), high / len(shards))
        loudness = loudness * jnp.repeat(jnp.exp(draws), dims[axis_at] // parts).reshape((-1,) + (1,) * (len(dims) - 1 - axis_at))
    return loudness


def setup_inputs(seed: int = 0, part: int = 0) -> dict:
    streams_of = jax.random.split(jax.random.key(seed), 10)
    part_splits = jax.random.split(jax.random.fold_in(streams_of[9], part), 10)
    sources = draw_sources(jax.random.fold_in(jax.random.fold_in(streams_of[9], part), 71), part)
    self_terms = jnp.clip(jnp.exp(math.log(2.0) - 1.3862944 * jax.random.uniform(streams_of[1], (2, PANELS), jnp.float32) ** level_of(streams_of[1], (2, PANELS), ((1, 16),), -0.2, 0.2)), 0.5, 2.0)
    near_tiles = draw_near_tiles(jax.random.fold_in(streams_of[9], 71), part)
    near_cols = draw_near_cols(jax.random.fold_in(streams_of[9], 71), part)
    near_count = draw_near_count(jax.random.fold_in(streams_of[9], 71), part)
    far_cols = draw_far_cols(jax.random.fold_in(streams_of[9], 71), part)
    basis_left = draw_basis_left(jax.random.fold_in(streams_of[9], 71), part)
    basis_right = draw_basis_right(jax.random.fold_in(streams_of[9], 71), part)
    couplings = draw_couplings(jax.random.fold_in(streams_of[9], 71), part)
    return {"sources": sources, "self_terms": self_terms, "near_tiles": near_tiles, "near_cols": near_cols, "near_count": near_count, "far_cols": far_cols, "basis_left": basis_left, "basis_right": basis_right, "couplings": couplings}


EPSILON = 1e-06

def apply_operator(inputs, self_terms, near_tiles, near_cols, near_count, far_cols, basis_left, basis_right, couplings):
    coeffs = jnp.einsum('bpr,kbps->kbrs', basis_right.astype(jnp.float32), inputs.astype(jnp.float32)).astype(jnp.bfloat16)
    slot_ids = jnp.arange(NEAR, dtype=jnp.int32)

    def one_block(row_id):
        tiles_row = near_tiles[:, row_id].astype(jnp.float32)
        taken = inputs[:, near_cols[row_id]].astype(jnp.float32)
        weight = (slot_ids < near_count[row_id]).astype(jnp.float32)
        taken = taken * weight[None, :, None, None]
        taken = jnp.broadcast_to(taken, (2,) + taken.shape[1:])
        near_part = jnp.einsum('okpq,okqs->ops', tiles_row, taken)
        picked = coeffs[:, far_cols[row_id]].astype(jnp.float32)
        picked = jnp.broadcast_to(picked, (2,) + picked.shape[1:])
        reduced = jnp.einsum('ofrq,ofqs->ors', couplings[:, row_id].astype(jnp.float32), picked).astype(jnp.bfloat16)
        far_part = jnp.einsum('pr,ors->ops', basis_left[row_id].astype(jnp.float32), reduced.astype(jnp.float32)).astype(jnp.bfloat16)
        return near_part + far_part.astype(jnp.float32)
    rows_out = lax.map(one_block, jnp.arange(BLOCKS, dtype=jnp.int32))
    diagonal = self_terms.reshape(2, BLOCKS, BLOCK)
    return jnp.transpose(rows_out, (1, 0, 2, 3)) + diagonal[..., None] * inputs.astype(jnp.float32)

def reference(sources, self_terms, near_tiles, near_cols, near_count, far_cols, basis_left, basis_right, couplings):
    operands = (self_terms, near_tiles, near_cols, near_count, far_cols, basis_left, basis_right, couplings)
    source_f = sources.astype(jnp.float32).reshape(BLOCKS, BLOCK, SOURCES)
    scale_sq = lax.optimization_barrier(jnp.sum(source_f * source_f, axis=(0, 1))) / PANELS
    first_vec = (source_f / jnp.sqrt(scale_sq + EPSILON)).astype(jnp.bfloat16)
    image_one = apply_operator(first_vec[None], *operands)
    first_f = first_vec.astype(jnp.float32)
    heights = lax.optimization_barrier(jnp.sum(first_f[None] * image_one, axis=(1, 2))) / PANELS
    remain = image_one - heights[:, None, None, :] * first_f[None]
    norms = jnp.sqrt(lax.optimization_barrier(jnp.sum(remain * remain, axis=(1, 2))) / PANELS + EPSILON)
    second_vec = (remain / norms[:, None, None, :]).astype(jnp.bfloat16)
    image_two = apply_operator(second_vec, *operands)
    return (image_two.reshape(2, PANELS, SOURCES), heights, norms)
```

```python
import functools

import jax
import jax.numpy as jnp
from jax import lax
from jax.experimental import pallas as pl
from jax.experimental.pallas import tpu as pltpu
from jax.sharding import PartitionSpec as P

REACH = 2
EPSILON = 1e-06
SLICE = 128
STATS = 16
F32 = jnp.float32
BF16 = jnp.bfloat16

VMEM = pl.BlockSpec(memory_space=pltpu.VMEM)
SMEM = pl.BlockSpec(memory_space=pltpu.SMEM)


def call(body, out_shape, in_specs, scratch=(), flops=0, nbytes=0):
    many = isinstance(out_shape, (list, tuple))
    return pl.pallas_call(
        body,
        out_shape=out_shape,
        in_specs=in_specs,
        out_specs=[VMEM] * len(out_shape) if many else VMEM,
        scratch_shapes=list(scratch),
        compiler_params=pltpu.CompilerParams(vmem_limit_bytes=40 * 1024 * 1024),
        cost_estimate=pl.CostEstimate(flops=flops, bytes_accessed=nbytes, transcendentals=0),
    )


def dot(a, b, dims=((1,), (0,))):
    return lax.dot_general(a, b, (dims, ((), ())), preferred_element_type=F32)


def split3(row):
    high = row.astype(BF16)
    rest = row - high.astype(F32)
    middle = rest.astype(BF16)
    low = (rest - middle.astype(F32)).astype(BF16)
    return [high, middle, low]


def join3(rows, at):
    return rows[..., 3 * at, :] + rows[..., 3 * at + 1, :] + rows[..., 3 * at + 2, :]


def order_tiles(all_blocks, cols, count, row0, tiles, out):
    ops, blocks, near, size, _ = tiles.shape
    for b in range(blocks):
        for k in range(near):
            rel = lax.rem(cols[b, k] - (row0[0] + b) + REACH + all_blocks, all_blocks)
            rel = lax.rem(rel, all_blocks)
            at = pl.multiple_of(rel * size, size)
            live = k < count[b]
            for o in range(ops):
                tile = tiles[o, b, k]
                out[b, o * size:(o + 1) * size, pl.ds(at, size)] = jnp.where(
                    live, tile, jnp.zeros_like(tile)
                )


def coeff_kernel(u, right, out):
    blocks, size, rank = right.shape
    n = out.shape[0]
    slices = u.shape[1] // SLICE
    for b in range(blocks):
        z = dot(right[b], u[b * size:(b + 1) * size, :], ((0,), (0,))).astype(BF16)
        for a in range(slices):
            part = z[:, a * SLICE:(a + 1) * SLICE]

            def put(g, _, part=part, a=a, b=b):
                out[a * (n // slices) + g, b * rank:(b + 1) * rank, :] = part
                return 0

            lax.fori_loop(0, n // slices, put, 0)


def couple(cols, coup, a, b, blocks, ops, rank, source):
    far = coup.shape[2] // rank
    at = (a * blocks + b) * far
    picked = []
    for f in range(far):
        start = pl.multiple_of(cols[at + f] * rank, rank)
        picked.append(source(start))
    return jnp.concatenate(picked, axis=0)


def first_couple(ops, blocks, rank, cols, z, coup, out):
    slices = out.shape[0]
    for a in range(slices):
        for b in range(blocks):
            picked = couple(cols, coup, a, b, blocks, ops, rank, lambda s: z[pl.ds(s, rank), :])
            lhs = coup[a, b * ops * rank:(b + 1) * ops * rank, :]
            res = dot(lhs, picked).astype(BF16)
            for o in range(ops):
                row = (o * blocks + b) * rank
                out[a, row:row + rank, :] = res[o * rank:(o + 1) * rank]


def image_kernel(n, w, low, own, high, diag, left, right, cmsg, vout, mout, ext, image, coef):
    ops = vout.shape[0] // own.shape[0]
    blocks, size, rank = right.shape
    rows, columns = own.shape
    slices = columns // SLICE
    ext[0:rows, :] = low[...]
    ext[rows:2 * rows, :] = own[...]
    ext[2 * rows:, :] = high[...]
    for a in range(slices):
        coef[:, a * SLICE:(a + 1) * SLICE] = cmsg[a]
    near = w.shape[2]
    inner = [None] * ops
    squares = None
    for b in range(blocks):
        base = rows + (b - REACH) * size
        product = dot(w[b], ext[base:base + near, :])
        ub = own[b * size:(b + 1) * size, :].astype(F32)
        part = jnp.sum(ub * ub, axis=0, keepdims=True)
        squares = part if squares is None else squares + part
        for o in range(ops):
            row = (o * blocks + b) * rank
            far = dot(left[b], coef[row:row + rank, :]).astype(BF16).astype(F32)
            value = (
                product[o * size:(o + 1) * size]
                + diag[b * size:(b + 1) * size, o:o + 1] * ub
                + far
            )
            image[o, b * size:(b + 1) * size, :] = value
            part = jnp.sum(ub * value, axis=0, keepdims=True)
            inner[o] = part if inner[o] is None else inner[o] + part
    stats = []
    shifts = []
    spreads = []
    good = squares > 0
    for o in range(ops):
        shift = jnp.where(good, inner[o] / jnp.where(good, squares, 1.0), 0.0)
        pieces = split3(shift)
        stats += pieces
        shift = pieces[0].astype(F32) + pieces[1].astype(F32) + pieces[2].astype(F32)
        shifts.append(pieces)
        spread = None
        for b in range(blocks):
            ub = own[b * size:(b + 1) * size, :].astype(F32)
            v = image[o, b * size:(b + 1) * size, :] - shift * ub
            part = jnp.sum(v * v, axis=0, keepdims=True)
            spread = part if spread is None else spread + part
            v = v.astype(BF16)
            vout[(o * blocks + b) * size:(o * blocks + b + 1) * size, :] = v
            z = dot(right[b], v, ((0,), (0,))).astype(BF16)
            row = (o * blocks + b) * rank
            for a in range(slices):
                part = z[:, a * SLICE:(a + 1) * SLICE]

                def put(g, _, part=part, a=a, row=row):
                    mout[a * (n // slices) + g, row:row + rank, :] = part
                    return 0

                lax.fori_loop(0, n // slices, put, 0)
        spreads.append(spread)
    zero = jnp.zeros((1, columns), BF16)
    edge = sum(shifts, [])
    vout[ops * rows:, :] = jnp.concatenate(edge + [zero] * (STATS - len(edge)), axis=0)
    stats += split3(squares)
    for spread in spreads:
        stats += split3(spread)
    stats = jnp.concatenate(stats + [zero] * (STATS - len(stats)), axis=0)
    base = ops * blocks * rank
    for a in range(slices):
        part = stats[:, a * SLICE:(a + 1) * SLICE]

        def put_stats(g, _, part=part, a=a):
            mout[a * (n // slices) + g, base:base + STATS, :] = part
            return 0

        lax.fori_loop(0, n // slices, put_stats, 0)


def second_couple(panels, ops, blocks, rank, cols, z1, msg, coup, out, zs):
    n = msg.shape[0]
    slices = out.shape[0]
    body = ops * blocks * rank
    st = msg[:, body:body + STATS, :].astype(F32)
    shift = [join3(st, o) for o in range(ops)]
    squares = join3(st, ops)
    scale_sq = jnp.sum(squares, axis=0, keepdims=True) / panels + EPSILON
    reverse = 1.0 / jnp.sqrt(scale_sq)
    heights, norms = [], []
    for o in range(ops):
        total = jnp.sum(shift[o] * squares, axis=0, keepdims=True) / panels
        height = total / scale_sq
        delta = shift[o] - height
        spread = join3(st, ops + 1 + o) + delta * delta * squares
        norm = jnp.sqrt(jnp.sum(spread, axis=0, keepdims=True) / panels / scale_sq + EPSILON)
        heights.append(height)
        norms.append(norm)
        factor = reverse / norm
        zs[ops, 0:n, :] = delta

        def put(d, _, o=o, factor=factor):
            change = zs[ops, pl.ds(d, 1), :]
            for b in range(blocks):
                row = (o * blocks + b) * rank
                at = pl.multiple_of((d * blocks + b) * rank, rank)
                z = msg[d, row:row + rank, :].astype(F32) + change * z1[pl.ds(at, rank), :].astype(F32)
                zs[o, pl.ds(at, rank), :] = z * factor
            return 0

        lax.fori_loop(0, n, put, 0, unroll=4)
    for a in range(slices):
        for b in range(blocks):
            for o in range(ops):
                picked = couple(
                    cols, coup, a, b, blocks, ops, rank, lambda s, o=o: zs[o, pl.ds(s, rank), :]
                ).astype(BF16)
                row = (b * ops + o) * rank
                res = dot(coup[a, row:row + rank, :], picked).astype(BF16)
                row = (o * blocks + b) * rank
                out[a, row:row + rank, :] = res
    rows = []
    for row in heights + norms + [reverse]:
        rows += split3(row)
    rows += [jnp.zeros_like(rows[0])] * (STATS - len(rows))
    rows = jnp.concatenate(rows, axis=0)
    for a in range(slices):
        out[a, body:body + STATS, :] = rows


def final_kernel(
    w, ulow, uown, uhigh, vlow, vown, vhigh, diag, left, cmsg, images, heights, norms, ext, coef, stat
):
    ops = images.shape[0]
    blocks, size, rank = left.shape
    rows, columns = uown.shape
    slices = columns // SLICE
    body = ops * blocks * rank
    for a in range(slices):
        coef[:, a * SLICE:(a + 1) * SLICE] = cmsg[a, 0:body, :]
        stat[:, a * SLICE:(a + 1) * SLICE] = cmsg[a, body:, :].astype(F32)
    st = stat[...]

    def row3(values, at):
        return values[3 * at:3 * at + 1] + values[3 * at + 1:3 * at + 2] + values[3 * at + 2:3 * at + 3]

    reverse = row3(st, 2 * ops)
    near = w.shape[2]
    for o in range(ops):
        height = row3(st, o)
        norm = row3(st, ops + o)
        heights[o:o + 1, :] = height
        norms[o:o + 1, :] = norm
        factor = reverse / norm
        for at, (u, v) in enumerate(((ulow, vlow), (uown, vown), (uhigh, vhigh))):
            shift = row3(v[ops * rows:, :].astype(F32), o)
            change = (shift - height) * factor
            value = v[o * rows:(o + 1) * rows, :].astype(F32) * factor + u[...].astype(F32) * change
            ext[at * rows:(at + 1) * rows, :] = value.astype(BF16)
        for b in range(blocks):
            base = rows + (b - REACH) * size
            product = dot(w[b, o * size:(o + 1) * size, :], ext[base:base + near, :])
            row = (o * blocks + b) * rank
            far = dot(left[b], coef[row:row + rank, :]).astype(BF16).astype(F32)
            mine = ext[rows + b * size:rows + (b + 1) * size, :].astype(F32)
            images[o, b * size:(b + 1) * size, :] = (
                product + diag[b * size:(b + 1) * size, o:o + 1] * mine + far
            )


def ring(block):
    count = lax.axis_size("store")
    forward = [(i, (i + 1) % count) for i in range(count)]
    backward = [(target, source) for source, target in forward]
    return lax.ppermute(block, "store", forward), lax.ppermute(block, "store", backward)


def shards(
    sources,
    self_terms,
    near_tiles,
    near_cols,
    near_count,
    far_cols,
    basis_left,
    basis_right,
    couplings,
):
    n = lax.axis_size("store")
    ops, blocks, near, size, _ = near_tiles.shape
    rank = basis_left.shape[2]
    far = far_cols.shape[1]
    rows, columns = sources.shape
    slices = columns // SLICE
    lanes = n // slices
    all_blocks = blocks * n
    groups = [[a * lanes + g for a in range(slices)] for g in range(lanes)]
    sds = jax.ShapeDtypeStruct

    def exchange(x, part):
        return lax.all_to_all(
            x, "store", 0, 0, axis_index_groups=groups if part else None, tiled=True
        )

    row0 = (lax.axis_index("store") * blocks).astype(jnp.int32).reshape(1)
    diag = self_terms.T

    z_out = call(coeff_kernel, sds((n, blocks * rank, SLICE), BF16), [VMEM, VMEM])(
        sources, basis_right
    )
    z1 = exchange(z_out, False).reshape(n * blocks * rank, SLICE)
    low, high = ring(sources)

    mine = jnp.transpose(couplings, (1, 0, 3, 2, 4)).reshape(blocks * ops * rank, far * rank)
    names = jnp.pad(far_cols.astype(BF16).reshape(1, blocks * far), ((0, STATS - 1), (0, far * rank - blocks * far)))
    mine = jnp.concatenate([mine, names], axis=0)
    held = exchange(jnp.broadcast_to(mine[None], (slices,) + mine.shape), True)
    cols = held[:, blocks * ops * rank, :blocks * far].astype(jnp.int32).reshape(-1)

    w = call(
        functools.partial(order_tiles, all_blocks),
        sds((blocks, ops * size, near * size), BF16),
        [SMEM, SMEM, SMEM, VMEM],
    )(near_cols, near_count, row0, near_tiles)

    body = ops * blocks * rank
    c1 = call(
        functools.partial(first_couple, ops, blocks, rank),
        sds((slices, body, SLICE), BF16),
        [SMEM, VMEM, VMEM],
    )(cols, z1, held)
    c1 = exchange(c1, True)

    v, msg = call(
        functools.partial(image_kernel, n),
        [sds((ops * rows + STATS, columns), BF16), sds((n, body + STATS, SLICE), BF16)],
        [VMEM] * 8,
        [
            pltpu.VMEM((3 * rows, columns), BF16),
            pltpu.VMEM((ops, rows, columns), F32),
            pltpu.VMEM((body, columns), BF16),
        ],
        flops=2 * ops * rows * near * size * columns,
    )(w, low, sources, high, diag, basis_left, basis_right, c1)
    msg = exchange(msg, False)
    vlow, vhigh = ring(v)

    c2 = call(
        functools.partial(second_couple, all_blocks * size, ops, blocks, rank),
        sds((slices, body + STATS, SLICE), BF16),
        [SMEM, VMEM, VMEM, VMEM],
        [pltpu.VMEM((ops + 1, n * blocks * rank, SLICE), F32)],
    )(cols, z1, msg, held)
    c2 = exchange(c2, True)

    images, heights, norms = call(
        final_kernel,
        [sds((ops, rows, columns), F32), sds((ops, columns), F32), sds((ops, columns), F32)],
        [VMEM] * 10,
        [
            pltpu.VMEM((3 * rows, columns), BF16),
            pltpu.VMEM((body, columns), BF16),
            pltpu.VMEM((STATS, columns), F32),
        ],
        flops=2 * ops * rows * near * size * columns,
    )(w, low, sources, high, vlow, v, vhigh, diag, basis_left, c2)
    return images, heights, norms


def solution(mesh):
    placed = (
        P(("groups", "store"), None),
        P(None, "store"),
        P(None, "store", None, None, None),
        P("store", None),
        P("store"),
        P("store", None),
        P("store", None, None),
        P("store", None, None),
        P(None, "store", None, None, None),
    )
    return jax.shard_map(
        shards,
        mesh=mesh,
        in_specs=placed,
        out_specs=(P(None, ("groups", "store"), None), P("groups", None), P("groups", None)),
        check_vma=False,
    )
```

```python
import functools

import jax
import jax.numpy as jnp
from jax import lax
from jax.experimental import pallas as pl
from jax.experimental.pallas import tpu as pltpu
from jax.sharding import PartitionSpec as P

REACH = 2
EPSILON = 1e-06
LANES = 128
HALF = 64
SLICES = 8
STATS = 16
F32 = jnp.float32
BF16 = jnp.bfloat16

VMEM = pl.BlockSpec(memory_space=pltpu.VMEM)
SMEM = pl.BlockSpec(memory_space=pltpu.SMEM)


def call(body, out_shape, in_specs, scratch=(), flops=0, nbytes=0):
    many = isinstance(out_shape, (list, tuple))
    return pl.pallas_call(
        body,
        out_shape=out_shape,
        in_specs=in_specs,
        out_specs=[VMEM] * len(out_shape) if many else VMEM,
        scratch_shapes=list(scratch),
        compiler_params=pltpu.CompilerParams(vmem_limit_bytes=20 * 1024 * 1024),
        cost_estimate=pl.CostEstimate(flops=flops, bytes_accessed=nbytes, transcendentals=0),
    )


def dot(a, b, dims=((1,), (0,))):
    return lax.dot_general(a, b, (dims, ((), ())), preferred_element_type=F32)


def split3(row):
    high = row.astype(BF16)
    rest = row - high.astype(F32)
    middle = rest.astype(BF16)
    low = (rest - middle.astype(F32)).astype(BF16)
    return [high, middle, low]


def join3(rows, at):
    return rows[..., 3 * at, :] + rows[..., 3 * at + 1, :] + rows[..., 3 * at + 2, :]


def row3(values, at):
    return values[3 * at:3 * at + 1] + values[3 * at + 1:3 * at + 2] + values[3 * at + 2:3 * at + 3]


def halves(x, y):
    left = lax.broadcasted_iota(jnp.int32, x.shape, x.ndim - 1) < HALF
    first = jnp.where(left, x, pltpu.roll(y, HALF, x.ndim - 1))
    second = jnp.where(left, pltpu.roll(x, HALF, x.ndim - 1), y)
    return first, second


def chunk(x, pair):
    return x[:, pair * LANES:(pair + 1) * LANES]


def send_all(out, rows, at, part):
    n = out.shape[0]

    def put(g, _):
        out[g * SLICES + at, rows, :] = part
        return 0

    lax.fori_loop(0, n // SLICES, put, 0, unroll=n == 2 * SLICES)


def order_tiles(all_blocks, cols, count, row0, tiles, out):
    ops, blocks, near, size, _ = tiles.shape
    for b in range(blocks):
        for k in range(near):
            rel = lax.rem(cols[b, k] - (row0[0] + b) + REACH + all_blocks, all_blocks)
            rel = lax.rem(rel, all_blocks)
            at = pl.multiple_of(rel * size, size)
            live = k < count[b]
            for o in range(ops):
                tile = tiles[o, b, k]
                out[b, o * size:(o + 1) * size, pl.ds(at, size)] = jnp.where(
                    live, tile, jnp.zeros_like(tile)
                )


def coeff_kernel(u, right, out):
    blocks, rank, size = right.shape
    z = [dot(right[b], u[b * size:(b + 1) * size, :]) for b in range(blocks)]
    for pair in range(SLICES // 2):
        first, second = halves(chunk(z[0], pair), chunk(z[1], pair))
        send_all(out, slice(0, rank), 2 * pair, first.astype(BF16))
        send_all(out, slice(0, rank), 2 * pair + 1, second.astype(BF16))


def share_kernel(far_cols, coup, out):
    ops, blocks, far, rank, _ = coup.shape
    rows = blocks * ops * rank
    parts = []
    for b in range(blocks):
        for o in range(ops):
            parts.append(jnp.concatenate([coup[o, b, f] for f in range(far)], axis=1))
    lane = lax.broadcasted_iota(jnp.int32, (STATS, far * rank), 1)
    names = jnp.zeros((STATS, far * rank), F32)
    for b in range(blocks):
        for f in range(far):
            names = jnp.where(lane == b * far + f, far_cols[b, f].astype(F32), names)
    whole = jnp.concatenate(parts + [names.astype(BF16)], axis=0)
    for s in range(out.shape[0]):
        out[s] = whole


def couple(cols, coup, s, b, ops, rank, z):
    blocks = 2
    far = coup.shape[2] // rank
    at = (s * blocks + b) * far
    picked = []
    for f in range(far):
        start = pl.multiple_of(cols[at + f] * rank, rank)
        picked.append([x[pl.ds(start, rank), :] for x in z])
    res = []
    if len(z) == 1:
        lhs = coup[s, b * ops * rank:(b + 1) * ops * rank, :]
        return dot(lhs, jnp.concatenate([p[0] for p in picked], axis=0))
    for o in range(ops):
        row = (b * ops + o) * rank
        rhs = jnp.concatenate([p[o] for p in picked], axis=0)
        res.append(dot(coup[s, row:row + rank, :], rhs))
    return jnp.concatenate(res, axis=0)


def spread_rows(source, target, rank):
    n = source.shape[0]
    x = source.reshape(n, rank, LANES)
    y = pltpu.roll(x, HALF, 2)
    both = jnp.concatenate([x[:, None], y[:, None]], axis=1)
    target[...] = both.reshape(n * 2 * rank, LANES).astype(BF16)


def first_couple(ops, rank, cols, z1, coup, out, zs):
    spread_rows(z1[...].astype(F32), zs, rank)
    for s in range(out.shape[0]):
        c = [couple(cols, coup, s, b, ops, rank, [zs]) for b in range(2)]
        out[s] = halves(c[0], c[1])[0].astype(BF16)


def take_coefs(cmsg, coef, rows):
    for pair in range(SLICES // 2):
        parts = halves(
            cmsg[2 * pair, 0:rows, :].astype(F32), cmsg[2 * pair + 1, 0:rows, :].astype(F32)
        )
        for b in range(2):
            coef[b, :, pair * LANES:(pair + 1) * LANES] = parts[b].astype(BF16)


def near_product(tiles, parts, b, blocks, size):
    total = None
    first = b - REACH
    at = 0
    for d, part in enumerate(parts):
        start = max((d - 1) * blocks, first)
        stop = min(d * blocks, first + 2 * REACH + 1)
        if stop <= start:
            continue
        begin = (start - (d - 1) * blocks) * size
        width = (stop - start) * size
        value = dot(tiles[:, at:at + width], part[begin:begin + width, :])
        total = value if total is None else total + value
        at += width
    return total


def diagonal_of(diag, o, b, size, columns):
    row = diag[o:o + 1, b * size:(b + 1) * size]
    column = jnp.transpose(jnp.broadcast_to(row, (LANES, size)))
    return jnp.concatenate([column] * (columns // LANES), axis=1)


def image_kernel(w, low, own, high, diag, left, right, cmsg, vout, mout, image, coef):
    ops = image.shape[0]
    blocks, rank, size = right.shape
    rows, columns = own.shape
    take_coefs(cmsg, coef, ops * rank)
    inner = [None] * ops
    squares = None
    for b in range(blocks):
        product = near_product(w.at[b], (low, own, high), b, blocks, size)
        ub = own[b * size:(b + 1) * size, :].astype(F32)
        part = jnp.sum(ub * ub, axis=0, keepdims=True)
        squares = part if squares is None else squares + part
        for o in range(ops):
            far = dot(left[b], coef[b, o * rank:(o + 1) * rank, :], ((0,), (0,)))
            value = (
                product[o * size:(o + 1) * size]
                + diagonal_of(diag, o, b, size, columns) * ub
                + far.astype(BF16).astype(F32)
            )
            image[o, b * size:(b + 1) * size, :] = value
            part = jnp.sum(ub * value, axis=0, keepdims=True)
            inner[o] = part if inner[o] is None else inner[o] + part
    stats = []
    spreads = []
    good = squares > 0
    for o in range(ops):
        shift = jnp.where(good, inner[o] / jnp.where(good, squares, 1.0), 0.0)
        pieces = split3(shift)
        stats += pieces
        shift = pieces[0].astype(F32) + pieces[1].astype(F32) + pieces[2].astype(F32)
        spread = None
        z = []
        for b in range(blocks):
            ub = own[b * size:(b + 1) * size, :].astype(F32)
            v = image[o, b * size:(b + 1) * size, :] - shift * ub
            part = jnp.sum(v * v, axis=0, keepdims=True)
            spread = part if spread is None else spread + part
            v = v.astype(BF16)
            vout[(o * blocks + b) * size:(o * blocks + b + 1) * size, :] = v
            z.append(dot(right[b], v))
        for pair in range(SLICES // 2):
            first, second = halves(chunk(z[0], pair), chunk(z[1], pair))
            send_all(mout, slice(o * rank, (o + 1) * rank), 2 * pair, first.astype(BF16))
            send_all(mout, slice(o * rank, (o + 1) * rank), 2 * pair + 1, second.astype(BF16))
        spreads.append(spread)
    zero = jnp.zeros((1, columns), BF16)
    vout[ops * rows:, :] = jnp.concatenate(stats + [zero] * (STATS - len(stats)), axis=0)
    stats += split3(squares)
    for spread in spreads:
        stats += split3(spread)
    stats = jnp.concatenate(stats + [zero] * (STATS - len(stats)), axis=0).astype(F32)
    for pair in range(SLICES // 2):
        part = chunk(stats, pair)
        first, second = halves(part, part)
        send_all(mout, slice(ops * rank, ops * rank + STATS), 2 * pair, first.astype(BF16))
        send_all(mout, slice(ops * rank, ops * rank + STATS), 2 * pair + 1, second.astype(BF16))


def second_couple(panels, ops, rank, cols, z1, msg, coup, out, zs):
    body = ops * rank
    st = msg[:, body:body + STATS, :].astype(F32)
    shift = [join3(st, o) for o in range(ops)]
    squares = join3(st, ops)
    scale_sq = jnp.sum(squares, axis=0, keepdims=True) / panels + EPSILON
    reverse = 1.0 / jnp.sqrt(scale_sq)
    heights, norms = [], []
    base = z1[...].astype(F32)
    for o in range(ops):
        total = jnp.sum(shift[o] * squares, axis=0, keepdims=True) / panels
        height = total / scale_sq
        delta = shift[o] - height
        spread = join3(st, ops + 1 + o) + delta * delta * squares
        norm = jnp.sqrt(jnp.sum(spread, axis=0, keepdims=True) / panels / scale_sq + EPSILON)
        heights.append(height)
        norms.append(norm)
        factor = reverse / norm
        z = msg[:, o * rank:(o + 1) * rank, :].astype(F32) + delta[:, None, :] * base
        spread_rows(z * factor[None], zs.at[o], rank)
    rows = []
    for row in heights + norms + [reverse]:
        rows += split3(row)
    rows += [jnp.zeros_like(rows[0])] * (STATS - len(rows))
    rows = jnp.concatenate(rows, axis=0)
    for s in range(out.shape[0]):
        c = [couple(cols, coup, s, b, ops, rank, [zs.at[o] for o in range(ops)]) for b in range(2)]
        out[s, 0:body, :] = halves(c[0], c[1])[0].astype(BF16)
        out[s, body:body + STATS, :] = rows


def final_kernel(
    w, ulow, uown, uhigh, vlow, vown, vhigh, diag, left, cmsg, images, heights, norms, ext, coef, stat
):
    ops = images.shape[0]
    blocks, rank, size = left.shape
    rows, columns = uown.shape
    body = ops * rank
    take_coefs(cmsg, coef, body)
    for pair in range(SLICES // 2):
        stat[:, pair * LANES:(pair + 1) * LANES] = halves(
            cmsg[2 * pair, body:body + STATS, :].astype(F32),
            cmsg[2 * pair + 1, body:body + STATS, :].astype(F32),
        )[0]
    st = stat[...]
    reverse = row3(st, 2 * ops)
    for o in range(ops):
        height = row3(st, o)
        norm = row3(st, ops + o)
        heights[o:o + 1, :] = height
        norms[o:o + 1, :] = norm
        factor = reverse / norm
        for at, (u, v) in enumerate(((ulow, vlow), (uown, vown), (uhigh, vhigh))):
            shift = row3(v[ops * rows:, :].astype(F32), o)
            change = (shift - height) * factor
            value = v[o * rows:(o + 1) * rows, :].astype(F32) * factor + u[...].astype(F32) * change
            ext[o, at] = value.astype(BF16)
        for b in range(blocks):
            parts = [ext.at[o, at] for at in range(3)]
            product = near_product(w.at[b, o * size:(o + 1) * size], parts, b, blocks, size)
            far = dot(left[b], coef[b, o * rank:(o + 1) * rank, :], ((0,), (0,)))
            mine = ext[o, 1, b * size:(b + 1) * size, :].astype(F32)
            images[o, b * size:(b + 1) * size, :] = (
                product
                + diagonal_of(diag, o, b, size, columns) * mine
                + far.astype(BF16).astype(F32)
            )


def ring(block):
    count = lax.axis_size("store")
    forward = [(i, (i + 1) % count) for i in range(count)]
    backward = [(target, source) for source, target in forward]
    return lax.ppermute(block, "store", forward), lax.ppermute(block, "store", backward)


def shards(
    sources,
    self_terms,
    near_tiles,
    near_cols,
    near_count,
    far_cols,
    basis_left,
    basis_right,
    couplings,
):
    n = lax.axis_size("store")
    ops, blocks, near, size, _ = near_tiles.shape
    rank = basis_left.shape[2]
    far = far_cols.shape[1]
    rows, columns = sources.shape
    all_blocks = blocks * n
    groups = [[g * SLICES + s for s in range(SLICES)] for g in range(n // SLICES)]
    sds = jax.ShapeDtypeStruct
    body = ops * rank

    def exchange(x, part):
        return lax.all_to_all(
            x, "store", 0, 0, axis_index_groups=groups if part else None, tiled=True
        )

    row0 = (lax.axis_index("store") * blocks).astype(jnp.int32).reshape(1)
    left = jnp.transpose(basis_left, (0, 2, 1))
    right = jnp.transpose(basis_right, (0, 2, 1))

    z1 = call(coeff_kernel, sds((n, rank, LANES), BF16), [VMEM, VMEM])(sources, right)
    z1 = exchange(z1, False)
    low, high = ring(sources)

    held = call(
        share_kernel, sds((SLICES, blocks * body + STATS, far * rank), BF16), [SMEM, VMEM]
    )(far_cols, couplings)
    held = exchange(held, True)
    cols = held[:, blocks * body, :blocks * far].astype(jnp.int32).reshape(-1)

    w = call(
        functools.partial(order_tiles, all_blocks),
        sds((blocks, ops * size, near * size), BF16),
        [SMEM, SMEM, SMEM, VMEM],
    )(near_cols, near_count, row0, near_tiles)

    c1 = call(
        functools.partial(first_couple, ops, rank),
        sds((SLICES, body, LANES), BF16),
        [SMEM, VMEM, VMEM],
        [pltpu.VMEM((n * blocks * rank, LANES), BF16)],
    )(cols, z1, held)
    c1 = exchange(c1, True)

    v, msg = call(
        image_kernel,
        [sds((ops * rows + STATS, columns), BF16), sds((n, body + STATS, LANES), BF16)],
        [VMEM] * 8,
        [
            pltpu.VMEM((ops, rows, columns), F32),
            pltpu.VMEM((blocks, body, columns), BF16),
        ],
        flops=2 * ops * rows * near * size * columns,
    )(w, low, sources, high, self_terms, left, right, c1)
    msg = exchange(msg, False)
    vlow, vhigh = ring(v)

    c2 = call(
        functools.partial(second_couple, all_blocks * size, ops, rank),
        sds((SLICES, body + STATS, LANES), BF16),
        [SMEM, VMEM, VMEM, VMEM],
        [pltpu.VMEM((ops, n * blocks * rank, LANES), BF16)],
    )(cols, z1, msg, held)
    c2 = exchange(c2, True)

    images, heights, norms = call(
        final_kernel,
        [sds((ops, rows, columns), F32), sds((ops, columns), F32), sds((ops, columns), F32)],
        [VMEM] * 10,
        [
            pltpu.VMEM((ops, 3, rows, columns), BF16),
            pltpu.VMEM((blocks, body, columns), BF16),
            pltpu.VMEM((STATS, columns), F32),
        ],
        flops=2 * ops * rows * near * size * columns,
    )(w, low, sources, high, vlow, v, vhigh, self_terms, left, c2)
    return images, heights, norms


def solution(mesh):
    placed = (
        P(("groups", "store"), None),
        P(None, "store"),
        P(None, "store", None, None, None),
        P("store", None),
        P("store"),
        P("store", None),
        P("store", None, None),
        P("store", None, None),
        P(None, "store", None, None, None),
    )
    return jax.shard_map(
        shards,
        mesh=mesh,
        in_specs=placed,
        out_specs=(P(None, ("groups", "store"), None), P("groups", None), P("groups", None)),
        check_vma=False,
    )
```

```python
import functools

import jax
import jax.numpy as jnp
from jax import lax
from jax.experimental import pallas as pl
from jax.experimental.pallas import tpu as pltpu
from jax.sharding import PartitionSpec as P

REACH = 2
EPSILON = 1e-06
LANES = 128
HALF = 64
SLICES = 8
STATS = 16
F32 = jnp.float32
BF16 = jnp.bfloat16

VMEM = pl.BlockSpec(memory_space=pltpu.VMEM)
SMEM = pl.BlockSpec(memory_space=pltpu.SMEM)


def call(body, out_shape, in_specs, scratch=(), flops=0, nbytes=0):
    many = isinstance(out_shape, (list, tuple))
    return pl.pallas_call(
        body,
        out_shape=out_shape,
        in_specs=in_specs,
        out_specs=[VMEM] * len(out_shape) if many else VMEM,
        scratch_shapes=list(scratch),
        compiler_params=pltpu.CompilerParams(vmem_limit_bytes=20 * 1024 * 1024),
        cost_estimate=pl.CostEstimate(flops=flops, bytes_accessed=nbytes, transcendentals=0),
    )


def dot(a, b, dims=((1,), (0,))):
    return lax.dot_general(a, b, (dims, ((), ())), preferred_element_type=F32)


def split3(row):
    high = row.astype(BF16)
    rest = row - high.astype(F32)
    middle = rest.astype(BF16)
    low = (rest - middle.astype(F32)).astype(BF16)
    return [high, middle, low]


def join3(rows, at):
    return rows[..., 3 * at, :] + rows[..., 3 * at + 1, :] + rows[..., 3 * at + 2, :]


def row3(values, at):
    return values[3 * at:3 * at + 1] + values[3 * at + 1:3 * at + 2] + values[3 * at + 2:3 * at + 3]


def halves(x, y):
    left = lax.broadcasted_iota(jnp.int32, x.shape, x.ndim - 1) < HALF
    first = jnp.where(left, x, pltpu.roll(y, HALF, x.ndim - 1))
    second = jnp.where(left, pltpu.roll(x, HALF, x.ndim - 1), y)
    return first, second


def chunk(x, pair):
    return x[:, pair * LANES:(pair + 1) * LANES]


def send_all(out, rows, at, part):
    n = out.shape[0]

    def put(g, _):
        out[g * SLICES + at, rows, :] = part
        return 0

    lax.fori_loop(0, n // SLICES, put, 0, unroll=n == 2 * SLICES)


def order_tiles(all_blocks, cols, count, row0, tiles, out):
    ops, blocks, near, size, _ = tiles.shape
    for b in range(blocks):
        for k in range(near):
            rel = lax.rem(cols[b, k] - (row0[0] + b) + REACH + all_blocks, all_blocks)
            rel = lax.rem(rel, all_blocks)
            at = pl.multiple_of(rel * size, size)
            live = k < count[b]
            for o in range(ops):
                tile = tiles[o, b, k]
                out[b, o * size:(o + 1) * size, pl.ds(at, size)] = jnp.where(
                    live, tile, jnp.zeros_like(tile)
                )


def coeff_kernel(u, right, out):
    blocks, rank, size = right.shape
    z = [dot(right[b], u[b * size:(b + 1) * size, :]) for b in range(blocks)]
    for pair in range(SLICES // 2):
        first, second = halves(chunk(z[0], pair), chunk(z[1], pair))
        send_all(out, slice(0, rank), 2 * pair, first.astype(BF16))
        send_all(out, slice(0, rank), 2 * pair + 1, second.astype(BF16))


def share_kernel(far_cols, coup, after, out):
    ops, blocks, far, rank, _ = coup.shape
    body = ops * rank
    whole, rest = [], []
    for b in range(blocks):
        tiles = [
            jnp.concatenate([coup[o, b, f] for f in range(far)], axis=1) for o in range(ops)
        ]
        tiles = jnp.concatenate(tiles, axis=0)
        whole.append(tiles[:, :LANES])
        rest.append(tiles[:, LANES:])
    lane = lax.broadcasted_iota(jnp.int32, (STATS, LANES), 1)
    names = jnp.zeros((STATS, LANES), F32)
    for b in range(blocks):
        for f in range(far):
            names = jnp.where(lane == b * far + f, far_cols[b, f].astype(F32), names)
    whole = jnp.concatenate(
        whole + [jnp.concatenate(rest, axis=1), names.astype(BF16)], axis=0
    )
    for s in range(out.shape[0]):
        out[s] = whole


def coupling_rows(coup, s, b, ops, rank):
    body = ops * rank
    first = coup[s, b * body:(b + 1) * body, :]
    rest = coup[s, 2 * body:3 * body, b * HALF:(b + 1) * HALF]
    return jnp.concatenate([first, rest], axis=1)


def couple(cols, coup, s, b, ops, rank, far, z):
    blocks = 2
    at = (s * blocks + b) * far
    lhs = coupling_rows(coup, s, b, ops, rank)
    starts = [pl.multiple_of(cols[at + f] * rank, rank) for f in range(far)]
    picked = [
        jnp.concatenate([x[pl.ds(start, rank), :] for start in starts], axis=0) for x in z
    ]
    if len(z) == 1:
        return dot(lhs, picked[0])
    return jnp.concatenate(
        [dot(lhs[o * rank:(o + 1) * rank], picked[o]) for o in range(ops)], axis=0
    )


def spread_rows(source, target, rank):
    n = source.shape[0]
    x = source.reshape(n, rank, LANES)
    y = pltpu.roll(x, HALF, 2)
    both = jnp.concatenate([x[:, None], y[:, None]], axis=1)
    target[...] = both.reshape(n * 2 * rank, LANES).astype(BF16)


def first_couple(ops, rank, far, cols, z1, coup, out, zs):
    spread_rows(z1[...].astype(F32), zs, rank)
    for s in range(out.shape[0]):
        c = [couple(cols, coup, s, b, ops, rank, far, [zs]) for b in range(2)]
        out[s] = halves(c[0], c[1])[0].astype(BF16)


def take_coefs(cmsg, coef, rows):
    for pair in range(SLICES // 2):
        parts = halves(
            cmsg[2 * pair, 0:rows, :].astype(F32), cmsg[2 * pair + 1, 0:rows, :].astype(F32)
        )
        for b in range(2):
            coef[b, :, pair * LANES:(pair + 1) * LANES] = parts[b].astype(BF16)


def near_product(tiles, parts, b, blocks, size):
    total = None
    first = b - REACH
    at = 0
    for d, part in enumerate(parts):
        start = max((d - 1) * blocks, first)
        stop = min(d * blocks, first + 2 * REACH + 1)
        if stop <= start:
            continue
        begin = (start - (d - 1) * blocks) * size
        width = (stop - start) * size
        value = dot(tiles[:, at:at + width], part[begin:begin + width, :])
        total = value if total is None else total + value
        at += width
    return total


def diagonal_of(diag, o, b, size, columns):
    row = diag[o:o + 1, b * size:(b + 1) * size]
    column = jnp.transpose(jnp.broadcast_to(row, (LANES, size)))
    return jnp.concatenate([column] * (columns // LANES), axis=1)


def near_kernel(w, low, own, high, diag, left, image, vout):
    ops = image.shape[0]
    blocks, rank, size = left.shape
    rows, columns = own.shape
    inner = [None] * ops
    squares = None
    for b in range(blocks):
        product = near_product(w.at[b], (low, own, high), b, blocks, size)
        ub = own[b * size:(b + 1) * size, :].astype(F32)
        part = jnp.sum(ub * ub, axis=0, keepdims=True)
        squares = part if squares is None else squares + part
        for o in range(ops):
            value = (
                product[o * size:(o + 1) * size]
                + diagonal_of(diag, o, b, size, columns) * ub
            )
            image[o, b * size:(b + 1) * size, :] = value
            part = jnp.sum(ub * value, axis=0, keepdims=True)
            inner[o] = part if inner[o] is None else inner[o] + part
    stats = []
    good = squares > 0
    for o in range(ops):
        shift = jnp.where(good, inner[o] / jnp.where(good, squares, 1.0), 0.0)
        pieces = split3(shift)
        stats += pieces
        shift = pieces[0].astype(F32) + pieces[1].astype(F32) + pieces[2].astype(F32)
        for b in range(blocks):
            ub = own[b * size:(b + 1) * size, :].astype(F32)
            v = image[o, b * size:(b + 1) * size, :] - shift * ub
            image[o, b * size:(b + 1) * size, :] = v
            vout[(o * blocks + b) * size:(o * blocks + b + 1) * size, :] = v.astype(BF16)
    zero = jnp.zeros((1, columns), BF16)
    at = ops * rows
    vout[at:at + STATS, :] = jnp.concatenate(stats + [zero] * (STATS - len(stats)), axis=0)
    for b in range(blocks):
        vout[at + STATS:at + STATS + rank, b * size:(b + 1) * size] = left[b]


def image_kernel(own, near, edge, left, right, cmsg, vout, mout, image, coef):
    ops = image.shape[0]
    blocks, rank, size = right.shape
    rows, columns = own.shape
    take_coefs(cmsg, coef, ops * rank)
    inner = [None] * ops
    squares = None
    for b in range(blocks):
        ub = own[b * size:(b + 1) * size, :].astype(F32)
        part = jnp.sum(ub * ub, axis=0, keepdims=True)
        squares = part if squares is None else squares + part
        for o in range(ops):
            far = dot(left[b], coef[b, o * rank:(o + 1) * rank, :], ((0,), (0,)))
            value = near[o, b * size:(b + 1) * size, :] + far.astype(BF16).astype(F32)
            image[o, b * size:(b + 1) * size, :] = value
            part = jnp.sum(ub * value, axis=0, keepdims=True)
            inner[o] = part if inner[o] is None else inner[o] + part
    stats = []
    spreads = []
    good = squares > 0
    edges = edge[0:STATS, :].astype(F32)
    for o in range(ops):
        before = row3(edges, o)
        change = jnp.where(good, inner[o] / jnp.where(good, squares, 1.0), 0.0)
        pieces = split3(before + change)
        stats += pieces
        shift = pieces[0].astype(F32) + pieces[1].astype(F32) + pieces[2].astype(F32) - before
        spread = None
        z = []
        for b in range(blocks):
            ub = own[b * size:(b + 1) * size, :].astype(F32)
            v = image[o, b * size:(b + 1) * size, :] - shift * ub
            part = jnp.sum(v * v, axis=0, keepdims=True)
            spread = part if spread is None else spread + part
            v = v.astype(BF16)
            vout[(o * blocks + b) * size:(o * blocks + b + 1) * size, :] = v
            z.append(dot(right[b], v))
        for pair in range(SLICES // 2):
            first, second = halves(chunk(z[0], pair), chunk(z[1], pair))
            send_all(mout, slice(o * rank, (o + 1) * rank), 2 * pair, first.astype(BF16))
            send_all(mout, slice(o * rank, (o + 1) * rank), 2 * pair + 1, second.astype(BF16))
        spreads.append(spread)
    zero = jnp.zeros((1, columns), BF16)
    vout[ops * rows:, :] = jnp.concatenate(stats + [zero] * (STATS - len(stats)), axis=0)
    stats += split3(squares)
    for spread in spreads:
        stats += split3(spread)
    stats = jnp.concatenate(stats + [zero] * (STATS - len(stats)), axis=0).astype(F32)
    for pair in range(SLICES // 2):
        part = chunk(stats, pair)
        first, second = halves(part, part)
        send_all(mout, slice(ops * rank, ops * rank + STATS), 2 * pair, first.astype(BF16))
        send_all(mout, slice(ops * rank, ops * rank + STATS), 2 * pair + 1, second.astype(BF16))


def neighbour_kernel(size, low, high, clow, chigh, olow, ohigh, coef):
    blocks, body, columns = coef.shape
    rows = blocks * size
    ops = (low.shape[0] - STATS) // rows
    rank = body // ops
    for v, cmsg, out in ((low, clow, olow), (high, chigh, ohigh)):
        take_coefs(cmsg, coef, body)
        for b in range(blocks):
            left = v[ops * rows + STATS:, b * size:(b + 1) * size]
            for o in range(ops):
                far = dot(left, coef[b, o * rank:(o + 1) * rank, :], ((0,), (0,)))
                at = (o * blocks + b) * size
                out[at:at + size, :] = (
                    v[at:at + size, :].astype(F32) + far.astype(BF16).astype(F32)
                ).astype(BF16)
        out[ops * rows:, :] = v[ops * rows:ops * rows + STATS, :]


def second_couple(panels, ops, rank, far, cols, z1, msg, coup, out, zs):
    body = ops * rank
    st = msg[:, body:body + STATS, :].astype(F32)
    shift = [join3(st, o) for o in range(ops)]
    squares = join3(st, ops)
    scale_sq = jnp.sum(squares, axis=0, keepdims=True) / panels + EPSILON
    reverse = 1.0 / jnp.sqrt(scale_sq)
    heights, norms = [], []
    base = z1[...].astype(F32)
    for o in range(ops):
        total = jnp.sum(shift[o] * squares, axis=0, keepdims=True) / panels
        height = total / scale_sq
        delta = shift[o] - height
        spread = join3(st, ops + 1 + o) + delta * delta * squares
        norm = jnp.sqrt(jnp.sum(spread, axis=0, keepdims=True) / panels / scale_sq + EPSILON)
        heights.append(height)
        norms.append(norm)
        factor = reverse / norm
        z = msg[:, o * rank:(o + 1) * rank, :].astype(F32) + delta[:, None, :] * base
        spread_rows(z * factor[None], zs.at[o], rank)
    rows = []
    for row in heights + norms + [reverse]:
        rows += split3(row)
    rows += [jnp.zeros_like(rows[0])] * (STATS - len(rows))
    rows = jnp.concatenate(rows, axis=0)
    for s in range(out.shape[0]):
        c = [couple(cols, coup, s, b, ops, rank, far, [zs.at[o] for o in range(ops)]) for b in range(2)]
        out[s, 0:body, :] = halves(c[0], c[1])[0].astype(BF16)
        out[s, body:body + STATS, :] = rows


def final_kernel(
    w, ulow, uown, uhigh, vlow, vown, vhigh, diag, left, cmsg, images, heights, norms, ext, coef, stat
):
    ops = images.shape[0]
    blocks, rank, size = left.shape
    rows, columns = uown.shape
    body = ops * rank
    take_coefs(cmsg, coef, body)
    for pair in range(SLICES // 2):
        stat[:, pair * LANES:(pair + 1) * LANES] = halves(
            cmsg[2 * pair, body:body + STATS, :].astype(F32),
            cmsg[2 * pair + 1, body:body + STATS, :].astype(F32),
        )[0]
    st = stat[...]
    reverse = row3(st, 2 * ops)
    for o in range(ops):
        height = row3(st, o)
        norm = row3(st, ops + o)
        heights[o:o + 1, :] = height
        norms[o:o + 1, :] = norm
        factor = reverse / norm
        for at, (u, v) in enumerate(((ulow, vlow), (uown, vown), (uhigh, vhigh))):
            shift = row3(v[ops * rows:, :].astype(F32), o)
            change = (shift - height) * factor
            value = v[o * rows:(o + 1) * rows, :].astype(F32) * factor + u[...].astype(F32) * change
            ext[o, at] = value.astype(BF16)
        for b in range(blocks):
            parts = [ext.at[o, at] for at in range(3)]
            product = near_product(w.at[b, o * size:(o + 1) * size], parts, b, blocks, size)
            far = dot(left[b], coef[b, o * rank:(o + 1) * rank, :], ((0,), (0,)))
            mine = ext[o, 1, b * size:(b + 1) * size, :].astype(F32)
            images[o, b * size:(b + 1) * size, :] = (
                product
                + diagonal_of(diag, o, b, size, columns) * mine
                + far.astype(BF16).astype(F32)
            )


def ring(block):
    count = lax.axis_size("store")
    forward = [(i, (i + 1) % count) for i in range(count)]
    backward = [(target, source) for source, target in forward]
    return lax.ppermute(block, "store", forward), lax.ppermute(block, "store", backward)


def shards(
    sources,
    self_terms,
    near_tiles,
    near_cols,
    near_count,
    far_cols,
    basis_left,
    basis_right,
    couplings,
):
    n = lax.axis_size("store")
    ops, blocks, near, size, _ = near_tiles.shape
    rank = basis_left.shape[2]
    far = far_cols.shape[1]
    rows, columns = sources.shape
    all_blocks = blocks * n
    groups = [[g * SLICES + s for s in range(SLICES)] for g in range(n // SLICES)]
    sds = jax.ShapeDtypeStruct
    body = ops * rank

    def exchange(x, part):
        return lax.all_to_all(
            x, "store", 0, 0, axis_index_groups=groups if part else None, tiled=True
        )

    row0 = (lax.axis_index("store") * blocks).astype(jnp.int32).reshape(1)
    left = jnp.transpose(basis_left, (0, 2, 1))
    right = jnp.transpose(basis_right, (0, 2, 1))

    low, high = ring(sources)
    z1 = call(coeff_kernel, sds((n, rank, LANES), BF16), [VMEM, VMEM])(sources, right)
    z1 = exchange(z1, False)

    held = call(
        share_kernel,
        sds((SLICES, (blocks + 1) * body + STATS, LANES), BF16),
        [SMEM, VMEM, pl.BlockSpec(memory_space=pl.ANY)],
    )(far_cols, couplings, z1)
    held = exchange(held, True)
    cols = held[:, (blocks + 1) * body, :blocks * far].astype(jnp.int32).reshape(-1)

    w = call(
        functools.partial(order_tiles, all_blocks),
        sds((blocks, ops * size, near * size), BF16),
        [SMEM, SMEM, SMEM, VMEM],
    )(near_cols, near_count, row0, near_tiles)

    work = 2 * ops * rows * near * size * columns
    image, edge = call(
        near_kernel,
        [sds((ops, rows, columns), F32), sds((ops * rows + STATS + rank, columns), BF16)],
        [VMEM] * 6,
        flops=work,
    )(w, low, sources, high, self_terms, left)
    vlow, vhigh = ring(edge)

    c1 = call(
        functools.partial(first_couple, ops, rank, far),
        sds((SLICES, body, LANES), BF16),
        [SMEM, VMEM, VMEM],
        [pltpu.VMEM((n * blocks * rank, LANES), BF16)],
    )(cols, z1, held)
    c1 = exchange(c1, True)
    clow, chigh = ring(c1)

    v, msg = call(
        image_kernel,
        [sds((ops * rows + STATS, columns), BF16), sds((n, body + STATS, LANES), BF16)],
        [VMEM, VMEM, pl.BlockSpec(memory_space=pltpu.VMEM), VMEM, VMEM, VMEM],
        [
            pltpu.VMEM((ops, rows, columns), F32),
            pltpu.VMEM((blocks, body, columns), BF16),
        ],
    )(sources, image, edge[ops * rows:ops * rows + STATS], left, right, c1)
    msg = exchange(msg, False)

    c2 = call(
        functools.partial(second_couple, all_blocks * size, ops, rank, far),
        sds((SLICES, body + STATS, LANES), BF16),
        [SMEM, VMEM, VMEM, VMEM],
        [pltpu.VMEM((ops, n * blocks * rank, LANES), BF16)],
    )(cols, z1, msg, held)
    c2 = exchange(c2, True)

    vlow, vhigh = call(
        functools.partial(neighbour_kernel, size),
        [sds((ops * rows + STATS, columns), BF16)] * 2,
        [VMEM] * 4,
        [pltpu.VMEM((blocks, body, columns), BF16)],
    )(vlow, vhigh, clow, chigh)

    images, heights, norms = call(
        final_kernel,
        [sds((ops, rows, columns), F32), sds((ops, columns), F32), sds((ops, columns), F32)],
        [VMEM] * 10,
        [
            pltpu.VMEM((ops, 3, rows, columns), BF16),
            pltpu.VMEM((blocks, body, columns), BF16),
            pltpu.VMEM((STATS, columns), F32),
        ],
        flops=work,
    )(w, low, sources, high, vlow, v, vhigh, self_terms, left, c2)
    return images, heights, norms


def solution(mesh):
    placed = (
        P(("groups", "store"), None),
        P(None, "store"),
        P(None, "store", None, None, None),
        P("store", None),
        P("store"),
        P("store", None),
        P("store", None, None),
        P("store", None, None),
        P(None, "store", None, None, None),
    )
    return jax.shard_map(
        shards,
        mesh=mesh,
        in_specs=placed,
        out_specs=(P(None, ("groups", "store"), None), P("groups", None), P("groups", None)),
        check_vma=False,
    )
```

```python
import functools

import jax
import jax.numpy as jnp
from jax import lax
from jax.experimental import pallas as pl
from jax.experimental.pallas import tpu as pltpu
from jax.sharding import PartitionSpec as P

REACH = 2
EPSILON = 1e-06
LANES = 128
HALF = 64
SLICES = 8
STATS = 16
F32 = jnp.float32
BF16 = jnp.bfloat16

VMEM = pl.BlockSpec(memory_space=pltpu.VMEM)
SMEM = pl.BlockSpec(memory_space=pltpu.SMEM)


def call(body, out_shape, in_specs, scratch=(), flops=0, nbytes=0):
    many = isinstance(out_shape, (list, tuple))
    return pl.pallas_call(
        body,
        out_shape=out_shape,
        in_specs=in_specs,
        out_specs=[VMEM] * len(out_shape) if many else VMEM,
        scratch_shapes=list(scratch),
        compiler_params=pltpu.CompilerParams(vmem_limit_bytes=20 * 1024 * 1024),
        cost_estimate=pl.CostEstimate(flops=flops, bytes_accessed=nbytes, transcendentals=0),
    )


def dot(a, b, dims=((1,), (0,))):
    return lax.dot_general(a, b, (dims, ((), ())), preferred_element_type=F32)


def split3(row):
    high = row.astype(BF16)
    rest = row - high.astype(F32)
    middle = rest.astype(BF16)
    low = (rest - middle.astype(F32)).astype(BF16)
    return [high, middle, low]


def join3(rows, at):
    return rows[..., 3 * at, :] + rows[..., 3 * at + 1, :] + rows[..., 3 * at + 2, :]


def row3(values, at):
    return values[3 * at:3 * at + 1] + values[3 * at + 1:3 * at + 2] + values[3 * at + 2:3 * at + 3]


def halves(x, y):
    left = lax.broadcasted_iota(jnp.int32, x.shape, x.ndim - 1) < HALF
    first = jnp.where(left, x, pltpu.roll(y, HALF, x.ndim - 1))
    second = jnp.where(left, pltpu.roll(x, HALF, x.ndim - 1), y)
    return first, second


def chunk(x, pair):
    return x[:, pair * LANES:(pair + 1) * LANES]


def order_tiles(all_blocks, cols, count, row0, tiles, out):
    ops, blocks, near, size, _ = tiles.shape
    for b in range(blocks):
        for k in range(near):
            rel = lax.rem(cols[b, k] - (row0[0] + b) + REACH + all_blocks, all_blocks)
            rel = lax.rem(rel, all_blocks)
            at = pl.multiple_of(rel * size, size)
            live = k < count[b]
            for o in range(ops):
                tile = tiles[o, b, k]
                out[b, o * size:(o + 1) * size, pl.ds(at, size)] = jnp.where(
                    live, tile, jnp.zeros_like(tile)
                )


def share_kernel(far_cols, u, right, coup, out):
    ops, blocks, far, rank, _ = coup.shape
    size = right.shape[2]
    z = [dot(right[b], u[b * size:(b + 1) * size, :]) for b in range(blocks)]
    for pair in range(SLICES // 2):
        first, second = halves(chunk(z[0], pair), chunk(z[1], pair))
        out[2 * pair, 0:rank, :] = first.astype(BF16)
        out[2 * pair + 1, 0:rank, :] = second.astype(BF16)
    whole, rest = [], []
    for b in range(blocks):
        tiles = [
            jnp.concatenate([coup[o, b, f] for f in range(far)], axis=1) for o in range(ops)
        ]
        tiles = jnp.concatenate(tiles, axis=0)
        whole.append(tiles[:, :LANES])
        rest.append(tiles[:, LANES:])
    lane = lax.broadcasted_iota(jnp.int32, (STATS, LANES), 1)
    names = jnp.zeros((STATS, LANES), F32)
    for b in range(blocks):
        for f in range(far):
            names = jnp.where(lane == b * far + f, far_cols[b, f].astype(F32), names)
    whole = jnp.concatenate(
        whole + [jnp.concatenate(rest, axis=1), names.astype(BF16)], axis=0
    )
    for s in range(SLICES):
        out[s, rank:, :] = whole


def relay_kernel(first, u, z, uout):
    z[...] = first[:, 0:z.shape[1], :]
    uout[...] = u[...]


def coupling_rows(held, s, b, ops, rank):
    body = ops * rank
    first = held[s, rank + b * body:rank + (b + 1) * body, :]
    rest = held[s, rank + 2 * body:rank + 3 * body, b * HALF:(b + 1) * HALF]
    return jnp.concatenate([first, rest], axis=1)


def couple(cols, held, s, b, ops, rank, far, z):
    at = (s * 2 + b) * far
    lhs = coupling_rows(held, s, b, ops, rank)
    starts = [pl.multiple_of(cols[at + f] * rank, rank) for f in range(far)]
    picked = [
        jnp.concatenate([x[pl.ds(start, rank), :] for start in starts], axis=0) for x in z
    ]
    if len(z) == 1:
        return dot(lhs, picked[0])
    return jnp.concatenate(
        [dot(lhs[o * rank:(o + 1) * rank], picked[o]) for o in range(ops)], axis=0
    )


def spread_rows(source, rank):
    count = source.shape[0]
    turned = pltpu.roll(source, HALF, 2)
    both = jnp.concatenate([source[:, None], turned[:, None]], axis=1)
    return both.reshape(count * 2 * rank, LANES).astype(BF16)


def group_at(group, m, groups, step):
    return pl.multiple_of(lax.rem(group[0] + (groups - m), groups) * step, step)


def first_couple(ops, rank, far, cols, group, held, *refs):
    parts, (out, zs) = refs[:-2], refs[-2:]
    step = SLICES * 2 * rank
    for m, part in enumerate(parts):
        at = group_at(group, m, len(parts), step)
        zs[pl.ds(at, step), :] = spread_rows(part[...].astype(F32), rank)
    for s in range(SLICES):
        c = [couple(cols, held, s, b, ops, rank, far, [zs]) for b in range(2)]
        out[s] = halves(c[0], c[1])[0].astype(BF16)


def take_coefs(cmsg, coef, rows):
    for pair in range(SLICES // 2):
        parts = halves(
            cmsg[2 * pair, 0:rows, :].astype(F32), cmsg[2 * pair + 1, 0:rows, :].astype(F32)
        )
        for b in range(2):
            coef[b, :, pair * LANES:(pair + 1) * LANES] = parts[b].astype(BF16)


def near_product(tiles, parts, b, blocks, size):
    total = None
    first = b - REACH
    at = 0
    for d, part in enumerate(parts):
        start = max((d - 1) * blocks, first)
        stop = min(d * blocks, first + 2 * REACH + 1)
        if stop <= start:
            continue
        begin = (start - (d - 1) * blocks) * size
        width = (stop - start) * size
        value = dot(tiles[:, at:at + width], part[begin:begin + width, :])
        total = value if total is None else total + value
        at += width
    return total


def diagonal_of(diag, o, b, size, columns):
    row = diag[o:o + 1, b * size:(b + 1) * size]
    column = jnp.transpose(jnp.broadcast_to(row, (LANES, size)))
    return jnp.concatenate([column] * (columns // LANES), axis=1)


def image_kernel(w, low, own, high, diag, left, right, cmsg, vout, mout, image, coef):
    ops = image.shape[0]
    blocks, rank, size = right.shape
    rows, columns = own.shape
    take_coefs(cmsg, coef, ops * rank)
    inner = [None] * ops
    squares = None
    for b in range(blocks):
        product = near_product(w.at[b], (low, own, high), b, blocks, size)
        ub = own[b * size:(b + 1) * size, :].astype(F32)
        part = jnp.sum(ub * ub, axis=0, keepdims=True)
        squares = part if squares is None else squares + part
        for o in range(ops):
            far = dot(left[b], coef[b, o * rank:(o + 1) * rank, :], ((0,), (0,)))
            value = (
                product[o * size:(o + 1) * size]
                + diagonal_of(diag, o, b, size, columns) * ub
                + far.astype(BF16).astype(F32)
            )
            image[o, b * size:(b + 1) * size, :] = value
            part = jnp.sum(ub * value, axis=0, keepdims=True)
            inner[o] = part if inner[o] is None else inner[o] + part
    stats = []
    spreads = []
    good = squares > 0
    for o in range(ops):
        shift = jnp.where(good, inner[o] / jnp.where(good, squares, 1.0), 0.0)
        pieces = split3(shift)
        stats += pieces
        shift = pieces[0].astype(F32) + pieces[1].astype(F32) + pieces[2].astype(F32)
        spread = None
        z = []
        for b in range(blocks):
            ub = own[b * size:(b + 1) * size, :].astype(F32)
            v = image[o, b * size:(b + 1) * size, :] - shift * ub
            part = jnp.sum(v * v, axis=0, keepdims=True)
            spread = part if spread is None else spread + part
            v = v.astype(BF16)
            vout[(o * blocks + b) * size:(o * blocks + b + 1) * size, :] = v
            z.append(dot(right[b], v))
        for pair in range(SLICES // 2):
            first, second = halves(chunk(z[0], pair), chunk(z[1], pair))
            mout[2 * pair, o * rank:(o + 1) * rank, :] = first.astype(BF16)
            mout[2 * pair + 1, o * rank:(o + 1) * rank, :] = second.astype(BF16)
        spreads.append(spread)
    zero = jnp.zeros((1, columns), BF16)
    vout[ops * rows:, :] = jnp.concatenate(stats + [zero] * (STATS - len(stats)), axis=0)
    stats += split3(squares)
    for spread in spreads:
        stats += split3(spread)
    stats = jnp.concatenate(stats + [zero] * (STATS - len(stats)), axis=0).astype(F32)
    for pair in range(SLICES // 2):
        part = chunk(stats, pair)
        first, second = halves(part, part)
        mout[2 * pair, ops * rank:ops * rank + STATS, :] = first.astype(BF16)
        mout[2 * pair + 1, ops * rank:ops * rank + STATS, :] = second.astype(BF16)


def second_couple(panels, ops, rank, far, cols, group, held, *refs):
    out, zs, st = refs[-3:]
    count = (len(refs) - 3) // 2
    z1, msgs = refs[:count], refs[count:2 * count]
    body = ops * rank
    step = SLICES * 2 * rank
    for m, msg in enumerate(msgs):
        at = group_at(group, m, count, SLICES)
        st[pl.ds(at, SLICES)] = msg[:, body:body + STATS, :].astype(F32)
    every = st[...]
    squares = join3(every, ops)
    scale_sq = jnp.sum(squares, axis=0, keepdims=True) / panels + EPSILON
    reverse = 1.0 / jnp.sqrt(scale_sq)
    heights, norms = [], []
    for o in range(ops):
        shift = join3(every, o)
        height = jnp.sum(shift * squares, axis=0, keepdims=True) / panels / scale_sq
        delta = shift - height
        spread = join3(every, ops + 1 + o) + delta * delta * squares
        norm = jnp.sqrt(jnp.sum(spread, axis=0, keepdims=True) / panels / scale_sq + EPSILON)
        heights.append(height)
        norms.append(norm)
    for m, (base, msg) in enumerate(zip(z1, msgs)):
        at = group_at(group, m, count, step)
        mine = msg[:, body:body + STATS, :].astype(F32)
        base = base[...].astype(F32)
        for o in range(ops):
            delta = join3(mine, o) - heights[o]
            z = msg[:, o * rank:(o + 1) * rank, :].astype(F32) + delta[:, None, :] * base
            z = z * (reverse / norms[o])[None]
            zs[o, pl.ds(at, step), :] = spread_rows(z, rank)
    rows = []
    for row in heights + norms + [reverse]:
        rows += split3(row)
    rows += [jnp.zeros_like(rows[0])] * (STATS - len(rows))
    rows = jnp.concatenate(rows, axis=0)
    for s in range(SLICES):
        c = [couple(cols, held, s, b, ops, rank, far, [zs.at[o] for o in range(ops)]) for b in range(2)]
        out[s, 0:body, :] = halves(c[0], c[1])[0].astype(BF16)
        out[s, body:body + STATS, :] = rows


def final_kernel(
    w, ulow, uown, uhigh, vlow, vown, vhigh, diag, left, cmsg, images, heights, norms, ext, coef, stat
):
    ops = images.shape[0]
    blocks, rank, size = left.shape
    rows, columns = uown.shape
    body = ops * rank
    take_coefs(cmsg, coef, body)
    for pair in range(SLICES // 2):
        stat[:, pair * LANES:(pair + 1) * LANES] = halves(
            cmsg[2 * pair, body:body + STATS, :].astype(F32),
            cmsg[2 * pair + 1, body:body + STATS, :].astype(F32),
        )[0]
    st = stat[...]
    reverse = row3(st, 2 * ops)
    for o in range(ops):
        height = row3(st, o)
        norm = row3(st, ops + o)
        heights[o:o + 1, :] = height
        norms[o:o + 1, :] = norm
        factor = reverse / norm
        for at, (u, v) in enumerate(((ulow, vlow), (uown, vown), (uhigh, vhigh))):
            shift = row3(v[ops * rows:, :].astype(F32), o)
            change = (shift - height) * factor
            value = v[o * rows:(o + 1) * rows, :].astype(F32) * factor + u[...].astype(F32) * change
            ext[o, at] = value.astype(BF16)
        for b in range(blocks):
            parts = [ext.at[o, at] for at in range(3)]
            product = near_product(w.at[b, o * size:(o + 1) * size], parts, b, blocks, size)
            far = dot(left[b], coef[b, o * rank:(o + 1) * rank, :], ((0,), (0,)))
            mine = ext[o, 1, b * size:(b + 1) * size, :].astype(F32)
            images[o, b * size:(b + 1) * size, :] = (
                product
                + diagonal_of(diag, o, b, size, columns) * mine
                + far.astype(BF16).astype(F32)
            )


def ring(block):
    count = lax.axis_size("store")
    forward = [(i, (i + 1) % count) for i in range(count)]
    backward = [(target, source) for source, target in forward]
    return lax.ppermute(block, "store", forward), lax.ppermute(block, "store", backward)


def shards(
    sources,
    self_terms,
    near_tiles,
    near_cols,
    near_count,
    far_cols,
    basis_left,
    basis_right,
    couplings,
):
    n = lax.axis_size("store")
    ops, blocks, near, size, _ = near_tiles.shape
    rank = basis_left.shape[2]
    far = far_cols.shape[1]
    rows, columns = sources.shape
    all_blocks = blocks * n
    count = n // SLICES
    groups = [[g * SLICES + s for s in range(SLICES)] for g in range(count)]
    sds = jax.ShapeDtypeStruct
    body = ops * rank

    def exchange(x):
        return lax.all_to_all(x, "store", 0, 0, axis_index_groups=groups, tiled=True)

    def across(x):
        parts = [x]
        for m in range(1, count):
            pairs = [(i, (i + m * SLICES) % n) for i in range(n)]
            parts.append(lax.ppermute(x, "store", pairs))
        return parts

    place = lax.axis_index("store").astype(jnp.int32)
    row0 = (place * blocks).reshape(1)
    group = lax.div(place, jnp.int32(SLICES)).reshape(1)
    left = jnp.transpose(basis_left, (0, 2, 1))
    right = jnp.transpose(basis_right, (0, 2, 1))

    shared = rank + (blocks + 1) * body
    held = call(
        share_kernel, sds((SLICES, shared + STATS, LANES), BF16), [SMEM, VMEM, VMEM, VMEM]
    )(far_cols, sources, right, couplings)
    held = exchange(held)
    cols = held[:, shared, :blocks * far].astype(jnp.int32).reshape(-1)
    z1, own = call(
        relay_kernel,
        [sds((SLICES, rank, LANES), BF16), sds((rows, columns), BF16)],
        [VMEM, VMEM],
    )(held, sources)
    z1 = across(z1)
    low, high = ring(own)

    w = call(
        functools.partial(order_tiles, all_blocks),
        sds((blocks, ops * size, near * size), BF16),
        [SMEM, SMEM, SMEM, VMEM],
    )(near_cols, near_count, row0, near_tiles)

    c1 = call(
        functools.partial(first_couple, ops, rank, far),
        sds((SLICES, body, LANES), BF16),
        [SMEM, SMEM] + [VMEM] * (1 + count),
        [pltpu.VMEM((n * blocks * rank, LANES), BF16)],
    )(cols, group, held, *z1)
    c1 = exchange(c1)

    work = 2 * ops * rows * near * size * columns
    v, msg = call(
        image_kernel,
        [sds((ops * rows + STATS, columns), BF16), sds((SLICES, body + STATS, LANES), BF16)],
        [VMEM] * 8,
        [
            pltpu.VMEM((ops, rows, columns), F32),
            pltpu.VMEM((blocks, body, columns), BF16),
        ],
        flops=work,
    )(w, low, own, high, self_terms, left, right, c1)
    msgs = across(exchange(msg))
    vlow, vhigh = ring(v)

    c2 = call(
        functools.partial(second_couple, all_blocks * size, ops, rank, far),
        sds((SLICES, body + STATS, LANES), BF16),
        [SMEM, SMEM] + [VMEM] * (1 + 2 * count),
        [
            pltpu.VMEM((ops, n * blocks * rank, LANES), BF16),
            pltpu.VMEM((n, STATS, LANES), F32),
        ],
    )(cols, group, held, *z1, *msgs)
    c2 = exchange(c2)

    images, heights, norms = call(
        final_kernel,
        [sds((ops, rows, columns), F32), sds((ops, columns), F32), sds((ops, columns), F32)],
        [VMEM] * 10,
        [
            pltpu.VMEM((ops, 3, rows, columns), BF16),
            pltpu.VMEM((blocks, body, columns), BF16),
            pltpu.VMEM((STATS, columns), F32),
        ],
        flops=work,
    )(w, low, own, high, vlow, v, vhigh, self_terms, left, c2)
    return images, heights, norms


def solution(mesh):
    placed = (
        P(("groups", "store"), None),
        P(None, "store"),
        P(None, "store", None, None, None),
        P("store", None),
        P("store"),
        P("store", None),
        P("store", None, None),
        P("store", None, None),
        P(None, "store", None, None, None),
    )
    return jax.shard_map(
        shards,
        mesh=mesh,
        in_specs=placed,
        out_specs=(P(None, ("groups", "store"), None), P("groups", None), P("groups", None)),
        check_vma=False,
    )
```

```python
import functools

import jax
import jax.numpy as jnp
from jax import lax
from jax.experimental import pallas as pl
from jax.experimental.pallas import tpu as pltpu
from jax.sharding import PartitionSpec as P

REACH = 2
EPSILON = 1e-06
LANES = 128
HALF = 64
SLICES = 8
STATS = 16
HBM_RATE = 3690000
F32 = jnp.float32
BF16 = jnp.bfloat16

VMEM = pl.BlockSpec(memory_space=pltpu.VMEM)
SMEM = pl.BlockSpec(memory_space=pltpu.SMEM)
HBM = pl.BlockSpec(memory_space=pltpu.HBM)


def call(body, out_shape, in_specs, scratch=(), micros=1.0):
    many = isinstance(out_shape, (list, tuple))
    return pl.pallas_call(
        body,
        out_shape=out_shape,
        in_specs=in_specs,
        out_specs=[VMEM] * len(out_shape) if many else VMEM,
        scratch_shapes=list(scratch),
        compiler_params=pltpu.CompilerParams(vmem_limit_bytes=20 * 1024 * 1024),
        cost_estimate=pl.CostEstimate(
            flops=0, bytes_accessed=int(micros * HBM_RATE), transcendentals=0
        ),
    )


def dot(a, b, dims=((1,), (0,))):
    return lax.dot_general(a, b, (dims, ((), ())), preferred_element_type=F32)


def split3(row):
    high = row.astype(BF16)
    rest = row - high.astype(F32)
    middle = rest.astype(BF16)
    low = (rest - middle.astype(F32)).astype(BF16)
    return [high, middle, low]


def join3(rows, at):
    return rows[..., 3 * at, :] + rows[..., 3 * at + 1, :] + rows[..., 3 * at + 2, :]


def row3(values, at):
    return values[3 * at:3 * at + 1] + values[3 * at + 1:3 * at + 2] + values[3 * at + 2:3 * at + 3]


def halves(x, y):
    left = lax.broadcasted_iota(jnp.int32, x.shape, x.ndim - 1) < HALF
    first = jnp.where(left, x, pltpu.roll(y, HALF, x.ndim - 1))
    second = jnp.where(left, pltpu.roll(x, HALF, x.ndim - 1), y)
    return first, second


def chunk(x, pair):
    return x[:, pair * LANES:(pair + 1) * LANES]


def order_tiles(all_blocks, cols, count, row0, tiles, out):
    ops, blocks, near, size, _ = tiles.shape
    for b in range(blocks):
        for k in range(near):
            rel = lax.rem(cols[b, k] - (row0[0] + b) + REACH + all_blocks, all_blocks)
            rel = lax.rem(rel, all_blocks)
            at = pl.multiple_of(rel * size, size)
            live = k < count[b]
            for o in range(ops):
                tile = tiles[o, b, k]
                out[b, o * size:(o + 1) * size, pl.ds(at, size)] = jnp.where(
                    live, tile, jnp.zeros_like(tile)
                )


def share_kernel(far_cols, u_in, right_in, coup_in, out, u, right, coup, sems):
    copies = [
        pltpu.make_async_copy(source, target, sems.at[i])
        for i, (source, target) in enumerate(((u_in, u), (right_in, right), (coup_in, coup)))
    ]
    for copy in copies:
        copy.start()
    for copy in copies:
        copy.wait()
    ops, blocks, far, rank, _ = coup.shape
    size = right.shape[2]
    z = [dot(right[b], u[b * size:(b + 1) * size, :]) for b in range(blocks)]
    for pair in range(SLICES // 2):
        first, second = halves(chunk(z[0], pair), chunk(z[1], pair))
        out[2 * pair, 0:rank, :] = first.astype(BF16)
        out[2 * pair + 1, 0:rank, :] = second.astype(BF16)
    whole, rest = [], []
    for b in range(blocks):
        tiles = [
            jnp.concatenate([coup[o, b, f] for f in range(far)], axis=1) for o in range(ops)
        ]
        tiles = jnp.concatenate(tiles, axis=0)
        whole.append(tiles[:, :LANES])
        rest.append(tiles[:, LANES:])
    lane = lax.broadcasted_iota(jnp.int32, (STATS, LANES), 1)
    names = jnp.zeros((STATS, LANES), F32)
    for b in range(blocks):
        for f in range(far):
            names = jnp.where(lane == b * far + f, far_cols[b, f].astype(F32), names)
    whole = jnp.concatenate(
        whole + [jnp.concatenate(rest, axis=1), names.astype(BF16)], axis=0
    )
    for s in range(SLICES):
        out[s, rank:, :] = whole


def relay_kernel(first, z):
    z[...] = first[:, 0:z.shape[1], :]


def copy_kernel(source, target):
    target[...] = source[...]


def coupling_rows(held, s, b, ops, rank):
    body = ops * rank
    first = held[s, rank + b * body:rank + (b + 1) * body, :]
    rest = held[s, rank + 2 * body:rank + 3 * body, b * HALF:(b + 1) * HALF]
    return jnp.concatenate([first, rest], axis=1)


def couple(cols, held, s, b, ops, rank, far, z):
    at = (s * 2 + b) * far
    lhs = coupling_rows(held, s, b, ops, rank)
    starts = [pl.multiple_of(cols[at + f] * rank, rank) for f in range(far)]
    picked = [
        jnp.concatenate([x[pl.ds(start, rank), :] for start in starts], axis=0) for x in z
    ]
    if len(z) == 1:
        return dot(lhs, picked[0])
    return jnp.concatenate(
        [dot(lhs[o * rank:(o + 1) * rank], picked[o]) for o in range(ops)], axis=0
    )


def spread_rows(source, rank):
    count = source.shape[0]
    turned = pltpu.roll(source, HALF, 2)
    both = jnp.concatenate([source[:, None], turned[:, None]], axis=1)
    return both.reshape(count * 2 * rank, LANES).astype(BF16)


def group_at(group, m, groups, step):
    return pl.multiple_of(lax.rem(group[0] + (groups - m), groups) * step, step)


def first_couple(ops, rank, far, cols, group, held, *refs):
    parts, (out, zs) = refs[:-2], refs[-2:]
    step = SLICES * 2 * rank
    for m, part in enumerate(parts):
        at = group_at(group, m, len(parts), step)
        zs[pl.ds(at, step), :] = spread_rows(part[...].astype(F32), rank)
    for s in range(SLICES):
        c = [couple(cols, held, s, b, ops, rank, far, [zs]) for b in range(2)]
        out[s] = halves(c[0], c[1])[0].astype(BF16)


def take_coefs(cmsg, coef, rows):
    for pair in range(SLICES // 2):
        parts = halves(
            cmsg[2 * pair, 0:rows, :].astype(F32), cmsg[2 * pair + 1, 0:rows, :].astype(F32)
        )
        for b in range(2):
            coef[b, :, pair * LANES:(pair + 1) * LANES] = parts[b].astype(BF16)


def near_product(tiles, parts, b, blocks, size):
    total = None
    first = b - REACH
    at = 0
    for d, part in enumerate(parts):
        start = max((d - 1) * blocks, first)
        stop = min(d * blocks, first + 2 * REACH + 1)
        if stop <= start:
            continue
        begin = (start - (d - 1) * blocks) * size
        width = (stop - start) * size
        value = dot(tiles[:, at:at + width], part[begin:begin + width, :])
        total = value if total is None else total + value
        at += width
    return total


def diagonal_of(diag, o, b, size, columns):
    row = diag[o:o + 1, b * size:(b + 1) * size]
    column = jnp.transpose(jnp.broadcast_to(row, (LANES, size)))
    return jnp.concatenate([column] * (columns // LANES), axis=1)


def image_kernel(w, low, own, high, diag, left, right, cmsg, vout, mout, image, coef):
    ops = image.shape[0]
    blocks, rank, size = right.shape
    rows, columns = own.shape
    take_coefs(cmsg, coef, ops * rank)
    inner = [None] * ops
    squares = None
    for b in range(blocks):
        product = near_product(w.at[b], (low, own, high), b, blocks, size)
        ub = own[b * size:(b + 1) * size, :].astype(F32)
        part = jnp.sum(ub * ub, axis=0, keepdims=True)
        squares = part if squares is None else squares + part
        for o in range(ops):
            far = dot(left[b], coef[b, o * rank:(o + 1) * rank, :], ((0,), (0,)))
            value = (
                product[o * size:(o + 1) * size]
                + diagonal_of(diag, o, b, size, columns) * ub
                + far.astype(BF16).astype(F32)
            )
            image[o, b * size:(b + 1) * size, :] = value
            part = jnp.sum(ub * value, axis=0, keepdims=True)
            inner[o] = part if inner[o] is None else inner[o] + part
    stats = []
    spreads = []
    good = squares > 0
    for o in range(ops):
        shift = jnp.where(good, inner[o] / jnp.where(good, squares, 1.0), 0.0)
        pieces = split3(shift)
        stats += pieces
        shift = pieces[0].astype(F32) + pieces[1].astype(F32) + pieces[2].astype(F32)
        spread = None
        z = []
        for b in range(blocks):
            ub = own[b * size:(b + 1) * size, :].astype(F32)
            v = image[o, b * size:(b + 1) * size, :] - shift * ub
            part = jnp.sum(v * v, axis=0, keepdims=True)
            spread = part if spread is None else spread + part
            v = v.astype(BF16)
            vout[(o * blocks + b) * size:(o * blocks + b + 1) * size, :] = v
            z.append(dot(right[b], v))
        for pair in range(SLICES // 2):
            first, second = halves(chunk(z[0], pair), chunk(z[1], pair))
            mout[2 * pair, o * rank:(o + 1) * rank, :] = first.astype(BF16)
            mout[2 * pair + 1, o * rank:(o + 1) * rank, :] = second.astype(BF16)
        spreads.append(spread)
    zero = jnp.zeros((1, columns), BF16)
    vout[ops * rows:, :] = jnp.concatenate(stats + [zero] * (STATS - len(stats)), axis=0)
    stats += split3(squares)
    for spread in spreads:
        stats += split3(spread)
    stats = jnp.concatenate(stats + [zero] * (STATS - len(stats)), axis=0).astype(F32)
    for pair in range(SLICES // 2):
        part = chunk(stats, pair)
        first, second = halves(part, part)
        mout[2 * pair, ops * rank:ops * rank + STATS, :] = first.astype(BF16)
        mout[2 * pair + 1, ops * rank:ops * rank + STATS, :] = second.astype(BF16)


def second_couple(panels, ops, rank, far, cols, group, held, *refs):
    out, zs, st = refs[-3:]
    count = (len(refs) - 3) // 2
    z1, msgs = refs[:count], refs[count:2 * count]
    body = ops * rank
    step = SLICES * 2 * rank
    for m, msg in enumerate(msgs):
        at = group_at(group, m, count, SLICES)
        st[pl.ds(at, SLICES)] = msg[:, body:body + STATS, :].astype(F32)
    every = st[...]
    squares = join3(every, ops)
    scale_sq = jnp.sum(squares, axis=0, keepdims=True) / panels + EPSILON
    reverse = 1.0 / jnp.sqrt(scale_sq)
    heights, norms = [], []
    for o in range(ops):
        shift = join3(every, o)
        height = jnp.sum(shift * squares, axis=0, keepdims=True) / panels / scale_sq
        delta = shift - height
        spread = join3(every, ops + 1 + o) + delta * delta * squares
        norm = jnp.sqrt(jnp.sum(spread, axis=0, keepdims=True) / panels / scale_sq + EPSILON)
        heights.append(height)
        norms.append(norm)
    for m, (base, msg) in enumerate(zip(z1, msgs)):
        at = group_at(group, m, count, step)
        mine = msg[:, body:body + STATS, :].astype(F32)
        base = base[...].astype(F32)
        for o in range(ops):
            delta = join3(mine, o) - heights[o]
            z = msg[:, o * rank:(o + 1) * rank, :].astype(F32) + delta[:, None, :] * base
            z = z * (reverse / norms[o])[None]
            zs[o, pl.ds(at, step), :] = spread_rows(z, rank)
    rows = []
    for row in heights + norms + [reverse]:
        rows += split3(row)
    rows += [jnp.zeros_like(rows[0])] * (STATS - len(rows))
    rows = jnp.concatenate(rows, axis=0)
    for s in range(SLICES):
        c = [couple(cols, held, s, b, ops, rank, far, [zs.at[o] for o in range(ops)]) for b in range(2)]
        out[s, 0:body, :] = halves(c[0], c[1])[0].astype(BF16)
        out[s, body:body + STATS, :] = rows


def final_kernel(
    w, ulow, uown, uhigh, vlow, vown, vhigh, diag, left, cmsg, images, heights, norms, ext, coef, stat
):
    ops = images.shape[0]
    blocks, rank, size = left.shape
    rows, columns = uown.shape
    body = ops * rank
    take_coefs(cmsg, coef, body)
    for pair in range(SLICES // 2):
        stat[:, pair * LANES:(pair + 1) * LANES] = halves(
            cmsg[2 * pair, body:body + STATS, :].astype(F32),
            cmsg[2 * pair + 1, body:body + STATS, :].astype(F32),
        )[0]
    st = stat[...]
    reverse = row3(st, 2 * ops)
    for o in range(ops):
        height = row3(st, o)
        norm = row3(st, ops + o)
        heights[o:o + 1, :] = height
        norms[o:o + 1, :] = norm
        factor = reverse / norm
        for at, (u, v) in enumerate(((ulow, vlow), (uown, vown), (uhigh, vhigh))):
            shift = row3(v[ops * rows:, :].astype(F32), o)
            change = (shift - height) * factor
            value = v[o * rows:(o + 1) * rows, :].astype(F32) * factor + u[...].astype(F32) * change
            ext[o, at] = value.astype(BF16)
        for b in range(blocks):
            parts = [ext.at[o, at] for at in range(3)]
            product = near_product(w.at[b, o * size:(o + 1) * size], parts, b, blocks, size)
            far = dot(left[b], coef[b, o * rank:(o + 1) * rank, :], ((0,), (0,)))
            mine = ext[o, 1, b * size:(b + 1) * size, :].astype(F32)
            images[o, b * size:(b + 1) * size, :] = (
                product
                + diagonal_of(diag, o, b, size, columns) * mine
                + far.astype(BF16).astype(F32)
            )


def ring(block):
    count = lax.axis_size("store")
    forward = [(i, (i + 1) % count) for i in range(count)]
    backward = [(target, source) for source, target in forward]
    return lax.ppermute(block, "store", forward), lax.ppermute(block, "store", backward)


def shards(
    sources,
    self_terms,
    near_tiles,
    near_cols,
    near_count,
    far_cols,
    basis_left,
    basis_right,
    couplings,
):
    n = lax.axis_size("store")
    ops, blocks, near, size, _ = near_tiles.shape
    rank = basis_left.shape[2]
    far = far_cols.shape[1]
    rows, columns = sources.shape
    all_blocks = blocks * n
    count = n // SLICES
    groups = [[g * SLICES + s for s in range(SLICES)] for g in range(count)]
    sds = jax.ShapeDtypeStruct
    body = ops * rank

    def exchange(x):
        return lax.all_to_all(x, "store", 0, 0, axis_index_groups=groups, tiled=True)

    def across(x):
        parts = [x]
        for m in range(1, count):
            pairs = [(i, (i + m * SLICES) % n) for i in range(n)]
            parts.append(lax.ppermute(x, "store", pairs))
        return parts

    place = lax.axis_index("store").astype(jnp.int32)
    row0 = (place * blocks).reshape(1)
    group = lax.div(place, jnp.int32(SLICES)).reshape(1)
    left = jnp.transpose(basis_left, (0, 2, 1))
    right = jnp.transpose(basis_right, (0, 2, 1))

    shared = rank + (blocks + 1) * body
    held = call(
        share_kernel,
        sds((SLICES, shared + STATS, LANES), BF16),
        [SMEM, HBM, HBM, HBM],
        [
            pltpu.VMEM(sources.shape, BF16),
            pltpu.VMEM(right.shape, BF16),
            pltpu.VMEM(couplings.shape, BF16),
            pltpu.SemaphoreType.DMA((3,)),
        ],
    )(far_cols, sources, right, couplings)
    held = exchange(held)
    cols = held[:, shared, :blocks * far].astype(jnp.int32).reshape(-1)
    z1 = across(call(relay_kernel, sds((SLICES, rank, LANES), BF16), [VMEM])(held))
    own = sources
    low, high = ring(own)

    w = call(
        functools.partial(order_tiles, all_blocks),
        sds((blocks, ops * size, near * size), BF16),
        [SMEM, SMEM, SMEM, VMEM],
        micros=2.5,
    )(near_cols, near_count, row0, near_tiles)

    c1 = call(
        functools.partial(first_couple, ops, rank, far),
        sds((SLICES, body, LANES), BF16),
        [SMEM, SMEM] + [VMEM] * (1 + count),
        [pltpu.VMEM((n * blocks * rank, LANES), BF16)],
    )(cols, group, held, *z1)
    c1 = exchange(c1)

    v, msg = call(
        image_kernel,
        [sds((ops * rows + STATS, columns), BF16), sds((SLICES, body + STATS, LANES), BF16)],
        [VMEM] * 8,
        [
            pltpu.VMEM((ops, rows, columns), F32),
            pltpu.VMEM((blocks, body, columns), BF16),
        ],
        micros=4.0,
    )(w, low, own, high, self_terms, left, right, c1)
    msgs = across(exchange(msg))
    bulk = call(copy_kernel, sds(v.shape, BF16), [VMEM], micros=4.0)(v)
    vlow, vhigh = ring(bulk)

    c2 = call(
        functools.partial(second_couple, all_blocks * size, ops, rank, far),
        sds((SLICES, body + STATS, LANES), BF16),
        [SMEM, SMEM] + [VMEM] * (1 + 2 * count),
        [
            pltpu.VMEM((ops, n * blocks * rank, LANES), BF16),
            pltpu.VMEM((n, STATS, LANES), F32),
        ],
    )(cols, group, held, *z1, *msgs)
    c2 = exchange(c2)

    images, heights, norms = call(
        final_kernel,
        [sds((ops, rows, columns), F32), sds((ops, columns), F32), sds((ops, columns), F32)],
        [VMEM] * 10,
        [
            pltpu.VMEM((ops, 3, rows, columns), BF16),
            pltpu.VMEM((blocks, body, columns), BF16),
            pltpu.VMEM((STATS, columns), F32),
        ],
        micros=4.0,
    )(w, low, own, high, vlow, v, vhigh, self_terms, left, c2)
    return images, heights, norms


def solution(mesh):
    placed = (
        P(("groups", "store"), None),
        P(None, "store"),
        P(None, "store", None, None, None),
        P("store", None),
        P("store"),
        P("store", None),
        P("store", None, None),
        P("store", None, None),
        P(None, "store", None, None, None),
    )
    return jax.shard_map(
        shards,
        mesh=mesh,
        in_specs=placed,
        out_specs=(P(None, ("groups", "store"), None), P("groups", None), P("groups", None)),
        check_vma=False,
    )
```

```python
import functools

import jax
import jax.numpy as jnp
from jax import lax
from jax.experimental import pallas as pl
from jax.experimental.pallas import tpu as pltpu
from jax.sharding import PartitionSpec as P

REACH = 2
EPSILON = 1e-06
LANES = 128
HALF = 64
SLICES = 8
STATS = 16
HBM_RATE = 3690000
F32 = jnp.float32
BF16 = jnp.bfloat16

VMEM = pl.BlockSpec(memory_space=pltpu.VMEM)
SMEM = pl.BlockSpec(memory_space=pltpu.SMEM)


def call(body, out_shape, in_specs, scratch=(), micros=1.0, megabytes=20):
    many = isinstance(out_shape, (list, tuple))
    return pl.pallas_call(
        body,
        out_shape=out_shape,
        in_specs=in_specs,
        out_specs=[VMEM] * len(out_shape) if many else VMEM,
        scratch_shapes=list(scratch),
        compiler_params=pltpu.CompilerParams(vmem_limit_bytes=megabytes * 1024 * 1024),
        cost_estimate=pl.CostEstimate(
            flops=0, bytes_accessed=int(micros * HBM_RATE), transcendentals=0
        ),
    )


def dot(a, b, dims=((1,), (0,))):
    return lax.dot_general(a, b, (dims, ((), ())), preferred_element_type=F32)


def split3(row):
    high = row.astype(BF16)
    rest = row - high.astype(F32)
    middle = rest.astype(BF16)
    low = (rest - middle.astype(F32)).astype(BF16)
    return [high, middle, low]


def join3(rows, at):
    return rows[..., 3 * at, :] + rows[..., 3 * at + 1, :] + rows[..., 3 * at + 2, :]


def row3(values, at):
    return values[3 * at:3 * at + 1] + values[3 * at + 1:3 * at + 2] + values[3 * at + 2:3 * at + 3]


def halves(x, y):
    left = lax.broadcasted_iota(jnp.int32, x.shape, x.ndim - 1) < HALF
    first = jnp.where(left, x, pltpu.roll(y, HALF, x.ndim - 1))
    second = jnp.where(left, pltpu.roll(x, HALF, x.ndim - 1), y)
    return first, second


def chunk(x, pair):
    return x[:, pair * LANES:(pair + 1) * LANES]


def order_tiles(all_blocks, cols, count, row0, tiles, out):
    ops, blocks, near, size, _ = tiles.shape
    for b in range(blocks):
        for k in range(near):
            rel = lax.rem(cols[b, k] - (row0[0] + b) + REACH + all_blocks, all_blocks)
            rel = lax.rem(rel, all_blocks)
            at = pl.multiple_of(rel * size, size)
            live = k < count[b]
            for o in range(ops):
                tile = tiles[o, b, k]
                out[b, o * size:(o + 1) * size, pl.ds(at, size)] = jnp.where(
                    live, tile, jnp.zeros_like(tile)
                )


def share_kernel(far_cols, u, right, coup, out):
    ops, blocks, far, rank, _ = coup.shape
    size = right.shape[2]
    z = [dot(right[b], u[b * size:(b + 1) * size, :]) for b in range(blocks)]
    for pair in range(SLICES // 2):
        first, second = halves(chunk(z[0], pair), chunk(z[1], pair))
        out[2 * pair, 0:rank, :] = first.astype(BF16)
        out[2 * pair + 1, 0:rank, :] = second.astype(BF16)
    whole, rest = [], []
    for b in range(blocks):
        tiles = [
            jnp.concatenate([coup[o, b, f] for f in range(far)], axis=1) for o in range(ops)
        ]
        tiles = jnp.concatenate(tiles, axis=0)
        whole.append(tiles[:, :LANES])
        rest.append(tiles[:, LANES:])
    lane = lax.broadcasted_iota(jnp.int32, (STATS, LANES), 1)
    names = jnp.zeros((STATS, LANES), F32)
    for b in range(blocks):
        for f in range(far):
            names = jnp.where(lane == b * far + f, far_cols[b, f].astype(F32), names)
    whole = jnp.concatenate(
        whole + [jnp.concatenate(rest, axis=1), names.astype(BF16)], axis=0
    )
    for s in range(SLICES):
        out[s, rank:, :] = whole


def relay_kernel(first, z):
    z[...] = first[:, 0:z.shape[1], :]


def copy_kernel(source, target):
    target[...] = source[...]


def coupling_rows(held, s, b, ops, rank):
    body = ops * rank
    first = held[s, rank + b * body:rank + (b + 1) * body, :]
    rest = held[s, rank + 2 * body:rank + 3 * body, b * HALF:(b + 1) * HALF]
    return jnp.concatenate([first, rest], axis=1)


def couple(cols, held, s, b, ops, rank, far, z):
    at = (s * 2 + b) * far
    lhs = coupling_rows(held, s, b, ops, rank)
    starts = [pl.multiple_of(cols[at + f] * rank, rank) for f in range(far)]
    picked = [
        jnp.concatenate([x[pl.ds(start, rank), :] for start in starts], axis=0) for x in z
    ]
    if len(z) == 1:
        return dot(lhs, picked[0])
    return jnp.concatenate(
        [dot(lhs[o * rank:(o + 1) * rank], picked[o]) for o in range(ops)], axis=0
    )


def spread_rows(source, rank):
    count = source.shape[0]
    turned = pltpu.roll(source, HALF, 2)
    both = jnp.concatenate([source[:, None], turned[:, None]], axis=1)
    return both.reshape(count * 2 * rank, LANES).astype(BF16)


def group_at(group, m, groups, step):
    return pl.multiple_of(lax.rem(group[0] + (groups - m), groups) * step, step)


def first_couple(ops, rank, far, cols, group, held, *refs):
    parts, (out, zs) = refs[:-2], refs[-2:]
    step = SLICES * 2 * rank
    for m, part in enumerate(parts):
        at = group_at(group, m, len(parts), step)
        zs[pl.ds(at, step), :] = spread_rows(part[...].astype(F32), rank)
    for s in range(SLICES):
        c = [couple(cols, held, s, b, ops, rank, far, [zs]) for b in range(2)]
        out[s] = halves(c[0], c[1])[0].astype(BF16)


def take_coefs(cmsg, coef, rows):
    for pair in range(SLICES // 2):
        parts = halves(
            cmsg[2 * pair, 0:rows, :].astype(F32), cmsg[2 * pair + 1, 0:rows, :].astype(F32)
        )
        for b in range(2):
            coef[b, :, pair * LANES:(pair + 1) * LANES] = parts[b].astype(BF16)


def near_product(tiles, parts, b, blocks, size):
    total = None
    first = b - REACH
    at = 0
    for d, part in enumerate(parts):
        start = max((d - 1) * blocks, first)
        stop = min(d * blocks, first + 2 * REACH + 1)
        if stop <= start:
            continue
        begin = (start - (d - 1) * blocks) * size
        width = (stop - start) * size
        value = dot(tiles[:, at:at + width], part[begin:begin + width, :])
        total = value if total is None else total + value
        at += width
    return total


def diagonal_of(diag, o, b, size, columns):
    row = diag[o:o + 1, b * size:(b + 1) * size]
    column = jnp.transpose(jnp.broadcast_to(row, (LANES, size)))
    return jnp.concatenate([column] * (columns // LANES), axis=1)


def image_kernel(w, low, own, high, diag, left, right, cmsg, vout, mout, image, coef):
    ops = image.shape[0]
    blocks, rank, size = right.shape
    rows, columns = own.shape
    take_coefs(cmsg, coef, ops * rank)
    inner = [None] * ops
    squares = None
    for b in range(blocks):
        product = near_product(w.at[b], (low, own, high), b, blocks, size)
        ub = own[b * size:(b + 1) * size, :].astype(F32)
        part = jnp.sum(ub * ub, axis=0, keepdims=True)
        squares = part if squares is None else squares + part
        for o in range(ops):
            far = dot(left[b], coef[b, o * rank:(o + 1) * rank, :], ((0,), (0,)))
            value = (
                product[o * size:(o + 1) * size]
                + diagonal_of(diag, o, b, size, columns) * ub
                + far.astype(BF16).astype(F32)
            )
            image[o, b * size:(b + 1) * size, :] = value
            part = jnp.sum(ub * value, axis=0, keepdims=True)
            inner[o] = part if inner[o] is None else inner[o] + part
    stats = []
    spreads = []
    good = squares > 0
    for o in range(ops):
        shift = jnp.where(good, inner[o] / jnp.where(good, squares, 1.0), 0.0)
        pieces = split3(shift)
        stats += pieces
        shift = pieces[0].astype(F32) + pieces[1].astype(F32) + pieces[2].astype(F32)
        spread = None
        z = []
        for b in range(blocks):
            ub = own[b * size:(b + 1) * size, :].astype(F32)
            v = image[o, b * size:(b + 1) * size, :] - shift * ub
            part = jnp.sum(v * v, axis=0, keepdims=True)
            spread = part if spread is None else spread + part
            v = v.astype(BF16)
            vout[(o * blocks + b) * size:(o * blocks + b + 1) * size, :] = v
            z.append(dot(right[b], v))
        for pair in range(SLICES // 2):
            first, second = halves(chunk(z[0], pair), chunk(z[1], pair))
            mout[2 * pair, o * rank:(o + 1) * rank, :] = first.astype(BF16)
            mout[2 * pair + 1, o * rank:(o + 1) * rank, :] = second.astype(BF16)
        spreads.append(spread)
    zero = jnp.zeros((1, columns), BF16)
    vout[ops * rows:, :] = jnp.concatenate(stats + [zero] * (STATS - len(stats)), axis=0)
    stats += split3(squares)
    for spread in spreads:
        stats += split3(spread)
    stats = jnp.concatenate(stats + [zero] * (STATS - len(stats)), axis=0).astype(F32)
    for pair in range(SLICES // 2):
        part = chunk(stats, pair)
        first, second = halves(part, part)
        mout[2 * pair, ops * rank:ops * rank + STATS, :] = first.astype(BF16)
        mout[2 * pair + 1, ops * rank:ops * rank + STATS, :] = second.astype(BF16)


def second_couple(panels, ops, rank, far, cols, group, held, *refs):
    out, zs, st = refs[-3:]
    count = (len(refs) - 3) // 2
    z1, msgs = refs[:count], refs[count:2 * count]
    body = ops * rank
    step = SLICES * 2 * rank
    for m, msg in enumerate(msgs):
        at = group_at(group, m, count, SLICES)
        st[pl.ds(at, SLICES)] = msg[:, body:body + STATS, :].astype(F32)
    every = st[...]
    squares = join3(every, ops)
    scale_sq = jnp.sum(squares, axis=0, keepdims=True) / panels + EPSILON
    reverse = 1.0 / jnp.sqrt(scale_sq)
    heights, norms = [], []
    for o in range(ops):
        shift = join3(every, o)
        height = jnp.sum(shift * squares, axis=0, keepdims=True) / panels / scale_sq
        delta = shift - height
        spread = join3(every, ops + 1 + o) + delta * delta * squares
        norm = jnp.sqrt(jnp.sum(spread, axis=0, keepdims=True) / panels / scale_sq + EPSILON)
        heights.append(height)
        norms.append(norm)
    for m, (base, msg) in enumerate(zip(z1, msgs)):
        at = group_at(group, m, count, step)
        mine = msg[:, body:body + STATS, :].astype(F32)
        base = base[...].astype(F32)
        for o in range(ops):
            delta = join3(mine, o) - heights[o]
            z = msg[:, o * rank:(o + 1) * rank, :].astype(F32) + delta[:, None, :] * base
            z = z * (reverse / norms[o])[None]
            zs[o, pl.ds(at, step), :] = spread_rows(z, rank)
    rows = []
    for row in heights + norms + [reverse]:
        rows += split3(row)
    rows += [jnp.zeros_like(rows[0])] * (STATS - len(rows))
    rows = jnp.concatenate(rows, axis=0)
    for s in range(SLICES):
        c = [couple(cols, held, s, b, ops, rank, far, [zs.at[o] for o in range(ops)]) for b in range(2)]
        out[s, 0:body, :] = halves(c[0], c[1])[0].astype(BF16)
        out[s, body:body + STATS, :] = rows


def final_kernel(
    w, ulow, uown, uhigh, vlow, vown, vhigh, diag, left, cmsg, images, heights, norms, ext, coef, stat
):
    ops = images.shape[0]
    blocks, rank, size = left.shape
    rows, columns = uown.shape
    body = ops * rank
    take_coefs(cmsg, coef, body)
    for pair in range(SLICES // 2):
        stat[:, pair * LANES:(pair + 1) * LANES] = halves(
            cmsg[2 * pair, body:body + STATS, :].astype(F32),
            cmsg[2 * pair + 1, body:body + STATS, :].astype(F32),
        )[0]
    st = stat[...]
    reverse = row3(st, 2 * ops)
    for o in range(ops):
        height = row3(st, o)
        norm = row3(st, ops + o)
        heights[o:o + 1, :] = height
        norms[o:o + 1, :] = norm
        factor = reverse / norm
        for at, (u, v) in enumerate(((ulow, vlow), (uown, vown), (uhigh, vhigh))):
            shift = row3(v[ops * rows:, :].astype(F32), o)
            change = (shift - height) * factor
            value = v[o * rows:(o + 1) * rows, :].astype(F32) * factor + u[...].astype(F32) * change
            ext[o, at] = value.astype(BF16)
        for b in range(blocks):
            parts = [ext.at[o, at] for at in range(3)]
            product = near_product(w.at[b, o * size:(o + 1) * size], parts, b, blocks, size)
            far = dot(left[b], coef[b, o * rank:(o + 1) * rank, :], ((0,), (0,)))
            mine = ext[o, 1, b * size:(b + 1) * size, :].astype(F32)
            images[o, b * size:(b + 1) * size, :] = (
                product
                + diagonal_of(diag, o, b, size, columns) * mine
                + far.astype(BF16).astype(F32)
            )


def ring(block):
    count = lax.axis_size("store")
    forward = [(i, (i + 1) % count) for i in range(count)]
    backward = [(target, source) for source, target in forward]
    return lax.ppermute(block, "store", forward), lax.ppermute(block, "store", backward)


def shards(
    sources,
    self_terms,
    near_tiles,
    near_cols,
    near_count,
    far_cols,
    basis_left,
    basis_right,
    couplings,
):
    n = lax.axis_size("store")
    ops, blocks, near, size, _ = near_tiles.shape
    rank = basis_left.shape[2]
    far = far_cols.shape[1]
    rows, columns = sources.shape
    all_blocks = blocks * n
    count = n // SLICES
    groups = [[g * SLICES + s for s in range(SLICES)] for g in range(count)]
    sds = jax.ShapeDtypeStruct
    body = ops * rank

    def exchange(x):
        return lax.all_to_all(x, "store", 0, 0, axis_index_groups=groups, tiled=True)

    def across(x):
        parts = [x]
        for m in range(1, count):
            pairs = [(i, (i + m * SLICES) % n) for i in range(n)]
            parts.append(lax.ppermute(x, "store", pairs))
        return parts

    place = lax.axis_index("store").astype(jnp.int32)
    row0 = (place * blocks).reshape(1)
    group = lax.div(place, jnp.int32(SLICES)).reshape(1)
    left = jnp.transpose(basis_left, (0, 2, 1))
    right = jnp.transpose(basis_right, (0, 2, 1))

    shared = rank + (blocks + 1) * body
    held = call(
        share_kernel,
        sds((SLICES, shared + STATS, LANES), BF16),
        [SMEM, VMEM, VMEM, VMEM],
        megabytes=60,
    )(far_cols, sources, right, couplings)
    held = exchange(held)
    cols = held[:, shared, :blocks * far].astype(jnp.int32).reshape(-1)
    z1 = across(call(relay_kernel, sds((SLICES, rank, LANES), BF16), [VMEM])(held))
    own = sources
    low, high = ring(own)

    w = call(
        functools.partial(order_tiles, all_blocks),
        sds((blocks, ops * size, near * size), BF16),
        [SMEM, SMEM, SMEM, VMEM],
        micros=2.5,
    )(near_cols, near_count, row0, near_tiles)

    c1 = call(
        functools.partial(first_couple, ops, rank, far),
        sds((SLICES, body, LANES), BF16),
        [SMEM, SMEM] + [VMEM] * (1 + count),
        [pltpu.VMEM((n * blocks * rank, LANES), BF16)],
    )(cols, group, held, *z1)
    c1 = exchange(c1)

    v, msg = call(
        image_kernel,
        [sds((ops * rows + STATS, columns), BF16), sds((SLICES, body + STATS, LANES), BF16)],
        [VMEM] * 8,
        [
            pltpu.VMEM((ops, rows, columns), F32),
            pltpu.VMEM((blocks, body, columns), BF16),
        ],
        micros=4.0,
    )(w, low, own, high, self_terms, left, right, c1)
    msg = exchange(msg)
    msgs = across(call(copy_kernel, sds(msg.shape, BF16), [VMEM], micros=40.0)(msg))
    vlow, vhigh = ring(v)

    c2 = call(
        functools.partial(second_couple, all_blocks * size, ops, rank, far),
        sds((SLICES, body + STATS, LANES), BF16),
        [SMEM, SMEM] + [VMEM] * (1 + 2 * count),
        [
            pltpu.VMEM((ops, n * blocks * rank, LANES), BF16),
            pltpu.VMEM((n, STATS, LANES), F32),
        ],
    )(cols, group, held, *z1, *msgs)
    c2 = exchange(c2)

    images, heights, norms = call(
        final_kernel,
        [sds((ops, rows, columns), F32), sds((ops, columns), F32), sds((ops, columns), F32)],
        [VMEM] * 10,
        [
            pltpu.VMEM((ops, 3, rows, columns), BF16),
            pltpu.VMEM((blocks, body, columns), BF16),
            pltpu.VMEM((STATS, columns), F32),
        ],
        micros=4.0,
    )(w, low, own, high, vlow, v, vhigh, self_terms, left, c2)
    return images, heights, norms


def solution(mesh):
    placed = (
        P(("groups", "store"), None),
        P(None, "store"),
        P(None, "store", None, None, None),
        P("store", None),
        P("store"),
        P("store", None),
        P("store", None, None),
        P("store", None, None),
        P(None, "store", None, None, None),
    )
    return jax.shard_map(
        shards,
        mesh=mesh,
        in_specs=placed,
        out_specs=(P(None, ("groups", "store"), None), P("groups", None), P("groups", None)),
        check_vma=False,
    )
```

```python
import functools

import jax
import jax.numpy as jnp
from jax import lax
from jax.experimental import pallas as pl
from jax.experimental.pallas import tpu as pltpu
from jax.sharding import PartitionSpec as P

REACH = 2
EPSILON = 1e-06
LANES = 128
HALF = 64
SLICES = 8
STATS = 16
HBM_RATE = 3690000
F32 = jnp.float32
BF16 = jnp.bfloat16

VMEM = pl.BlockSpec(memory_space=pltpu.VMEM)
SMEM = pl.BlockSpec(memory_space=pltpu.SMEM)


def call(body, out_shape, in_specs, scratch=(), micros=1.0, megabytes=20):
    many = isinstance(out_shape, (list, tuple))
    return pl.pallas_call(
        body,
        out_shape=out_shape,
        in_specs=in_specs,
        out_specs=[VMEM] * len(out_shape) if many else VMEM,
        scratch_shapes=list(scratch),
        compiler_params=pltpu.CompilerParams(vmem_limit_bytes=megabytes * 1024 * 1024),
        cost_estimate=pl.CostEstimate(
            flops=0, bytes_accessed=int(micros * HBM_RATE), transcendentals=0
        ),
    )


def dot(a, b, dims=((1,), (0,))):
    return lax.dot_general(a, b, (dims, ((), ())), preferred_element_type=F32)


def split3(row):
    high = row.astype(BF16)
    rest = row - high.astype(F32)
    middle = rest.astype(BF16)
    low = (rest - middle.astype(F32)).astype(BF16)
    return [high, middle, low]


def join3(rows, at):
    return rows[..., 3 * at, :] + rows[..., 3 * at + 1, :] + rows[..., 3 * at + 2, :]


def row3(values, at):
    return values[3 * at:3 * at + 1] + values[3 * at + 1:3 * at + 2] + values[3 * at + 2:3 * at + 3]


def halves(x, y):
    left = lax.broadcasted_iota(jnp.int32, x.shape, x.ndim - 1) < HALF
    first = jnp.where(left, x, pltpu.roll(y, HALF, x.ndim - 1))
    second = jnp.where(left, pltpu.roll(x, HALF, x.ndim - 1), y)
    return first, second


def chunk(x, pair):
    return x[:, pair * LANES:(pair + 1) * LANES]


def order_tiles(all_blocks, cols, count, row0, tiles, out):
    ops, blocks, near, size, _ = tiles.shape
    for b in range(blocks):
        for k in range(near):
            rel = lax.rem(cols[b, k] - (row0[0] + b) + REACH + all_blocks, all_blocks)
            rel = lax.rem(rel, all_blocks)
            at = pl.multiple_of(rel * size, size)
            live = k < count[b]
            for o in range(ops):
                tile = tiles[o, b, k]
                out[b, o * size:(o + 1) * size, pl.ds(at, size)] = jnp.where(
                    live, tile, jnp.zeros_like(tile)
                )


def coeff_kernel(u, right, out):
    blocks, rank, size = right.shape
    z = [dot(right[b], u[b * size:(b + 1) * size, :]) for b in range(blocks)]
    for pair in range(SLICES // 2):
        first, second = halves(chunk(z[0], pair), chunk(z[1], pair))
        out[2 * pair] = first.astype(BF16)
        out[2 * pair + 1] = second.astype(BF16)


def pack_kernel(far_cols, coup, out):
    ops, blocks, far, rank, _ = coup.shape
    whole, rest = [], []
    for b in range(blocks):
        tiles = [
            jnp.concatenate([coup[o, b, f] for f in range(far)], axis=1) for o in range(ops)
        ]
        tiles = jnp.concatenate(tiles, axis=0)
        whole.append(tiles[:, :LANES])
        rest.append(tiles[:, LANES:])
    lane = lax.broadcasted_iota(jnp.int32, (STATS, LANES), 1)
    names = jnp.zeros((STATS, LANES), F32)
    for b in range(blocks):
        for f in range(far):
            names = jnp.where(lane == b * far + f, far_cols[b, f].astype(F32), names)
    out[...] = jnp.concatenate(
        whole + [jnp.concatenate(rest, axis=1), names.astype(BF16)], axis=0
    )


def share_kernel(packed, *refs):
    parts, out = refs[:-1], refs[-1]
    rows = packed.shape[0]
    rank = parts[0].shape[1]
    for s in range(SLICES):
        out[s, 0:rows, :] = packed[...]
    for m, part in enumerate(parts):
        out[:, rows + m * rank:rows + (m + 1) * rank, :] = part[...]


def copy_kernel(source, after, target):
    target[...] = source[...]


def coupling_rows(held, s, b, ops, rank):
    body = ops * rank
    first = held[s, b * body:(b + 1) * body, :]
    rest = held[s, 2 * body:3 * body, b * HALF:(b + 1) * HALF]
    return jnp.concatenate([first, rest], axis=1)


def couple(cols, held, s, b, ops, rank, far, z):
    at = (s * 2 + b) * far
    lhs = coupling_rows(held, s, b, ops, rank)
    starts = [pl.multiple_of(cols[at + f] * rank, rank) for f in range(far)]
    picked = [
        jnp.concatenate([x[pl.ds(start, rank), :] for start in starts], axis=0) for x in z
    ]
    if len(z) == 1:
        return dot(lhs, picked[0])
    return jnp.concatenate(
        [dot(lhs[o * rank:(o + 1) * rank], picked[o]) for o in range(ops)], axis=0
    )


def spread_rows(source, rank):
    count = source.shape[0]
    turned = pltpu.roll(source, HALF, 2)
    both = jnp.concatenate([source[:, None], turned[:, None]], axis=1)
    return both.reshape(count * 2 * rank, LANES).astype(BF16)


def held_part(held, m, ops, rank):
    at = 3 * ops * rank + STATS + m * rank
    return held[:, at:at + rank, :].astype(F32)


def group_at(group, m, groups, step):
    return pl.multiple_of(lax.rem(group[0] + (groups - m), groups) * step, step)


def first_couple(ops, rank, far, cols, group, held, out, zs):
    step = SLICES * 2 * rank
    count = zs.shape[0] // step
    for m in range(count):
        at = group_at(group, m, count, step)
        zs[pl.ds(at, step), :] = spread_rows(held_part(held, m, ops, rank), rank)
    for s in range(SLICES):
        c = [couple(cols, held, s, b, ops, rank, far, [zs]) for b in range(2)]
        out[s] = halves(c[0], c[1])[0].astype(BF16)


def take_coefs(cmsg, coef, rows):
    for pair in range(SLICES // 2):
        parts = halves(
            cmsg[2 * pair, 0:rows, :].astype(F32), cmsg[2 * pair + 1, 0:rows, :].astype(F32)
        )
        for b in range(2):
            coef[b, :, pair * LANES:(pair + 1) * LANES] = parts[b].astype(BF16)


def near_product(tiles, parts, b, blocks, size):
    total = None
    first = b - REACH
    at = 0
    for d, part in enumerate(parts):
        start = max((d - 1) * blocks, first)
        stop = min(d * blocks, first + 2 * REACH + 1)
        if stop <= start:
            continue
        begin = (start - (d - 1) * blocks) * size
        width = (stop - start) * size
        value = dot(tiles[:, at:at + width], part[begin:begin + width, :])
        total = value if total is None else total + value
        at += width
    return total


def diagonal_of(diag, o, b, size, columns):
    row = diag[o:o + 1, b * size:(b + 1) * size]
    column = jnp.transpose(jnp.broadcast_to(row, (LANES, size)))
    return jnp.concatenate([column] * (columns // LANES), axis=1)


def image_kernel(w, low, own, high, diag, left, right, cmsg, vout, mout, image, coef):
    ops = image.shape[0]
    blocks, rank, size = right.shape
    rows, columns = own.shape
    take_coefs(cmsg, coef, ops * rank)
    inner = [None] * ops
    squares = None
    for b in range(blocks):
        product = near_product(w.at[b], (low, own, high), b, blocks, size)
        ub = own[b * size:(b + 1) * size, :].astype(F32)
        part = jnp.sum(ub * ub, axis=0, keepdims=True)
        squares = part if squares is None else squares + part
        for o in range(ops):
            far = dot(left[b], coef[b, o * rank:(o + 1) * rank, :], ((0,), (0,)))
            value = (
                product[o * size:(o + 1) * size]
                + diagonal_of(diag, o, b, size, columns) * ub
                + far.astype(BF16).astype(F32)
            )
            image[o, b * size:(b + 1) * size, :] = value
            part = jnp.sum(ub * value, axis=0, keepdims=True)
            inner[o] = part if inner[o] is None else inner[o] + part
    stats = []
    spreads = []
    good = squares > 0
    for o in range(ops):
        shift = jnp.where(good, inner[o] / jnp.where(good, squares, 1.0), 0.0)
        pieces = split3(shift)
        stats += pieces
        shift = pieces[0].astype(F32) + pieces[1].astype(F32) + pieces[2].astype(F32)
        spread = None
        z = []
        for b in range(blocks):
            ub = own[b * size:(b + 1) * size, :].astype(F32)
            v = image[o, b * size:(b + 1) * size, :] - shift * ub
            part = jnp.sum(v * v, axis=0, keepdims=True)
            spread = part if spread is None else spread + part
            v = v.astype(BF16)
            vout[(o * blocks + b) * size:(o * blocks + b + 1) * size, :] = v
            z.append(dot(right[b], v))
        for pair in range(SLICES // 2):
            first, second = halves(chunk(z[0], pair), chunk(z[1], pair))
            mout[2 * pair, o * rank:(o + 1) * rank, :] = first.astype(BF16)
            mout[2 * pair + 1, o * rank:(o + 1) * rank, :] = second.astype(BF16)
        spreads.append(spread)
    zero = jnp.zeros((1, columns), BF16)
    vout[ops * rows:, :] = jnp.concatenate(stats + [zero] * (STATS - len(stats)), axis=0)
    stats += split3(squares)
    for spread in spreads:
        stats += split3(spread)
    stats = jnp.concatenate(stats + [zero] * (STATS - len(stats)), axis=0).astype(F32)
    for pair in range(SLICES // 2):
        part = chunk(stats, pair)
        first, second = halves(part, part)
        mout[2 * pair, ops * rank:ops * rank + STATS, :] = first.astype(BF16)
        mout[2 * pair + 1, ops * rank:ops * rank + STATS, :] = second.astype(BF16)


def second_couple(panels, ops, rank, far, cols, group, held, *refs):
    msgs, (out, zs, st) = refs[:-3], refs[-3:]
    count = len(msgs)
    body = ops * rank
    step = SLICES * 2 * rank
    for m, msg in enumerate(msgs):
        at = group_at(group, m, count, SLICES)
        st[pl.ds(at, SLICES)] = msg[:, body:body + STATS, :].astype(F32)
    every = st[...]
    squares = join3(every, ops)
    scale_sq = jnp.sum(squares, axis=0, keepdims=True) / panels + EPSILON
    reverse = 1.0 / jnp.sqrt(scale_sq)
    heights, norms = [], []
    for o in range(ops):
        shift = join3(every, o)
        height = jnp.sum(shift * squares, axis=0, keepdims=True) / panels / scale_sq
        delta = shift - height
        spread = join3(every, ops + 1 + o) + delta * delta * squares
        norm = jnp.sqrt(jnp.sum(spread, axis=0, keepdims=True) / panels / scale_sq + EPSILON)
        heights.append(height)
        norms.append(norm)
    for m, msg in enumerate(msgs):
        at = group_at(group, m, count, step)
        mine = msg[:, body:body + STATS, :].astype(F32)
        base = held_part(held, m, ops, rank)
        for o in range(ops):
            delta = join3(mine, o) - heights[o]
            z = msg[:, o * rank:(o + 1) * rank, :].astype(F32) + delta[:, None, :] * base
            z = z * (reverse / norms[o])[None]
            zs[o, pl.ds(at, step), :] = spread_rows(z, rank)
    rows = []
    for row in heights + norms + [reverse]:
        rows += split3(row)
    rows += [jnp.zeros_like(rows[0])] * (STATS - len(rows))
    rows = jnp.concatenate(rows, axis=0)
    for s in range(SLICES):
        c = [couple(cols, held, s, b, ops, rank, far, [zs.at[o] for o in range(ops)]) for b in range(2)]
        out[s, 0:body, :] = halves(c[0], c[1])[0].astype(BF16)
        out[s, body:body + STATS, :] = rows


def final_kernel(
    w, ulow, uown, uhigh, vlow, vown, vhigh, diag, left, cmsg, images, heights, norms, ext, coef, stat
):
    ops = images.shape[0]
    blocks, rank, size = left.shape
    rows, columns = uown.shape
    body = ops * rank
    take_coefs(cmsg, coef, body)
    for pair in range(SLICES // 2):
        stat[:, pair * LANES:(pair + 1) * LANES] = halves(
            cmsg[2 * pair, body:body + STATS, :].astype(F32),
            cmsg[2 * pair + 1, body:body + STATS, :].astype(F32),
        )[0]
    st = stat[...]
    reverse = row3(st, 2 * ops)
    for o in range(ops):
        height = row3(st, o)
        norm = row3(st, ops + o)
        heights[o:o + 1, :] = height
        norms[o:o + 1, :] = norm
        factor = reverse / norm
        for at, (u, v) in enumerate(((ulow, vlow), (uown, vown), (uhigh, vhigh))):
            shift = row3(v[ops * rows:, :].astype(F32), o)
            change = (shift - height) * factor
            value = v[o * rows:(o + 1) * rows, :].astype(F32) * factor + u[...].astype(F32) * change
            ext[o, at] = value.astype(BF16)
        for b in range(blocks):
            parts = [ext.at[o, at] for at in range(3)]
            product = near_product(w.at[b, o * size:(o + 1) * size], parts, b, blocks, size)
            far = dot(left[b], coef[b, o * rank:(o + 1) * rank, :], ((0,), (0,)))
            mine = ext[o, 1, b * size:(b + 1) * size, :].astype(F32)
            images[o, b * size:(b + 1) * size, :] = (
                product
                + diagonal_of(diag, o, b, size, columns) * mine
                + far.astype(BF16).astype(F32)
            )


def ring(block):
    count = lax.axis_size("store")
    forward = [(i, (i + 1) % count) for i in range(count)]
    backward = [(target, source) for source, target in forward]
    return lax.ppermute(block, "store", forward), lax.ppermute(block, "store", backward)


def shards(
    sources,
    self_terms,
    near_tiles,
    near_cols,
    near_count,
    far_cols,
    basis_left,
    basis_right,
    couplings,
):
    n = lax.axis_size("store")
    ops, blocks, near, size, _ = near_tiles.shape
    rank = basis_left.shape[2]
    far = far_cols.shape[1]
    rows, columns = sources.shape
    all_blocks = blocks * n
    count = n // SLICES
    groups = [[g * SLICES + s for s in range(SLICES)] for g in range(count)]
    sds = jax.ShapeDtypeStruct
    body = ops * rank

    def exchange(x):
        return lax.all_to_all(x, "store", 0, 0, axis_index_groups=groups, tiled=True)

    def across(x):
        parts = [x]
        for m in range(1, count):
            pairs = [(i, (i + m * SLICES) % n) for i in range(n)]
            parts.append(lax.ppermute(x, "store", pairs))
        return parts

    place = lax.axis_index("store").astype(jnp.int32)
    row0 = (place * blocks).reshape(1)
    group = lax.div(place, jnp.int32(SLICES)).reshape(1)
    left = jnp.transpose(basis_left, (0, 2, 1))
    right = jnp.transpose(basis_right, (0, 2, 1))

    low, high = ring(sources)
    z1 = call(coeff_kernel, sds((SLICES, rank, LANES), BF16), [VMEM, VMEM], megabytes=60)(
        sources, right
    )
    z1 = across(z1)
    shared = (blocks + 1) * body
    packed = call(pack_kernel, sds((shared + STATS, LANES), BF16), [SMEM, VMEM])(
        far_cols, couplings
    )
    held = call(
        share_kernel,
        sds((SLICES, shared + STATS + count * rank, LANES), BF16),
        [VMEM] * (1 + count),
    )(packed, *z1)
    held = exchange(held)
    cols = held[:, shared, :blocks * far].astype(jnp.int32).reshape(-1)

    w = call(
        functools.partial(order_tiles, all_blocks),
        sds((blocks, ops * size, near * size), BF16),
        [SMEM, SMEM, SMEM, VMEM],
        micros=2.5,
    )(near_cols, near_count, row0, near_tiles)

    c1 = call(
        functools.partial(first_couple, ops, rank, far),
        sds((SLICES, body, LANES), BF16),
        [SMEM, SMEM, VMEM],
        [pltpu.VMEM((n * blocks * rank, LANES), BF16)],
    )(cols, group, held)
    c1 = exchange(c1)

    v, msg = call(
        image_kernel,
        [sds((ops * rows + STATS, columns), BF16), sds((SLICES, body + STATS, LANES), BF16)],
        [VMEM] * 8,
        [
            pltpu.VMEM((ops, rows, columns), F32),
            pltpu.VMEM((blocks, body, columns), BF16),
        ],
        micros=4.0,
    )(w, low, sources, high, self_terms, left, right, c1)
    msg = exchange(msg)
    msgs = across(msg)
    bulk = call(
        copy_kernel, sds(v.shape, BF16), [VMEM, pl.BlockSpec(memory_space=pl.ANY)], micros=8.0
    )(v, msg)
    vlow, vhigh = ring(bulk)

    c2 = call(
        functools.partial(second_couple, all_blocks * size, ops, rank, far),
        sds((SLICES, body + STATS, LANES), BF16),
        [SMEM, SMEM] + [VMEM] * (1 + count),
        [
            pltpu.VMEM((ops, n * blocks * rank, LANES), BF16),
            pltpu.VMEM((n, STATS, LANES), F32),
        ],
    )(cols, group, held, *msgs)
    c2 = exchange(c2)

    images, heights, norms = call(
        final_kernel,
        [sds((ops, rows, columns), F32), sds((ops, columns), F32), sds((ops, columns), F32)],
        [VMEM] * 10,
        [
            pltpu.VMEM((ops, 3, rows, columns), BF16),
            pltpu.VMEM((blocks, body, columns), BF16),
            pltpu.VMEM((STATS, columns), F32),
        ],
        micros=4.0,
    )(w, low, sources, high, vlow, v, vhigh, self_terms, left, c2)
    return images, heights, norms


def solution(mesh):
    placed = (
        P(("groups", "store"), None),
        P(None, "store"),
        P(None, "store", None, None, None),
        P("store", None),
        P("store"),
        P("store", None),
        P("store", None, None),
        P("store", None, None),
        P(None, "store", None, None, None),
    )
    return jax.shard_map(
        shards,
        mesh=mesh,
        in_specs=placed,
        out_specs=(P(None, ("groups", "store"), None), P("groups", None), P("groups", None)),
        check_vma=False,
    )
```

```python
import functools

import jax
import jax.numpy as jnp
from jax import lax
from jax.experimental import pallas as pl
from jax.experimental.pallas import tpu as pltpu
from jax.sharding import PartitionSpec as P

REACH = 2
EPSILON = 1e-06
LANES = 128
HALF = 64
SLICES = 8
STATS = 16
HBM_RATE = 3690000
F32 = jnp.float32
BF16 = jnp.bfloat16

VMEM = pl.BlockSpec(memory_space=pltpu.VMEM)
SMEM = pl.BlockSpec(memory_space=pltpu.SMEM)


def call(body, out_shape, in_specs, scratch=(), micros=1.0, megabytes=20):
    many = isinstance(out_shape, (list, tuple))
    return pl.pallas_call(
        body,
        out_shape=out_shape,
        in_specs=in_specs,
        out_specs=[VMEM] * len(out_shape) if many else VMEM,
        scratch_shapes=list(scratch),
        compiler_params=pltpu.CompilerParams(vmem_limit_bytes=megabytes * 1024 * 1024),
        cost_estimate=pl.CostEstimate(
            flops=0, bytes_accessed=int(micros * HBM_RATE), transcendentals=0
        ),
    )


def dot(a, b, dims=((1,), (0,))):
    return lax.dot_general(a, b, (dims, ((), ())), preferred_element_type=F32)


def split3(row):
    high = row.astype(BF16)
    rest = row - high.astype(F32)
    middle = rest.astype(BF16)
    low = (rest - middle.astype(F32)).astype(BF16)
    return [high, middle, low]


def join3(rows, at):
    return rows[..., 3 * at, :] + rows[..., 3 * at + 1, :] + rows[..., 3 * at + 2, :]


def row3(values, at):
    return values[3 * at:3 * at + 1] + values[3 * at + 1:3 * at + 2] + values[3 * at + 2:3 * at + 3]


def halves(x, y):
    left = lax.broadcasted_iota(jnp.int32, x.shape, x.ndim - 1) < HALF
    first = jnp.where(left, x, pltpu.roll(y, HALF, x.ndim - 1))
    second = jnp.where(left, pltpu.roll(x, HALF, x.ndim - 1), y)
    return first, second


def chunk(x, pair):
    return x[:, pair * LANES:(pair + 1) * LANES]


def order_tiles(all_blocks, cols, count, row0, tiles, out):
    ops, blocks, near, size, _ = tiles.shape
    for b in range(blocks):
        for k in range(near):
            rel = lax.rem(cols[b, k] - (row0[0] + b) + REACH + all_blocks, all_blocks)
            rel = lax.rem(rel, all_blocks)
            at = pl.multiple_of(rel * size, size)
            live = k < count[b]
            for o in range(ops):
                tile = tiles[o, b, k]
                out[b, o * size:(o + 1) * size, pl.ds(at, size)] = jnp.where(
                    live, tile, jnp.zeros_like(tile)
                )


def coeff_kernel(u, right, out):
    blocks, rank, size = right.shape
    z = [dot(right[b], u[b * size:(b + 1) * size, :]) for b in range(blocks)]
    for pair in range(SLICES // 2):
        first, second = halves(chunk(z[0], pair), chunk(z[1], pair))
        out[2 * pair] = first.astype(BF16)
        out[2 * pair + 1] = second.astype(BF16)


def pack_kernel(far_cols, coup, left, right, out):
    ops, blocks, far, rank, _ = coup.shape
    whole, rest = [], []
    for b in range(blocks):
        tiles = [
            jnp.concatenate([coup[o, b, f] for f in range(far)], axis=1) for o in range(ops)
        ]
        tiles = jnp.concatenate(tiles, axis=0)
        whole.append(tiles[:, :LANES])
        rest.append(tiles[:, LANES:])
    lane = lax.broadcasted_iota(jnp.int32, (STATS, LANES), 1)
    names = jnp.zeros((STATS, LANES), F32)
    for b in range(blocks):
        for f in range(far):
            names = jnp.where(lane == b * far + f, far_cols[b, f].astype(F32), names)
    mixed = [dot(right[b], left[b], ((1,), (1,))) for b in range(blocks)]
    high = [m.astype(BF16) for m in mixed]
    low = [(m - h.astype(F32)).astype(BF16) for m, h in zip(mixed, high)]
    out[...] = jnp.concatenate(
        whole
        + [jnp.concatenate(rest, axis=1), names.astype(BF16), jnp.concatenate(high + low, axis=1)],
        axis=0,
    )


def share_kernel(packed, *refs):
    parts, out = refs[:-1], refs[-1]
    rows = packed.shape[0]
    rank = parts[0].shape[1]
    for s in range(SLICES):
        out[s, 0:rows, :] = packed[...]
    for m, part in enumerate(parts):
        out[:, rows + m * rank:rows + (m + 1) * rank, :] = part[...]


def coupling_rows(held, s, b, ops, rank):
    body = ops * rank
    first = held[s, b * body:(b + 1) * body, :]
    rest = held[s, 2 * body:3 * body, b * HALF:(b + 1) * HALF]
    return jnp.concatenate([first, rest], axis=1)


def couple(cols, held, s, b, ops, rank, far, z):
    at = (s * 2 + b) * far
    lhs = coupling_rows(held, s, b, ops, rank)
    starts = [pl.multiple_of(cols[at + f] * rank, rank) for f in range(far)]
    picked = [
        jnp.concatenate([x[pl.ds(start, rank), :] for start in starts], axis=0) for x in z
    ]
    if len(z) == 1:
        return dot(lhs, picked[0])
    return jnp.concatenate(
        [dot(lhs[o * rank:(o + 1) * rank], picked[o]) for o in range(ops)], axis=0
    )


def spread_rows(source, rank):
    count = source.shape[0]
    turned = pltpu.roll(source, HALF, 2)
    both = jnp.concatenate([source[:, None], turned[:, None]], axis=1)
    return both.reshape(count * 2 * rank, LANES).astype(BF16)


def held_part(held, m, ops, rank):
    at = 3 * ops * rank + STATS + (m + 1) * rank
    return held[:, at:at + rank, :].astype(F32)


def group_at(group, m, groups, step):
    return pl.multiple_of(lax.rem(group[0] + (groups - m), groups) * step, step)


def first_couple(ops, rank, far, cols, group, held, out, mixed, zs):
    step = SLICES * 2 * rank
    count = zs.shape[0] // step
    for m in range(count):
        at = group_at(group, m, count, step)
        zs[pl.ds(at, step), :] = spread_rows(held_part(held, m, ops, rank), rank)
    at = 3 * ops * rank + STATS
    first = lax.broadcasted_iota(jnp.int32, (rank, LANES), 1) < HALF
    for s in range(SLICES):
        c = [couple(cols, held, s, b, ops, rank, far, [zs]) for b in range(2)]
        c = halves(c[0], c[1])[0]
        out[s] = c.astype(BF16)
        for o in range(ops):
            x = c[o * rank:(o + 1) * rank]
            parts = [jnp.where(first, x, 0.0), jnp.where(first, 0.0, x)] * 2
            parts = jnp.concatenate(parts, axis=0).astype(BF16)
            mixed[s, o * rank:(o + 1) * rank, :] = dot(held[s, at:at + rank, :], parts)


def take_coefs(cmsg, coef, rows):
    for pair in range(SLICES // 2):
        parts = halves(
            cmsg[2 * pair, 0:rows, :].astype(F32), cmsg[2 * pair + 1, 0:rows, :].astype(F32)
        )
        for b in range(2):
            coef[b, :, pair * LANES:(pair + 1) * LANES] = parts[b].astype(BF16)


def near_product(tiles, parts, b, blocks, size):
    total = None
    first = b - REACH
    at = 0
    for d, part in enumerate(parts):
        start = max((d - 1) * blocks, first)
        stop = min(d * blocks, first + 2 * REACH + 1)
        if stop <= start:
            continue
        begin = (start - (d - 1) * blocks) * size
        width = (stop - start) * size
        value = dot(tiles[:, at:at + width], part[begin:begin + width, :])
        total = value if total is None else total + value
        at += width
    return total


def diagonal_of(diag, o, b, size, columns):
    row = diag[o:o + 1, b * size:(b + 1) * size]
    column = jnp.transpose(jnp.broadcast_to(row, (LANES, size)))
    return jnp.concatenate([column] * (columns // LANES), axis=1)


def pieces_of(values):
    rows = []
    for value in values:
        rows += split3(value)
    zero = jnp.zeros_like(rows[0])
    return jnp.concatenate(rows + [zero] * (STATS - len(rows)), axis=0)


def spread_pairs(out, rows, x, y):
    for pair in range(SLICES // 2):
        first, second = halves(chunk(x, pair), chunk(y, pair))
        out[2 * pair, rows, :] = first.astype(BF16)
        out[2 * pair + 1, rows, :] = second.astype(BF16)


def ratio(inner, squares):
    good = squares > 0
    return jnp.where(good, inner / jnp.where(good, squares, 1.0), 0.0)


def near_kernel(w, low, own, high, diag, right, c1, image, first, second, edge, msg):
    ops = image.shape[0]
    blocks, rank, size = right.shape
    rows, columns = own.shape
    body = ops * rank
    inner = [None] * ops
    squares = None
    for b in range(blocks):
        product = near_product(w.at[b], (low, own, high), b, blocks, size)
        ub = own[b * size:(b + 1) * size, :].astype(F32)
        part = jnp.sum(ub * ub, axis=0, keepdims=True)
        squares = part if squares is None else squares + part
        for o in range(ops):
            value = (
                product[o * size:(o + 1) * size]
                + diagonal_of(diag, o, b, size, columns) * ub
            )
            image[o, b * size:(b + 1) * size, :] = value
            part = jnp.sum(ub * value, axis=0, keepdims=True)
            inner[o] = part if inner[o] is None else inner[o] + part
    shifts = [ratio(x, squares) for x in inner]
    edges = pieces_of(shifts + [squares])
    edge[...] = edges
    first[rows:, :] = edges
    edges = edges.astype(F32)
    msg[:, 0:body, :] = c1[...]
    for o, out in enumerate((first, second)):
        shift = row3(edges, o)
        z = []
        for b in range(blocks):
            ub = own[b * size:(b + 1) * size, :].astype(F32)
            v = image[o, b * size:(b + 1) * size, :] - shift * ub
            image[o, b * size:(b + 1) * size, :] = v
            v = v.astype(BF16)
            out[b * size:(b + 1) * size, :] = v
            z.append(dot(right[b], v))
        spread_pairs(msg, slice(body + o * rank, body + (o + 1) * rank), z[0], z[1])
    spread_pairs(msg, slice(2 * body, 2 * body + STATS), edges, edges)


def image_kernel(own, near, edge, left, got, mixed, after_low, after_high, vout, stats, cown, xmsg, image, coef):
    ops = near.shape[0]
    blocks, rank, size = left.shape
    rows, columns = own.shape
    body = ops * rank
    for s in range(SLICES):
        xmsg[s * body:(s + 1) * body, :] = (
            got[s, body:2 * body, :].astype(F32) + mixed[s]
        ).astype(BF16)
        at = SLICES * body + s * STATS
        xmsg[at:at + STATS, :] = got[s, 2 * body:2 * body + STATS, :]
    take_coefs(got, coef, body)
    edges = edge[...].astype(F32)
    squares = row3(edges, ops)
    shifts, spreads = [], []
    for o in range(ops):
        inner = None
        for b in range(blocks):
            cown[(o * blocks + b) * rank:(o * blocks + b + 1) * rank, :] = coef[
                b, o * rank:(o + 1) * rank, :
            ]
            far = dot(left[b], coef[b, o * rank:(o + 1) * rank, :], ((0,), (0,)))
            value = near[o, b * size:(b + 1) * size, :] + far.astype(BF16).astype(F32)
            image[b * size:(b + 1) * size, :] = value
            ub = own[b * size:(b + 1) * size, :].astype(F32)
            part = jnp.sum(ub * value, axis=0, keepdims=True)
            inner = part if inner is None else inner + part
        before = row3(edges, o)
        after = before + ratio(inner, squares)
        shifts.append(after)
        change = sum(x.astype(F32) for x in split3(after)) - before
        spread = None
        for b in range(blocks):
            ub = own[b * size:(b + 1) * size, :].astype(F32)
            v = image[b * size:(b + 1) * size, :] - change * ub
            part = jnp.sum(v * v, axis=0, keepdims=True)
            spread = part if spread is None else spread + part
            vout[(o * blocks + b) * size:(o * blocks + b + 1) * size, :] = v.astype(BF16)
        spreads.append(spread)
    every = pieces_of(shifts + [squares] + spreads)
    stats[...] = every
    at = SLICES * (body + STATS)
    for j in range(columns // LANES):
        xmsg[at + j * STATS:at + (j + 1) * STATS, :] = chunk(every, j)


def bulk_kernel(near, cown, left, edge, after, out):
    rows = near.shape[0]
    blocks, rank, size = left.shape
    at = rows + cown.shape[0]
    out[0:rows, :] = near[...]
    out[rows:at, :] = cown[...]
    for b in range(blocks):
        out[at:at + rank, b * size:(b + 1) * size] = left[b]
    out[at + rank:, :] = edge[...]


def second_couple(panels, ops, rank, far, cols, group, held, *refs):
    parts, (out, zs) = refs[:-2], refs[-2:]
    count = len(parts)
    body = ops * rank
    step = SLICES * 2 * rank
    at = SLICES * body
    edges = [
        x[at:at + SLICES * STATS, :].astype(F32).reshape(SLICES, STATS, LANES) for x in parts
    ]
    scale_sq = EPSILON
    totals = [0.0] * ops
    for x in edges:
        squares = join3(x, ops)
        scale_sq = scale_sq + jnp.sum(squares, axis=0, keepdims=True) / panels
        for o in range(ops):
            totals[o] = totals[o] + jnp.sum(join3(x, o) * squares, axis=0, keepdims=True) / panels
    rough = pieces_of([total / scale_sq for total in totals])
    for m, x in enumerate(parts):
        row = group_at(group, m, count, step)
        base = held_part(held, m, ops, rank)
        z = x[0:at, :].astype(F32).reshape(SLICES, body, LANES)
        for o in range(ops):
            delta = join3(edges[m], o) - row3(rough.astype(F32), o)
            value = z[:, o * rank:(o + 1) * rank, :] + delta[:, None, :] * base
            zs[o, pl.ds(row, step), :] = spread_rows(value, rank)
    start = at + SLICES * STATS
    for s in range(SLICES):
        c = [couple(cols, held, s, b, ops, rank, far, [zs.at[o] for o in range(ops)]) for b in range(2)]
        out[s, 0:body, :] = halves(c[0], c[1])[0].astype(BF16)
        out[s, body:body + STATS, :] = rough
        for m, x in enumerate(parts):
            height = x.shape[0] - start
            row = body + STATS + m * height
            out[s, row:row + height, :] = x[start:, :]


def final_kernel(
    panels,
    group,
    w,
    ulow,
    uown,
    uhigh,
    low0,
    low1,
    vown,
    high0,
    high1,
    mine,
    diag,
    left,
    cown,
    cmsg,
    images,
    heights,
    norms,
    ext,
    coef,
    st,
):
    ops = images.shape[0]
    blocks, rank, size = left.shape
    rows, columns = uown.shape
    body = ops * rank
    wide = columns // LANES
    height = wide * STATS
    count = (cmsg.shape[1] - body - STATS) // height
    take_coefs(cmsg, coef, body)
    for m in range(count):
        at = group_at(group, m, count, SLICES)
        for j in range(wide):
            row = body + STATS + m * height + j * STATS
            st[pl.ds(at, SLICES), :, j * LANES:(j + 1) * LANES] = cmsg[
                :, row:row + STATS, :
            ].astype(F32)
    rough = jnp.concatenate(
        [
            halves(
                cmsg[2 * pair, body:body + STATS, :].astype(F32),
                cmsg[2 * pair + 1, body:body + STATS, :].astype(F32),
            )[0]
            for pair in range(wide)
        ],
        axis=1,
    )
    every = st[...]
    squares = join3(every, ops)
    scale_sq = jnp.sum(squares, axis=0, keepdims=True) / panels + EPSILON
    reverse = 1.0 / jnp.sqrt(scale_sq)
    for o in range(ops):
        shift = join3(every, o)
        high = jnp.sum(shift * squares, axis=0, keepdims=True) / panels / scale_sq
        delta = shift - high
        spread = join3(every, ops + 1 + o) + delta * delta * squares
        norm = jnp.sqrt(jnp.sum(spread, axis=0, keepdims=True) / panels / scale_sq + EPSILON)
        heights[o:o + 1, :] = high
        norms[o:o + 1, :] = norm
        factor = reverse / norm
        for at, u, v, more in ((0, ulow, (low0, low1)[o], low1), (2, uhigh, (high0, high1)[o], high1)):
            start = rows + ops * blocks * rank
            edges = more[start + rank:, :].astype(F32)
            change = (row3(edges, o) - high) * factor
            for b in range(blocks):
                row = rows + (o * blocks + b) * rank
                far = dot(
                    more[start:start + rank, b * size:(b + 1) * size],
                    more[row:row + rank, :],
                    ((0,), (0,)),
                ).astype(BF16).astype(F32)
                here = slice(b * size, (b + 1) * size)
                value = (v[here, :].astype(F32) + far) * factor + u[here, :].astype(F32) * change
                ext[at, here, :] = value.astype(BF16)
        change = (row3(mine[...].astype(F32), o) - high) * factor
        value = vown[o * rows:(o + 1) * rows, :].astype(F32) * factor
        ext[1] = (value + uown[...].astype(F32) * change).astype(BF16)
        offset = high - row3(rough, o)
        for b in range(blocks):
            parts = [ext.at[at] for at in range(3)]
            product = near_product(w.at[b, o * size:(o + 1) * size], parts, b, blocks, size)
            row = (o * blocks + b) * rank
            c = coef[b, o * rank:(o + 1) * rank, :].astype(F32)
            c = (c - offset * cown[row:row + rank, :].astype(F32)) * factor
            far = dot(left[b], c.astype(BF16), ((0,), (0,)))
            own = ext[1, b * size:(b + 1) * size, :].astype(F32)
            images[o, b * size:(b + 1) * size, :] = (
                product
                + diagonal_of(diag, o, b, size, columns) * own
                + far.astype(BF16).astype(F32)
            )


def ring(block):
    count = lax.axis_size("store")
    forward = [(i, (i + 1) % count) for i in range(count)]
    backward = [(target, source) for source, target in forward]
    return lax.ppermute(block, "store", forward), lax.ppermute(block, "store", backward)


def shards(
    sources,
    self_terms,
    near_tiles,
    near_cols,
    near_count,
    far_cols,
    basis_left,
    basis_right,
    couplings,
):
    n = lax.axis_size("store")
    ops, blocks, near, size, _ = near_tiles.shape
    rank = basis_left.shape[2]
    far = far_cols.shape[1]
    rows, columns = sources.shape
    all_blocks = blocks * n
    count = n // SLICES
    groups = [[g * SLICES + s for s in range(SLICES)] for g in range(count)]
    sds = jax.ShapeDtypeStruct
    body = ops * rank

    def exchange(x):
        return lax.all_to_all(x, "store", 0, 0, axis_index_groups=groups, tiled=True)

    def across(x):
        parts = [x]
        for m in range(1, count):
            pairs = [(i, (i + m * SLICES) % n) for i in range(n)]
            parts.append(lax.ppermute(x, "store", pairs))
        return parts

    place = lax.axis_index("store").astype(jnp.int32)
    row0 = (place * blocks).reshape(1)
    group = lax.div(place, jnp.int32(SLICES)).reshape(1)
    left = jnp.transpose(basis_left, (0, 2, 1))
    right = jnp.transpose(basis_right, (0, 2, 1))

    low, high = ring(sources)
    z1 = call(coeff_kernel, sds((SLICES, rank, LANES), BF16), [VMEM, VMEM], megabytes=60)(
        sources, right
    )
    z1 = across(z1)
    shared = (blocks + 1) * body
    lead = shared + STATS + rank
    packed = call(pack_kernel, sds((lead, LANES), BF16), [SMEM, VMEM, VMEM, VMEM])(
        far_cols, couplings, left, right
    )
    held = call(
        share_kernel, sds((SLICES, lead + count * rank, LANES), BF16), [VMEM] * (1 + count)
    )(packed, *z1)
    held = exchange(held)
    cols = held[:, shared, :blocks * far].astype(jnp.int32).reshape(-1)

    w = call(
        functools.partial(order_tiles, all_blocks),
        sds((blocks, ops * size, near * size), BF16),
        [SMEM, SMEM, SMEM, VMEM],
        micros=2.5,
    )(near_cols, near_count, row0, near_tiles)

    c1, mixed = call(
        functools.partial(first_couple, ops, rank, far),
        [sds((SLICES, body, LANES), BF16), sds((SLICES, body, LANES), F32)],
        [SMEM, SMEM, VMEM],
        [pltpu.VMEM((n * blocks * rank, LANES), BF16)],
    )(cols, group, held)

    image, first, second, edge, msg = call(
        near_kernel,
        [
            sds((ops, rows, columns), F32),
            sds((rows + STATS, columns), BF16),
            sds((rows, columns), BF16),
            sds((STATS, columns), BF16),
            sds((SLICES, 2 * body + STATS, LANES), BF16),
        ],
        [VMEM] * 7,
        micros=4.0,
    )(w, low, sources, high, self_terms, right, c1)
    low0, high0 = ring(first)
    got = exchange(msg)

    own_rows = ops * blocks * rank
    v, stats, cown, xmsg = call(
        image_kernel,
        [
            sds((ops * rows, columns), BF16),
            sds((STATS, columns), BF16),
            sds((own_rows, columns), BF16),
            sds((SLICES * (body + STATS) + columns // LANES * STATS, LANES), BF16),
        ],
        [VMEM] * 6 + [pl.BlockSpec(memory_space=pl.ANY)] * 2,
        [pltpu.VMEM((rows, columns), F32), pltpu.VMEM((blocks, body, columns), BF16)],
        micros=3.0,
    )(sources, image, edge, left, got, mixed, low0, high0)
    parts = across(xmsg)

    bulk = call(
        bulk_kernel,
        sds((rows + own_rows + rank + STATS, columns), BF16),
        [VMEM] * 4 + [pl.BlockSpec(memory_space=pl.ANY)],
    )(second, cown, left, edge, parts[-1])
    low1, high1 = ring(bulk)

    panels = all_blocks * size
    c2 = call(
        functools.partial(second_couple, panels, ops, rank, far),
        sds((SLICES, body + STATS + count * columns // LANES * STATS, LANES), BF16),
        [SMEM, SMEM] + [VMEM] * (1 + count),
        [pltpu.VMEM((ops, n * blocks * rank, LANES), BF16)],
    )(cols, group, held, *parts)
    c2 = exchange(c2)

    images, heights, norms = call(
        functools.partial(final_kernel, panels),
        [sds((ops, rows, columns), F32), sds((ops, columns), F32), sds((ops, columns), F32)],
        [SMEM] + [VMEM] * 14,
        [
            pltpu.VMEM((3, rows, columns), BF16),
            pltpu.VMEM((blocks, body, columns), BF16),
            pltpu.VMEM((n, STATS, columns), F32),
        ],
        micros=5.0,
    )(
        group,
        w,
        low,
        sources,
        high,
        low0,
        low1,
        v,
        high0,
        high1,
        stats,
        self_terms,
        left,
        cown,
        c2,
    )
    return images, heights, norms


def solution(mesh):
    placed = (
        P(("groups", "store"), None),
        P(None, "store"),
        P(None, "store", None, None, None),
        P("store", None),
        P("store"),
        P("store", None),
        P("store", None, None),
        P("store", None, None),
        P(None, "store", None, None, None),
    )
    return jax.shard_map(
        shards,
        mesh=mesh,
        in_specs=placed,
        out_specs=(P(None, ("groups", "store"), None), P("groups", None), P("groups", None)),
        check_vma=False,
    )
```

```python
import functools

import jax
import jax.numpy as jnp
from jax import lax
from jax.experimental import pallas as pl
from jax.experimental.pallas import tpu as pltpu
from jax.sharding import PartitionSpec as P

REACH = 2
EPSILON = 1e-06
LANES = 128
HALF = 64
SLICES = 8
STATS = 16
HBM_RATE = 3690000
F32 = jnp.float32
BF16 = jnp.bfloat16

VMEM = pl.BlockSpec(memory_space=pltpu.VMEM)
SMEM = pl.BlockSpec(memory_space=pltpu.SMEM)
ANY = pl.BlockSpec(memory_space=pl.ANY)


def call(body, out_shape, in_specs, scratch=(), micros=1.0, megabytes=20, out_specs=None, alias=None):
    many = isinstance(out_shape, (list, tuple))
    if out_specs is None:
        out_specs = [VMEM] * len(out_shape) if many else VMEM
    return pl.pallas_call(
        body,
        out_shape=out_shape,
        in_specs=in_specs,
        out_specs=out_specs,
        input_output_aliases=alias or {},
        scratch_shapes=list(scratch),
        compiler_params=pltpu.CompilerParams(vmem_limit_bytes=megabytes * 1024 * 1024),
        cost_estimate=pl.CostEstimate(
            flops=0, bytes_accessed=int(micros * HBM_RATE), transcendentals=0
        ),
    )


def dot(a, b, dims=((1,), (0,))):
    return lax.dot_general(a, b, (dims, ((), ())), preferred_element_type=F32)


def split3(row):
    high = row.astype(BF16)
    rest = row - high.astype(F32)
    middle = rest.astype(BF16)
    low = (rest - middle.astype(F32)).astype(BF16)
    return [high, middle, low]


def join3(rows, at):
    return rows[..., 3 * at, :] + rows[..., 3 * at + 1, :] + rows[..., 3 * at + 2, :]


def row3(values, at):
    return values[3 * at:3 * at + 1] + values[3 * at + 1:3 * at + 2] + values[3 * at + 2:3 * at + 3]


def halves(x, y):
    left = lax.broadcasted_iota(jnp.int32, x.shape, x.ndim - 1) < HALF
    first = jnp.where(left, x, pltpu.roll(y, HALF, x.ndim - 1))
    second = jnp.where(left, pltpu.roll(x, HALF, x.ndim - 1), y)
    return first, second


def chunk(x, pair):
    return x[:, pair * LANES:(pair + 1) * LANES]


def order_tiles(all_blocks, cols, count, row0, tiles, out):
    ops, blocks, near, size, _ = tiles.shape
    for b in range(blocks):
        for k in range(near):
            rel = lax.rem(cols[b, k] - (row0[0] + b) + REACH + all_blocks, all_blocks)
            rel = lax.rem(rel, all_blocks)
            at = pl.multiple_of(rel * size, size)
            live = k < count[b]
            for o in range(ops):
                tile = tiles[o, b, k]
                out[b, o * size:(o + 1) * size, pl.ds(at, size)] = jnp.where(
                    live, tile, jnp.zeros_like(tile)
                )


def coeff_kernel(far_cols, u, left, right, coup, z_out, out):
    ops, blocks, far, rank, _ = coup.shape
    size = right.shape[2]
    z = [dot(right[b], u[b * size:(b + 1) * size, :]) for b in range(blocks)]
    for pair in range(SLICES // 2):
        first, second = halves(chunk(z[0], pair), chunk(z[1], pair))
        z_out[2 * pair] = first.astype(BF16)
        z_out[2 * pair + 1] = second.astype(BF16)
    whole, rest = [], []
    for b in range(blocks):
        tiles = [
            jnp.concatenate([coup[o, b, f] for f in range(far)], axis=1) for o in range(ops)
        ]
        tiles = jnp.concatenate(tiles, axis=0)
        whole.append(tiles[:, :LANES])
        rest.append(tiles[:, LANES:])
    lane = lax.broadcasted_iota(jnp.int32, (STATS, LANES), 1)
    names = jnp.zeros((STATS, LANES), F32)
    for b in range(blocks):
        for f in range(far):
            names = jnp.where(lane == b * far + f, far_cols[b, f].astype(F32), names)
    mixed = [dot(right[b], left[b], ((1,), (1,))) for b in range(blocks)]
    high = [m.astype(BF16) for m in mixed]
    low = [(m - h.astype(F32)).astype(BF16) for m, h in zip(mixed, high)]
    out[...] = jnp.concatenate(
        whole
        + [jnp.concatenate(rest, axis=1), names.astype(BF16), jnp.concatenate(high + low, axis=1)],
        axis=0,
    )


def share_kernel(packed, after_low, after_high, *refs):
    parts, out = refs[:-1], refs[-1]
    rows = packed.shape[0]
    rank = parts[0].shape[1]
    for s in range(SLICES):
        out[s, 0:rows, :] = packed[...]
    for m, part in enumerate(parts):
        out[:, rows + m * rank:rows + (m + 1) * rank, :] = part[...]


def coupling_rows(held, s, b, ops, rank):
    body = ops * rank
    first = held[s, b * body:(b + 1) * body, :]
    rest = held[s, 2 * body:3 * body, b * HALF:(b + 1) * HALF]
    return jnp.concatenate([first, rest], axis=1)


def couple(cols, held, s, b, ops, rank, far, z):
    at = (s * 2 + b) * far
    lhs = coupling_rows(held, s, b, ops, rank)
    starts = [pl.multiple_of(cols[at + f] * rank, rank) for f in range(far)]
    picked = [
        jnp.concatenate([x[pl.ds(start, rank), :] for start in starts], axis=0) for x in z
    ]
    if len(z) == 1:
        return dot(lhs, picked[0])
    return jnp.concatenate(
        [dot(lhs[o * rank:(o + 1) * rank], picked[o]) for o in range(ops)], axis=0
    )


def spread_rows(source, rank):
    count = source.shape[0]
    turned = pltpu.roll(source, HALF, 2)
    both = jnp.concatenate([source[:, None], turned[:, None]], axis=1)
    return both.reshape(count * 2 * rank, LANES).astype(BF16)


def held_part(held, m, ops, rank):
    at = 3 * ops * rank + STATS + (m + 1) * rank
    return held[:, at:at + rank, :].astype(F32)


def group_at(group, m, groups, step):
    return pl.multiple_of(lax.rem(group[0] + (groups - m), groups) * step, step)


def first_couple(ops, rank, far, cols, group, held, out, mixed, zs):
    step = SLICES * 2 * rank
    count = zs.shape[0] // step
    for m in range(count):
        at = group_at(group, m, count, step)
        zs[pl.ds(at, step), :] = spread_rows(held_part(held, m, ops, rank), rank)
    at = 3 * ops * rank + STATS
    first = lax.broadcasted_iota(jnp.int32, (rank, LANES), 1) < HALF
    for s in range(SLICES):
        c = [couple(cols, held, s, b, ops, rank, far, [zs]) for b in range(2)]
        c = halves(c[0], c[1])[0]
        out[s] = c.astype(BF16)
        for o in range(ops):
            x = c[o * rank:(o + 1) * rank]
            parts = [jnp.where(first, x, 0.0), jnp.where(first, 0.0, x)] * 2
            parts = jnp.concatenate(parts, axis=0).astype(BF16)
            mixed[s, o * rank:(o + 1) * rank, :] = dot(held[s, at:at + rank, :], parts)


def take_coefs(cmsg, coef, rows):
    for pair in range(SLICES // 2):
        parts = halves(
            cmsg[2 * pair, 0:rows, :].astype(F32), cmsg[2 * pair + 1, 0:rows, :].astype(F32)
        )
        for b in range(2):
            coef[b, :, pair * LANES:(pair + 1) * LANES] = parts[b].astype(BF16)


def near_product(tiles, parts, b, blocks, size):
    total = None
    first = b - REACH
    at = 0
    for d, part in enumerate(parts):
        start = max((d - 1) * blocks, first)
        stop = min(d * blocks, first + 2 * REACH + 1)
        if stop <= start:
            continue
        begin = (start - (d - 1) * blocks) * size
        width = (stop - start) * size
        value = dot(tiles[:, at:at + width], part[begin:begin + width, :])
        total = value if total is None else total + value
        at += width
    return total


def diagonal_of(diag, o, b, size, columns):
    row = diag[o:o + 1, b * size:(b + 1) * size]
    column = jnp.transpose(jnp.broadcast_to(row, (LANES, size)))
    return jnp.concatenate([column] * (columns // LANES), axis=1)


def pieces_of(values):
    rows = []
    for value in values:
        rows += split3(value)
    zero = jnp.zeros_like(rows[0])
    return jnp.concatenate(rows + [zero] * (STATS - len(rows)), axis=0)


def spread_pairs(out, rows, x, y):
    for pair in range(SLICES // 2):
        first, second = halves(chunk(x, pair), chunk(y, pair))
        out[2 * pair, rows, :] = first.astype(BF16)
        out[2 * pair + 1, rows, :] = second.astype(BF16)


def ratio(inner, squares):
    good = squares > 0
    return jnp.where(good, inner / jnp.where(good, squares, 1.0), 0.0)


def near_kernel(w, low, own, high, diag, right, c1, image, edge, msg):
    ops = image.shape[0]
    blocks, rank, size = right.shape
    rows, columns = own.shape
    body = ops * rank
    inner = [None] * ops
    squares = None
    for b in range(blocks):
        product = near_product(w.at[b], (low, own, high), b, blocks, size)
        ub = own[b * size:(b + 1) * size, :].astype(F32)
        part = jnp.sum(ub * ub, axis=0, keepdims=True)
        squares = part if squares is None else squares + part
        for o in range(ops):
            value = (
                product[o * size:(o + 1) * size]
                + diagonal_of(diag, o, b, size, columns) * ub
            )
            image[o, b * size:(b + 1) * size, :] = value
            part = jnp.sum(ub * value, axis=0, keepdims=True)
            inner[o] = part if inner[o] is None else inner[o] + part
    shifts = [ratio(x, squares) for x in inner]
    edges = pieces_of(shifts + [squares])
    edge[...] = edges
    edges = edges.astype(F32)
    msg[:, 0:body, :] = c1[...]
    for o in range(ops):
        shift = row3(edges, o)
        z = []
        for b in range(blocks):
            ub = own[b * size:(b + 1) * size, :].astype(F32)
            v = image[o, b * size:(b + 1) * size, :] - shift * ub
            image[o, b * size:(b + 1) * size, :] = v
            z.append(dot(right[b], v.astype(BF16)))
        spread_pairs(msg, slice(body + o * rank, body + (o + 1) * rank), z[0], z[1])
    spread_pairs(msg, slice(2 * body, 2 * body + STATS), edges, edges)


def image_kernel(own, near, edge, left, got, mixed, first, second, cown, xmsg, image, coef):
    ops = near.shape[0]
    blocks, rank, size = left.shape
    rows, columns = own.shape
    body = ops * rank
    for s in range(SLICES):
        xmsg[s * body:(s + 1) * body, :] = (
            got[s, body:2 * body, :].astype(F32) + mixed[s]
        ).astype(BF16)
        at = SLICES * body + s * STATS
        xmsg[at:at + STATS, :] = got[s, 2 * body:2 * body + STATS, :]
    take_coefs(got, coef, body)
    edges = edge[...].astype(F32)
    squares = row3(edges, ops)
    shifts, spreads = [], []
    for o in range(ops):
        inner = None
        for b in range(blocks):
            cown[(o * blocks + b) * rank:(o * blocks + b + 1) * rank, :] = coef[
                b, o * rank:(o + 1) * rank, :
            ]
            far = dot(left[b], coef[b, o * rank:(o + 1) * rank, :], ((0,), (0,)))
            value = near[o, b * size:(b + 1) * size, :] + far.astype(BF16).astype(F32)
            image[b * size:(b + 1) * size, :] = value
            ub = own[b * size:(b + 1) * size, :].astype(F32)
            part = jnp.sum(ub * value, axis=0, keepdims=True)
            inner = part if inner is None else inner + part
        before = row3(edges, o)
        after = before + ratio(inner, squares)
        shifts.append(after)
        change = sum(x.astype(F32) for x in split3(after)) - before
        spread = None
        for b in range(blocks):
            ub = own[b * size:(b + 1) * size, :].astype(F32)
            v = image[b * size:(b + 1) * size, :] - change * ub
            part = jnp.sum(v * v, axis=0, keepdims=True)
            spread = part if spread is None else spread + part
            (first, second)[o][b * size:(b + 1) * size, :] = v.astype(BF16)
        spreads.append(spread)
    every = pieces_of(shifts + [squares] + spreads)
    first[rows:, :] = every
    at = SLICES * (body + STATS)
    for j in range(columns // LANES):
        xmsg[at + j * STATS:at + (j + 1) * STATS, :] = chunk(every, j)


def second_couple(panels, ops, rank, far, cols, group, held, *refs):
    parts, (out, zs) = refs[:-2], refs[-2:]
    count = len(parts)
    body = ops * rank
    step = SLICES * 2 * rank
    at = SLICES * body
    edges = [
        x[at:at + SLICES * STATS, :].astype(F32).reshape(SLICES, STATS, LANES) for x in parts
    ]
    scale_sq = EPSILON
    totals = [0.0] * ops
    for x in edges:
        squares = join3(x, ops)
        scale_sq = scale_sq + jnp.sum(squares, axis=0, keepdims=True) / panels
        for o in range(ops):
            totals[o] = totals[o] + jnp.sum(join3(x, o) * squares, axis=0, keepdims=True) / panels
    rough = pieces_of([total / scale_sq for total in totals])
    for m, x in enumerate(parts):
        row = group_at(group, m, count, step)
        base = held_part(held, m, ops, rank)
        z = x[0:at, :].astype(F32).reshape(SLICES, body, LANES)
        for o in range(ops):
            delta = join3(edges[m], o) - row3(rough.astype(F32), o)
            value = z[:, o * rank:(o + 1) * rank, :] + delta[:, None, :] * base
            zs[o, pl.ds(row, step), :] = spread_rows(value, rank)
    start = at + SLICES * STATS
    for s in range(SLICES):
        c = [couple(cols, held, s, b, ops, rank, far, [zs.at[o] for o in range(ops)]) for b in range(2)]
        out[s, 0:body, :] = halves(c[0], c[1])[0].astype(BF16)
        out[s, body:body + STATS, :] = rough
        for m, x in enumerate(parts):
            height = x.shape[0] - start
            row = body + STATS + m * height
            out[s, row:row + height, :] = x[start:, :]


def apply_second(o, rows3, u3, v3, w, diag, left, cown, cmsg, images, ext, coef, out, sem):
    blocks, rank, size = left.shape
    rows, columns = u3[1].shape
    ops = w.shape[1] // size
    factor, changes, offset = rows3
    copies = []
    for at, (u, v) in enumerate(zip(u3, v3)):
        value = v[0:rows, :].astype(F32) * factor + u[...].astype(F32) * changes[at]
        ext[at] = value.astype(BF16)
    take_coefs(cmsg, coef, ops * rank)
    for b in range(blocks):
        parts = [ext.at[at] for at in range(3)]
        product = near_product(w.at[b, o * size:(o + 1) * size], parts, b, blocks, size)
        row = (o * blocks + b) * rank
        c = coef[b, o * rank:(o + 1) * rank, :].astype(F32) * factor
        c = c - offset * cown[row:row + rank, :].astype(F32)
        far = dot(left[b], c.astype(BF16), ((0,), (0,)))
        here = slice(b * size, (b + 1) * size)
        out[here, :] = (
            product
            + diagonal_of(diag, o, b, size, columns) * ext[1, here, :].astype(F32)
            + far.astype(BF16).astype(F32)
        )
        copies.append(pltpu.make_async_copy(out.at[here], images.at[o, here], sem.at[b]))
        copies[-1].start()
    for copy in copies:
        copy.wait()


def final_first(
    panels,
    group,
    w,
    ulow,
    uown,
    uhigh,
    vlow,
    vown,
    vhigh,
    diag,
    left,
    cown,
    cmsg,
    images,
    heights,
    norms,
    aux,
    ext,
    coef,
    out,
    st,
    sem,
):
    blocks, rank, size = left.shape
    rows, columns = uown.shape
    ops = w.shape[1] // size
    body = ops * rank
    wide = columns // LANES
    height = wide * STATS
    count = (cmsg.shape[1] - body - STATS) // height
    for m in range(count):
        at = group_at(group, m, count, SLICES)
        for j in range(wide):
            row = body + STATS + m * height + j * STATS
            st[pl.ds(at, SLICES), :, j * LANES:(j + 1) * LANES] = cmsg[
                :, row:row + STATS, :
            ].astype(F32)
    rough = jnp.concatenate(
        [
            halves(
                cmsg[2 * pair, body:body + STATS, :].astype(F32),
                cmsg[2 * pair + 1, body:body + STATS, :].astype(F32),
            )[0]
            for pair in range(wide)
        ],
        axis=1,
    )
    every = st[...]
    squares = join3(every, ops)
    scale_sq = jnp.sum(squares, axis=0, keepdims=True) / panels + EPSILON
    reverse = 1.0 / jnp.sqrt(scale_sq)
    found = []
    for o in range(ops):
        shift = join3(every, o)
        high = jnp.sum(shift * squares, axis=0, keepdims=True) / panels / scale_sq
        delta = shift - high
        spread = join3(every, ops + 1 + o) + delta * delta * squares
        norm = jnp.sqrt(jnp.sum(spread, axis=0, keepdims=True) / panels / scale_sq + EPSILON)
        heights[o:o + 1, :] = high
        norms[o:o + 1, :] = norm
        factor = reverse / norm
        changes = [
            (row3(v[rows:rows + STATS, :].astype(F32), o) - high) * factor
            for v in (vlow, vown, vhigh)
        ]
        found.append((factor, changes, (high - row3(rough, o)) * factor))
    factor, changes, offset = found[1]
    aux[0:1, :] = factor
    aux[1:2, :] = offset
    for at in range(3):
        aux[2 + at:3 + at, :] = changes[at]
    apply_second(
        0,
        found[0],
        (ulow, uown, uhigh),
        (vlow, vown, vhigh),
        w,
        diag,
        left,
        cown,
        cmsg,
        images,
        ext,
        coef,
        out,
        sem,
    )


def final_second(
    begun,
    w,
    ulow,
    uown,
    uhigh,
    vlow,
    vown,
    vhigh,
    diag,
    left,
    cown,
    cmsg,
    aux,
    images,
    ext,
    coef,
    out,
    sem,
):
    rows3 = aux[0:1, :], [aux[2 + at:3 + at, :] for at in range(3)], aux[1:2, :]
    apply_second(
        1,
        rows3,
        (ulow, uown, uhigh),
        (vlow, vown, vhigh),
        w,
        diag,
        left,
        cown,
        cmsg,
        images,
        ext,
        coef,
        out,
        sem,
    )


def ring(block):
    count = lax.axis_size("store")
    forward = [(i, (i + 1) % count) for i in range(count)]
    backward = [(target, source) for source, target in forward]
    return lax.ppermute(block, "store", forward), lax.ppermute(block, "store", backward)


def shards(
    sources,
    self_terms,
    near_tiles,
    near_cols,
    near_count,
    far_cols,
    basis_left,
    basis_right,
    couplings,
):
    n = lax.axis_size("store")
    ops, blocks, near, size, _ = near_tiles.shape
    rank = basis_left.shape[2]
    far = far_cols.shape[1]
    rows, columns = sources.shape
    all_blocks = blocks * n
    count = n // SLICES
    groups = [[g * SLICES + s for s in range(SLICES)] for g in range(count)]
    sds = jax.ShapeDtypeStruct
    body = ops * rank

    def exchange(x):
        return lax.all_to_all(x, "store", 0, 0, axis_index_groups=groups, tiled=True)

    def across(x):
        parts = [x]
        for m in range(1, count):
            pairs = [(i, (i + m * SLICES) % n) for i in range(n)]
            parts.append(lax.ppermute(x, "store", pairs))
        return parts

    place = lax.axis_index("store").astype(jnp.int32)
    row0 = (place * blocks).reshape(1)
    group = lax.div(place, jnp.int32(SLICES)).reshape(1)
    left = jnp.transpose(basis_left, (0, 2, 1))
    right = jnp.transpose(basis_right, (0, 2, 1))

    low, high = ring(sources)
    shared = (blocks + 1) * body
    lead = shared + STATS + rank
    z1, packed = call(
        coeff_kernel,
        [sds((SLICES, rank, LANES), BF16), sds((lead, LANES), BF16)],
        [SMEM] + [VMEM] * 4,
        megabytes=60,
    )(far_cols, sources, left, right, couplings)
    z1 = across(z1)
    held = call(
        share_kernel,
        sds((SLICES, lead + count * rank, LANES), BF16),
        [VMEM, ANY, ANY] + [VMEM] * count,
        megabytes=60,
    )(packed, low, high, *z1)
    held = exchange(held)
    cols = held[:, shared, :blocks * far].astype(jnp.int32).reshape(-1)

    w = call(
        functools.partial(order_tiles, all_blocks),
        sds((blocks, ops * size, near * size), BF16),
        [SMEM, SMEM, SMEM, VMEM],
        micros=2.5,
    )(near_cols, near_count, row0, near_tiles)

    c1, mixed = call(
        functools.partial(first_couple, ops, rank, far),
        [sds((SLICES, body, LANES), BF16), sds((SLICES, body, LANES), F32)],
        [SMEM, SMEM, VMEM],
        [pltpu.VMEM((n * blocks * rank, LANES), BF16)],
    )(cols, group, held)

    image, edge, msg = call(
        near_kernel,
        [
            sds((ops, rows, columns), F32),
            sds((STATS, columns), BF16),
            sds((SLICES, 2 * body + STATS, LANES), BF16),
        ],
        [VMEM] * 7,
        micros=4.0,
    )(w, low, sources, high, self_terms, right, c1)
    got = exchange(msg)

    first, second, cown, xmsg = call(
        image_kernel,
        [
            sds((rows + STATS, columns), BF16),
            sds((rows, columns), BF16),
            sds((ops * blocks * rank, columns), BF16),
            sds((SLICES * (body + STATS) + columns // LANES * STATS, LANES), BF16),
        ],
        [VMEM] * 6,
        [pltpu.VMEM((rows, columns), F32), pltpu.VMEM((blocks, body, columns), BF16)],
        micros=3.0,
    )(sources, image, edge, left, got, mixed)
    parts = across(xmsg)
    low0, high0 = ring(first)
    low1, high1 = ring(second)

    panels = all_blocks * size
    c2 = call(
        functools.partial(second_couple, panels, ops, rank, far),
        sds((SLICES, body + STATS + count * columns // LANES * STATS, LANES), BF16),
        [SMEM, SMEM] + [VMEM] * (1 + count),
        [pltpu.VMEM((ops, n * blocks * rank, LANES), BF16)],
    )(cols, group, held, *parts)
    c2 = exchange(c2)

    outs = sds((ops, rows, columns), F32)
    scratch = [
        pltpu.VMEM((3, rows, columns), BF16),
        pltpu.VMEM((blocks, body, columns), BF16),
        pltpu.VMEM((rows, columns), F32),
    ]
    images, heights, norms, aux = call(
        functools.partial(final_first, panels),
        [outs, sds((ops, columns), F32), sds((ops, columns), F32), sds((8, columns), F32)],
        [SMEM] + [VMEM] * 11,
        scratch + [pltpu.VMEM((n, STATS, columns), F32), pltpu.SemaphoreType.DMA((blocks,))],
        micros=4.0,
        megabytes=60,
        out_specs=[ANY, VMEM, VMEM, VMEM],
    )(group, w, low, sources, high, low0, first, high0, self_terms, left, cown, c2)
    images = call(
        final_second,
        outs,
        [ANY] + [VMEM] * 12,
        scratch + [pltpu.SemaphoreType.DMA((blocks,))],
        micros=4.0,
        megabytes=60,
        out_specs=ANY,
        alias={0: 0},
    )(images, w, low, sources, high, low1, second, high1, self_terms, left, cown, c2, aux)
    return images, heights, norms


def solution(mesh):
    placed = (
        P(("groups", "store"), None),
        P(None, "store"),
        P(None, "store", None, None, None),
        P("store", None),
        P("store"),
        P("store", None),
        P("store", None, None),
        P("store", None, None),
        P(None, "store", None, None, None),
    )
    return jax.shard_map(
        shards,
        mesh=mesh,
        in_specs=placed,
        out_specs=(P(None, ("groups", "store"), None), P("groups", None), P("groups", None)),
        check_vma=False,
    )
```

```python
import functools

import jax
import jax.numpy as jnp
from jax import lax
from jax.experimental import pallas as pl
from jax.experimental.pallas import tpu as pltpu
from jax.sharding import PartitionSpec as P

REACH = 2
EPSILON = 1e-06
LANES = 128
HALF = 64
SLICES = 8
STATS = 16
FLOP_RATE = 1150000000
F32 = jnp.float32
BF16 = jnp.bfloat16

VMEM = pl.BlockSpec(memory_space=pltpu.VMEM)
SMEM = pl.BlockSpec(memory_space=pltpu.SMEM)
ANY = pl.BlockSpec(memory_space=pl.ANY)


def call(body, out_shape, in_specs, scratch=(), micros=1.0, megabytes=20):
    many = isinstance(out_shape, (list, tuple))
    return pl.pallas_call(
        body,
        out_shape=out_shape,
        in_specs=in_specs,
        out_specs=[VMEM] * len(out_shape) if many else VMEM,
        scratch_shapes=list(scratch),
        compiler_params=pltpu.CompilerParams(vmem_limit_bytes=megabytes * 1024 * 1024),
        cost_estimate=pl.CostEstimate(
            flops=int(micros * FLOP_RATE), bytes_accessed=0, transcendentals=0
        ),
    )


def dot(a, b, dims=((1,), (0,))):
    return lax.dot_general(a, b, (dims, ((), ())), preferred_element_type=F32)


def split3(row):
    high = row.astype(BF16)
    rest = row - high.astype(F32)
    middle = rest.astype(BF16)
    low = (rest - middle.astype(F32)).astype(BF16)
    return [high, middle, low]


def join3(rows, at):
    return rows[..., 3 * at, :] + rows[..., 3 * at + 1, :] + rows[..., 3 * at + 2, :]


def row3(values, at):
    return values[3 * at:3 * at + 1] + values[3 * at + 1:3 * at + 2] + values[3 * at + 2:3 * at + 3]


def halves(x, y):
    left = lax.broadcasted_iota(jnp.int32, x.shape, x.ndim - 1) < HALF
    first = jnp.where(left, x, pltpu.roll(y, HALF, x.ndim - 1))
    second = jnp.where(left, pltpu.roll(x, HALF, x.ndim - 1), y)
    return first, second


def chunk(x, pair):
    return x[:, pair * LANES:(pair + 1) * LANES]


def order_tiles(all_blocks, cols, count, row0, tiles, out):
    ops, blocks, near, size, _ = tiles.shape
    for b in range(blocks):
        for k in range(near):
            rel = lax.rem(cols[b, k] - (row0[0] + b) + REACH + all_blocks, all_blocks)
            rel = lax.rem(rel, all_blocks)
            at = pl.multiple_of(rel * size, size)
            live = k < count[b]
            for o in range(ops):
                tile = tiles[o, b, k]
                out[b, o * size:(o + 1) * size, pl.ds(at, size)] = jnp.where(
                    live, tile, jnp.zeros_like(tile)
                )


def coeff_kernel(u, right, out):
    blocks, rank, size = right.shape
    z = [dot(right[b], u[b * size:(b + 1) * size, :]) for b in range(blocks)]
    for pair in range(SLICES // 2):
        first, second = halves(chunk(z[0], pair), chunk(z[1], pair))
        out[2 * pair] = first.astype(BF16)
        out[2 * pair + 1] = second.astype(BF16)


def pack_kernel(far_cols, coup, out):
    ops, blocks, far, rank, _ = coup.shape
    whole, rest = [], []
    for b in range(blocks):
        tiles = [
            jnp.concatenate([coup[o, b, f] for f in range(far)], axis=1) for o in range(ops)
        ]
        tiles = jnp.concatenate(tiles, axis=0)
        whole.append(tiles[:, :LANES])
        rest.append(tiles[:, LANES:])
    lane = lax.broadcasted_iota(jnp.int32, (STATS, LANES), 1)
    names = jnp.zeros((STATS, LANES), F32)
    for b in range(blocks):
        for f in range(far):
            names = jnp.where(lane == b * far + f, far_cols[b, f].astype(F32), names)
    out[...] = jnp.concatenate(
        whole + [jnp.concatenate(rest, axis=1), names.astype(BF16)], axis=0
    )


def share_kernel(packed, *refs):
    parts, out = refs[:-1], refs[-1]
    rows = packed.shape[0]
    rank = parts[0].shape[1]
    for s in range(SLICES):
        out[s, 0:rows, :] = packed[...]
    for m, part in enumerate(parts):
        out[:, rows + m * rank:rows + (m + 1) * rank, :] = part[...]


def copy_kernel(source, target):
    target[...] = source[...]


def coupling_rows(held, s, b, ops, rank):
    body = ops * rank
    first = held[s, b * body:(b + 1) * body, :]
    rest = held[s, 2 * body:3 * body, b * HALF:(b + 1) * HALF]
    return jnp.concatenate([first, rest], axis=1)


def couple(cols, held, s, b, ops, rank, far, z):
    at = (s * 2 + b) * far
    lhs = coupling_rows(held, s, b, ops, rank)
    starts = [pl.multiple_of(cols[at + f] * rank, rank) for f in range(far)]
    picked = [
        jnp.concatenate([x[pl.ds(start, rank), :] for start in starts], axis=0) for x in z
    ]
    if len(z) == 1:
        return dot(lhs, picked[0])
    return jnp.concatenate(
        [dot(lhs[o * rank:(o + 1) * rank], picked[o]) for o in range(ops)], axis=0
    )


def spread_rows(source, rank):
    count = source.shape[0]
    turned = pltpu.roll(source, HALF, 2)
    both = jnp.concatenate([source[:, None], turned[:, None]], axis=1)
    return both.reshape(count * 2 * rank, LANES).astype(BF16)


def held_part(held, m, ops, rank):
    at = 3 * ops * rank + STATS + m * rank
    return held[:, at:at + rank, :].astype(F32)


def group_at(group, m, groups, step):
    return pl.multiple_of(lax.rem(group[0] + (groups - m), groups) * step, step)


def first_couple(ops, rank, far, cols, group, held, out, zs):
    step = SLICES * 2 * rank
    count = zs.shape[0] // step
    for m in range(count):
        at = group_at(group, m, count, step)
        zs[pl.ds(at, step), :] = spread_rows(held_part(held, m, ops, rank), rank)
    for s in range(SLICES):
        c = [couple(cols, held, s, b, ops, rank, far, [zs]) for b in range(2)]
        out[s] = halves(c[0], c[1])[0].astype(BF16)


def take_coefs(cmsg, coef, rows):
    for pair in range(SLICES // 2):
        parts = halves(
            cmsg[2 * pair, 0:rows, :].astype(F32), cmsg[2 * pair + 1, 0:rows, :].astype(F32)
        )
        for b in range(2):
            coef[b, :, pair * LANES:(pair + 1) * LANES] = parts[b].astype(BF16)


def near_product(tiles, parts, b, blocks, size):
    total = None
    first = b - REACH
    at = 0
    for d, part in enumerate(parts):
        start = max((d - 1) * blocks, first)
        stop = min(d * blocks, first + 2 * REACH + 1)
        if stop <= start:
            continue
        begin = (start - (d - 1) * blocks) * size
        width = (stop - start) * size
        value = dot(tiles[:, at:at + width], part[begin:begin + width, :])
        total = value if total is None else total + value
        at += width
    return total


def diagonal_of(diag, o, b, size, columns):
    row = diag[o:o + 1, b * size:(b + 1) * size]
    column = jnp.transpose(jnp.broadcast_to(row, (LANES, size)))
    return jnp.concatenate([column] * (columns // LANES), axis=1)


def near_kernel(w, low, own, high, diag, image):
    ops, rows, columns = image.shape
    size = w.shape[1] // ops
    blocks = rows // size
    for b in range(blocks):
        product = near_product(w.at[b], (low, own, high), b, blocks, size)
        here = slice(b * size, (b + 1) * size)
        ub = own[here, :].astype(F32)
        for o in range(ops):
            image[o, here, :] = (
                product[o * size:(o + 1) * size] + diagonal_of(diag, o, b, size, columns) * ub
            )


def image_kernel(own, near, left, right, cmsg, out0, out1, mout, image, coef):
    ops = image.shape[0]
    blocks, rank, size = right.shape
    rows, columns = own.shape
    take_coefs(cmsg, coef, ops * rank)
    inner = [None] * ops
    squares = None
    for b in range(blocks):
        here = slice(b * size, (b + 1) * size)
        ub = own[here, :].astype(F32)
        part = jnp.sum(ub * ub, axis=0, keepdims=True)
        squares = part if squares is None else squares + part
        for o in range(ops):
            far = dot(left[b], coef[b, o * rank:(o + 1) * rank, :], ((0,), (0,)))
            value = near[o, here, :] + far.astype(BF16).astype(F32)
            image[o, here, :] = value
            part = jnp.sum(ub * value, axis=0, keepdims=True)
            inner[o] = part if inner[o] is None else inner[o] + part
    stats = []
    spreads = []
    good = squares > 0
    for o in range(ops):
        shift = jnp.where(good, inner[o] / jnp.where(good, squares, 1.0), 0.0)
        pieces = split3(shift)
        stats += pieces
        shift = pieces[0].astype(F32) + pieces[1].astype(F32) + pieces[2].astype(F32)
        spread = None
        z = []
        for b in range(blocks):
            ub = own[b * size:(b + 1) * size, :].astype(F32)
            v = image[o, b * size:(b + 1) * size, :] - shift * ub
            part = jnp.sum(v * v, axis=0, keepdims=True)
            spread = part if spread is None else spread + part
            v = v.astype(BF16)
            (out0, out1)[o][b * size:(b + 1) * size, :] = v
            z.append(dot(right[b], v))
        for pair in range(SLICES // 2):
            first, second = halves(chunk(z[0], pair), chunk(z[1], pair))
            mout[2 * pair, o * rank:(o + 1) * rank, :] = first.astype(BF16)
            mout[2 * pair + 1, o * rank:(o + 1) * rank, :] = second.astype(BF16)
        spreads.append(spread)
    zero = jnp.zeros((1, columns), BF16)
    out0[rows:, :] = jnp.concatenate(stats + [zero] * (STATS - len(stats)), axis=0)
    stats += split3(squares)
    for spread in spreads:
        stats += split3(spread)
    stats = jnp.concatenate(stats + [zero] * (STATS - len(stats)), axis=0).astype(F32)
    for pair in range(SLICES // 2):
        part = chunk(stats, pair)
        first, second = halves(part, part)
        mout[2 * pair, ops * rank:ops * rank + STATS, :] = first.astype(BF16)
        mout[2 * pair + 1, ops * rank:ops * rank + STATS, :] = second.astype(BF16)


def second_couple(panels, ops, rank, far, cols, group, after_low, after_high, held, *refs):
    msgs, (out, zs, st) = refs[:-3], refs[-3:]
    count = len(msgs)
    body = ops * rank
    step = SLICES * 2 * rank
    for m, msg in enumerate(msgs):
        at = group_at(group, m, count, SLICES)
        st[pl.ds(at, SLICES)] = msg[:, body:body + STATS, :].astype(F32)
    every = st[...]
    squares = join3(every, ops)
    scale_sq = jnp.sum(squares, axis=0, keepdims=True) / panels + EPSILON
    reverse = 1.0 / jnp.sqrt(scale_sq)
    heights, norms = [], []
    for o in range(ops):
        shift = join3(every, o)
        height = jnp.sum(shift * squares, axis=0, keepdims=True) / panels / scale_sq
        delta = shift - height
        spread = join3(every, ops + 1 + o) + delta * delta * squares
        norm = jnp.sqrt(jnp.sum(spread, axis=0, keepdims=True) / panels / scale_sq + EPSILON)
        heights.append(height)
        norms.append(norm)
    for m, msg in enumerate(msgs):
        at = group_at(group, m, count, step)
        mine = msg[:, body:body + STATS, :].astype(F32)
        base = held_part(held, m, ops, rank)
        for o in range(ops):
            delta = join3(mine, o) - heights[o]
            z = msg[:, o * rank:(o + 1) * rank, :].astype(F32) + delta[:, None, :] * base
            z = z * (reverse / norms[o])[None]
            zs[o, pl.ds(at, step), :] = spread_rows(z, rank)
    rows = []
    for row in heights + norms + [reverse]:
        rows += split3(row)
    rows += [jnp.zeros_like(rows[0])] * (STATS - len(rows))
    rows = jnp.concatenate(rows, axis=0)
    for s in range(SLICES):
        c = [couple(cols, held, s, b, ops, rank, far, [zs.at[o] for o in range(ops)]) for b in range(2)]
        out[s, 0:body, :] = halves(c[0], c[1])[0].astype(BF16)
        out[s, body:body + STATS, :] = rows


def final_kernel(
    w,
    ulow,
    uown,
    uhigh,
    low0,
    first,
    high0,
    low1,
    second,
    high1,
    diag,
    left,
    cmsg,
    images,
    heights,
    norms,
    ext,
    coef,
    stat,
):
    ops = images.shape[0]
    blocks, rank, size = left.shape
    rows, columns = uown.shape
    body = ops * rank
    take_coefs(cmsg, coef, body)
    for pair in range(SLICES // 2):
        stat[:, pair * LANES:(pair + 1) * LANES] = halves(
            cmsg[2 * pair, body:body + STATS, :].astype(F32),
            cmsg[2 * pair + 1, body:body + STATS, :].astype(F32),
        )[0]
    st = stat[...]
    reverse = row3(st, 2 * ops)
    for o in range(ops):
        height = row3(st, o)
        norm = row3(st, ops + o)
        heights[o:o + 1, :] = height
        norms[o:o + 1, :] = norm
        factor = reverse / norm
        triples = (ulow, low0, low1), (uown, first, second), (uhigh, high0, high1)
        for at, (u, v0, v1) in enumerate(triples):
            shift = row3(v0[rows:, :].astype(F32), o)
            change = (shift - height) * factor
            v = (v0, v1)[o][0:rows, :].astype(F32)
            value = v * factor + u[...].astype(F32) * change
            ext[o, at] = value.astype(BF16)
        for b in range(blocks):
            parts = [ext.at[o, at] for at in range(3)]
            product = near_product(w.at[b, o * size:(o + 1) * size], parts, b, blocks, size)
            far = dot(left[b], coef[b, o * rank:(o + 1) * rank, :], ((0,), (0,)))
            mine = ext[o, 1, b * size:(b + 1) * size, :].astype(F32)
            images[o, b * size:(b + 1) * size, :] = (
                product
                + diagonal_of(diag, o, b, size, columns) * mine
                + far.astype(BF16).astype(F32)
            )


def ring(block):
    count = lax.axis_size("store")
    forward = [(i, (i + 1) % count) for i in range(count)]
    backward = [(target, source) for source, target in forward]
    return lax.ppermute(block, "store", forward), lax.ppermute(block, "store", backward)


def shards(
    sources,
    self_terms,
    near_tiles,
    near_cols,
    near_count,
    far_cols,
    basis_left,
    basis_right,
    couplings,
):
    n = lax.axis_size("store")
    ops, blocks, near, size, _ = near_tiles.shape
    rank = basis_left.shape[2]
    far = far_cols.shape[1]
    rows, columns = sources.shape
    all_blocks = blocks * n
    count = n // SLICES
    groups = [[g * SLICES + s for s in range(SLICES)] for g in range(count)]
    sds = jax.ShapeDtypeStruct
    body = ops * rank

    def exchange(x):
        return lax.all_to_all(x, "store", 0, 0, axis_index_groups=groups, tiled=True)

    def across(x):
        parts = [x]
        for m in range(1, count):
            pairs = [(i, (i + m * SLICES) % n) for i in range(n)]
            parts.append(lax.ppermute(x, "store", pairs))
        return parts

    place = lax.axis_index("store").astype(jnp.int32)
    row0 = (place * blocks).reshape(1)
    group = lax.div(place, jnp.int32(SLICES)).reshape(1)
    left = jnp.transpose(basis_left, (0, 2, 1))
    right = jnp.transpose(basis_right, (0, 2, 1))

    low, high = ring(sources)
    z1 = call(coeff_kernel, sds((SLICES, rank, LANES), BF16), [VMEM, VMEM], megabytes=60)(
        sources, right
    )
    z1 = across(z1)
    shared = (blocks + 1) * body
    packed = call(pack_kernel, sds((shared + STATS, LANES), BF16), [SMEM, VMEM])(
        far_cols, couplings
    )
    held = call(
        share_kernel,
        sds((SLICES, shared + STATS + count * rank, LANES), BF16),
        [VMEM] * (1 + count),
    )(packed, *z1)
    held = exchange(held)
    cols = held[:, shared, :blocks * far].astype(jnp.int32).reshape(-1)

    w = call(
        functools.partial(order_tiles, all_blocks),
        sds((blocks, ops * size, near * size), BF16),
        [SMEM, SMEM, SMEM, VMEM],
        micros=2.5,
    )(near_cols, near_count, row0, near_tiles)

    c1 = call(
        functools.partial(first_couple, ops, rank, far),
        sds((SLICES, body, LANES), BF16),
        [SMEM, SMEM, VMEM],
        [pltpu.VMEM((n * blocks * rank, LANES), BF16)],
    )(cols, group, held)
    c1 = exchange(c1)

    image = call(near_kernel, sds((ops, rows, columns), F32), [VMEM] * 5, micros=3.0)(
        w, low, sources, high, self_terms
    )
    first, second, msg = call(
        image_kernel,
        [
            sds((rows + STATS, columns), BF16),
            sds((rows, columns), BF16),
            sds((SLICES, body + STATS, LANES), BF16),
        ],
        [VMEM] * 5,
        [
            pltpu.VMEM((ops, rows, columns), F32),
            pltpu.VMEM((blocks, body, columns), BF16),
        ],
        micros=2.0,
    )(sources, image, left, right, c1)
    msg = exchange(msg)
    msgs = across(call(copy_kernel, sds(msg.shape, BF16), [VMEM], micros=30.0)(msg))
    low0, high0 = ring(first)
    low1, high1 = ring(second)

    c2 = call(
        functools.partial(second_couple, all_blocks * size, ops, rank, far),
        sds((SLICES, body + STATS, LANES), BF16),
        [SMEM, SMEM, ANY, ANY] + [VMEM] * (1 + count),
        [
            pltpu.VMEM((ops, n * blocks * rank, LANES), BF16),
            pltpu.VMEM((n, STATS, LANES), F32),
        ],
        micros=30.0,
    )(cols, group, low0, high0, held, *msgs)
    c2 = exchange(c2)

    images, heights, norms = call(
        final_kernel,
        [sds((ops, rows, columns), F32), sds((ops, columns), F32), sds((ops, columns), F32)],
        [VMEM] * 13,
        [
            pltpu.VMEM((ops, 3, rows, columns), BF16),
            pltpu.VMEM((blocks, body, columns), BF16),
            pltpu.VMEM((STATS, columns), F32),
        ],
        micros=4.0,
    )(w, low, sources, high, low0, first, high0, low1, second, high1, self_terms, left, c2)
    return images, heights, norms


def solution(mesh):
    placed = (
        P(("groups", "store"), None),
        P(None, "store"),
        P(None, "store", None, None, None),
        P("store", None),
        P("store"),
        P("store", None),
        P("store", None, None),
        P("store", None, None),
        P(None, "store", None, None, None),
    )
    return jax.shard_map(
        shards,
        mesh=mesh,
        in_specs=placed,
        out_specs=(P(None, ("groups", "store"), None), P("groups", None), P("groups", None)),
        check_vma=False,
    )
```

```python
import functools

import jax
import jax.numpy as jnp
from jax import lax
from jax.experimental import pallas as pl
from jax.experimental.pallas import tpu as pltpu
from jax.sharding import PartitionSpec as P

REACH = 2
EPSILON = 1e-06
LANES = 128
HALF = 64
SLICES = 8
STATS = 16
FLOP_RATE = 1150000000
F32 = jnp.float32
BF16 = jnp.bfloat16

VMEM = pl.BlockSpec(memory_space=pltpu.VMEM)
SMEM = pl.BlockSpec(memory_space=pltpu.SMEM)
ANY = pl.BlockSpec(memory_space=pl.ANY)


def call(body, out_shape, in_specs, scratch=(), micros=1.0, megabytes=20, out_specs=None):
    many = isinstance(out_shape, (list, tuple))
    if out_specs is None:
        out_specs = [VMEM] * len(out_shape) if many else VMEM
    return pl.pallas_call(
        body,
        out_shape=out_shape,
        in_specs=in_specs,
        out_specs=out_specs,
        scratch_shapes=list(scratch),
        compiler_params=pltpu.CompilerParams(vmem_limit_bytes=megabytes * 1024 * 1024),
        cost_estimate=pl.CostEstimate(
            flops=int(micros * FLOP_RATE), bytes_accessed=0, transcendentals=0
        ),
    )


def dot(a, b, dims=((1,), (0,))):
    return lax.dot_general(a, b, (dims, ((), ())), preferred_element_type=F32)


def split3(row):
    high = row.astype(BF16)
    rest = row - high.astype(F32)
    middle = rest.astype(BF16)
    low = (rest - middle.astype(F32)).astype(BF16)
    return [high, middle, low]


def join3(rows, at):
    return rows[..., 3 * at, :] + rows[..., 3 * at + 1, :] + rows[..., 3 * at + 2, :]


def row3(values, at):
    return values[3 * at:3 * at + 1] + values[3 * at + 1:3 * at + 2] + values[3 * at + 2:3 * at + 3]


def halves(x, y):
    left = lax.broadcasted_iota(jnp.int32, x.shape, x.ndim - 1) < HALF
    first = jnp.where(left, x, pltpu.roll(y, HALF, x.ndim - 1))
    second = jnp.where(left, pltpu.roll(x, HALF, x.ndim - 1), y)
    return first, second


def chunk(x, pair):
    return x[:, pair * LANES:(pair + 1) * LANES]


def fetch_tiles(all_blocks, cols, count, row0, tiles, w, sems):
    ops, blocks, near, size, _ = tiles.shape
    steps = []
    for b in range(blocks):
        for k in range(near):
            rel = lax.rem(cols[b, k] - (row0[0] + b) + REACH + all_blocks, all_blocks)
            at = pl.multiple_of(lax.rem(rel, all_blocks) * size, size)
            live = k < count[b]
            for o in range(ops):
                place = w.at[b, o * size:(o + 1) * size, pl.ds(at, size)]
                copy = pltpu.make_async_copy(tiles.at[o, b, k], place, sems.at[b, k, o])
                steps.append((live, copy, place))
    for live, copy, place in steps:

        @pl.when(live)
        def _(copy=copy):
            copy.start()

        @pl.when(jnp.logical_not(live))
        def _(place=place):
            place[...] = jnp.zeros_like(place)

    def wait():
        for live, copy, _ in steps:

            @pl.when(live)
            def _(copy=copy):
                copy.wait()

    return wait


def coeff_kernel(far_cols, u, right, coup, z_out, out):
    ops, blocks, far, rank, _ = coup.shape
    size = right.shape[2]
    z = [dot(right[b], u[b * size:(b + 1) * size, :]) for b in range(blocks)]
    for pair in range(SLICES // 2):
        first, second = halves(chunk(z[0], pair), chunk(z[1], pair))
        z_out[2 * pair] = first.astype(BF16)
        z_out[2 * pair + 1] = second.astype(BF16)
    whole, rest = [], []
    for b in range(blocks):
        tiles = [
            jnp.concatenate([coup[o, b, f] for f in range(far)], axis=1) for o in range(ops)
        ]
        tiles = jnp.concatenate(tiles, axis=0)
        whole.append(tiles[:, :LANES])
        rest.append(tiles[:, LANES:])
    lane = lax.broadcasted_iota(jnp.int32, (STATS, LANES), 1)
    names = jnp.zeros((STATS, LANES), F32)
    for b in range(blocks):
        for f in range(far):
            names = jnp.where(lane == b * far + f, far_cols[b, f].astype(F32), names)
    out[...] = jnp.concatenate(
        whole + [jnp.concatenate(rest, axis=1), names.astype(BF16)], axis=0
    )


def share_kernel(packed, *refs):
    parts, out = refs[:-1], refs[-1]
    rows = packed.shape[0]
    rank = parts[0].shape[1]
    for s in range(SLICES):
        out[s, 0:rows, :] = packed[...]
    for m, part in enumerate(parts):
        out[:, rows + m * rank:rows + (m + 1) * rank, :] = part[...]


def coupling_rows(held, s, b, ops, rank):
    body = ops * rank
    first = held[s, b * body:(b + 1) * body, :]
    rest = held[s, 2 * body:3 * body, b * HALF:(b + 1) * HALF]
    return jnp.concatenate([first, rest], axis=1)


def couple(cols, held, s, b, ops, rank, far, z):
    at = (s * 2 + b) * far
    lhs = coupling_rows(held, s, b, ops, rank)
    starts = [pl.multiple_of(cols[at + f] * rank, rank) for f in range(far)]
    picked = [
        jnp.concatenate([x[pl.ds(start, rank), :] for start in starts], axis=0) for x in z
    ]
    if len(z) == 1:
        return dot(lhs, picked[0])
    return jnp.concatenate(
        [dot(lhs[o * rank:(o + 1) * rank], picked[o]) for o in range(ops)], axis=0
    )


def spread_rows(source, rank):
    count = source.shape[0]
    turned = pltpu.roll(source, HALF, 2)
    both = jnp.concatenate([source[:, None], turned[:, None]], axis=1)
    return both.reshape(count * 2 * rank, LANES).astype(BF16)


def held_part(held, m, ops, rank):
    at = 3 * ops * rank + STATS + m * rank
    return held[:, at:at + rank, :].astype(F32)


def group_at(group, m, groups, step):
    return pl.multiple_of(lax.rem(group[0] + (groups - m), groups) * step, step)


def first_couple(ops, rank, far, cols, group, held, out, zs):
    step = SLICES * 2 * rank
    count = zs.shape[0] // step
    for m in range(count):
        at = group_at(group, m, count, step)
        zs[pl.ds(at, step), :] = spread_rows(held_part(held, m, ops, rank), rank)
    for s in range(SLICES):
        c = [couple(cols, held, s, b, ops, rank, far, [zs]) for b in range(2)]
        out[s] = halves(c[0], c[1])[0].astype(BF16)


def take_coefs(cmsg, coef, rows):
    for pair in range(SLICES // 2):
        parts = halves(
            cmsg[2 * pair, 0:rows, :].astype(F32), cmsg[2 * pair + 1, 0:rows, :].astype(F32)
        )
        for b in range(2):
            coef[b, :, pair * LANES:(pair + 1) * LANES] = parts[b].astype(BF16)


def near_product(tiles, parts, b, blocks, size):
    total = None
    first = b - REACH
    at = 0
    for d, part in enumerate(parts):
        start = max((d - 1) * blocks, first)
        stop = min(d * blocks, first + 2 * REACH + 1)
        if stop <= start:
            continue
        begin = (start - (d - 1) * blocks) * size
        width = (stop - start) * size
        value = dot(tiles[:, at:at + width], part[begin:begin + width, :])
        total = value if total is None else total + value
        at += width
    return total


def diagonal_of(diag, o, b, size, columns):
    row = diag[o:o + 1, b * size:(b + 1) * size]
    column = jnp.transpose(jnp.broadcast_to(row, (LANES, size)))
    return jnp.concatenate([column] * (columns // LANES), axis=1)


def image_kernel(
    all_blocks,
    cols,
    count,
    row0,
    tiles,
    low,
    own,
    high,
    diag,
    left,
    right,
    cmsg,
    vout,
    mout,
    image,
    coef,
    w,
    sems,
):
    wait = fetch_tiles(all_blocks, cols, count, row0, tiles, w, sems)
    ops = image.shape[0]
    blocks, rank, size = right.shape
    rows, columns = own.shape
    take_coefs(cmsg, coef, ops * rank)
    wait()
    inner = [None] * ops
    squares = None
    for b in range(blocks):
        product = near_product(w.at[b], (low, own, high), b, blocks, size)
        ub = own[b * size:(b + 1) * size, :].astype(F32)
        part = jnp.sum(ub * ub, axis=0, keepdims=True)
        squares = part if squares is None else squares + part
        for o in range(ops):
            far = dot(left[b], coef[b, o * rank:(o + 1) * rank, :], ((0,), (0,)))
            value = (
                product[o * size:(o + 1) * size]
                + diagonal_of(diag, o, b, size, columns) * ub
                + far.astype(BF16).astype(F32)
            )
            image[o, b * size:(b + 1) * size, :] = value
            part = jnp.sum(ub * value, axis=0, keepdims=True)
            inner[o] = part if inner[o] is None else inner[o] + part
    stats = []
    spreads = []
    good = squares > 0
    for o in range(ops):
        shift = jnp.where(good, inner[o] / jnp.where(good, squares, 1.0), 0.0)
        pieces = split3(shift)
        stats += pieces
        shift = pieces[0].astype(F32) + pieces[1].astype(F32) + pieces[2].astype(F32)
        spread = None
        z = []
        for b in range(blocks):
            ub = own[b * size:(b + 1) * size, :].astype(F32)
            v = image[o, b * size:(b + 1) * size, :] - shift * ub
            part = jnp.sum(v * v, axis=0, keepdims=True)
            spread = part if spread is None else spread + part
            v = v.astype(BF16)
            vout[(o * blocks + b) * size:(o * blocks + b + 1) * size, :] = v
            z.append(dot(right[b], v))
        for pair in range(SLICES // 2):
            first, second = halves(chunk(z[0], pair), chunk(z[1], pair))
            mout[2 * pair, o * rank:(o + 1) * rank, :] = first.astype(BF16)
            mout[2 * pair + 1, o * rank:(o + 1) * rank, :] = second.astype(BF16)
        spreads.append(spread)
    zero = jnp.zeros((1, columns), BF16)
    vout[ops * rows:, :] = jnp.concatenate(stats + [zero] * (STATS - len(stats)), axis=0)
    stats += split3(squares)
    for spread in spreads:
        stats += split3(spread)
    stats = jnp.concatenate(stats + [zero] * (STATS - len(stats)), axis=0).astype(F32)
    for pair in range(SLICES // 2):
        part = chunk(stats, pair)
        first, second = halves(part, part)
        mout[2 * pair, ops * rank:ops * rank + STATS, :] = first.astype(BF16)
        mout[2 * pair + 1, ops * rank:ops * rank + STATS, :] = second.astype(BF16)


def second_couple(panels, ops, rank, far, cols, group, held, *refs):
    msgs, (out, zs, st) = refs[:-3], refs[-3:]
    count = len(msgs)
    body = ops * rank
    step = SLICES * 2 * rank
    for m, msg in enumerate(msgs):
        at = group_at(group, m, count, SLICES)
        st[pl.ds(at, SLICES)] = msg[:, body:body + STATS, :].astype(F32)
    every = st[...]
    squares = join3(every, ops)
    scale_sq = jnp.sum(squares, axis=0, keepdims=True) / panels + EPSILON
    reverse = 1.0 / jnp.sqrt(scale_sq)
    heights, norms = [], []
    for o in range(ops):
        shift = join3(every, o)
        height = jnp.sum(shift * squares, axis=0, keepdims=True) / panels / scale_sq
        delta = shift - height
        spread = join3(every, ops + 1 + o) + delta * delta * squares
        norm = jnp.sqrt(jnp.sum(spread, axis=0, keepdims=True) / panels / scale_sq + EPSILON)
        heights.append(height)
        norms.append(norm)
    for m, msg in enumerate(msgs):
        at = group_at(group, m, count, step)
        mine = msg[:, body:body + STATS, :].astype(F32)
        base = held_part(held, m, ops, rank)
        for o in range(ops):
            delta = join3(mine, o) - heights[o]
            z = msg[:, o * rank:(o + 1) * rank, :].astype(F32) + delta[:, None, :] * base
            z = z * (reverse / norms[o])[None]
            zs[o, pl.ds(at, step), :] = spread_rows(z, rank)
    rows = []
    for row in heights + norms + [reverse]:
        rows += split3(row)
    rows += [jnp.zeros_like(rows[0])] * (STATS - len(rows))
    rows = jnp.concatenate(rows, axis=0)
    for s in range(SLICES):
        c = [couple(cols, held, s, b, ops, rank, far, [zs.at[o] for o in range(ops)]) for b in range(2)]
        out[s, 0:body, :] = halves(c[0], c[1])[0].astype(BF16)
        out[s, body:body + STATS, :] = rows


def final_kernel(
    all_blocks,
    cols,
    count,
    row0,
    tiles,
    ulow,
    uown,
    uhigh,
    vlow,
    vown,
    vhigh,
    diag,
    left,
    cmsg,
    images,
    heights,
    norms,
    ext,
    coef,
    stat,
    out,
    w,
    sems,
    outs,
):
    wait = fetch_tiles(all_blocks, cols, count, row0, tiles, w, sems)
    copies = []
    ops = images.shape[0]
    blocks, rank, size = left.shape
    rows, columns = uown.shape
    body = ops * rank
    take_coefs(cmsg, coef, body)
    for pair in range(SLICES // 2):
        stat[:, pair * LANES:(pair + 1) * LANES] = halves(
            cmsg[2 * pair, body:body + STATS, :].astype(F32),
            cmsg[2 * pair + 1, body:body + STATS, :].astype(F32),
        )[0]
    st = stat[...]
    reverse = row3(st, 2 * ops)
    for o in range(ops):
        height = row3(st, o)
        norm = row3(st, ops + o)
        heights[o:o + 1, :] = height
        norms[o:o + 1, :] = norm
        factor = reverse / norm
        for at, (u, v) in enumerate(((ulow, vlow), (uown, vown), (uhigh, vhigh))):
            shift = row3(v[ops * rows:, :].astype(F32), o)
            change = (shift - height) * factor
            value = v[o * rows:(o + 1) * rows, :].astype(F32) * factor + u[...].astype(F32) * change
            ext[o, at] = value.astype(BF16)
        if o == 0:
            wait()
        for b in range(blocks):
            parts = [ext.at[o, at] for at in range(3)]
            product = near_product(w.at[b, o * size:(o + 1) * size], parts, b, blocks, size)
            far = dot(left[b], coef[b, o * rank:(o + 1) * rank, :], ((0,), (0,)))
            mine = ext[o, 1, b * size:(b + 1) * size, :].astype(F32)
            here = slice(b * size, (b + 1) * size)
            out[o, here, :] = (
                product
                + diagonal_of(diag, o, b, size, columns) * mine
                + far.astype(BF16).astype(F32)
            )
            copy = pltpu.make_async_copy(out.at[o, here], images.at[o, here], outs.at[o, b])
            copy.start()
            copies.append(copy)
    for copy in copies:
        copy.wait()


def ring(block):
    count = lax.axis_size("store")
    forward = [(i, (i + 1) % count) for i in range(count)]
    backward = [(target, source) for source, target in forward]
    return lax.ppermute(block, "store", forward), lax.ppermute(block, "store", backward)


def shards(
    sources,
    self_terms,
    near_tiles,
    near_cols,
    near_count,
    far_cols,
    basis_left,
    basis_right,
    couplings,
):
    n = lax.axis_size("store")
    ops, blocks, near, size, _ = near_tiles.shape
    rank = basis_left.shape[2]
    far = far_cols.shape[1]
    rows, columns = sources.shape
    all_blocks = blocks * n
    count = n // SLICES
    groups = [[g * SLICES + s for s in range(SLICES)] for g in range(count)]
    sds = jax.ShapeDtypeStruct
    body = ops * rank

    def exchange(x):
        return lax.all_to_all(x, "store", 0, 0, axis_index_groups=groups, tiled=True)

    def across(x):
        parts = [x]
        for m in range(1, count):
            pairs = [(i, (i + m * SLICES) % n) for i in range(n)]
            parts.append(lax.ppermute(x, "store", pairs))
        return parts

    place = lax.axis_index("store").astype(jnp.int32)
    row0 = (place * blocks).reshape(1)
    group = lax.div(place, jnp.int32(SLICES)).reshape(1)
    left = jnp.transpose(basis_left, (0, 2, 1))
    right = jnp.transpose(basis_right, (0, 2, 1))

    low, high = ring(sources)
    shared = (blocks + 1) * body
    z1, packed = call(
        coeff_kernel,
        [sds((SLICES, rank, LANES), BF16), sds((shared + STATS, LANES), BF16)],
        [SMEM, VMEM, VMEM, VMEM],
        megabytes=60,
    )(far_cols, sources, right, couplings)
    z1 = across(z1)
    held = call(
        share_kernel,
        sds((SLICES, shared + STATS + count * rank, LANES), BF16),
        [VMEM] * (1 + count),
    )(packed, *z1)
    held = exchange(held)
    cols = held[:, shared, :blocks * far].astype(jnp.int32).reshape(-1)

    c1 = call(
        functools.partial(first_couple, ops, rank, far),
        sds((SLICES, body, LANES), BF16),
        [SMEM, SMEM, VMEM],
        [pltpu.VMEM((n * blocks * rank, LANES), BF16)],
    )(cols, group, held)
    c1 = exchange(c1)

    places = [SMEM, SMEM, SMEM, ANY]
    tile_scratch = [
        pltpu.VMEM((blocks, ops * size, near * size), BF16),
        pltpu.SemaphoreType.DMA((blocks, near, ops)),
    ]
    v, msg = call(
        functools.partial(image_kernel, all_blocks),
        [sds((ops * rows + STATS, columns), BF16), sds((SLICES, body + STATS, LANES), BF16)],
        places + [VMEM] * 7,
        [
            pltpu.VMEM((ops, rows, columns), F32),
            pltpu.VMEM((blocks, body, columns), BF16),
        ]
        + tile_scratch,
        micros=4.0,
    )(near_cols, near_count, row0, near_tiles, low, sources, high, self_terms, left, right, c1)
    msgs = across(exchange(msg))
    vlow, vhigh = ring(v)

    c2 = call(
        functools.partial(second_couple, all_blocks * size, ops, rank, far),
        sds((SLICES, body + STATS, LANES), BF16),
        [SMEM, SMEM] + [VMEM] * (1 + count),
        [
            pltpu.VMEM((ops, n * blocks * rank, LANES), BF16),
            pltpu.VMEM((n, STATS, LANES), F32),
        ],
        micros=30.0,
    )(cols, group, held, *msgs)
    c2 = exchange(c2)

    images, heights, norms = call(
        functools.partial(final_kernel, all_blocks),
        [sds((ops, rows, columns), F32), sds((ops, columns), F32), sds((ops, columns), F32)],
        places + [VMEM] * 9,
        [
            pltpu.VMEM((ops, 3, rows, columns), BF16),
            pltpu.VMEM((blocks, body, columns), BF16),
            pltpu.VMEM((STATS, columns), F32),
            pltpu.VMEM((ops, rows, columns), F32),
        ]
        + tile_scratch
        + [pltpu.SemaphoreType.DMA((ops, blocks))],
        micros=4.0,
        out_specs=[ANY, VMEM, VMEM],
    )(
        near_cols,
        near_count,
        row0,
        near_tiles,
        low,
        sources,
        high,
        vlow,
        v,
        vhigh,
        self_terms,
        left,
        c2,
    )
    return images, heights, norms


def solution(mesh):
    placed = (
        P(("groups", "store"), None),
        P(None, "store"),
        P(None, "store", None, None, None),
        P("store", None),
        P("store"),
        P("store", None),
        P("store", None, None),
        P("store", None, None),
        P(None, "store", None, None, None),
    )
    return jax.shard_map(
        shards,
        mesh=mesh,
        in_specs=placed,
        out_specs=(P(None, ("groups", "store"), None), P("groups", None), P("groups", None)),
        check_vma=False,
    )
```

```python
import functools

import jax
import jax.numpy as jnp
from jax import lax
from jax.experimental import pallas as pl
from jax.experimental.pallas import tpu as pltpu
from jax.sharding import PartitionSpec as P

REACH = 2
EPSILON = 1e-06
LANES = 128
HALF = 64
SLICES = 8
STATS = 16
FLOP_RATE = 1150000000
F32 = jnp.float32
BF16 = jnp.bfloat16

VMEM = pl.BlockSpec(memory_space=pltpu.VMEM)
SMEM = pl.BlockSpec(memory_space=pltpu.SMEM)
ANY = pl.BlockSpec(memory_space=pl.ANY)


def call(body, out_shape, in_specs, scratch=(), micros=1.0, megabytes=20, out_specs=None):
    many = isinstance(out_shape, (list, tuple))
    if out_specs is None:
        out_specs = [VMEM] * len(out_shape) if many else VMEM
    return pl.pallas_call(
        body,
        out_shape=out_shape,
        in_specs=in_specs,
        out_specs=out_specs,
        scratch_shapes=list(scratch),
        compiler_params=pltpu.CompilerParams(vmem_limit_bytes=megabytes * 1024 * 1024),
        cost_estimate=pl.CostEstimate(
            flops=int(micros * FLOP_RATE), bytes_accessed=0, transcendentals=0
        ),
    )


def dot(a, b, dims=((1,), (0,))):
    return lax.dot_general(a, b, (dims, ((), ())), preferred_element_type=F32)


def split3(row):
    high = row.astype(BF16)
    rest = row - high.astype(F32)
    middle = rest.astype(BF16)
    low = (rest - middle.astype(F32)).astype(BF16)
    return [high, middle, low]


def join3(rows, at):
    return rows[..., 3 * at, :] + rows[..., 3 * at + 1, :] + rows[..., 3 * at + 2, :]


def row3(values, at):
    return values[3 * at:3 * at + 1] + values[3 * at + 1:3 * at + 2] + values[3 * at + 2:3 * at + 3]


def halves(x, y):
    left = lax.broadcasted_iota(jnp.int32, x.shape, x.ndim - 1) < HALF
    first = jnp.where(left, x, pltpu.roll(y, HALF, x.ndim - 1))
    second = jnp.where(left, pltpu.roll(x, HALF, x.ndim - 1), y)
    return first, second


def chunk(x, pair):
    return x[:, pair * LANES:(pair + 1) * LANES]


def order_tiles(all_blocks, cols, count, row0, tiles, out):
    ops, blocks, near, size, _ = tiles.shape
    for b in range(blocks):
        for k in range(near):
            rel = lax.rem(cols[b, k] - (row0[0] + b) + REACH + all_blocks, all_blocks)
            rel = lax.rem(rel, all_blocks)
            at = pl.multiple_of(rel * size, size)
            live = k < count[b]
            for o in range(ops):
                tile = tiles[o, b, k]
                out[b, o * size:(o + 1) * size, pl.ds(at, size)] = jnp.where(
                    live, tile, jnp.zeros_like(tile)
                )


def coeff_kernel(count, far_cols, u, right, coup, z_out, out):
    ops, blocks, far, rank, _ = coup.shape
    size = right.shape[2]
    z = [dot(right[b], u[b * size:(b + 1) * size, :]) for b in range(blocks)]
    for pair in range(SLICES // 2):
        first, second = halves(chunk(z[0], pair), chunk(z[1], pair))
        z_out[2 * pair] = first.astype(BF16)
        z_out[2 * pair + 1] = second.astype(BF16)
    whole, rest = [], []
    for b in range(blocks):
        tiles = [
            jnp.concatenate([coup[o, b, f] for f in range(far)], axis=1) for o in range(ops)
        ]
        tiles = jnp.concatenate(tiles, axis=0)
        whole.append(tiles[:, :LANES])
        rest.append(tiles[:, LANES:])
    lane = lax.broadcasted_iota(jnp.int32, (STATS, LANES), 1)
    names = jnp.zeros((STATS, LANES), F32)
    for b in range(blocks):
        for f in range(far):
            col = far_cols[b, f]
            device = lax.div(col, blocks)
            slot = lax.rem(device, count) * SLICES + lax.div(device, count)
            name = (slot * blocks + lax.rem(col, blocks)).astype(F32)
            names = jnp.where(lane == b * far + f, name, names)
    out[...] = jnp.concatenate(
        whole + [jnp.concatenate(rest, axis=1), names.astype(BF16)], axis=0
    )


def share_kernel(packed, *refs):
    parts, out = refs[:-1], refs[-1]
    rows = packed.shape[0]
    rank = parts[0].shape[1]
    for s in range(SLICES):
        out[s, 0:rows, :] = packed[...]
    for m, part in enumerate(parts):
        out[:, rows + m * rank:rows + (m + 1) * rank, :] = part[...]


def coupling_rows(held, s, b, ops, rank):
    body = ops * rank
    first = held[s, b * body:(b + 1) * body, :]
    rest = held[s, 2 * body:3 * body, b * HALF:(b + 1) * HALF]
    return jnp.concatenate([first, rest], axis=1)


def couple(cols, held, s, b, ops, rank, far, z):
    at = (s * 2 + b) * far
    lhs = coupling_rows(held, s, b, ops, rank)
    starts = [pl.multiple_of(cols[at + f] * rank, rank) for f in range(far)]
    picked = [
        jnp.concatenate([x[pl.ds(start, rank), :] for start in starts], axis=0) for x in z
    ]
    if len(z) == 1:
        return dot(lhs, picked[0])
    return jnp.concatenate(
        [dot(lhs[o * rank:(o + 1) * rank], picked[o]) for o in range(ops)], axis=0
    )


def spread_rows(source, rank):
    count = source.shape[0]
    turned = pltpu.roll(source, HALF, 2)
    both = jnp.concatenate([source[:, None], turned[:, None]], axis=1)
    return both.reshape(count * 2 * rank, LANES).astype(BF16)


def held_part(held, m, ops, rank):
    at = 3 * ops * rank + STATS + m * rank
    return held[:, at:at + rank, :].astype(F32)


def group_at(group, m, groups, step):
    return pl.multiple_of(lax.rem(group[0] + (groups - m), groups) * step, step)


def first_couple(ops, rank, far, cols, group, held, out, zs):
    step = SLICES * 2 * rank
    count = zs.shape[0] // step
    for m in range(count):
        at = group_at(group, m, count, step)
        zs[pl.ds(at, step), :] = spread_rows(held_part(held, m, ops, rank), rank)
    for s in range(SLICES):
        c = [couple(cols, held, s, b, ops, rank, far, [zs]) for b in range(2)]
        out[s] = halves(c[0], c[1])[0].astype(BF16)


def take_coefs(cmsg, coef, rows):
    for pair in range(SLICES // 2):
        parts = halves(
            cmsg[2 * pair, 0:rows, :].astype(F32), cmsg[2 * pair + 1, 0:rows, :].astype(F32)
        )
        for b in range(2):
            coef[b, :, pair * LANES:(pair + 1) * LANES] = parts[b].astype(BF16)


def near_product(tiles, parts, b, blocks, size):
    total = None
    first = b - REACH
    at = 0
    for d, part in enumerate(parts):
        start = max((d - 1) * blocks, first)
        stop = min(d * blocks, first + 2 * REACH + 1)
        if stop <= start:
            continue
        begin = (start - (d - 1) * blocks) * size
        width = (stop - start) * size
        value = dot(tiles[:, at:at + width], part[begin:begin + width, :])
        total = value if total is None else total + value
        at += width
    return total


def diagonal_of(diag, o, b, size, columns):
    row = diag[o:o + 1, b * size:(b + 1) * size]
    column = jnp.transpose(jnp.broadcast_to(row, (LANES, size)))
    return jnp.concatenate([column] * (columns // LANES), axis=1)


def image_kernel(w, low, own, high, diag, left, right, cmsg, vout, mout, image, coef):
    ops = image.shape[0]
    blocks, rank, size = right.shape
    rows, columns = own.shape
    take_coefs(cmsg, coef, ops * rank)
    inner = [None] * ops
    squares = None
    for b in range(blocks):
        product = near_product(w.at[b], (low, own, high), b, blocks, size)
        ub = own[b * size:(b + 1) * size, :].astype(F32)
        part = jnp.sum(ub * ub, axis=0, keepdims=True)
        squares = part if squares is None else squares + part
        for o in range(ops):
            far = dot(left[b], coef[b, o * rank:(o + 1) * rank, :], ((0,), (0,)))
            value = (
                product[o * size:(o + 1) * size]
                + diagonal_of(diag, o, b, size, columns) * ub
                + far.astype(BF16).astype(F32)
            )
            image[o, b * size:(b + 1) * size, :] = value
            part = jnp.sum(ub * value, axis=0, keepdims=True)
            inner[o] = part if inner[o] is None else inner[o] + part
    stats = []
    spreads = []
    good = squares > 0
    for o in range(ops):
        shift = jnp.where(good, inner[o] / jnp.where(good, squares, 1.0), 0.0)
        pieces = split3(shift)
        stats += pieces
        shift = pieces[0].astype(F32) + pieces[1].astype(F32) + pieces[2].astype(F32)
        spread = None
        z = []
        for b in range(blocks):
            ub = own[b * size:(b + 1) * size, :].astype(F32)
            v = image[o, b * size:(b + 1) * size, :] - shift * ub
            part = jnp.sum(v * v, axis=0, keepdims=True)
            spread = part if spread is None else spread + part
            v = v.astype(BF16)
            vout[(o * blocks + b) * size:(o * blocks + b + 1) * size, :] = v
            z.append(dot(right[b], v))
        for pair in range(SLICES // 2):
            first, second = halves(chunk(z[0], pair), chunk(z[1], pair))
            mout[2 * pair, o * rank:(o + 1) * rank, :] = first.astype(BF16)
            mout[2 * pair + 1, o * rank:(o + 1) * rank, :] = second.astype(BF16)
        spreads.append(spread)
    zero = jnp.zeros((1, columns), BF16)
    vout[ops * rows:, :] = jnp.concatenate(stats + [zero] * (STATS - len(stats)), axis=0)
    stats += split3(squares)
    for spread in spreads:
        stats += split3(spread)
    stats = jnp.concatenate(stats + [zero] * (STATS - len(stats)), axis=0).astype(F32)
    for pair in range(SLICES // 2):
        part = chunk(stats, pair)
        first, second = halves(part, part)
        mout[2 * pair, ops * rank:ops * rank + STATS, :] = first.astype(BF16)
        mout[2 * pair + 1, ops * rank:ops * rank + STATS, :] = second.astype(BF16)


def second_couple(panels, ops, rank, far, cols, group, held, *refs):
    msgs, (out, zs, st) = refs[:-3], refs[-3:]
    count = len(msgs)
    body = ops * rank
    step = SLICES * 2 * rank
    for m, msg in enumerate(msgs):
        at = group_at(group, m, count, SLICES)
        st[pl.ds(at, SLICES)] = msg[:, body:body + STATS, :].astype(F32)
    every = st[...]
    squares = join3(every, ops)
    scale_sq = jnp.sum(squares, axis=0, keepdims=True) / panels + EPSILON
    reverse = 1.0 / jnp.sqrt(scale_sq)
    heights, norms = [], []
    for o in range(ops):
        shift = join3(every, o)
        height = jnp.sum(shift * squares, axis=0, keepdims=True) / panels / scale_sq
        delta = shift - height
        spread = join3(every, ops + 1 + o) + delta * delta * squares
        norm = jnp.sqrt(jnp.sum(spread, axis=0, keepdims=True) / panels / scale_sq + EPSILON)
        heights.append(height)
        norms.append(norm)
    for m, msg in enumerate(msgs):
        at = group_at(group, m, count, step)
        mine = msg[:, body:body + STATS, :].astype(F32)
        base = held_part(held, m, ops, rank)
        for o in range(ops):
            delta = join3(mine, o) - heights[o]
            z = msg[:, o * rank:(o + 1) * rank, :].astype(F32) + delta[:, None, :] * base
            z = z * (reverse / norms[o])[None]
            zs[o, pl.ds(at, step), :] = spread_rows(z, rank)
    rows = []
    for row in heights + norms + [reverse]:
        rows += split3(row)
    rows += [jnp.zeros_like(rows[0])] * (STATS - len(rows))
    rows = jnp.concatenate(rows, axis=0)
    for s in range(SLICES):
        c = [couple(cols, held, s, b, ops, rank, far, [zs.at[o] for o in range(ops)]) for b in range(2)]
        out[s, 0:body, :] = halves(c[0], c[1])[0].astype(BF16)
        out[s, body:body + STATS, :] = rows


def final_kernel(
    w,
    ulow,
    uown,
    uhigh,
    vlow,
    vown,
    vhigh,
    diag,
    left,
    cmsg,
    images,
    heights,
    norms,
    ext,
    coef,
    stat,
    out,
    outs,
):
    copies = []
    ops = images.shape[0]
    blocks, rank, size = left.shape
    rows, columns = uown.shape
    body = ops * rank
    take_coefs(cmsg, coef, body)
    for pair in range(SLICES // 2):
        stat[:, pair * LANES:(pair + 1) * LANES] = halves(
            cmsg[2 * pair, body:body + STATS, :].astype(F32),
            cmsg[2 * pair + 1, body:body + STATS, :].astype(F32),
        )[0]
    st = stat[...]
    reverse = row3(st, 2 * ops)
    for o in range(ops):
        height = row3(st, o)
        norm = row3(st, ops + o)
        heights[o:o + 1, :] = height
        norms[o:o + 1, :] = norm
        factor = reverse / norm
        for at, (u, v) in enumerate(((ulow, vlow), (uown, vown), (uhigh, vhigh))):
            shift = row3(v[ops * rows:, :].astype(F32), o)
            change = (shift - height) * factor
            value = v[o * rows:(o + 1) * rows, :].astype(F32) * factor + u[...].astype(F32) * change
            ext[o, at] = value.astype(BF16)
        for b in range(blocks):
            parts = [ext.at[o, at] for at in range(3)]
            product = near_product(w.at[b, o * size:(o + 1) * size], parts, b, blocks, size)
            far = dot(left[b], coef[b, o * rank:(o + 1) * rank, :], ((0,), (0,)))
            mine = ext[o, 1, b * size:(b + 1) * size, :].astype(F32)
            here = slice(b * size, (b + 1) * size)
            out[o, here, :] = (
                product
                + diagonal_of(diag, o, b, size, columns) * mine
                + far.astype(BF16).astype(F32)
            )
            copy = pltpu.make_async_copy(out.at[o, here], images.at[o, here], outs.at[o, b])
            copy.start()
            copies.append(copy)
    for copy in copies:
        copy.wait()


def ring(block):
    count = lax.axis_size("store")
    forward = [(i, (i + 1) % count) for i in range(count)]
    backward = [(target, source) for source, target in forward]
    return lax.ppermute(block, "store", forward), lax.ppermute(block, "store", backward)


def shards(
    sources,
    self_terms,
    near_tiles,
    near_cols,
    near_count,
    far_cols,
    basis_left,
    basis_right,
    couplings,
):
    n = lax.axis_size("store")
    ops, blocks, near, size, _ = near_tiles.shape
    rank = basis_left.shape[2]
    far = far_cols.shape[1]
    rows, columns = sources.shape
    all_blocks = blocks * n
    count = n // SLICES
    groups = [[s * count + g for s in range(SLICES)] for g in range(count)]
    sds = jax.ShapeDtypeStruct
    body = ops * rank

    def exchange(x):
        return lax.all_to_all(x, "store", 0, 0, axis_index_groups=groups, tiled=True)

    def across(x):
        parts = [x]
        for m in range(1, count):
            pairs = [(i, i - i % count + (i + m) % count) for i in range(n)]
            parts.append(lax.ppermute(x, "store", pairs))
        return parts

    place = lax.axis_index("store").astype(jnp.int32)
    row0 = (place * blocks).reshape(1)
    group = lax.rem(place, jnp.int32(count)).reshape(1)
    left = jnp.transpose(basis_left, (0, 2, 1))
    right = jnp.transpose(basis_right, (0, 2, 1))

    low, high = ring(sources)
    shared = (blocks + 1) * body
    z1, packed = call(
        functools.partial(coeff_kernel, count),
        [sds((SLICES, rank, LANES), BF16), sds((shared + STATS, LANES), BF16)],
        [SMEM, VMEM, VMEM, VMEM],
        megabytes=60,
    )(far_cols, sources, right, couplings)
    z1 = across(z1)
    held = call(
        share_kernel,
        sds((SLICES, shared + STATS + count * rank, LANES), BF16),
        [VMEM] * (1 + count),
    )(packed, *z1)
    held = exchange(held)
    cols = held[:, shared, :blocks * far].astype(jnp.int32).reshape(-1)

    c1 = call(
        functools.partial(first_couple, ops, rank, far),
        sds((SLICES, body, LANES), BF16),
        [SMEM, SMEM, VMEM],
        [pltpu.VMEM((n * blocks * rank, LANES), BF16)],
    )(cols, group, held)
    c1 = exchange(c1)

    w = call(
        functools.partial(order_tiles, all_blocks),
        sds((blocks, ops * size, near * size), BF16),
        [SMEM, SMEM, SMEM, VMEM],
        micros=2.5,
    )(near_cols, near_count, row0, near_tiles)

    v, msg = call(
        image_kernel,
        [sds((ops * rows + STATS, columns), BF16), sds((SLICES, body + STATS, LANES), BF16)],
        [VMEM] * 8,
        [
            pltpu.VMEM((ops, rows, columns), F32),
            pltpu.VMEM((blocks, body, columns), BF16),
        ],
        micros=4.0,
    )(w, low, sources, high, self_terms, left, right, c1)
    msgs = across(exchange(msg))
    vlow, vhigh = ring(v)

    c2 = call(
        functools.partial(second_couple, all_blocks * size, ops, rank, far),
        sds((SLICES, body + STATS, LANES), BF16),
        [SMEM, SMEM] + [VMEM] * (1 + count),
        [
            pltpu.VMEM((ops, n * blocks * rank, LANES), BF16),
            pltpu.VMEM((n, STATS, LANES), F32),
        ],
        micros=30.0,
    )(cols, group, held, *msgs)
    c2 = exchange(c2)

    images, heights, norms = call(
        final_kernel,
        [sds((ops, rows, columns), F32), sds((ops, columns), F32), sds((ops, columns), F32)],
        [VMEM] * 10,
        [
            pltpu.VMEM((ops, 3, rows, columns), BF16),
            pltpu.VMEM((blocks, body, columns), BF16),
            pltpu.VMEM((STATS, columns), F32),
            pltpu.VMEM((ops, rows, columns), F32),
            pltpu.SemaphoreType.DMA((ops, blocks)),
        ],
        micros=4.0,
        out_specs=[ANY, VMEM, VMEM],
    )(w, low, sources, high, vlow, v, vhigh, self_terms, left, c2)
    return images, heights, norms


def solution(mesh):
    placed = (
        P(("groups", "store"), None),
        P(None, "store"),
        P(None, "store", None, None, None),
        P("store", None),
        P("store"),
        P("store", None),
        P("store", None, None),
        P("store", None, None),
        P(None, "store", None, None, None),
    )
    return jax.shard_map(
        shards,
        mesh=mesh,
        in_specs=placed,
        out_specs=(P(None, ("groups", "store"), None), P("groups", None), P("groups", None)),
        check_vma=False,
    )
```

```python
import functools

import jax
import jax.numpy as jnp
from jax import lax
from jax.experimental import pallas as pl
from jax.experimental.pallas import tpu as pltpu
from jax.sharding import PartitionSpec as P

REACH = 2
EPSILON = 1e-06
LANES = 128
HALF = 64
SLICES = 8
STATS = 16
FLOP_RATE = 1150000000
F32 = jnp.float32
BF16 = jnp.bfloat16

VMEM = pl.BlockSpec(memory_space=pltpu.VMEM)
SMEM = pl.BlockSpec(memory_space=pltpu.SMEM)
ANY = pl.BlockSpec(memory_space=pl.ANY)


def call(body, out_shape, in_specs, scratch=(), micros=1.0, megabytes=20, out_specs=None):
    many = isinstance(out_shape, (list, tuple))
    if out_specs is None:
        out_specs = [VMEM] * len(out_shape) if many else VMEM
    return pl.pallas_call(
        body,
        out_shape=out_shape,
        in_specs=in_specs,
        out_specs=out_specs,
        scratch_shapes=list(scratch),
        compiler_params=pltpu.CompilerParams(vmem_limit_bytes=megabytes * 1024 * 1024),
        cost_estimate=pl.CostEstimate(
            flops=int(micros * FLOP_RATE), bytes_accessed=0, transcendentals=0
        ),
    )


def dot(a, b, dims=((1,), (0,))):
    return lax.dot_general(a, b, (dims, ((), ())), preferred_element_type=F32)


def split3(row):
    high = row.astype(BF16)
    rest = row - high.astype(F32)
    middle = rest.astype(BF16)
    low = (rest - middle.astype(F32)).astype(BF16)
    return [high, middle, low]


def join3(rows, at):
    return rows[..., 3 * at, :] + rows[..., 3 * at + 1, :] + rows[..., 3 * at + 2, :]


def row3(values, at):
    return values[3 * at:3 * at + 1] + values[3 * at + 1:3 * at + 2] + values[3 * at + 2:3 * at + 3]


def halves(x, y):
    left = lax.broadcasted_iota(jnp.int32, x.shape, x.ndim - 1) < HALF
    first = jnp.where(left, x, pltpu.roll(y, HALF, x.ndim - 1))
    second = jnp.where(left, pltpu.roll(x, HALF, x.ndim - 1), y)
    return first, second


def chunk(x, pair):
    return x[:, pair * LANES:(pair + 1) * LANES]


def order_tiles(all_blocks, cols, count, row0, tiles, out):
    ops, blocks, near, size, _ = tiles.shape
    for b in range(blocks):
        for k in range(near):
            rel = lax.rem(cols[b, k] - (row0[0] + b) + REACH + all_blocks, all_blocks)
            rel = lax.rem(rel, all_blocks)
            at = pl.multiple_of(rel * size, size)
            live = k < count[b]
            for o in range(ops):
                tile = tiles[o, b, k]
                out[b, o * size:(o + 1) * size, pl.ds(at, size)] = jnp.where(
                    live, tile, jnp.zeros_like(tile)
                )


def coeff_kernel(count, far_cols, u, right, coup, z_out, out):
    ops, blocks, far, rank, _ = coup.shape
    size = right.shape[2]
    z = [dot(right[b], u[b * size:(b + 1) * size, :]) for b in range(blocks)]
    for pair in range(SLICES // 2):
        first, second = halves(chunk(z[0], pair), chunk(z[1], pair))
        z_out[2 * pair] = first.astype(BF16)
        z_out[2 * pair + 1] = second.astype(BF16)
    whole, rest = [], []
    for b in range(blocks):
        tiles = [
            jnp.concatenate([coup[o, b, f] for f in range(far)], axis=1) for o in range(ops)
        ]
        tiles = jnp.concatenate(tiles, axis=0)
        whole.append(tiles[:, :LANES])
        rest.append(tiles[:, LANES:])
    lane = lax.broadcasted_iota(jnp.int32, (STATS, LANES), 1)
    names = jnp.zeros((STATS, LANES), F32)
    for b in range(blocks):
        for f in range(far):
            col = far_cols[b, f]
            device = lax.div(col, blocks)
            slot = lax.rem(device, count) * SLICES + lax.div(device, count)
            name = (slot * blocks + lax.rem(col, blocks)).astype(F32)
            names = jnp.where(lane == b * far + f, name, names)
    out[...] = jnp.concatenate(
        whole + [jnp.concatenate(rest, axis=1), names.astype(BF16)], axis=0
    )


def share_kernel(packed, *refs):
    parts, out = refs[:-1], refs[-1]
    rows = packed.shape[0]
    rank = parts[0].shape[1]
    for s in range(SLICES):
        out[s, 0:rows, :] = packed[...]
    for m, part in enumerate(parts):
        out[:, rows + m * rank:rows + (m + 1) * rank, :] = part[...]


def coupling_rows(held, s, b, ops, rank):
    body = ops * rank
    first = held[s, b * body:(b + 1) * body, :]
    rest = held[s, 2 * body:3 * body, b * HALF:(b + 1) * HALF]
    return jnp.concatenate([first, rest], axis=1)


def couple(cols, held, s, b, ops, rank, far, z):
    at = (s * 2 + b) * far
    lhs = coupling_rows(held, s, b, ops, rank)
    starts = [pl.multiple_of(cols[at + f] * rank, rank) for f in range(far)]
    picked = [
        jnp.concatenate([x[pl.ds(start, rank), :] for start in starts], axis=0) for x in z
    ]
    if len(z) == 1:
        return dot(lhs, picked[0])
    return jnp.concatenate(
        [dot(lhs[o * rank:(o + 1) * rank], picked[o]) for o in range(ops)], axis=0
    )


def spread_rows(source, rank):
    count = source.shape[0]
    turned = pltpu.roll(source, HALF, 2)
    both = jnp.concatenate([source[:, None], turned[:, None]], axis=1)
    return both.reshape(count * 2 * rank, LANES).astype(BF16)


def held_part(held, m, ops, rank):
    at = 3 * ops * rank + STATS + m * rank
    return held[:, at:at + rank, :].astype(F32)


def group_at(group, m, groups, step):
    return pl.multiple_of(lax.rem(group[0] + (groups - m), groups) * step, step)


def first_couple(ops, rank, far, cols, group, after, held, out, zs):
    step = SLICES * 2 * rank
    count = zs.shape[0] // step
    for m in range(count):
        at = group_at(group, m, count, step)
        zs[pl.ds(at, step), :] = spread_rows(held_part(held, m, ops, rank), rank)
    for s in range(SLICES):
        c = [couple(cols, held, s, b, ops, rank, far, [zs]) for b in range(2)]
        out[s] = halves(c[0], c[1])[0].astype(BF16)


def take_coefs(cmsg, coef, rows):
    for pair in range(SLICES // 2):
        parts = halves(
            cmsg[2 * pair, 0:rows, :].astype(F32), cmsg[2 * pair + 1, 0:rows, :].astype(F32)
        )
        for b in range(2):
            coef[b, :, pair * LANES:(pair + 1) * LANES] = parts[b].astype(BF16)


def near_product(tiles, parts, b, blocks, size):
    total = None
    first = b - REACH
    at = 0
    for d, part in enumerate(parts):
        start = max((d - 1) * blocks, first)
        stop = min(d * blocks, first + 2 * REACH + 1)
        if stop <= start:
            continue
        begin = (start - (d - 1) * blocks) * size
        width = (stop - start) * size
        value = dot(tiles[:, at:at + width], part[begin:begin + width, :])
        total = value if total is None else total + value
        at += width
    return total


def diagonal_of(diag, o, b, size, columns):
    row = diag[o:o + 1, b * size:(b + 1) * size]
    column = jnp.transpose(jnp.broadcast_to(row, (LANES, size)))
    return jnp.concatenate([column] * (columns // LANES), axis=1)


def near_kernel(w, low, own, high, diag, image):
    ops, rows, columns = image.shape
    size = w.shape[1] // ops
    blocks = rows // size
    for b in range(blocks):
        product = near_product(w.at[b], (low, own, high), b, blocks, size)
        here = slice(b * size, (b + 1) * size)
        ub = own[here, :].astype(F32)
        for o in range(ops):
            image[o, here, :] = (
                product[o * size:(o + 1) * size] + diagonal_of(diag, o, b, size, columns) * ub
            )


def image_kernel(own, near, left, right, cmsg, out0, out1, mout, image, coef):
    ops = image.shape[0]
    blocks, rank, size = right.shape
    rows, columns = own.shape
    take_coefs(cmsg, coef, ops * rank)
    inner = [None] * ops
    squares = None
    for b in range(blocks):
        here = slice(b * size, (b + 1) * size)
        ub = own[here, :].astype(F32)
        part = jnp.sum(ub * ub, axis=0, keepdims=True)
        squares = part if squares is None else squares + part
        for o in range(ops):
            far = dot(left[b], coef[b, o * rank:(o + 1) * rank, :], ((0,), (0,)))
            value = near[o, here, :] + far.astype(BF16).astype(F32)
            image[o, here, :] = value
            part = jnp.sum(ub * value, axis=0, keepdims=True)
            inner[o] = part if inner[o] is None else inner[o] + part
    stats = []
    spreads = []
    good = squares > 0
    for o in range(ops):
        shift = jnp.where(good, inner[o] / jnp.where(good, squares, 1.0), 0.0)
        pieces = split3(shift)
        stats += pieces
        shift = pieces[0].astype(F32) + pieces[1].astype(F32) + pieces[2].astype(F32)
        spread = None
        z = []
        for b in range(blocks):
            ub = own[b * size:(b + 1) * size, :].astype(F32)
            v = image[o, b * size:(b + 1) * size, :] - shift * ub
            part = jnp.sum(v * v, axis=0, keepdims=True)
            spread = part if spread is None else spread + part
            v = v.astype(BF16)
            (out0, out1)[o][b * size:(b + 1) * size, :] = v
            z.append(dot(right[b], v))
        for pair in range(SLICES // 2):
            first, second = halves(chunk(z[0], pair), chunk(z[1], pair))
            mout[2 * pair, o * rank:(o + 1) * rank, :] = first.astype(BF16)
            mout[2 * pair + 1, o * rank:(o + 1) * rank, :] = second.astype(BF16)
        spreads.append(spread)
    zero = jnp.zeros((1, columns), BF16)
    out0[rows:, :] = jnp.concatenate(stats + [zero] * (STATS - len(stats)), axis=0)
    stats += split3(squares)
    for spread in spreads:
        stats += split3(spread)
    stats = jnp.concatenate(stats + [zero] * (STATS - len(stats)), axis=0).astype(F32)
    for pair in range(SLICES // 2):
        part = chunk(stats, pair)
        first, second = halves(part, part)
        mout[2 * pair, ops * rank:ops * rank + STATS, :] = first.astype(BF16)
        mout[2 * pair + 1, ops * rank:ops * rank + STATS, :] = second.astype(BF16)


def second_couple(panels, ops, rank, far, cols, group, after_low, after_high, held, *refs):
    msgs, (out, zs, st) = refs[:-3], refs[-3:]
    count = len(msgs)
    body = ops * rank
    step = SLICES * 2 * rank
    for m, msg in enumerate(msgs):
        at = group_at(group, m, count, SLICES)
        st[pl.ds(at, SLICES)] = msg[:, body:body + STATS, :].astype(F32)
    every = st[...]
    squares = join3(every, ops)
    scale_sq = jnp.sum(squares, axis=0, keepdims=True) / panels + EPSILON
    reverse = 1.0 / jnp.sqrt(scale_sq)
    heights, norms = [], []
    for o in range(ops):
        shift = join3(every, o)
        height = jnp.sum(shift * squares, axis=0, keepdims=True) / panels / scale_sq
        delta = shift - height
        spread = join3(every, ops + 1 + o) + delta * delta * squares
        norm = jnp.sqrt(jnp.sum(spread, axis=0, keepdims=True) / panels / scale_sq + EPSILON)
        heights.append(height)
        norms.append(norm)
    for m, msg in enumerate(msgs):
        at = group_at(group, m, count, step)
        mine = msg[:, body:body + STATS, :].astype(F32)
        base = held_part(held, m, ops, rank)
        for o in range(ops):
            delta = join3(mine, o) - heights[o]
            z = msg[:, o * rank:(o + 1) * rank, :].astype(F32) + delta[:, None, :] * base
            z = z * (reverse / norms[o])[None]
            zs[o, pl.ds(at, step), :] = spread_rows(z, rank)
    rows = []
    for row in heights + norms + [reverse]:
        rows += split3(row)
    rows += [jnp.zeros_like(rows[0])] * (STATS - len(rows))
    rows = jnp.concatenate(rows, axis=0)
    for s in range(SLICES):
        c = [couple(cols, held, s, b, ops, rank, far, [zs.at[o] for o in range(ops)]) for b in range(2)]
        out[s, 0:body, :] = halves(c[0], c[1])[0].astype(BF16)
        out[s, body:body + STATS, :] = rows


def final_kernel(
    w,
    ulow,
    uown,
    uhigh,
    low0,
    first,
    high0,
    low1,
    second,
    high1,
    diag,
    left,
    cmsg,
    images,
    heights,
    norms,
    ext,
    coef,
    stat,
    out,
    outs,
):
    copies = []
    ops = images.shape[0]
    blocks, rank, size = left.shape
    rows, columns = uown.shape
    body = ops * rank
    take_coefs(cmsg, coef, body)
    for pair in range(SLICES // 2):
        stat[:, pair * LANES:(pair + 1) * LANES] = halves(
            cmsg[2 * pair, body:body + STATS, :].astype(F32),
            cmsg[2 * pair + 1, body:body + STATS, :].astype(F32),
        )[0]
    st = stat[...]
    reverse = row3(st, 2 * ops)
    for o in range(ops):
        height = row3(st, o)
        norm = row3(st, ops + o)
        heights[o:o + 1, :] = height
        norms[o:o + 1, :] = norm
        factor = reverse / norm
        triples = (ulow, low0, low1), (uown, first, second), (uhigh, high0, high1)
        for at, (u, v0, v1) in enumerate(triples):
            shift = row3(v0[rows:, :].astype(F32), o)
            change = (shift - height) * factor
            v = (v0, v1)[o][0:rows, :].astype(F32)
            value = v * factor + u[...].astype(F32) * change
            ext[o, at] = value.astype(BF16)
        for b in range(blocks):
            parts = [ext.at[o, at] for at in range(3)]
            product = near_product(w.at[b, o * size:(o + 1) * size], parts, b, blocks, size)
            far = dot(left[b], coef[b, o * rank:(o + 1) * rank, :], ((0,), (0,)))
            mine = ext[o, 1, b * size:(b + 1) * size, :].astype(F32)
            here = slice(b * size, (b + 1) * size)
            out[o, here, :] = (
                product
                + diagonal_of(diag, o, b, size, columns) * mine
                + far.astype(BF16).astype(F32)
            )
            copy = pltpu.make_async_copy(out.at[o, here], images.at[o, here], outs.at[o, b])
            copy.start()
            copies.append(copy)
    for copy in copies:
        copy.wait()


def ring(block):
    count = lax.axis_size("store")
    forward = [(i, (i + 1) % count) for i in range(count)]
    backward = [(target, source) for source, target in forward]
    return lax.ppermute(block, "store", forward), lax.ppermute(block, "store", backward)


def shards(
    sources,
    self_terms,
    near_tiles,
    near_cols,
    near_count,
    far_cols,
    basis_left,
    basis_right,
    couplings,
):
    n = lax.axis_size("store")
    ops, blocks, near, size, _ = near_tiles.shape
    rank = basis_left.shape[2]
    far = far_cols.shape[1]
    rows, columns = sources.shape
    all_blocks = blocks * n
    count = n // SLICES
    groups = [[s * count + g for s in range(SLICES)] for g in range(count)]
    sds = jax.ShapeDtypeStruct
    body = ops * rank

    def exchange(x):
        return lax.all_to_all(x, "store", 0, 0, axis_index_groups=groups, tiled=True)

    def across(x):
        parts = [x]
        for m in range(1, count):
            pairs = [(i, i - i % count + (i + m) % count) for i in range(n)]
            parts.append(lax.ppermute(x, "store", pairs))
        return parts

    place = lax.axis_index("store").astype(jnp.int32)
    row0 = (place * blocks).reshape(1)
    group = lax.rem(place, jnp.int32(count)).reshape(1)
    left = jnp.transpose(basis_left, (0, 2, 1))
    right = jnp.transpose(basis_right, (0, 2, 1))

    low, high = ring(sources)
    shared = (blocks + 1) * body
    z1, packed = call(
        functools.partial(coeff_kernel, count),
        [sds((SLICES, rank, LANES), BF16), sds((shared + STATS, LANES), BF16)],
        [SMEM, VMEM, VMEM, VMEM],
        megabytes=60,
    )(far_cols, sources, right, couplings)
    z1 = across(z1)
    held = call(
        share_kernel,
        sds((SLICES, shared + STATS + count * rank, LANES), BF16),
        [VMEM] * (1 + count),
    )(packed, *z1)
    held = exchange(held)
    cols = held[:, shared, :blocks * far].astype(jnp.int32).reshape(-1)

    w = call(
        functools.partial(order_tiles, all_blocks),
        sds((blocks, ops * size, near * size), BF16),
        [SMEM, SMEM, SMEM, VMEM],
        micros=2.5,
    )(near_cols, near_count, row0, near_tiles)
    image = call(near_kernel, sds((ops, rows, columns), F32), [VMEM] * 5, micros=3.0)(
        w, low, sources, high, self_terms
    )

    c1 = call(
        functools.partial(first_couple, ops, rank, far),
        sds((SLICES, body, LANES), BF16),
        [SMEM, SMEM, ANY, VMEM],
        [pltpu.VMEM((n * blocks * rank, LANES), BF16)],
    )(cols, group, image, held)
    c1 = exchange(c1)

    first, second, msg = call(
        image_kernel,
        [
            sds((rows + STATS, columns), BF16),
            sds((rows, columns), BF16),
            sds((SLICES, body + STATS, LANES), BF16),
        ],
        [VMEM] * 5,
        [
            pltpu.VMEM((ops, rows, columns), F32),
            pltpu.VMEM((blocks, body, columns), BF16),
        ],
        micros=2.0,
    )(sources, image, left, right, c1)
    low0, high0 = ring(first)
    low1, high1 = ring(second)
    msgs = across(exchange(msg))

    c2 = call(
        functools.partial(second_couple, all_blocks * size, ops, rank, far),
        sds((SLICES, body + STATS, LANES), BF16),
        [SMEM, SMEM, ANY, ANY] + [VMEM] * (1 + count),
        [
            pltpu.VMEM((ops, n * blocks * rank, LANES), BF16),
            pltpu.VMEM((n, STATS, LANES), F32),
        ],
        micros=30.0,
    )(cols, group, low0, high0, held, *msgs)
    c2 = exchange(c2)

    images, heights, norms = call(
        final_kernel,
        [sds((ops, rows, columns), F32), sds((ops, columns), F32), sds((ops, columns), F32)],
        [VMEM] * 13,
        [
            pltpu.VMEM((ops, 3, rows, columns), BF16),
            pltpu.VMEM((blocks, body, columns), BF16),
            pltpu.VMEM((STATS, columns), F32),
            pltpu.VMEM((ops, rows, columns), F32),
            pltpu.SemaphoreType.DMA((ops, blocks)),
        ],
        micros=4.0,
        out_specs=[ANY, VMEM, VMEM],
    )(w, low, sources, high, low0, first, high0, low1, second, high1, self_terms, left, c2)
    return images, heights, norms


def solution(mesh):
    placed = (
        P(("groups", "store"), None),
        P(None, "store"),
        P(None, "store", None, None, None),
        P("store", None),
        P("store"),
        P("store", None),
        P("store", None, None),
        P("store", None, None),
        P(None, "store", None, None, None),
    )
    return jax.shard_map(
        shards,
        mesh=mesh,
        in_specs=placed,
        out_specs=(P(None, ("groups", "store"), None), P("groups", None), P("groups", None)),
        check_vma=False,
    )
```

```python
import functools

import jax
import jax.numpy as jnp
from jax import lax
from jax.experimental import pallas as pl
from jax.experimental.pallas import tpu as pltpu
from jax.sharding import PartitionSpec as P

REACH = 2
EPSILON = 1e-06
LANES = 128
HALF = 64
SLICES = 8
STATS = 16
FLOP_RATE = 1150000000
F32 = jnp.float32
BF16 = jnp.bfloat16

VMEM = pl.BlockSpec(memory_space=pltpu.VMEM)
SMEM = pl.BlockSpec(memory_space=pltpu.SMEM)
ANY = pl.BlockSpec(memory_space=pl.ANY)


def call(body, out_shape, in_specs, scratch=(), micros=0.0, megabytes=20, out_specs=None):
    many = isinstance(out_shape, (list, tuple))
    if out_specs is None:
        out_specs = [VMEM] * len(out_shape) if many else VMEM
    return pl.pallas_call(
        body,
        out_shape=out_shape,
        in_specs=in_specs,
        out_specs=out_specs,
        scratch_shapes=list(scratch),
        compiler_params=pltpu.CompilerParams(vmem_limit_bytes=megabytes * 1024 * 1024),
        cost_estimate=pl.CostEstimate(
            flops=int(micros * FLOP_RATE), bytes_accessed=0, transcendentals=0
        ),
    )


def dot(a, b, dims=((1,), (0,))):
    return lax.dot_general(a, b, (dims, ((), ())), preferred_element_type=F32)


def split3(row):
    high = row.astype(BF16)
    rest = row - high.astype(F32)
    middle = rest.astype(BF16)
    low = (rest - middle.astype(F32)).astype(BF16)
    return [high, middle, low]


def join3(rows, at):
    return rows[..., 3 * at, :] + rows[..., 3 * at + 1, :] + rows[..., 3 * at + 2, :]


def row3(values, at):
    return values[3 * at:3 * at + 1] + values[3 * at + 1:3 * at + 2] + values[3 * at + 2:3 * at + 3]


def halves(x, y):
    left = lax.broadcasted_iota(jnp.int32, x.shape, x.ndim - 1) < HALF
    first = jnp.where(left, x, pltpu.roll(y, HALF, x.ndim - 1))
    second = jnp.where(left, pltpu.roll(x, HALF, x.ndim - 1), y)
    return first, second


def chunk(x, pair):
    return x[:, pair * LANES:(pair + 1) * LANES]


def order_tiles(all_blocks, cols, count, row0, tiles, out):
    ops, blocks, near, size, _ = tiles.shape
    for b in range(blocks):
        for k in range(near):
            rel = lax.rem(cols[b, k] - (row0[0] + b) + REACH + all_blocks, all_blocks)
            rel = lax.rem(rel, all_blocks)
            at = pl.multiple_of(rel * size, size)
            live = k < count[b]
            for o in range(ops):
                tile = tiles[o, b, k]
                out[b, o * size:(o + 1) * size, pl.ds(at, size)] = jnp.where(
                    live, tile, jnp.zeros_like(tile)
                )


def coeff_kernel(count, far_cols, u, right, coup, z_out, out):
    ops, blocks, far, rank, _ = coup.shape
    size = right.shape[2]
    z = [dot(right[b], u[b * size:(b + 1) * size, :]) for b in range(blocks)]
    for pair in range(SLICES // 2):
        first, second = halves(chunk(z[0], pair), chunk(z[1], pair))
        z_out[2 * pair] = first.astype(BF16)
        z_out[2 * pair + 1] = second.astype(BF16)
    whole, rest = [], []
    for b in range(blocks):
        tiles = [
            jnp.concatenate([coup[o, b, f] for f in range(far)], axis=1) for o in range(ops)
        ]
        tiles = jnp.concatenate(tiles, axis=0)
        whole.append(tiles[:, :LANES])
        rest.append(tiles[:, LANES:])
    lane = lax.broadcasted_iota(jnp.int32, (STATS, LANES), 1)
    names = jnp.zeros((STATS, LANES), F32)
    for b in range(blocks):
        for f in range(far):
            col = far_cols[b, f]
            device = lax.div(col, blocks)
            slot = lax.rem(device, count) * SLICES + lax.div(device, count)
            name = (slot * blocks + lax.rem(col, blocks)).astype(F32)
            names = jnp.where(lane == b * far + f, name, names)
    out[...] = jnp.concatenate(
        whole + [jnp.concatenate(rest, axis=1), names.astype(BF16)], axis=0
    )


def share_kernel(packed, *refs):
    parts, out = refs[:-1], refs[-1]
    rows = packed.shape[0]
    rank = parts[0].shape[1]
    for s in range(SLICES):
        out[s, 0:rows, :] = packed[...]
    for m, part in enumerate(parts):
        out[:, rows + m * rank:rows + (m + 1) * rank, :] = part[...]


def coupling_rows(held, s, b, ops, rank):
    body = ops * rank
    first = held[s, b * body:(b + 1) * body, :]
    rest = held[s, 2 * body:3 * body, b * HALF:(b + 1) * HALF]
    return jnp.concatenate([first, rest], axis=1)


def couple(cols, held, s, b, ops, rank, far, z):
    at = (s * 2 + b) * far
    lhs = coupling_rows(held, s, b, ops, rank)
    starts = [pl.multiple_of(cols[at + f] * rank, rank) for f in range(far)]
    picked = [
        jnp.concatenate([x[pl.ds(start, rank), :] for start in starts], axis=0) for x in z
    ]
    if len(z) == 1:
        return dot(lhs, picked[0])
    return jnp.concatenate(
        [dot(lhs[o * rank:(o + 1) * rank], picked[o]) for o in range(ops)], axis=0
    )


def spread_rows(source, rank):
    count = source.shape[0]
    turned = pltpu.roll(source, HALF, 2)
    both = jnp.concatenate([source[:, None], turned[:, None]], axis=1)
    return both.reshape(count * 2 * rank, LANES).astype(BF16)


def held_part(held, m, ops, rank):
    at = 3 * ops * rank + STATS + m * rank
    return held[:, at:at + rank, :].astype(F32)


def group_at(group, m, groups, step):
    return pl.multiple_of(lax.rem(group[0] + (groups - m), groups) * step, step)


def first_couple(ops, rank, far, cols, group, after, held, out, zs):
    step = SLICES * 2 * rank
    count = zs.shape[0] // step
    for m in range(count):
        at = group_at(group, m, count, step)
        zs[pl.ds(at, step), :] = spread_rows(held_part(held, m, ops, rank), rank)
    for s in range(SLICES):
        c = [couple(cols, held, s, b, ops, rank, far, [zs]) for b in range(2)]
        out[s] = halves(c[0], c[1])[0].astype(BF16)


def take_coefs(cmsg, coef, rows):
    for pair in range(SLICES // 2):
        parts = halves(
            cmsg[2 * pair, 0:rows, :].astype(F32), cmsg[2 * pair + 1, 0:rows, :].astype(F32)
        )
        for b in range(2):
            coef[b, :, pair * LANES:(pair + 1) * LANES] = parts[b].astype(BF16)


def near_product(tiles, parts, b, blocks, size):
    total = None
    first = b - REACH
    at = 0
    for d, part in enumerate(parts):
        start = max((d - 1) * blocks, first)
        stop = min(d * blocks, first + 2 * REACH + 1)
        if stop <= start:
            continue
        begin = (start - (d - 1) * blocks) * size
        width = (stop - start) * size
        value = dot(tiles[:, at:at + width], part[begin:begin + width, :])
        total = value if total is None else total + value
        at += width
    return total


def diagonal_of(diag, o, b, size, columns):
    row = diag[o:o + 1, b * size:(b + 1) * size]
    column = jnp.transpose(jnp.broadcast_to(row, (LANES, size)))
    return jnp.concatenate([column] * (columns // LANES), axis=1)


def near_kernel(w, low, own, high, diag, image, token):
    token[...] = jnp.zeros_like(token)
    ops, rows, columns = image.shape
    size = w.shape[1] // ops
    blocks = rows // size
    for b in range(blocks):
        product = near_product(w.at[b], (low, own, high), b, blocks, size)
        here = slice(b * size, (b + 1) * size)
        ub = own[here, :].astype(F32)
        for o in range(ops):
            image[o, here, :] = (
                product[o * size:(o + 1) * size] + diagonal_of(diag, o, b, size, columns) * ub
            )


def image_kernel(own, near, left, right, cmsg, out0, out1, mout, image, coef):
    ops = image.shape[0]
    blocks, rank, size = right.shape
    rows, columns = own.shape
    take_coefs(cmsg, coef, ops * rank)
    inner = [None] * ops
    squares = None
    for b in range(blocks):
        here = slice(b * size, (b + 1) * size)
        ub = own[here, :].astype(F32)
        part = jnp.sum(ub * ub, axis=0, keepdims=True)
        squares = part if squares is None else squares + part
        for o in range(ops):
            far = dot(left[b], coef[b, o * rank:(o + 1) * rank, :], ((0,), (0,)))
            value = near[o, here, :] + far.astype(BF16).astype(F32)
            image[o, here, :] = value
            part = jnp.sum(ub * value, axis=0, keepdims=True)
            inner[o] = part if inner[o] is None else inner[o] + part
    stats = []
    spreads = []
    good = squares > 0
    for o in range(ops):
        shift = jnp.where(good, inner[o] / jnp.where(good, squares, 1.0), 0.0)
        pieces = split3(shift)
        stats += pieces
        shift = pieces[0].astype(F32) + pieces[1].astype(F32) + pieces[2].astype(F32)
        spread = None
        z = []
        for b in range(blocks):
            ub = own[b * size:(b + 1) * size, :].astype(F32)
            v = image[o, b * size:(b + 1) * size, :] - shift * ub
            part = jnp.sum(v * v, axis=0, keepdims=True)
            spread = part if spread is None else spread + part
            v = v.astype(BF16)
            (out0, out1)[o][b * size:(b + 1) * size, :] = v
            z.append(dot(right[b], v))
        for pair in range(SLICES // 2):
            first, second = halves(chunk(z[0], pair), chunk(z[1], pair))
            mout[2 * pair, o * rank:(o + 1) * rank, :] = first.astype(BF16)
            mout[2 * pair + 1, o * rank:(o + 1) * rank, :] = second.astype(BF16)
        spreads.append(spread)
    zero = jnp.zeros((1, columns), BF16)
    out0[rows:, :] = jnp.concatenate(stats + [zero] * (STATS - len(stats)), axis=0)
    stats += split3(squares)
    for spread in spreads:
        stats += split3(spread)
    stats = jnp.concatenate(stats + [zero] * (STATS - len(stats)), axis=0).astype(F32)
    for pair in range(SLICES // 2):
        part = chunk(stats, pair)
        first, second = halves(part, part)
        mout[2 * pair, ops * rank:ops * rank + STATS, :] = first.astype(BF16)
        mout[2 * pair + 1, ops * rank:ops * rank + STATS, :] = second.astype(BF16)


def second_couple(panels, ops, rank, far, cols, group, after_low, after_high, held, *refs):
    msgs, (out, zs, st) = refs[:-3], refs[-3:]
    count = len(msgs)
    body = ops * rank
    step = SLICES * 2 * rank
    for m, msg in enumerate(msgs):
        at = group_at(group, m, count, SLICES)
        st[pl.ds(at, SLICES)] = msg[:, body:body + STATS, :].astype(F32)
    every = st[...]
    squares = join3(every, ops)
    scale_sq = jnp.sum(squares, axis=0, keepdims=True) / panels + EPSILON
    reverse = 1.0 / jnp.sqrt(scale_sq)
    heights, norms = [], []
    for o in range(ops):
        shift = join3(every, o)
        height = jnp.sum(shift * squares, axis=0, keepdims=True) / panels / scale_sq
        delta = shift - height
        spread = join3(every, ops + 1 + o) + delta * delta * squares
        norm = jnp.sqrt(jnp.sum(spread, axis=0, keepdims=True) / panels / scale_sq + EPSILON)
        heights.append(height)
        norms.append(norm)
    for m, msg in enumerate(msgs):
        at = group_at(group, m, count, step)
        mine = msg[:, body:body + STATS, :].astype(F32)
        base = held_part(held, m, ops, rank)
        for o in range(ops):
            delta = join3(mine, o) - heights[o]
            z = msg[:, o * rank:(o + 1) * rank, :].astype(F32) + delta[:, None, :] * base
            z = z * (reverse / norms[o])[None]
            zs[o, pl.ds(at, step), :] = spread_rows(z, rank)
    rows = []
    for row in heights + norms + [reverse]:
        rows += split3(row)
    rows += [jnp.zeros_like(rows[0])] * (STATS - len(rows))
    rows = jnp.concatenate(rows, axis=0)
    for s in range(SLICES):
        c = [couple(cols, held, s, b, ops, rank, far, [zs.at[o] for o in range(ops)]) for b in range(2)]
        out[s, 0:body, :] = halves(c[0], c[1])[0].astype(BF16)
        out[s, body:body + STATS, :] = rows


def final_kernel(
    w,
    ulow,
    uown,
    uhigh,
    low0,
    first,
    high0,
    low1,
    second,
    high1,
    diag,
    left,
    cmsg,
    images,
    heights,
    norms,
    ext,
    coef,
    stat,
    out,
    outs,
):
    copies = []
    ops = images.shape[0]
    blocks, rank, size = left.shape
    rows, columns = uown.shape
    body = ops * rank
    take_coefs(cmsg, coef, body)
    for pair in range(SLICES // 2):
        stat[:, pair * LANES:(pair + 1) * LANES] = halves(
            cmsg[2 * pair, body:body + STATS, :].astype(F32),
            cmsg[2 * pair + 1, body:body + STATS, :].astype(F32),
        )[0]
    st = stat[...]
    reverse = row3(st, 2 * ops)
    for o in range(ops):
        height = row3(st, o)
        norm = row3(st, ops + o)
        heights[o:o + 1, :] = height
        norms[o:o + 1, :] = norm
        factor = reverse / norm
        triples = (ulow, low0, low1), (uown, first, second), (uhigh, high0, high1)
        for at, (u, v0, v1) in enumerate(triples):
            shift = row3(v0[rows:, :].astype(F32), o)
            change = (shift - height) * factor
            v = (v0, v1)[o][0:rows, :].astype(F32)
            value = v * factor + u[...].astype(F32) * change
            ext[o, at] = value.astype(BF16)
        for b in range(blocks):
            parts = [ext.at[o, at] for at in range(3)]
            product = near_product(w.at[b, o * size:(o + 1) * size], parts, b, blocks, size)
            far = dot(left[b], coef[b, o * rank:(o + 1) * rank, :], ((0,), (0,)))
            mine = ext[o, 1, b * size:(b + 1) * size, :].astype(F32)
            here = slice(b * size, (b + 1) * size)
            out[o, here, :] = (
                product
                + diagonal_of(diag, o, b, size, columns) * mine
                + far.astype(BF16).astype(F32)
            )
            copy = pltpu.make_async_copy(out.at[o, here], images.at[o, here], outs.at[o, b])
            copy.start()
            copies.append(copy)
    for copy in copies:
        copy.wait()


def ring(block):
    count = lax.axis_size("store")
    forward = [(i, (i + 1) % count) for i in range(count)]
    backward = [(target, source) for source, target in forward]
    return lax.ppermute(block, "store", forward), lax.ppermute(block, "store", backward)


def shards(
    sources,
    self_terms,
    near_tiles,
    near_cols,
    near_count,
    far_cols,
    basis_left,
    basis_right,
    couplings,
):
    n = lax.axis_size("store")
    ops, blocks, near, size, _ = near_tiles.shape
    rank = basis_left.shape[2]
    far = far_cols.shape[1]
    rows, columns = sources.shape
    all_blocks = blocks * n
    count = n // SLICES
    groups = [[s * count + g for s in range(SLICES)] for g in range(count)]
    sds = jax.ShapeDtypeStruct
    body = ops * rank

    def exchange(x):
        return lax.all_to_all(x, "store", 0, 0, axis_index_groups=groups, tiled=True)

    def across(x):
        parts = [x]
        for m in range(1, count):
            pairs = [(i, i - i % count + (i + m) % count) for i in range(n)]
            parts.append(lax.ppermute(x, "store", pairs))
        return parts

    place = lax.axis_index("store").astype(jnp.int32)
    row0 = (place * blocks).reshape(1)
    group = lax.rem(place, jnp.int32(count)).reshape(1)
    left = jnp.transpose(basis_left, (0, 2, 1))
    right = jnp.transpose(basis_right, (0, 2, 1))

    low, high = ring(sources)
    shared = (blocks + 1) * body
    z1, packed = call(
        functools.partial(coeff_kernel, count),
        [sds((SLICES, rank, LANES), BF16), sds((shared + STATS, LANES), BF16)],
        [SMEM, VMEM, VMEM, VMEM],
        megabytes=60,
    )(far_cols, sources, right, couplings)
    z1 = across(z1)
    held = call(
        share_kernel,
        sds((SLICES, shared + STATS + count * rank, LANES), BF16),
        [VMEM] * (1 + count),
    )(packed, *z1)
    held = exchange(held)
    cols = held[:, shared, :blocks * far].astype(jnp.int32).reshape(-1)

    w = call(
        functools.partial(order_tiles, all_blocks),
        sds((blocks, ops * size, near * size), BF16),
        [SMEM, SMEM, SMEM, VMEM],
        micros=0.0,
        megabytes=60,
    )(near_cols, near_count, row0, near_tiles)
    image, token = call(
        near_kernel,
        [sds((ops, rows, columns), F32), sds((8, LANES), F32)],
        [VMEM] * 5,
        micros=10.0,
        megabytes=60,
    )(w, low, sources, high, self_terms)

    c1 = call(
        functools.partial(first_couple, ops, rank, far),
        sds((SLICES, body, LANES), BF16),
        [SMEM, SMEM, ANY, VMEM],
        [pltpu.VMEM((n * blocks * rank, LANES), BF16)],
    )(cols, group, token, held)
    c1 = exchange(c1)

    first, second, msg = call(
        image_kernel,
        [
            sds((rows + STATS, columns), BF16),
            sds((rows, columns), BF16),
            sds((SLICES, body + STATS, LANES), BF16),
        ],
        [VMEM] * 5,
        [
            pltpu.VMEM((ops, rows, columns), F32),
            pltpu.VMEM((blocks, body, columns), BF16),
        ],
        micros=2.0,
    )(sources, image, left, right, c1)
    low0, high0 = ring(first)
    low1, high1 = ring(second)
    msgs = across(exchange(msg))

    c2 = call(
        functools.partial(second_couple, all_blocks * size, ops, rank, far),
        sds((SLICES, body + STATS, LANES), BF16),
        [SMEM, SMEM, ANY, ANY] + [VMEM] * (1 + count),
        [
            pltpu.VMEM((ops, n * blocks * rank, LANES), BF16),
            pltpu.VMEM((n, STATS, LANES), F32),
        ],
        micros=30.0,
    )(cols, group, low0, high0, held, *msgs)
    c2 = exchange(c2)

    images, heights, norms = call(
        final_kernel,
        [sds((ops, rows, columns), F32), sds((ops, columns), F32), sds((ops, columns), F32)],
        [VMEM] * 13,
        [
            pltpu.VMEM((ops, 3, rows, columns), BF16),
            pltpu.VMEM((blocks, body, columns), BF16),
            pltpu.VMEM((STATS, columns), F32),
            pltpu.VMEM((ops, rows, columns), F32),
            pltpu.SemaphoreType.DMA((ops, blocks)),
        ],
        micros=4.0,
        out_specs=[ANY, VMEM, VMEM],
    )(w, low, sources, high, low0, first, high0, low1, second, high1, self_terms, left, c2)
    return images, heights, norms


def solution(mesh):
    placed = (
        P(("groups", "store"), None),
        P(None, "store"),
        P(None, "store", None, None, None),
        P("store", None),
        P("store"),
        P("store", None),
        P("store", None, None),
        P("store", None, None),
        P(None, "store", None, None, None),
    )
    return jax.shard_map(
        shards,
        mesh=mesh,
        in_specs=placed,
        out_specs=(P(None, ("groups", "store"), None), P("groups", None), P("groups", None)),
        check_vma=False,
    )
```

```python
import functools

import jax
import jax.numpy as jnp
from jax import lax
from jax.experimental import pallas as pl
from jax.experimental.pallas import tpu as pltpu
from jax.sharding import PartitionSpec as P

REACH = 2
EPSILON = 1e-06
LANES = 128
HALF = 64
SLICES = 8
STATS = 16
FLOP_RATE = 1150000000
F32 = jnp.float32
BF16 = jnp.bfloat16

VMEM = pl.BlockSpec(memory_space=pltpu.VMEM)
SMEM = pl.BlockSpec(memory_space=pltpu.SMEM)
ANY = pl.BlockSpec(memory_space=pl.ANY)


def call(body, out_shape, in_specs, scratch=(), micros=0.0, megabytes=20, out_specs=None, alias=None):
    many = isinstance(out_shape, (list, tuple))
    if out_specs is None:
        out_specs = [VMEM] * len(out_shape) if many else VMEM
    return pl.pallas_call(
        body,
        out_shape=out_shape,
        in_specs=in_specs,
        out_specs=out_specs,
        input_output_aliases=alias or {},
        scratch_shapes=list(scratch),
        compiler_params=pltpu.CompilerParams(vmem_limit_bytes=megabytes * 1024 * 1024),
        cost_estimate=pl.CostEstimate(
            flops=int(micros * FLOP_RATE), bytes_accessed=0, transcendentals=0
        ),
    )


def dot(a, b, dims=((1,), (0,))):
    return lax.dot_general(a, b, (dims, ((), ())), preferred_element_type=F32)


def split3(row):
    high = row.astype(BF16)
    rest = row - high.astype(F32)
    middle = rest.astype(BF16)
    low = (rest - middle.astype(F32)).astype(BF16)
    return [high, middle, low]


def join3(rows, at):
    return rows[..., 3 * at, :] + rows[..., 3 * at + 1, :] + rows[..., 3 * at + 2, :]


def row3(values, at):
    return values[3 * at:3 * at + 1] + values[3 * at + 1:3 * at + 2] + values[3 * at + 2:3 * at + 3]


def halves(x, y):
    left = lax.broadcasted_iota(jnp.int32, x.shape, x.ndim - 1) < HALF
    first = jnp.where(left, x, pltpu.roll(y, HALF, x.ndim - 1))
    second = jnp.where(left, pltpu.roll(x, HALF, x.ndim - 1), y)
    return first, second


def chunk(x, pair):
    return x[:, pair * LANES:(pair + 1) * LANES]


def order_tiles(all_blocks, cols, count, row0, tiles, after, out):
    ops, blocks, near, size, _ = tiles.shape
    for b in range(blocks):
        for k in range(near):
            rel = lax.rem(cols[b, k] - (row0[0] + b) + REACH + all_blocks, all_blocks)
            rel = lax.rem(rel, all_blocks)
            at = pl.multiple_of(rel * size, size)
            live = k < count[b]
            for o in range(ops):
                tile = tiles[o, b, k]
                out[b, o * size:(o + 1) * size, pl.ds(at, size)] = jnp.where(
                    live, tile, jnp.zeros_like(tile)
                )


def coeff_kernel(count, far_cols, u, right, coup, z_out, out):
    ops, blocks, far, rank, _ = coup.shape
    size = right.shape[2]
    z = [dot(right[b], u[b * size:(b + 1) * size, :]) for b in range(blocks)]
    for pair in range(SLICES // 2):
        first, second = halves(chunk(z[0], pair), chunk(z[1], pair))
        z_out[2 * pair] = first.astype(BF16)
        z_out[2 * pair + 1] = second.astype(BF16)
    whole, rest = [], []
    for b in range(blocks):
        tiles = [
            jnp.concatenate([coup[o, b, f] for f in range(far)], axis=1) for o in range(ops)
        ]
        tiles = jnp.concatenate(tiles, axis=0)
        whole.append(tiles[:, :LANES])
        rest.append(tiles[:, LANES:])
    lane = lax.broadcasted_iota(jnp.int32, (STATS, LANES), 1)
    names = jnp.zeros((STATS, LANES), F32)
    for b in range(blocks):
        for f in range(far):
            col = far_cols[b, f]
            device = lax.div(col, blocks)
            slot = lax.rem(device, count) * SLICES + lax.div(device, count)
            name = (slot * blocks + lax.rem(col, blocks)).astype(F32)
            names = jnp.where(lane == b * far + f, name, names)
    out[...] = jnp.concatenate(
        whole + [jnp.concatenate(rest, axis=1), names.astype(BF16)], axis=0
    )


def share_kernel(packed, *refs):
    parts, out = refs[:-1], refs[-1]
    rows = packed.shape[0]
    rank = parts[0].shape[1]
    for s in range(SLICES):
        out[s, 0:rows, :] = packed[...]
    for m, part in enumerate(parts):
        out[:, rows + m * rank:rows + (m + 1) * rank, :] = part[...]


def coupling_rows(held, s, b, ops, rank):
    body = ops * rank
    first = held[s, b * body:(b + 1) * body, :]
    rest = held[s, 2 * body:3 * body, b * HALF:(b + 1) * HALF]
    return jnp.concatenate([first, rest], axis=1)


def couple(cols, held, s, b, ops, rank, far, z):
    at = (s * 2 + b) * far
    lhs = coupling_rows(held, s, b, ops, rank)
    starts = [pl.multiple_of(cols[at + f] * rank, rank) for f in range(far)]
    picked = [
        jnp.concatenate([x[pl.ds(start, rank), :] for start in starts], axis=0) for x in z
    ]
    if len(z) == 1:
        return dot(lhs, picked[0])
    return jnp.concatenate(
        [dot(lhs[o * rank:(o + 1) * rank], picked[o]) for o in range(ops)], axis=0
    )


def spread_rows(source, rank):
    count = source.shape[0]
    turned = pltpu.roll(source, HALF, 2)
    both = jnp.concatenate([source[:, None], turned[:, None]], axis=1)
    return both.reshape(count * 2 * rank, LANES).astype(BF16)


def held_part(held, m, ops, rank):
    at = 3 * ops * rank + STATS + m * rank
    return held[:, at:at + rank, :].astype(F32)


def group_at(group, m, groups, step):
    return pl.multiple_of(lax.rem(group[0] + (groups - m), groups) * step, step)


def first_couple(ops, rank, far, cols, group, after, held, out, zs):
    step = SLICES * 2 * rank
    count = zs.shape[0] // step
    for m in range(count):
        at = group_at(group, m, count, step)
        zs[pl.ds(at, step), :] = spread_rows(held_part(held, m, ops, rank), rank)
    for s in range(SLICES):
        c = [couple(cols, held, s, b, ops, rank, far, [zs]) for b in range(2)]
        out[s] = halves(c[0], c[1])[0].astype(BF16)


def take_coefs(cmsg, coef, rows):
    for pair in range(SLICES // 2):
        parts = halves(
            cmsg[2 * pair, 0:rows, :].astype(F32), cmsg[2 * pair + 1, 0:rows, :].astype(F32)
        )
        for b in range(2):
            coef[b, :, pair * LANES:(pair + 1) * LANES] = parts[b].astype(BF16)


def near_product(tiles, parts, b, blocks, size):
    total = None
    first = b - REACH
    at = 0
    for d, part in enumerate(parts):
        start = max((d - 1) * blocks, first)
        stop = min(d * blocks, first + 2 * REACH + 1)
        if stop <= start:
            continue
        begin = (start - (d - 1) * blocks) * size
        width = (stop - start) * size
        value = dot(tiles[:, at:at + width], part[begin:begin + width, :])
        total = value if total is None else total + value
        at += width
    return total


def diagonal_of(diag, o, b, size, columns):
    row = diag[o:o + 1, b * size:(b + 1) * size]
    column = jnp.transpose(jnp.broadcast_to(row, (LANES, size)))
    return jnp.concatenate([column] * (columns // LANES), axis=1)


def near_kernel(w, low, own, high, diag, image, token):
    token[...] = jnp.zeros_like(token)
    ops, rows, columns = image.shape
    size = w.shape[1] // ops
    blocks = rows // size
    for b in range(blocks):
        product = near_product(w.at[b], (low, own, high), b, blocks, size)
        here = slice(b * size, (b + 1) * size)
        ub = own[here, :].astype(F32)
        for o in range(ops):
            image[o, here, :] = (
                product[o * size:(o + 1) * size] + diagonal_of(diag, o, b, size, columns) * ub
            )


def image_kernel(own, near, left, right, cmsg, out0, out1, mout, image, coef):
    ops = image.shape[0]
    blocks, rank, size = right.shape
    rows, columns = own.shape
    take_coefs(cmsg, coef, ops * rank)
    inner = [None] * ops
    squares = None
    for b in range(blocks):
        here = slice(b * size, (b + 1) * size)
        ub = own[here, :].astype(F32)
        part = jnp.sum(ub * ub, axis=0, keepdims=True)
        squares = part if squares is None else squares + part
        for o in range(ops):
            far = dot(left[b], coef[b, o * rank:(o + 1) * rank, :], ((0,), (0,)))
            value = near[o, here, :] + far.astype(BF16).astype(F32)
            image[o, here, :] = value
            part = jnp.sum(ub * value, axis=0, keepdims=True)
            inner[o] = part if inner[o] is None else inner[o] + part
    stats = []
    spreads = []
    good = squares > 0
    for o in range(ops):
        shift = jnp.where(good, inner[o] / jnp.where(good, squares, 1.0), 0.0)
        pieces = split3(shift)
        stats += pieces
        shift = pieces[0].astype(F32) + pieces[1].astype(F32) + pieces[2].astype(F32)
        spread = None
        z = []
        for b in range(blocks):
            ub = own[b * size:(b + 1) * size, :].astype(F32)
            v = image[o, b * size:(b + 1) * size, :] - shift * ub
            part = jnp.sum(v * v, axis=0, keepdims=True)
            spread = part if spread is None else spread + part
            v = v.astype(BF16)
            (out0, out1)[o][b * size:(b + 1) * size, :] = v
            z.append(dot(right[b], v))
        for pair in range(SLICES // 2):
            first, second = halves(chunk(z[0], pair), chunk(z[1], pair))
            mout[2 * pair, o * rank:(o + 1) * rank, :] = first.astype(BF16)
            mout[2 * pair + 1, o * rank:(o + 1) * rank, :] = second.astype(BF16)
        spreads.append(spread)
    zero = jnp.zeros((1, columns), BF16)
    out0[rows:, :] = jnp.concatenate(stats + [zero] * (STATS - len(stats)), axis=0)
    stats += split3(squares)
    for spread in spreads:
        stats += split3(spread)
    stats = jnp.concatenate(stats + [zero] * (STATS - len(stats)), axis=0).astype(F32)
    for pair in range(SLICES // 2):
        part = chunk(stats, pair)
        first, second = halves(part, part)
        mout[2 * pair, ops * rank:ops * rank + STATS, :] = first.astype(BF16)
        mout[2 * pair + 1, ops * rank:ops * rank + STATS, :] = second.astype(BF16)


def second_couple(panels, ops, rank, far, cols, group, after_low, after_high, held, *refs):
    msgs, (out, zs, st) = refs[:-3], refs[-3:]
    count = len(msgs)
    body = ops * rank
    step = SLICES * 2 * rank
    for m, msg in enumerate(msgs):
        at = group_at(group, m, count, SLICES)
        st[pl.ds(at, SLICES)] = msg[:, body:body + STATS, :].astype(F32)
    every = st[...]
    squares = join3(every, ops)
    scale_sq = jnp.sum(squares, axis=0, keepdims=True) / panels + EPSILON
    reverse = 1.0 / jnp.sqrt(scale_sq)
    heights, norms = [], []
    for o in range(ops):
        shift = join3(every, o)
        height = jnp.sum(shift * squares, axis=0, keepdims=True) / panels / scale_sq
        delta = shift - height
        spread = join3(every, ops + 1 + o) + delta * delta * squares
        norm = jnp.sqrt(jnp.sum(spread, axis=0, keepdims=True) / panels / scale_sq + EPSILON)
        heights.append(height)
        norms.append(norm)
    for m, msg in enumerate(msgs):
        at = group_at(group, m, count, step)
        mine = msg[:, body:body + STATS, :].astype(F32)
        base = held_part(held, m, ops, rank)
        for o in range(ops):
            delta = join3(mine, o) - heights[o]
            z = msg[:, o * rank:(o + 1) * rank, :].astype(F32) + delta[:, None, :] * base
            z = z * (reverse / norms[o])[None]
            zs[o, pl.ds(at, step), :] = spread_rows(z, rank)
    rows = []
    for row in heights + norms + [reverse]:
        rows += split3(row)
    rows += [jnp.zeros_like(rows[0])] * (STATS - len(rows))
    rows = jnp.concatenate(rows, axis=0)
    for s in range(SLICES):
        c = [couple(cols, held, s, b, ops, rank, far, [zs.at[o] for o in range(ops)]) for b in range(2)]
        out[s, 0:body, :] = halves(c[0], c[1])[0].astype(BF16)
        out[s, body:body + STATS, :] = rows


def apply_second(o, factor, changes, u3, v3, w, diag, left, cmsg, images, ext, coef, out, sems):
    blocks, rank, size = left.shape
    rows, columns = u3[1].shape
    ops = w.shape[1] // size
    take_coefs(cmsg, coef, ops * rank)
    for at, (u, v) in enumerate(zip(u3, v3)):
        value = v[0:rows, :].astype(F32) * factor + u[...].astype(F32) * changes[at]
        ext[at] = value.astype(BF16)
    copies = []
    for b in range(blocks):
        parts = [ext.at[at] for at in range(3)]
        product = near_product(w.at[b, o * size:(o + 1) * size], parts, b, blocks, size)
        far = dot(left[b], coef[b, o * rank:(o + 1) * rank, :], ((0,), (0,)))
        here = slice(b * size, (b + 1) * size)
        out[here, :] = (
            product
            + diagonal_of(diag, o, b, size, columns) * ext[1, here, :].astype(F32)
            + far.astype(BF16).astype(F32)
        )
        copies.append(pltpu.make_async_copy(out.at[here], images.at[o, here], sems.at[b]))
        copies[-1].start()
    for copy in copies:
        copy.wait()


def final_first(
    w,
    ulow,
    uown,
    uhigh,
    vlow,
    vown,
    vhigh,
    diag,
    left,
    cmsg,
    images,
    heights,
    norms,
    aux,
    ext,
    coef,
    out,
    stat,
    sems,
):
    blocks, rank, size = left.shape
    rows, columns = uown.shape
    ops = w.shape[1] // size
    body = ops * rank
    for pair in range(SLICES // 2):
        stat[:, pair * LANES:(pair + 1) * LANES] = halves(
            cmsg[2 * pair, body:body + STATS, :].astype(F32),
            cmsg[2 * pair + 1, body:body + STATS, :].astype(F32),
        )[0]
    st = stat[...]
    reverse = row3(st, 2 * ops)
    scales = []
    for o in range(ops):
        height = row3(st, o)
        norm = row3(st, ops + o)
        heights[o:o + 1, :] = height
        norms[o:o + 1, :] = norm
        factor = reverse / norm
        changes = [
            (row3(v[rows:, :].astype(F32), o) - height) * factor for v in (vlow, vown, vhigh)
        ]
        scales.append((factor, changes))
    factor, changes = scales[1]
    aux[0:1, :] = factor
    for at in range(3):
        aux[1 + at:2 + at, :] = changes[at]
    factor, changes = scales[0]
    u3, v3 = (ulow, uown, uhigh), (vlow, vown, vhigh)
    apply_second(0, factor, changes, u3, v3, w, diag, left, cmsg, images, ext, coef, out, sems)


def final_second(
    begun,
    w,
    ulow,
    uown,
    uhigh,
    vlow,
    vown,
    vhigh,
    diag,
    left,
    cmsg,
    aux,
    images,
    ext,
    coef,
    out,
    sems,
):
    factor, changes = aux[0:1, :], [aux[1 + at:2 + at, :] for at in range(3)]
    u3, v3 = (ulow, uown, uhigh), (vlow, vown, vhigh)
    apply_second(1, factor, changes, u3, v3, w, diag, left, cmsg, images, ext, coef, out, sems)


def ring(block):
    count = lax.axis_size("store")
    forward = [(i, (i + 1) % count) for i in range(count)]
    backward = [(target, source) for source, target in forward]
    return lax.ppermute(block, "store", forward), lax.ppermute(block, "store", backward)


def shards(
    sources,
    self_terms,
    near_tiles,
    near_cols,
    near_count,
    far_cols,
    basis_left,
    basis_right,
    couplings,
):
    n = lax.axis_size("store")
    ops, blocks, near, size, _ = near_tiles.shape
    rank = basis_left.shape[2]
    far = far_cols.shape[1]
    rows, columns = sources.shape
    all_blocks = blocks * n
    count = n // SLICES
    groups = [[s * count + g for s in range(SLICES)] for g in range(count)]
    sds = jax.ShapeDtypeStruct
    body = ops * rank

    def exchange(x):
        return lax.all_to_all(x, "store", 0, 0, axis_index_groups=groups, tiled=True)

    def across(x):
        parts = [x]
        for m in range(1, count):
            pairs = [(i, i - i % count + (i + m) % count) for i in range(n)]
            parts.append(lax.ppermute(x, "store", pairs))
        return parts

    place = lax.axis_index("store").astype(jnp.int32)
    row0 = (place * blocks).reshape(1)
    group = lax.rem(place, jnp.int32(count)).reshape(1)
    left = jnp.transpose(basis_left, (0, 2, 1))
    right = jnp.transpose(basis_right, (0, 2, 1))

    low, high = ring(sources)
    shared = (blocks + 1) * body
    z1, packed = call(
        functools.partial(coeff_kernel, count),
        [sds((SLICES, rank, LANES), BF16), sds((shared + STATS, LANES), BF16)],
        [SMEM, VMEM, VMEM, VMEM],
        megabytes=60,
    )(far_cols, sources, right, couplings)
    z1 = across(z1)
    mine = call(
        share_kernel,
        sds((SLICES, shared + STATS + count * rank, LANES), BF16),
        [VMEM] * (1 + count),
    )(packed, *z1)
    held = exchange(mine)
    cols = held[:, shared, :blocks * far].astype(jnp.int32).reshape(-1)

    w = call(
        functools.partial(order_tiles, all_blocks),
        sds((blocks, ops * size, near * size), BF16),
        [SMEM, SMEM, SMEM, VMEM, ANY],
        megabytes=60,
    )(near_cols, near_count, row0, near_tiles, mine)
    image, token = call(
        near_kernel,
        [sds((ops, rows, columns), F32), sds((8, LANES), F32)],
        [VMEM] * 5,
        micros=10.0,
        megabytes=60,
    )(w, low, sources, high, self_terms)

    c1 = call(
        functools.partial(first_couple, ops, rank, far),
        sds((SLICES, body, LANES), BF16),
        [SMEM, SMEM, ANY, VMEM],
        [pltpu.VMEM((n * blocks * rank, LANES), BF16)],
    )(cols, group, token, held)
    c1 = exchange(c1)

    first, second, msg = call(
        image_kernel,
        [
            sds((rows + STATS, columns), BF16),
            sds((rows, columns), BF16),
            sds((SLICES, body + STATS, LANES), BF16),
        ],
        [VMEM] * 5,
        [
            pltpu.VMEM((ops, rows, columns), F32),
            pltpu.VMEM((blocks, body, columns), BF16),
        ],
        micros=2.0,
    )(sources, image, left, right, c1)
    low0, high0 = ring(first)
    low1, high1 = ring(second)
    msgs = across(exchange(msg))

    c2 = call(
        functools.partial(second_couple, all_blocks * size, ops, rank, far),
        sds((SLICES, body + STATS, LANES), BF16),
        [SMEM, SMEM, ANY, ANY] + [VMEM] * (1 + count),
        [
            pltpu.VMEM((ops, n * blocks * rank, LANES), BF16),
            pltpu.VMEM((n, STATS, LANES), F32),
        ],
        micros=30.0,
    )(cols, group, low0, high0, held, *msgs)
    c2 = exchange(c2)

    outs = sds((ops, rows, columns), F32)
    scratch = [
        pltpu.VMEM((3, rows, columns), BF16),
        pltpu.VMEM((blocks, body, columns), BF16),
        pltpu.VMEM((rows, columns), F32),
    ]
    images, heights, norms, aux = call(
        final_first,
        [outs, sds((ops, columns), F32), sds((ops, columns), F32), sds((8, columns), F32)],
        [VMEM] * 10,
        scratch + [pltpu.VMEM((STATS, columns), F32), pltpu.SemaphoreType.DMA((blocks,))],
        micros=10.0,
        out_specs=[ANY, VMEM, VMEM, VMEM],
    )(w, low, sources, high, low0, first, high0, self_terms, left, c2)
    images = call(
        final_second,
        outs,
        [ANY] + [VMEM] * 11,
        scratch + [pltpu.SemaphoreType.DMA((blocks,))],
        micros=4.0,
        out_specs=ANY,
        alias={0: 0},
    )(images, w, low, sources, high, low1, second, high1, self_terms, left, c2, aux)
    return images, heights, norms


def solution(mesh):
    placed = (
        P(("groups", "store"), None),
        P(None, "store"),
        P(None, "store", None, None, None),
        P("store", None),
        P("store"),
        P("store", None),
        P("store", None, None),
        P("store", None, None),
        P(None, "store", None, None, None),
    )
    return jax.shard_map(
        shards,
        mesh=mesh,
        in_specs=placed,
        out_specs=(P(None, ("groups", "store"), None), P("groups", None), P("groups", None)),
        check_vma=False,
    )
```

```python
import functools

import jax
import jax.numpy as jnp
from jax import lax
from jax.experimental import pallas as pl
from jax.experimental.pallas import tpu as pltpu
from jax.sharding import PartitionSpec as P

REACH = 2
EPSILON = 1e-06
LANES = 128
HALF = 64
SLICES = 8
STATS = 16
FLOP_RATE = 1150000000
F32 = jnp.float32
BF16 = jnp.bfloat16

VMEM = pl.BlockSpec(memory_space=pltpu.VMEM)
SMEM = pl.BlockSpec(memory_space=pltpu.SMEM)
ANY = pl.BlockSpec(memory_space=pl.ANY)


def call(body, out_shape, in_specs, scratch=(), micros=0.0, megabytes=20, out_specs=None, alias=None):
    many = isinstance(out_shape, (list, tuple))
    if out_specs is None:
        out_specs = [VMEM] * len(out_shape) if many else VMEM
    return pl.pallas_call(
        body,
        out_shape=out_shape,
        in_specs=in_specs,
        out_specs=out_specs,
        input_output_aliases=alias or {},
        scratch_shapes=list(scratch),
        compiler_params=pltpu.CompilerParams(vmem_limit_bytes=megabytes * 1024 * 1024),
        cost_estimate=pl.CostEstimate(
            flops=int(micros * FLOP_RATE), bytes_accessed=0, transcendentals=0
        ),
    )


def dot(a, b, dims=((1,), (0,))):
    return lax.dot_general(a, b, (dims, ((), ())), preferred_element_type=F32)


def split3(row):
    high = row.astype(BF16)
    rest = row - high.astype(F32)
    middle = rest.astype(BF16)
    low = (rest - middle.astype(F32)).astype(BF16)
    return [high, middle, low]


def join3(rows, at):
    return rows[..., 3 * at, :] + rows[..., 3 * at + 1, :] + rows[..., 3 * at + 2, :]


def row3(values, at):
    return values[3 * at:3 * at + 1] + values[3 * at + 1:3 * at + 2] + values[3 * at + 2:3 * at + 3]


def halves(x, y):
    left = lax.broadcasted_iota(jnp.int32, x.shape, x.ndim - 1) < HALF
    first = jnp.where(left, x, pltpu.roll(y, HALF, x.ndim - 1))
    second = jnp.where(left, pltpu.roll(x, HALF, x.ndim - 1), y)
    return first, second


def chunk(x, pair):
    return x[:, pair * LANES:(pair + 1) * LANES]


def order_tiles(all_blocks, cols, count, row0, tiles, after, out):
    ops, blocks, near, size, _ = tiles.shape
    for b in range(blocks):
        for k in range(near):
            rel = lax.rem(cols[b, k] - (row0[0] + b) + REACH + all_blocks, all_blocks)
            rel = lax.rem(rel, all_blocks)
            at = pl.multiple_of(rel * size, size)
            live = k < count[b]
            for o in range(ops):
                tile = tiles[o, b, k]
                out[b, o * size:(o + 1) * size, pl.ds(at, size)] = jnp.where(
                    live, tile, jnp.zeros_like(tile)
                )


def coeff_kernel(count, far_cols, u, right, coup, z_out, out):
    ops, blocks, far, rank, _ = coup.shape
    size = right.shape[2]
    z = [dot(right[b], u[b * size:(b + 1) * size, :]) for b in range(blocks)]
    for pair in range(SLICES // 2):
        first, second = halves(chunk(z[0], pair), chunk(z[1], pair))
        z_out[2 * pair] = first.astype(BF16)
        z_out[2 * pair + 1] = second.astype(BF16)
    whole, rest = [], []
    for b in range(blocks):
        tiles = [
            jnp.concatenate([coup[o, b, f] for f in range(far)], axis=1) for o in range(ops)
        ]
        tiles = jnp.concatenate(tiles, axis=0)
        whole.append(tiles[:, :LANES])
        rest.append(tiles[:, LANES:])
    lane = lax.broadcasted_iota(jnp.int32, (STATS, LANES), 1)
    names = jnp.zeros((STATS, LANES), F32)
    for b in range(blocks):
        for f in range(far):
            col = far_cols[b, f]
            device = lax.div(col, blocks)
            slot = lax.rem(device, count) * SLICES + lax.div(device, count)
            name = (slot * blocks + lax.rem(col, blocks)).astype(F32)
            names = jnp.where(lane == b * far + f, name, names)
    out[...] = jnp.concatenate(
        whole + [jnp.concatenate(rest, axis=1), names.astype(BF16)], axis=0
    )


def share_kernel(packed, *refs):
    parts, out = refs[:-1], refs[-1]
    rows = packed.shape[0]
    rank = parts[0].shape[1]
    for s in range(SLICES):
        out[s, 0:rows, :] = packed[...]
    for m, part in enumerate(parts):
        out[:, rows + m * rank:rows + (m + 1) * rank, :] = part[...]


def coupling_rows(held, s, b, ops, rank):
    body = ops * rank
    first = held[s, b * body:(b + 1) * body, :]
    rest = held[s, 2 * body:3 * body, b * HALF:(b + 1) * HALF]
    return jnp.concatenate([first, rest], axis=1)


def couple(cols, held, s, b, ops, rank, far, z):
    at = (s * 2 + b) * far
    lhs = coupling_rows(held, s, b, ops, rank)
    starts = [pl.multiple_of(cols[at + f] * rank, rank) for f in range(far)]
    picked = [
        jnp.concatenate([x[pl.ds(start, rank), :] for start in starts], axis=0) for x in z
    ]
    if len(z) == 1:
        return dot(lhs, picked[0])
    return jnp.concatenate(
        [dot(lhs[o * rank:(o + 1) * rank], picked[o]) for o in range(ops)], axis=0
    )


def spread_rows(source, rank):
    count = source.shape[0]
    turned = pltpu.roll(source, HALF, 2)
    both = jnp.concatenate([source[:, None], turned[:, None]], axis=1)
    return both.reshape(count * 2 * rank, LANES).astype(BF16)


def held_part(held, m, ops, rank):
    at = 3 * ops * rank + STATS + m * rank
    return held[:, at:at + rank, :].astype(F32)


def group_at(group, m, groups, step):
    return pl.multiple_of(lax.rem(group[0] + (groups - m), groups) * step, step)


def first_couple(ops, rank, far, cols, group, after, held, out, zs):
    step = SLICES * 2 * rank
    count = zs.shape[0] // step
    for m in range(count):
        at = group_at(group, m, count, step)
        zs[pl.ds(at, step), :] = spread_rows(held_part(held, m, ops, rank), rank)
    for s in range(SLICES):
        c = [couple(cols, held, s, b, ops, rank, far, [zs]) for b in range(2)]
        out[s] = halves(c[0], c[1])[0].astype(BF16)


def take_coefs(cmsg, coef, rows):
    for pair in range(SLICES // 2):
        parts = halves(
            cmsg[2 * pair, 0:rows, :].astype(F32), cmsg[2 * pair + 1, 0:rows, :].astype(F32)
        )
        for b in range(2):
            coef[b, :, pair * LANES:(pair + 1) * LANES] = parts[b].astype(BF16)


def near_product(tiles, parts, b, blocks, size):
    total = None
    first = b - REACH
    at = 0
    for d, part in enumerate(parts):
        start = max((d - 1) * blocks, first)
        stop = min(d * blocks, first + 2 * REACH + 1)
        if stop <= start:
            continue
        begin = (start - (d - 1) * blocks) * size
        width = (stop - start) * size
        value = dot(tiles[:, at:at + width], part[begin:begin + width, :])
        total = value if total is None else total + value
        at += width
    return total


def diagonal_of(diag, o, b, size, columns):
    row = diag[o:o + 1, b * size:(b + 1) * size]
    column = jnp.transpose(jnp.broadcast_to(row, (LANES, size)))
    return jnp.concatenate([column] * (columns // LANES), axis=1)


def near_kernel(w, low, own, high, diag, image, token):
    token[...] = jnp.zeros_like(token)
    ops, rows, columns = image.shape
    size = w.shape[1] // ops
    blocks = rows // size
    for b in range(blocks):
        product = near_product(w.at[b], (low, own, high), b, blocks, size)
        here = slice(b * size, (b + 1) * size)
        ub = own[here, :].astype(F32)
        for o in range(ops):
            image[o, here, :] = (
                product[o * size:(o + 1) * size] + diagonal_of(diag, o, b, size, columns) * ub
            )


def image_kernel(own, near, left, right, cmsg, out0, out1, mout, image, coef):
    ops = image.shape[0]
    blocks, rank, size = right.shape
    rows, columns = own.shape
    take_coefs(cmsg, coef, ops * rank)
    inner = [None] * ops
    squares = None
    for b in range(blocks):
        here = slice(b * size, (b + 1) * size)
        ub = own[here, :].astype(F32)
        part = jnp.sum(ub * ub, axis=0, keepdims=True)
        squares = part if squares is None else squares + part
        for o in range(ops):
            far = dot(left[b], coef[b, o * rank:(o + 1) * rank, :], ((0,), (0,)))
            value = near[o, here, :] + far.astype(BF16).astype(F32)
            image[o, here, :] = value
            part = jnp.sum(ub * value, axis=0, keepdims=True)
            inner[o] = part if inner[o] is None else inner[o] + part
    stats = []
    spreads = []
    good = squares > 0
    for o in range(ops):
        shift = jnp.where(good, inner[o] / jnp.where(good, squares, 1.0), 0.0)
        pieces = split3(shift)
        stats += pieces
        shift = pieces[0].astype(F32) + pieces[1].astype(F32) + pieces[2].astype(F32)
        spread = None
        z = []
        for b in range(blocks):
            ub = own[b * size:(b + 1) * size, :].astype(F32)
            v = image[o, b * size:(b + 1) * size, :] - shift * ub
            part = jnp.sum(v * v, axis=0, keepdims=True)
            spread = part if spread is None else spread + part
            v = v.astype(BF16)
            (out0, out1)[o][b * size:(b + 1) * size, :] = v
            z.append(dot(right[b], v))
        for pair in range(SLICES // 2):
            first, second = halves(chunk(z[0], pair), chunk(z[1], pair))
            mout[2 * pair, o * rank:(o + 1) * rank, :] = first.astype(BF16)
            mout[2 * pair + 1, o * rank:(o + 1) * rank, :] = second.astype(BF16)
        spreads.append(spread)
    zero = jnp.zeros((1, columns), BF16)
    out0[rows:, :] = jnp.concatenate(stats + [zero] * (STATS - len(stats)), axis=0)
    stats += split3(squares)
    for spread in spreads:
        stats += split3(spread)
    stats = jnp.concatenate(stats + [zero] * (STATS - len(stats)), axis=0).astype(F32)
    for pair in range(SLICES // 2):
        part = chunk(stats, pair)
        first, second = halves(part, part)
        mout[2 * pair, ops * rank:ops * rank + STATS, :] = first.astype(BF16)
        mout[2 * pair + 1, ops * rank:ops * rank + STATS, :] = second.astype(BF16)


def second_couple(panels, ops, rank, far, cols, group, after_low, after_high, held, *refs):
    msgs, (out, zs, st) = refs[:-3], refs[-3:]
    count = len(msgs)
    body = ops * rank
    step = SLICES * 2 * rank
    for m, msg in enumerate(msgs):
        at = group_at(group, m, count, SLICES)
        st[pl.ds(at, SLICES)] = msg[:, body:body + STATS, :].astype(F32)
    every = st[...]
    squares = join3(every, ops)
    scale_sq = jnp.sum(squares, axis=0, keepdims=True) / panels + EPSILON
    reverse = 1.0 / jnp.sqrt(scale_sq)
    heights, norms = [], []
    for o in range(ops):
        shift = join3(every, o)
        height = jnp.sum(shift * squares, axis=0, keepdims=True) / panels / scale_sq
        delta = shift - height
        spread = join3(every, ops + 1 + o) + delta * delta * squares
        norm = jnp.sqrt(jnp.sum(spread, axis=0, keepdims=True) / panels / scale_sq + EPSILON)
        heights.append(height)
        norms.append(norm)
    for m, msg in enumerate(msgs):
        at = group_at(group, m, count, step)
        mine = msg[:, body:body + STATS, :].astype(F32)
        base = held_part(held, m, ops, rank)
        for o in range(ops):
            delta = join3(mine, o) - heights[o]
            z = msg[:, o * rank:(o + 1) * rank, :].astype(F32) + delta[:, None, :] * base
            z = z * (reverse / norms[o])[None]
            zs[o, pl.ds(at, step), :] = spread_rows(z, rank)
    rows = []
    for row in heights + norms + [reverse]:
        rows += split3(row)
    rows += [jnp.zeros_like(rows[0])] * (STATS - len(rows))
    rows = jnp.concatenate(rows, axis=0)
    for s in range(SLICES):
        c = [couple(cols, held, s, b, ops, rank, far, [zs.at[o] for o in range(ops)]) for b in range(2)]
        out[s, 0:body, :] = halves(c[0], c[1])[0].astype(BF16)
        out[s, body:body + STATS, :] = rows


def apply_second(o, factor, changes, u3, v3, w, diag, left, cmsg, images, ext, coef, out, sems):
    blocks, rank, size = left.shape
    rows, columns = u3[1].shape
    ops = w.shape[1] // size
    take_coefs(cmsg, coef, ops * rank)
    for at, (u, v) in enumerate(zip(u3, v3)):
        value = v[0:rows, :].astype(F32) * factor + u[...].astype(F32) * changes[at]
        ext[at] = value.astype(BF16)
    copies = []
    for b in range(blocks):
        parts = [ext.at[at] for at in range(3)]
        product = near_product(w.at[b, o * size:(o + 1) * size], parts, b, blocks, size)
        far = dot(left[b], coef[b, o * rank:(o + 1) * rank, :], ((0,), (0,)))
        here = slice(b * size, (b + 1) * size)
        out[here, :] = (
            product
            + diagonal_of(diag, o, b, size, columns) * ext[1, here, :].astype(F32)
            + far.astype(BF16).astype(F32)
        )
        copies.append(pltpu.make_async_copy(out.at[here], images.at[o, here], sems.at[b]))
        copies[-1].start()
    for copy in copies:
        copy.wait()


def final_first(
    w,
    ulow,
    uown,
    uhigh,
    vlow,
    vown,
    vhigh,
    diag,
    left,
    cmsg,
    images,
    heights,
    norms,
    aux,
    ext,
    coef,
    out,
    stat,
    sems,
):
    blocks, rank, size = left.shape
    rows, columns = uown.shape
    ops = w.shape[1] // size
    body = ops * rank
    for pair in range(SLICES // 2):
        stat[:, pair * LANES:(pair + 1) * LANES] = halves(
            cmsg[2 * pair, body:body + STATS, :].astype(F32),
            cmsg[2 * pair + 1, body:body + STATS, :].astype(F32),
        )[0]
    st = stat[...]
    reverse = row3(st, 2 * ops)
    scales = []
    for o in range(ops):
        height = row3(st, o)
        norm = row3(st, ops + o)
        heights[o:o + 1, :] = height
        norms[o:o + 1, :] = norm
        factor = reverse / norm
        changes = [
            (row3(v[rows:, :].astype(F32), o) - height) * factor for v in (vlow, vown, vhigh)
        ]
        scales.append((factor, changes))
    factor, changes = scales[1]
    aux[0:1, :] = factor
    for at in range(3):
        aux[1 + at:2 + at, :] = changes[at]
    factor, changes = scales[0]
    u3, v3 = (ulow, uown, uhigh), (vlow, vown, vhigh)
    apply_second(0, factor, changes, u3, v3, w, diag, left, cmsg, images, ext, coef, out, sems)


def final_second(
    begun,
    w,
    ulow,
    uown,
    uhigh,
    vlow,
    vown,
    vhigh,
    diag,
    left,
    cmsg,
    aux,
    images,
    ext,
    coef,
    out,
    sems,
):
    factor, changes = aux[0:1, :], [aux[1 + at:2 + at, :] for at in range(3)]
    u3, v3 = (ulow, uown, uhigh), (vlow, vown, vhigh)
    apply_second(1, factor, changes, u3, v3, w, diag, left, cmsg, images, ext, coef, out, sems)


def ring(block):
    count = lax.axis_size("store")
    forward = [(i, (i + 1) % count) for i in range(count)]
    backward = [(target, source) for source, target in forward]
    return lax.ppermute(block, "store", forward), lax.ppermute(block, "store", backward)


def shards(
    sources,
    self_terms,
    near_tiles,
    near_cols,
    near_count,
    far_cols,
    basis_left,
    basis_right,
    couplings,
):
    n = lax.axis_size("store")
    ops, blocks, near, size, _ = near_tiles.shape
    rank = basis_left.shape[2]
    far = far_cols.shape[1]
    rows, columns = sources.shape
    all_blocks = blocks * n
    count = n // SLICES
    groups = [[s * count + g for s in range(SLICES)] for g in range(count)]
    sds = jax.ShapeDtypeStruct
    body = ops * rank

    def exchange(x):
        return lax.all_to_all(x, "store", 0, 0, axis_index_groups=groups, tiled=True)

    def across(x):
        parts = [x]
        for m in range(1, count):
            pairs = [(i, i - i % count + (i + m) % count) for i in range(n)]
            parts.append(lax.ppermute(x, "store", pairs))
        return parts

    place = lax.axis_index("store").astype(jnp.int32)
    row0 = (place * blocks).reshape(1)
    group = lax.rem(place, jnp.int32(count)).reshape(1)
    left = jnp.transpose(basis_left, (0, 2, 1))
    right = jnp.transpose(basis_right, (0, 2, 1))

    low, high = ring(sources)
    shared = (blocks + 1) * body
    z1, packed = call(
        functools.partial(coeff_kernel, count),
        [sds((SLICES, rank, LANES), BF16), sds((shared + STATS, LANES), BF16)],
        [SMEM, VMEM, VMEM, VMEM],
        megabytes=60,
    )(far_cols, sources, right, couplings)
    z1 = across(z1)
    mine = call(
        share_kernel,
        sds((SLICES, shared + STATS + count * rank, LANES), BF16),
        [VMEM] * (1 + count),
        megabytes=60,
    )(packed, *z1)
    held = exchange(mine)
    cols = held[:, shared, :blocks * far].astype(jnp.int32).reshape(-1)

    w = call(
        functools.partial(order_tiles, all_blocks),
        sds((blocks, ops * size, near * size), BF16),
        [SMEM, SMEM, SMEM, VMEM, ANY],
        megabytes=60,
    )(near_cols, near_count, row0, near_tiles, mine)
    image, token = call(
        near_kernel,
        [sds((ops, rows, columns), F32), sds((8, LANES), F32)],
        [VMEM] * 5,
        micros=10.0,
        megabytes=60,
    )(w, low, sources, high, self_terms)

    c1 = call(
        functools.partial(first_couple, ops, rank, far),
        sds((SLICES, body, LANES), BF16),
        [SMEM, SMEM, ANY, VMEM],
        [pltpu.VMEM((n * blocks * rank, LANES), BF16)],
    )(cols, group, token, held)
    c1 = exchange(c1)

    first, second, msg = call(
        image_kernel,
        [
            sds((rows + STATS, columns), BF16),
            sds((rows, columns), BF16),
            sds((SLICES, body + STATS, LANES), BF16),
        ],
        [VMEM] * 5,
        [
            pltpu.VMEM((ops, rows, columns), F32),
            pltpu.VMEM((blocks, body, columns), BF16),
        ],
        micros=2.0,
    )(sources, image, left, right, c1)
    low0, high0 = ring(first)
    low1, high1 = ring(second)
    msgs = across(exchange(msg))

    c2 = call(
        functools.partial(second_couple, all_blocks * size, ops, rank, far),
        sds((SLICES, body + STATS, LANES), BF16),
        [SMEM, SMEM, ANY, ANY] + [VMEM] * (1 + count),
        [
            pltpu.VMEM((ops, n * blocks * rank, LANES), BF16),
            pltpu.VMEM((n, STATS, LANES), F32),
        ],
        micros=30.0,
    )(cols, group, low0, high0, held, *msgs)
    c2 = exchange(c2)

    outs = sds((ops, rows, columns), F32)
    scratch = [
        pltpu.VMEM((3, rows, columns), BF16),
        pltpu.VMEM((blocks, body, columns), BF16),
        pltpu.VMEM((rows, columns), F32),
    ]
    images, heights, norms, aux = call(
        final_first,
        [outs, sds((ops, columns), F32), sds((ops, columns), F32), sds((8, columns), F32)],
        [VMEM] * 10,
        scratch + [pltpu.VMEM((STATS, columns), F32), pltpu.SemaphoreType.DMA((blocks,))],
        out_specs=[ANY, VMEM, VMEM, VMEM],
    )(w, low, sources, high, low0, first, high0, self_terms, left, c2)
    images = call(
        final_second,
        outs,
        [ANY] + [VMEM] * 11,
        scratch + [pltpu.SemaphoreType.DMA((blocks,))],
        out_specs=ANY,
        alias={0: 0},
    )(images, w, low, sources, high, low1, second, high1, self_terms, left, c2, aux)
    return images, heights, norms


def solution(mesh):
    placed = (
        P(("groups", "store"), None),
        P(None, "store"),
        P(None, "store", None, None, None),
        P("store", None),
        P("store"),
        P("store", None),
        P("store", None, None),
        P("store", None, None),
        P(None, "store", None, None, None),
    )
    return jax.shard_map(
        shards,
        mesh=mesh,
        in_specs=placed,
        out_specs=(P(None, ("groups", "store"), None), P("groups", None), P("groups", None)),
        check_vma=False,
    )
```

```python
import functools

import jax
import jax.numpy as jnp
from jax import lax
from jax.experimental import pallas as pl
from jax.experimental.pallas import tpu as pltpu
from jax.sharding import PartitionSpec as P

REACH = 2
EPSILON = 1e-06
LANES = 128
HALF = 64
SLICES = 8
STATS = 16
FLOP_RATE = 1150000000
F32 = jnp.float32
BF16 = jnp.bfloat16

VMEM = pl.BlockSpec(memory_space=pltpu.VMEM)
SMEM = pl.BlockSpec(memory_space=pltpu.SMEM)
ANY = pl.BlockSpec(memory_space=pl.ANY)


def call(body, out_shape, in_specs, scratch=(), micros=0.0, megabytes=20, out_specs=None, alias=None):
    many = isinstance(out_shape, (list, tuple))
    if out_specs is None:
        out_specs = [VMEM] * len(out_shape) if many else VMEM
    return pl.pallas_call(
        body,
        out_shape=out_shape,
        in_specs=in_specs,
        out_specs=out_specs,
        input_output_aliases=alias or {},
        scratch_shapes=list(scratch),
        compiler_params=pltpu.CompilerParams(vmem_limit_bytes=megabytes * 1024 * 1024),
        cost_estimate=pl.CostEstimate(
            flops=int(micros * FLOP_RATE), bytes_accessed=0, transcendentals=0
        ),
    )


def dot(a, b, dims=((1,), (0,))):
    return lax.dot_general(a, b, (dims, ((), ())), preferred_element_type=F32)


def split3(row):
    high = row.astype(BF16)
    rest = row - high.astype(F32)
    middle = rest.astype(BF16)
    low = (rest - middle.astype(F32)).astype(BF16)
    return [high, middle, low]


def join3(rows, at):
    return rows[..., 3 * at, :] + rows[..., 3 * at + 1, :] + rows[..., 3 * at + 2, :]


def row3(values, at):
    return values[3 * at:3 * at + 1] + values[3 * at + 1:3 * at + 2] + values[3 * at + 2:3 * at + 3]


def halves(x, y):
    left = lax.broadcasted_iota(jnp.int32, x.shape, x.ndim - 1) < HALF
    first = jnp.where(left, x, pltpu.roll(y, HALF, x.ndim - 1))
    second = jnp.where(left, pltpu.roll(x, HALF, x.ndim - 1), y)
    return first, second


def chunk(x, pair):
    return x[:, pair * LANES:(pair + 1) * LANES]


def order_tiles(all_blocks, cols, count, row0, tiles, after, out):
    ops, blocks, near, size, _ = tiles.shape
    for b in range(blocks):
        for k in range(near):
            rel = lax.rem(cols[b, k] - (row0[0] + b) + REACH + all_blocks, all_blocks)
            rel = lax.rem(rel, all_blocks)
            at = pl.multiple_of(rel * size, size)
            live = k < count[b]
            for o in range(ops):
                tile = tiles[o, b, k]
                out[b, o * size:(o + 1) * size, pl.ds(at, size)] = jnp.where(
                    live, tile, jnp.zeros_like(tile)
                )


def coeff_kernel(count, far_cols, u, left, right, coup, out, u_out):
    ops, blocks, far, rank, _ = coup.shape
    size = right.shape[2]
    u_out[...] = u[...]
    z = [dot(right[b], u[b * size:(b + 1) * size, :]) for b in range(blocks)]
    at = 3 * ops * rank + STATS + rank
    for pair in range(SLICES // 2):
        first, second = halves(chunk(z[0], pair), chunk(z[1], pair))
        out[2 * pair, at:at + rank, :] = first.astype(BF16)
        out[2 * pair + 1, at:at + rank, :] = second.astype(BF16)
    whole, rest = [], []
    for b in range(blocks):
        tiles = [
            jnp.concatenate([coup[o, b, f] for f in range(far)], axis=1) for o in range(ops)
        ]
        tiles = jnp.concatenate(tiles, axis=0)
        whole.append(tiles[:, :LANES])
        rest.append(tiles[:, LANES:])
    lane = lax.broadcasted_iota(jnp.int32, (STATS, LANES), 1)
    names = jnp.zeros((STATS, LANES), F32)
    for b in range(blocks):
        for f in range(far):
            col = far_cols[b, f]
            device = lax.div(col, blocks)
            slot = lax.rem(device, count) * SLICES + lax.div(device, count)
            name = (slot * blocks + lax.rem(col, blocks)).astype(F32)
            names = jnp.where(lane == b * far + f, name, names)
    mixed = [dot(right[b], left[b], ((1,), (1,))) for b in range(blocks)]
    high = [m.astype(BF16) for m in mixed]
    low = [(m - h.astype(F32)).astype(BF16) for m, h in zip(mixed, high)]
    whole = jnp.concatenate(
        whole
        + [jnp.concatenate(rest, axis=1), names.astype(BF16), jnp.concatenate(high + low, axis=1)],
        axis=0,
    )
    for s in range(SLICES):
        out[s, 0:at, :] = whole


def take_kernel(held, after, out):
    out[...] = held[:, held.shape[1] - out.shape[1]:, :]


def coupling_rows(held, s, b, ops, rank):
    body = ops * rank
    first = held[s, b * body:(b + 1) * body, :]
    rest = held[s, 2 * body:3 * body, b * HALF:(b + 1) * HALF]
    return jnp.concatenate([first, rest], axis=1)


def couple(cols, held, s, b, ops, rank, far, z):
    at = (s * 2 + b) * far
    lhs = coupling_rows(held, s, b, ops, rank)
    starts = [pl.multiple_of(cols[at + f] * rank, rank) for f in range(far)]
    picked = [
        jnp.concatenate([x[pl.ds(start, rank), :] for start in starts], axis=0) for x in z
    ]
    if len(z) == 1:
        return dot(lhs, picked[0])
    return jnp.concatenate(
        [dot(lhs[o * rank:(o + 1) * rank], picked[o]) for o in range(ops)], axis=0
    )


def spread_rows(source, rank):
    count = source.shape[0]
    turned = pltpu.roll(source, HALF, 2)
    both = jnp.concatenate([source[:, None], turned[:, None]], axis=1)
    return both.reshape(count * 2 * rank, LANES).astype(BF16)


def group_at(group, m, groups, step):
    return pl.multiple_of(lax.rem(group[0] + (groups - m), groups) * step, step)


def first_couple(ops, rank, far, cols, group, held, late, *refs):
    parts, (out, mixed, zs) = refs[:-3], refs[-3:]
    step = SLICES * 2 * rank
    body = ops * rank
    for m, part in enumerate(parts):
        at = group_at(group, m, len(parts), step)
        zs[pl.ds(at, step), :] = spread_rows(part[...].astype(F32), rank)
    out[:, body:, :] = late[...]
    at = 3 * ops * rank + STATS
    first = lax.broadcasted_iota(jnp.int32, (rank, LANES), 1) < HALF
    for s in range(SLICES):
        c = [couple(cols, held, s, b, ops, rank, far, [zs]) for b in range(2)]
        c = halves(c[0], c[1])[0]
        out[s, 0:body, :] = c.astype(BF16)
        for o in range(ops):
            x = c[o * rank:(o + 1) * rank]
            parts = [jnp.where(first, x, 0.0), jnp.where(first, 0.0, x)] * 2
            parts = jnp.concatenate(parts, axis=0).astype(BF16)
            mixed[s, o * rank:(o + 1) * rank, :] = dot(held[s, at:at + rank, :], parts)


def take_coefs(cmsg, coef, rows):
    for pair in range(SLICES // 2):
        parts = halves(
            cmsg[2 * pair, 0:rows, :].astype(F32), cmsg[2 * pair + 1, 0:rows, :].astype(F32)
        )
        for b in range(2):
            coef[b, :, pair * LANES:(pair + 1) * LANES] = parts[b].astype(BF16)


def near_product(tiles, parts, b, blocks, size):
    total = None
    first = b - REACH
    at = 0
    for d, part in enumerate(parts):
        start = max((d - 1) * blocks, first)
        stop = min(d * blocks, first + 2 * REACH + 1)
        if stop <= start:
            continue
        begin = (start - (d - 1) * blocks) * size
        width = (stop - start) * size
        value = dot(tiles[:, at:at + width], part[begin:begin + width, :])
        total = value if total is None else total + value
        at += width
    return total


def diagonal_of(diag, o, b, size, columns):
    row = diag[o:o + 1, b * size:(b + 1) * size]
    column = jnp.transpose(jnp.broadcast_to(row, (LANES, size)))
    return jnp.concatenate([column] * (columns // LANES), axis=1)


def pieces_of(values):
    rows = []
    for value in values:
        rows += split3(value)
    zero = jnp.zeros_like(rows[0])
    return jnp.concatenate(rows + [zero] * (STATS - len(rows)), axis=0)


def spread_pairs(out, rows, x, y):
    for pair in range(SLICES // 2):
        first, second = halves(chunk(x, pair), chunk(y, pair))
        out[2 * pair, rows, :] = first.astype(BF16)
        out[2 * pair + 1, rows, :] = second.astype(BF16)


def ratio(inner, squares):
    good = squares > 0
    return jnp.where(good, inner / jnp.where(good, squares, 1.0), 0.0)


def near_kernel(w, low, own, high, diag, right, image, edge, msg):
    ops = image.shape[0]
    blocks, rank, size = right.shape
    rows, columns = own.shape
    body = ops * rank
    inner = [None] * ops
    squares = None
    for b in range(blocks):
        product = near_product(w.at[b], (low, own, high), b, blocks, size)
        ub = own[b * size:(b + 1) * size, :].astype(F32)
        part = jnp.sum(ub * ub, axis=0, keepdims=True)
        squares = part if squares is None else squares + part
        for o in range(ops):
            value = (
                product[o * size:(o + 1) * size]
                + diagonal_of(diag, o, b, size, columns) * ub
            )
            image[o, b * size:(b + 1) * size, :] = value
            part = jnp.sum(ub * value, axis=0, keepdims=True)
            inner[o] = part if inner[o] is None else inner[o] + part
    shifts = [ratio(x, squares) for x in inner]
    edges = pieces_of(shifts + [squares])
    edge[...] = edges
    edges = edges.astype(F32)
    for o in range(ops):
        shift = row3(edges, o)
        z = []
        for b in range(blocks):
            ub = own[b * size:(b + 1) * size, :].astype(F32)
            v = image[o, b * size:(b + 1) * size, :] - shift * ub
            image[o, b * size:(b + 1) * size, :] = v
            z.append(dot(right[b], v.astype(BF16)))
        spread_pairs(msg, slice(o * rank, (o + 1) * rank), z[0], z[1])
    spread_pairs(msg, slice(body, body + STATS), edges, edges)


def image_kernel(own, near, edge, left, got, mixed, vout, cown, xmsg, image, coef):
    ops = near.shape[0]
    blocks, rank, size = left.shape
    rows, columns = own.shape
    body = ops * rank
    for s in range(SLICES):
        xmsg[s * body:(s + 1) * body, :] = (
            got[s, body:2 * body, :].astype(F32) + mixed[s]
        ).astype(BF16)
        at = SLICES * body + s * STATS
        xmsg[at:at + STATS, :] = got[s, 2 * body:2 * body + STATS, :]
    take_coefs(got, coef, body)
    edges = edge[...].astype(F32)
    squares = row3(edges, ops)
    shifts, spreads = [], []
    for o in range(ops):
        inner = None
        for b in range(blocks):
            cown[(o * blocks + b) * rank:(o * blocks + b + 1) * rank, :] = coef[
                b, o * rank:(o + 1) * rank, :
            ]
            far = dot(left[b], coef[b, o * rank:(o + 1) * rank, :], ((0,), (0,)))
            value = near[o, b * size:(b + 1) * size, :] + far.astype(BF16).astype(F32)
            image[b * size:(b + 1) * size, :] = value
            ub = own[b * size:(b + 1) * size, :].astype(F32)
            part = jnp.sum(ub * value, axis=0, keepdims=True)
            inner = part if inner is None else inner + part
        before = row3(edges, o)
        after = before + ratio(inner, squares)
        shifts.append(after)
        change = sum(x.astype(F32) for x in split3(after)) - before
        spread = None
        for b in range(blocks):
            ub = own[b * size:(b + 1) * size, :].astype(F32)
            v = image[b * size:(b + 1) * size, :] - change * ub
            part = jnp.sum(v * v, axis=0, keepdims=True)
            spread = part if spread is None else spread + part
            vout[(o * blocks + b) * size:(o * blocks + b + 1) * size, :] = v.astype(BF16)
        spreads.append(spread)
    every = pieces_of(shifts + [squares] + spreads)
    vout[ops * rows:, :] = every
    at = SLICES * (body + STATS)
    for j in range(columns // LANES):
        xmsg[at + j * STATS:at + (j + 1) * STATS, :] = chunk(every, j)


def second_couple(panels, ops, rank, far, cols, group, held, *refs):
    out, zs = refs[-2:]
    count = (len(refs) - 2) // 2
    z1, parts = refs[:count], refs[count:2 * count]
    body = ops * rank
    step = SLICES * 2 * rank
    at = SLICES * body
    edges = [
        x[at:at + SLICES * STATS, :].astype(F32).reshape(SLICES, STATS, LANES) for x in parts
    ]
    scale_sq = EPSILON
    totals = [0.0] * ops
    for x in edges:
        squares = join3(x, ops)
        scale_sq = scale_sq + jnp.sum(squares, axis=0, keepdims=True) / panels
        for o in range(ops):
            totals[o] = totals[o] + jnp.sum(join3(x, o) * squares, axis=0, keepdims=True) / panels
    rough = pieces_of([total / scale_sq for total in totals])
    for m, x in enumerate(parts):
        row = group_at(group, m, count, step)
        base = z1[m][...].astype(F32)
        z = x[0:at, :].astype(F32).reshape(SLICES, body, LANES)
        for o in range(ops):
            delta = join3(edges[m], o) - row3(rough.astype(F32), o)
            value = z[:, o * rank:(o + 1) * rank, :] + delta[:, None, :] * base
            zs[o, pl.ds(row, step), :] = spread_rows(value, rank)
    start = at + SLICES * STATS
    for s in range(SLICES):
        c = [couple(cols, held, s, b, ops, rank, far, [zs.at[o] for o in range(ops)]) for b in range(2)]
        out[s, 0:body, :] = halves(c[0], c[1])[0].astype(BF16)
        out[s, body:body + STATS, :] = rough
        for m, x in enumerate(parts):
            height = x.shape[0] - start
            row = body + STATS + m * height
            out[s, row:row + height, :] = x[start:, :]


def apply_second(o, rows3, u3, v3, w, diag, left, cown, cmsg, images, ext, coef, out, sem):
    blocks, rank, size = left.shape
    rows, columns = u3[1].shape
    ops = w.shape[1] // size
    factor, changes, offset = rows3
    copies = []
    for at, (u, v) in enumerate(zip(u3, v3)):
        v = v[o * rows:(o + 1) * rows, :].astype(F32)
        value = v * factor + u[...].astype(F32) * changes[at]
        ext[at] = value.astype(BF16)
    take_coefs(cmsg, coef, ops * rank)
    for b in range(blocks):
        parts = [ext.at[at] for at in range(3)]
        product = near_product(w.at[b, o * size:(o + 1) * size], parts, b, blocks, size)
        row = (o * blocks + b) * rank
        c = coef[b, o * rank:(o + 1) * rank, :].astype(F32) * factor
        c = c - offset * cown[row:row + rank, :].astype(F32)
        far = dot(left[b], c.astype(BF16), ((0,), (0,)))
        here = slice(b * size, (b + 1) * size)
        out[o, here, :] = (
            product
            + diagonal_of(diag, o, b, size, columns) * ext[1, here, :].astype(F32)
            + far.astype(BF16).astype(F32)
        )
        copies.append(pltpu.make_async_copy(out.at[o, here], images.at[o, here], sem.at[o, b]))
        copies[-1].start()
    return copies


def final_kernel(
    panels,
    group,
    w,
    ulow,
    uown,
    uhigh,
    vlow,
    vown,
    vhigh,
    diag,
    left,
    cown,
    cmsg,
    images,
    heights,
    norms,
    ext,
    coef,
    out,
    st,
    sem,
):
    blocks, rank, size = left.shape
    rows, columns = uown.shape
    ops = w.shape[1] // size
    body = ops * rank
    wide = columns // LANES
    height = wide * STATS
    count = (cmsg.shape[1] - body - STATS) // height
    for m in range(count):
        at = group_at(group, m, count, SLICES)
        for j in range(wide):
            row = body + STATS + m * height + j * STATS
            st[pl.ds(at, SLICES), :, j * LANES:(j + 1) * LANES] = cmsg[
                :, row:row + STATS, :
            ].astype(F32)
    rough = jnp.concatenate(
        [
            halves(
                cmsg[2 * pair, body:body + STATS, :].astype(F32),
                cmsg[2 * pair + 1, body:body + STATS, :].astype(F32),
            )[0]
            for pair in range(wide)
        ],
        axis=1,
    )
    every = st[...]
    squares = join3(every, ops)
    scale_sq = jnp.sum(squares, axis=0, keepdims=True) / panels + EPSILON
    reverse = 1.0 / jnp.sqrt(scale_sq)
    found = []
    for o in range(ops):
        shift = join3(every, o)
        high = jnp.sum(shift * squares, axis=0, keepdims=True) / panels / scale_sq
        delta = shift - high
        spread = join3(every, ops + 1 + o) + delta * delta * squares
        norm = jnp.sqrt(jnp.sum(spread, axis=0, keepdims=True) / panels / scale_sq + EPSILON)
        heights[o:o + 1, :] = high
        norms[o:o + 1, :] = norm
        factor = reverse / norm
        changes = [
            (row3(v[ops * rows:, :].astype(F32), o) - high) * factor
            for v in (vlow, vown, vhigh)
        ]
        found.append((factor, changes, (high - row3(rough, o)) * factor))
    copies = []
    for o in range(ops):
        copies += apply_second(
            o,
            found[o],
            (ulow, uown, uhigh),
            (vlow, vown, vhigh),
            w,
            diag,
            left,
            cown,
            cmsg,
            images,
            ext,
            coef,
            out,
            sem,
        )
    for copy in copies:
        copy.wait()


def ring(block):
    count = lax.axis_size("store")
    forward = [(i, (i + 1) % count) for i in range(count)]
    backward = [(target, source) for source, target in forward]
    return lax.ppermute(block, "store", forward), lax.ppermute(block, "store", backward)


def shards(
    sources,
    self_terms,
    near_tiles,
    near_cols,
    near_count,
    far_cols,
    basis_left,
    basis_right,
    couplings,
):
    n = lax.axis_size("store")
    ops, blocks, near, size, _ = near_tiles.shape
    rank = basis_left.shape[2]
    far = far_cols.shape[1]
    rows, columns = sources.shape
    all_blocks = blocks * n
    count = n // SLICES
    groups = [[s * count + g for s in range(SLICES)] for g in range(count)]
    sds = jax.ShapeDtypeStruct
    body = ops * rank

    def exchange(x):
        return lax.all_to_all(x, "store", 0, 0, axis_index_groups=groups, tiled=True)

    def across(x):
        parts = [x]
        for m in range(1, count):
            pairs = [(i, i - i % count + (i + m) % count) for i in range(n)]
            parts.append(lax.ppermute(x, "store", pairs))
        return parts

    place = lax.axis_index("store").astype(jnp.int32)
    row0 = (place * blocks).reshape(1)
    group = lax.rem(place, jnp.int32(count)).reshape(1)
    left = jnp.transpose(basis_left, (0, 2, 1))
    right = jnp.transpose(basis_right, (0, 2, 1))

    shared = (blocks + 1) * body
    lead = shared + STATS + rank
    mine, own = call(
        functools.partial(coeff_kernel, count),
        [sds((SLICES, lead + rank, LANES), BF16), sds(sources.shape, BF16)],
        [SMEM] + [VMEM] * 4,
        megabytes=60,
    )(far_cols, sources, left, right, couplings)
    low, high = ring(own)
    held = exchange(mine)
    cols = held[:, shared, :blocks * far].astype(jnp.int32).reshape(-1)

    w = call(
        functools.partial(order_tiles, all_blocks),
        sds((blocks, ops * size, near * size), BF16),
        [SMEM, SMEM, SMEM, VMEM, ANY],
        megabytes=60,
    )(near_cols, near_count, row0, near_tiles, mine)
    image, edge, late = call(
        near_kernel,
        [
            sds((ops, rows, columns), F32),
            sds((STATS, columns), BF16),
            sds((SLICES, body + STATS, LANES), BF16),
        ],
        [VMEM] * 6,
        micros=10.0,
        megabytes=60,
    )(w, low, sources, high, self_terms, right)

    z1 = across(call(take_kernel, sds((SLICES, rank, LANES), BF16), [VMEM, ANY])(held, edge))
    msg, mixed = call(
        functools.partial(first_couple, ops, rank, far),
        [sds((SLICES, 2 * body + STATS, LANES), BF16), sds((SLICES, body, LANES), F32)],
        [SMEM, SMEM] + [VMEM] * (2 + count),
        [pltpu.VMEM((n * blocks * rank, LANES), BF16)],
    )(cols, group, held, late, *z1)
    got = exchange(msg)

    v, cown, xmsg = call(
        image_kernel,
        [
            sds((ops * rows + STATS, columns), BF16),
            sds((ops * blocks * rank, columns), BF16),
            sds((SLICES * (body + STATS) + columns // LANES * STATS, LANES), BF16),
        ],
        [VMEM] * 6,
        [pltpu.VMEM((rows, columns), F32), pltpu.VMEM((blocks, body, columns), BF16)],
        micros=2.0,
    )(sources, image, edge, left, got, mixed)
    parts = across(xmsg)
    vlow, vhigh = ring(v)

    panels = all_blocks * size
    c2 = call(
        functools.partial(second_couple, panels, ops, rank, far),
        sds((SLICES, body + STATS + count * columns // LANES * STATS, LANES), BF16),
        [SMEM, SMEM] + [VMEM] * (1 + 2 * count),
        [pltpu.VMEM((ops, n * blocks * rank, LANES), BF16)],
        micros=30.0,
    )(cols, group, held, *z1, *parts)
    c2 = exchange(c2)

    images, heights, norms = call(
        functools.partial(final_kernel, panels),
        [sds((ops, rows, columns), F32), sds((ops, columns), F32), sds((ops, columns), F32)],
        [SMEM] + [VMEM] * 11,
        [
            pltpu.VMEM((3, rows, columns), BF16),
            pltpu.VMEM((blocks, body, columns), BF16),
            pltpu.VMEM((ops, rows, columns), F32),
            pltpu.VMEM((n, STATS, columns), F32),
            pltpu.SemaphoreType.DMA((ops, blocks)),
        ],
        out_specs=[ANY, VMEM, VMEM],
    )(group, w, low, sources, high, vlow, v, vhigh, self_terms, left, cown, c2)
    return images, heights, norms


def solution(mesh):
    placed = (
        P(("groups", "store"), None),
        P(None, "store"),
        P(None, "store", None, None, None),
        P("store", None),
        P("store"),
        P("store", None),
        P("store", None, None),
        P("store", None, None),
        P(None, "store", None, None, None),
    )
    return jax.shard_map(
        shards,
        mesh=mesh,
        in_specs=placed,
        out_specs=(P(None, ("groups", "store"), None), P("groups", None), P("groups", None)),
        check_vma=False,
    )
```

```python
import functools

import jax
import jax.numpy as jnp
from jax import lax
from jax.experimental import pallas as pl
from jax.experimental.pallas import tpu as pltpu
from jax.sharding import PartitionSpec as P

REACH = 2
EPSILON = 1e-06
LANES = 128
HALF = 64
SLICES = 8
STATS = 16
FLOP_RATE = 1150000000
F32 = jnp.float32
BF16 = jnp.bfloat16

VMEM = pl.BlockSpec(memory_space=pltpu.VMEM)
SMEM = pl.BlockSpec(memory_space=pltpu.SMEM)
ANY = pl.BlockSpec(memory_space=pl.ANY)


def call(body, out_shape, in_specs, scratch=(), micros=0.0, megabytes=20, out_specs=None, alias=None):
    many = isinstance(out_shape, (list, tuple))
    if out_specs is None:
        out_specs = [VMEM] * len(out_shape) if many else VMEM
    return pl.pallas_call(
        body,
        out_shape=out_shape,
        in_specs=in_specs,
        out_specs=out_specs,
        input_output_aliases=alias or {},
        scratch_shapes=list(scratch),
        compiler_params=pltpu.CompilerParams(vmem_limit_bytes=megabytes * 1024 * 1024),
        cost_estimate=pl.CostEstimate(
            flops=int(micros * FLOP_RATE), bytes_accessed=0, transcendentals=0
        ),
    )


def dot(a, b, dims=((1,), (0,))):
    return lax.dot_general(a, b, (dims, ((), ())), preferred_element_type=F32)


def split3(row):
    high = row.astype(BF16)
    rest = row - high.astype(F32)
    middle = rest.astype(BF16)
    low = (rest - middle.astype(F32)).astype(BF16)
    return [high, middle, low]


def join3(rows, at):
    return rows[..., 3 * at, :] + rows[..., 3 * at + 1, :] + rows[..., 3 * at + 2, :]


def row3(values, at):
    return values[3 * at:3 * at + 1] + values[3 * at + 1:3 * at + 2] + values[3 * at + 2:3 * at + 3]


def halves(x, y):
    left = lax.broadcasted_iota(jnp.int32, x.shape, x.ndim - 1) < HALF
    first = jnp.where(left, x, pltpu.roll(y, HALF, x.ndim - 1))
    second = jnp.where(left, pltpu.roll(x, HALF, x.ndim - 1), y)
    return first, second


def chunk(x, pair):
    return x[:, pair * LANES:(pair + 1) * LANES]


def order_tiles(all_blocks, cols, count, row0, tiles, after, out):
    ops, blocks, near, size, _ = tiles.shape
    for b in range(blocks):
        for k in range(near):
            rel = lax.rem(cols[b, k] - (row0[0] + b) + REACH + all_blocks, all_blocks)
            rel = lax.rem(rel, all_blocks)
            at = pl.multiple_of(rel * size, size)
            live = k < count[b]
            for o in range(ops):
                tile = tiles[o, b, k]
                out[b, o * size:(o + 1) * size, pl.ds(at, size)] = jnp.where(
                    live, tile, jnp.zeros_like(tile)
                )


def coeff_kernel(count, far_cols, u, right, coup, out, u_out):
    ops, blocks, far, rank, _ = coup.shape
    size = right.shape[2]
    u_out[...] = u[...]
    z = [dot(right[b], u[b * size:(b + 1) * size, :]) for b in range(blocks)]
    at = 3 * ops * rank + STATS
    for pair in range(SLICES // 2):
        first, second = halves(chunk(z[0], pair), chunk(z[1], pair))
        out[2 * pair, at:at + rank, :] = first.astype(BF16)
        out[2 * pair + 1, at:at + rank, :] = second.astype(BF16)
    whole, rest = [], []
    for b in range(blocks):
        tiles = [
            jnp.concatenate([coup[o, b, f] for f in range(far)], axis=1) for o in range(ops)
        ]
        tiles = jnp.concatenate(tiles, axis=0)
        whole.append(tiles[:, :LANES])
        rest.append(tiles[:, LANES:])
    lane = lax.broadcasted_iota(jnp.int32, (STATS, LANES), 1)
    names = jnp.zeros((STATS, LANES), F32)
    for b in range(blocks):
        for f in range(far):
            col = far_cols[b, f]
            device = lax.div(col, blocks)
            slot = lax.rem(device, count) * SLICES + lax.div(device, count)
            name = (slot * blocks + lax.rem(col, blocks)).astype(F32)
            names = jnp.where(lane == b * far + f, name, names)
    whole = jnp.concatenate(
        whole + [jnp.concatenate(rest, axis=1), names.astype(BF16)], axis=0
    )
    for s in range(SLICES):
        out[s, 0:at, :] = whole


def take_kernel(held, after, out):
    out[...] = held[:, held.shape[1] - out.shape[1]:, :]


def coupling_rows(held, s, b, ops, rank):
    body = ops * rank
    first = held[s, b * body:(b + 1) * body, :]
    rest = held[s, 2 * body:3 * body, b * HALF:(b + 1) * HALF]
    return jnp.concatenate([first, rest], axis=1)


def couple(cols, held, s, b, ops, rank, far, z):
    at = (s * 2 + b) * far
    lhs = coupling_rows(held, s, b, ops, rank)
    starts = [pl.multiple_of(cols[at + f] * rank, rank) for f in range(far)]
    picked = [
        jnp.concatenate([x[pl.ds(start, rank), :] for start in starts], axis=0) for x in z
    ]
    if len(z) == 1:
        return dot(lhs, picked[0])
    return jnp.concatenate(
        [dot(lhs[o * rank:(o + 1) * rank], picked[o]) for o in range(ops)], axis=0
    )


def spread_rows(source, rank):
    count = source.shape[0]
    turned = pltpu.roll(source, HALF, 2)
    both = jnp.concatenate([source[:, None], turned[:, None]], axis=1)
    return both.reshape(count * 2 * rank, LANES).astype(BF16)


def group_at(group, m, groups, step):
    return pl.multiple_of(lax.rem(group[0] + (groups - m), groups) * step, step)


def first_couple(ops, rank, far, cols, group, held, *refs):
    parts, (out, zs) = refs[:-2], refs[-2:]
    step = SLICES * 2 * rank
    for m, part in enumerate(parts):
        at = group_at(group, m, len(parts), step)
        zs[pl.ds(at, step), :] = spread_rows(part[...].astype(F32), rank)
    for s in range(SLICES):
        c = [couple(cols, held, s, b, ops, rank, far, [zs]) for b in range(2)]
        out[s] = halves(c[0], c[1])[0].astype(BF16)


def take_coefs(cmsg, coef, rows):
    for pair in range(SLICES // 2):
        parts = halves(
            cmsg[2 * pair, 0:rows, :].astype(F32), cmsg[2 * pair + 1, 0:rows, :].astype(F32)
        )
        for b in range(2):
            coef[b, :, pair * LANES:(pair + 1) * LANES] = parts[b].astype(BF16)


def near_product(tiles, parts, b, blocks, size):
    total = None
    first = b - REACH
    at = 0
    for d, part in enumerate(parts):
        start = max((d - 1) * blocks, first)
        stop = min(d * blocks, first + 2 * REACH + 1)
        if stop <= start:
            continue
        begin = (start - (d - 1) * blocks) * size
        width = (stop - start) * size
        value = dot(tiles[:, at:at + width], part[begin:begin + width, :])
        total = value if total is None else total + value
        at += width
    return total


def diagonal_of(diag, o, b, size, columns):
    row = diag[o:o + 1, b * size:(b + 1) * size]
    column = jnp.transpose(jnp.broadcast_to(row, (LANES, size)))
    return jnp.concatenate([column] * (columns // LANES), axis=1)


def near_kernel(w, low, own, high, diag, image, token):
    token[...] = jnp.zeros_like(token)
    ops, rows, columns = image.shape
    size = w.shape[1] // ops
    blocks = rows // size
    for b in range(blocks):
        product = near_product(w.at[b], (low, own, high), b, blocks, size)
        here = slice(b * size, (b + 1) * size)
        ub = own[here, :].astype(F32)
        for o in range(ops):
            image[o, here, :] = (
                product[o * size:(o + 1) * size] + diagonal_of(diag, o, b, size, columns) * ub
            )


def image_kernel(own, near, left, right, cmsg, out0, out1, mout, image, coef):
    ops = image.shape[0]
    blocks, rank, size = right.shape
    rows, columns = own.shape
    take_coefs(cmsg, coef, ops * rank)
    inner = [None] * ops
    squares = None
    for b in range(blocks):
        here = slice(b * size, (b + 1) * size)
        ub = own[here, :].astype(F32)
        part = jnp.sum(ub * ub, axis=0, keepdims=True)
        squares = part if squares is None else squares + part
        for o in range(ops):
            far = dot(left[b], coef[b, o * rank:(o + 1) * rank, :], ((0,), (0,)))
            value = near[o, here, :] + far.astype(BF16).astype(F32)
            image[o, here, :] = value
            part = jnp.sum(ub * value, axis=0, keepdims=True)
            inner[o] = part if inner[o] is None else inner[o] + part
    stats = []
    spreads = []
    good = squares > 0
    for o in range(ops):
        shift = jnp.where(good, inner[o] / jnp.where(good, squares, 1.0), 0.0)
        pieces = split3(shift)
        stats += pieces
        shift = pieces[0].astype(F32) + pieces[1].astype(F32) + pieces[2].astype(F32)
        spread = None
        z = []
        for b in range(blocks):
            ub = own[b * size:(b + 1) * size, :].astype(F32)
            v = image[o, b * size:(b + 1) * size, :] - shift * ub
            part = jnp.sum(v * v, axis=0, keepdims=True)
            spread = part if spread is None else spread + part
            v = v.astype(BF16)
            (out0, out1)[o][b * size:(b + 1) * size, :] = v
            z.append(dot(right[b], v))
        for pair in range(SLICES // 2):
            first, second = halves(chunk(z[0], pair), chunk(z[1], pair))
            mout[2 * pair, o * rank:(o + 1) * rank, :] = first.astype(BF16)
            mout[2 * pair + 1, o * rank:(o + 1) * rank, :] = second.astype(BF16)
        spreads.append(spread)
    zero = jnp.zeros((1, columns), BF16)
    out0[rows:, :] = jnp.concatenate(stats + [zero] * (STATS - len(stats)), axis=0)
    stats += split3(squares)
    for spread in spreads:
        stats += split3(spread)
    stats = jnp.concatenate(stats + [zero] * (STATS - len(stats)), axis=0).astype(F32)
    for pair in range(SLICES // 2):
        part = chunk(stats, pair)
        first, second = halves(part, part)
        mout[2 * pair, ops * rank:ops * rank + STATS, :] = first.astype(BF16)
        mout[2 * pair + 1, ops * rank:ops * rank + STATS, :] = second.astype(BF16)


def second_couple(panels, ops, rank, far, cols, group, after_low, after_high, held, *refs):
    out, zs, st = refs[-3:]
    count = (len(refs) - 3) // 2
    z1, msgs = refs[:count], refs[count:2 * count]
    body = ops * rank
    step = SLICES * 2 * rank
    for m, msg in enumerate(msgs):
        at = group_at(group, m, count, SLICES)
        st[pl.ds(at, SLICES)] = msg[:, body:body + STATS, :].astype(F32)
    every = st[...]
    squares = join3(every, ops)
    scale_sq = jnp.sum(squares, axis=0, keepdims=True) / panels + EPSILON
    reverse = 1.0 / jnp.sqrt(scale_sq)
    heights, norms = [], []
    for o in range(ops):
        shift = join3(every, o)
        height = jnp.sum(shift * squares, axis=0, keepdims=True) / panels / scale_sq
        delta = shift - height
        spread = join3(every, ops + 1 + o) + delta * delta * squares
        norm = jnp.sqrt(jnp.sum(spread, axis=0, keepdims=True) / panels / scale_sq + EPSILON)
        heights.append(height)
        norms.append(norm)
    for m, msg in enumerate(msgs):
        at = group_at(group, m, count, step)
        mine = msg[:, body:body + STATS, :].astype(F32)
        base = z1[m][...].astype(F32)
        for o in range(ops):
            delta = join3(mine, o) - heights[o]
            z = msg[:, o * rank:(o + 1) * rank, :].astype(F32) + delta[:, None, :] * base
            z = z * (reverse / norms[o])[None]
            zs[o, pl.ds(at, step), :] = spread_rows(z, rank)
    rows = []
    for row in heights + norms + [reverse]:
        rows += split3(row)
    rows += [jnp.zeros_like(rows[0])] * (STATS - len(rows))
    rows = jnp.concatenate(rows, axis=0)
    for s in range(SLICES):
        c = [couple(cols, held, s, b, ops, rank, far, [zs.at[o] for o in range(ops)]) for b in range(2)]
        out[s, 0:body, :] = halves(c[0], c[1])[0].astype(BF16)
        out[s, body:body + STATS, :] = rows


def apply_second(o, factor, changes, u3, v3, w, diag, left, cmsg, images, ext, coef, out, sems):
    blocks, rank, size = left.shape
    rows, columns = u3[1].shape
    ops = w.shape[1] // size
    take_coefs(cmsg, coef, ops * rank)
    for at, (u, v) in enumerate(zip(u3, v3)):
        value = v[0:rows, :].astype(F32) * factor + u[...].astype(F32) * changes[at]
        ext[at] = value.astype(BF16)
    copies = []
    for b in range(blocks):
        parts = [ext.at[at] for at in range(3)]
        product = near_product(w.at[b, o * size:(o + 1) * size], parts, b, blocks, size)
        far = dot(left[b], coef[b, o * rank:(o + 1) * rank, :], ((0,), (0,)))
        here = slice(b * size, (b + 1) * size)
        out[here, :] = (
            product
            + diagonal_of(diag, o, b, size, columns) * ext[1, here, :].astype(F32)
            + far.astype(BF16).astype(F32)
        )
        copies.append(pltpu.make_async_copy(out.at[here], images.at[o, here], sems.at[b]))
        copies[-1].start()
    for copy in copies:
        copy.wait()


def final_first(
    w,
    ulow,
    uown,
    uhigh,
    vlow,
    vown,
    vhigh,
    diag,
    left,
    cmsg,
    images,
    heights,
    norms,
    aux,
    ext,
    coef,
    out,
    stat,
    sems,
):
    blocks, rank, size = left.shape
    rows, columns = uown.shape
    ops = w.shape[1] // size
    body = ops * rank
    for pair in range(SLICES // 2):
        stat[:, pair * LANES:(pair + 1) * LANES] = halves(
            cmsg[2 * pair, body:body + STATS, :].astype(F32),
            cmsg[2 * pair + 1, body:body + STATS, :].astype(F32),
        )[0]
    st = stat[...]
    reverse = row3(st, 2 * ops)
    scales = []
    for o in range(ops):
        height = row3(st, o)
        norm = row3(st, ops + o)
        heights[o:o + 1, :] = height
        norms[o:o + 1, :] = norm
        factor = reverse / norm
        changes = [
            (row3(v[rows:, :].astype(F32), o) - height) * factor for v in (vlow, vown, vhigh)
        ]
        scales.append((factor, changes))
    factor, changes = scales[1]
    aux[0:1, :] = factor
    for at in range(3):
        aux[1 + at:2 + at, :] = changes[at]
    factor, changes = scales[0]
    u3, v3 = (ulow, uown, uhigh), (vlow, vown, vhigh)
    apply_second(0, factor, changes, u3, v3, w, diag, left, cmsg, images, ext, coef, out, sems)


def final_second(
    begun,
    w,
    ulow,
    uown,
    uhigh,
    vlow,
    vown,
    vhigh,
    diag,
    left,
    cmsg,
    aux,
    images,
    ext,
    coef,
    out,
    sems,
):
    factor, changes = aux[0:1, :], [aux[1 + at:2 + at, :] for at in range(3)]
    u3, v3 = (ulow, uown, uhigh), (vlow, vown, vhigh)
    apply_second(1, factor, changes, u3, v3, w, diag, left, cmsg, images, ext, coef, out, sems)


def ring(block):
    count = lax.axis_size("store")
    forward = [(i, (i + 1) % count) for i in range(count)]
    backward = [(target, source) for source, target in forward]
    return lax.ppermute(block, "store", forward), lax.ppermute(block, "store", backward)


def shards(
    sources,
    self_terms,
    near_tiles,
    near_cols,
    near_count,
    far_cols,
    basis_left,
    basis_right,
    couplings,
):
    n = lax.axis_size("store")
    ops, blocks, near, size, _ = near_tiles.shape
    rank = basis_left.shape[2]
    far = far_cols.shape[1]
    rows, columns = sources.shape
    all_blocks = blocks * n
    count = n // SLICES
    groups = [[s * count + g for s in range(SLICES)] for g in range(count)]
    sds = jax.ShapeDtypeStruct
    body = ops * rank

    def exchange(x):
        return lax.all_to_all(x, "store", 0, 0, axis_index_groups=groups, tiled=True)

    def across(x):
        parts = [x]
        for m in range(1, count):
            pairs = [(i, i - i % count + (i + m) % count) for i in range(n)]
            parts.append(lax.ppermute(x, "store", pairs))
        return parts

    place = lax.axis_index("store").astype(jnp.int32)
    row0 = (place * blocks).reshape(1)
    group = lax.rem(place, jnp.int32(count)).reshape(1)
    left = jnp.transpose(basis_left, (0, 2, 1))
    right = jnp.transpose(basis_right, (0, 2, 1))

    shared = (blocks + 1) * body
    mine, own = call(
        functools.partial(coeff_kernel, count),
        [sds((SLICES, shared + STATS + rank, LANES), BF16), sds(sources.shape, BF16)],
        [SMEM] + [VMEM] * 3,
        megabytes=60,
    )(far_cols, sources, right, couplings)
    low, high = ring(own)
    held = exchange(mine)
    cols = held[:, shared, :blocks * far].astype(jnp.int32).reshape(-1)

    w = call(
        functools.partial(order_tiles, all_blocks),
        sds((blocks, ops * size, near * size), BF16),
        [SMEM, SMEM, SMEM, VMEM, ANY],
        megabytes=60,
    )(near_cols, near_count, row0, near_tiles, mine)
    image, token = call(
        near_kernel,
        [sds((ops, rows, columns), F32), sds((8, LANES), F32)],
        [VMEM] * 5,
        micros=10.0,
    )(w, low, sources, high, self_terms)
    z1 = across(call(take_kernel, sds((SLICES, rank, LANES), BF16), [VMEM, ANY])(held, token))

    c1 = call(
        functools.partial(first_couple, ops, rank, far),
        sds((SLICES, body, LANES), BF16),
        [SMEM, SMEM] + [VMEM] * (1 + count),
        [pltpu.VMEM((n * blocks * rank, LANES), BF16)],
    )(cols, group, held, *z1)
    c1 = exchange(c1)

    first, second, msg = call(
        image_kernel,
        [
            sds((rows + STATS, columns), BF16),
            sds((rows, columns), BF16),
            sds((SLICES, body + STATS, LANES), BF16),
        ],
        [VMEM] * 5,
        [
            pltpu.VMEM((ops, rows, columns), F32),
            pltpu.VMEM((blocks, body, columns), BF16),
        ],
        micros=2.0,
    )(sources, image, left, right, c1)
    low0, high0 = ring(first)
    low1, high1 = ring(second)
    msgs = across(exchange(msg))

    c2 = call(
        functools.partial(second_couple, all_blocks * size, ops, rank, far),
        sds((SLICES, body + STATS, LANES), BF16),
        [SMEM, SMEM, ANY, ANY] + [VMEM] * (1 + 2 * count),
        [
            pltpu.VMEM((ops, n * blocks * rank, LANES), BF16),
            pltpu.VMEM((n, STATS, LANES), F32),
        ],
        micros=30.0,
    )(cols, group, low0, high0, held, *z1, *msgs)
    c2 = exchange(c2)

    outs = sds((ops, rows, columns), F32)
    scratch = [
        pltpu.VMEM((3, rows, columns), BF16),
        pltpu.VMEM((blocks, body, columns), BF16),
        pltpu.VMEM((rows, columns), F32),
    ]
    images, heights, norms, aux = call(
        final_first,
        [outs, sds((ops, columns), F32), sds((ops, columns), F32), sds((8, columns), F32)],
        [VMEM] * 10,
        scratch + [pltpu.VMEM((STATS, columns), F32), pltpu.SemaphoreType.DMA((blocks,))],
        out_specs=[ANY, VMEM, VMEM, VMEM],
    )(w, low, sources, high, low0, first, high0, self_terms, left, c2)
    images = call(
        final_second,
        outs,
        [ANY] + [VMEM] * 11,
        scratch + [pltpu.SemaphoreType.DMA((blocks,))],
        out_specs=ANY,
        alias={0: 0},
    )(images, w, low, sources, high, low1, second, high1, self_terms, left, c2, aux)
    return images, heights, norms


def solution(mesh):
    placed = (
        P(("groups", "store"), None),
        P(None, "store"),
        P(None, "store", None, None, None),
        P("store", None),
        P("store"),
        P("store", None),
        P("store", None, None),
        P("store", None, None),
        P(None, "store", None, None, None),
    )
    return jax.shard_map(
        shards,
        mesh=mesh,
        in_specs=placed,
        out_specs=(P(None, ("groups", "store"), None), P("groups", None), P("groups", None)),
        check_vma=False,
    )
```

```python
import functools

import jax
import jax.numpy as jnp
from jax import lax
from jax.experimental import pallas as pl
from jax.experimental.pallas import tpu as pltpu
from jax.sharding import PartitionSpec as P

REACH = 2
EPSILON = 1e-06
LANES = 128
HALF = 64
SLICES = 8
STATS = 16
FLOP_RATE = 1150000000
F32 = jnp.float32
BF16 = jnp.bfloat16

VMEM = pl.BlockSpec(memory_space=pltpu.VMEM)
SMEM = pl.BlockSpec(memory_space=pltpu.SMEM)
ANY = pl.BlockSpec(memory_space=pl.ANY)


def call(body, out_shape, in_specs, scratch=(), micros=0.0, megabytes=20, out_specs=None, alias=None):
    many = isinstance(out_shape, (list, tuple))
    if out_specs is None:
        out_specs = [VMEM] * len(out_shape) if many else VMEM
    return pl.pallas_call(
        body,
        out_shape=out_shape,
        in_specs=in_specs,
        out_specs=out_specs,
        input_output_aliases=alias or {},
        scratch_shapes=list(scratch),
        compiler_params=pltpu.CompilerParams(vmem_limit_bytes=megabytes * 1024 * 1024),
        cost_estimate=pl.CostEstimate(
            flops=int(micros * FLOP_RATE), bytes_accessed=0, transcendentals=0
        ),
    )


def dot(a, b, dims=((1,), (0,))):
    return lax.dot_general(a, b, (dims, ((), ())), preferred_element_type=F32)


def split3(row):
    high = row.astype(BF16)
    rest = row - high.astype(F32)
    middle = rest.astype(BF16)
    low = (rest - middle.astype(F32)).astype(BF16)
    return [high, middle, low]


def join3(rows, at):
    return rows[..., 3 * at, :] + rows[..., 3 * at + 1, :] + rows[..., 3 * at + 2, :]


def row3(values, at):
    return values[3 * at:3 * at + 1] + values[3 * at + 1:3 * at + 2] + values[3 * at + 2:3 * at + 3]


def halves(x, y):
    left = lax.broadcasted_iota(jnp.int32, x.shape, x.ndim - 1) < HALF
    first = jnp.where(left, x, pltpu.roll(y, HALF, x.ndim - 1))
    second = jnp.where(left, pltpu.roll(x, HALF, x.ndim - 1), y)
    return first, second


def chunk(x, pair):
    return x[:, pair * LANES:(pair + 1) * LANES]


def order_tiles(all_blocks, cols, count, row0, tiles, after, out):
    ops, blocks, near, size, _ = tiles.shape
    for b in range(blocks):
        for k in range(near):
            rel = lax.rem(cols[b, k] - (row0[0] + b) + REACH + all_blocks, all_blocks)
            rel = lax.rem(rel, all_blocks)
            at = pl.multiple_of(rel * size, size)
            live = k < count[b]
            for o in range(ops):
                tile = tiles[o, b, k]
                out[b, o * size:(o + 1) * size, pl.ds(at, size)] = jnp.where(
                    live, tile, jnp.zeros_like(tile)
                )


def coeff_kernel(count, far_cols, u, right, coup, out, u_out):
    ops, blocks, far, rank, _ = coup.shape
    size = right.shape[2]
    u_out[...] = u[...]
    z = [dot(right[b], u[b * size:(b + 1) * size, :]) for b in range(blocks)]
    at = 3 * ops * rank + STATS
    for pair in range(SLICES // 2):
        first, second = halves(chunk(z[0], pair), chunk(z[1], pair))
        out[2 * pair, at:at + rank, :] = first.astype(BF16)
        out[2 * pair + 1, at:at + rank, :] = second.astype(BF16)
    whole, rest = [], []
    for b in range(blocks):
        tiles = [
            jnp.concatenate([coup[o, b, f] for f in range(far)], axis=1) for o in range(ops)
        ]
        tiles = jnp.concatenate(tiles, axis=0)
        whole.append(tiles[:, :LANES])
        rest.append(tiles[:, LANES:])
    lane = lax.broadcasted_iota(jnp.int32, (STATS, LANES), 1)
    names = jnp.zeros((STATS, LANES), F32)
    for b in range(blocks):
        for f in range(far):
            col = far_cols[b, f]
            device = lax.div(col, blocks)
            slot = lax.rem(device, count) * SLICES + lax.div(device, count)
            name = (slot * blocks + lax.rem(col, blocks)).astype(F32)
            names = jnp.where(lane == b * far + f, name, names)
    whole = jnp.concatenate(
        whole + [jnp.concatenate(rest, axis=1), names.astype(BF16)], axis=0
    )
    for s in range(SLICES):
        out[s, 0:at, :] = whole


def take_kernel(held, after, out):
    out[...] = held[:, held.shape[1] - out.shape[1]:, :]


def coupling_rows(held, s, b, ops, rank):
    body = ops * rank
    first = held[s, b * body:(b + 1) * body, :]
    rest = held[s, 2 * body:3 * body, b * HALF:(b + 1) * HALF]
    return jnp.concatenate([first, rest], axis=1)


def couple(cols, held, s, b, ops, rank, far, z):
    at = (s * 2 + b) * far
    lhs = coupling_rows(held, s, b, ops, rank)
    starts = [pl.multiple_of(cols[at + f] * rank, rank) for f in range(far)]
    picked = [
        jnp.concatenate([x[pl.ds(start, rank), :] for start in starts], axis=0) for x in z
    ]
    if len(z) == 1:
        return dot(lhs, picked[0])
    return jnp.concatenate(
        [dot(lhs[o * rank:(o + 1) * rank], picked[o]) for o in range(ops)], axis=0
    )


def spread_rows(source, rank):
    count = source.shape[0]
    turned = pltpu.roll(source, HALF, 2)
    both = jnp.concatenate([source[:, None], turned[:, None]], axis=1)
    return both.reshape(count * 2 * rank, LANES).astype(BF16)


def group_at(group, m, groups, step):
    return pl.multiple_of(lax.rem(group[0] + (groups - m), groups) * step, step)


def first_couple(ops, rank, far, cols, group, after, held, *refs):
    parts, (out, zs) = refs[:-2], refs[-2:]
    step = SLICES * 2 * rank
    for m, part in enumerate(parts):
        at = group_at(group, m, len(parts), step)
        zs[pl.ds(at, step), :] = spread_rows(part[...].astype(F32), rank)
    for s in range(SLICES):
        c = [couple(cols, held, s, b, ops, rank, far, [zs]) for b in range(2)]
        out[s] = halves(c[0], c[1])[0].astype(BF16)


def take_coefs(cmsg, coef, rows):
    for pair in range(SLICES // 2):
        parts = halves(
            cmsg[2 * pair, 0:rows, :].astype(F32), cmsg[2 * pair + 1, 0:rows, :].astype(F32)
        )
        for b in range(2):
            coef[b, :, pair * LANES:(pair + 1) * LANES] = parts[b].astype(BF16)


def near_product(tiles, parts, b, blocks, size):
    total = None
    first = b - REACH
    at = 0
    for d, part in enumerate(parts):
        start = max((d - 1) * blocks, first)
        stop = min(d * blocks, first + 2 * REACH + 1)
        if stop <= start:
            continue
        begin = (start - (d - 1) * blocks) * size
        width = (stop - start) * size
        value = dot(tiles[:, at:at + width], part[begin:begin + width, :])
        total = value if total is None else total + value
        at += width
    return total


def diagonal_of(diag, o, b, size, columns):
    row = diag[o:o + 1, b * size:(b + 1) * size]
    column = jnp.transpose(jnp.broadcast_to(row, (LANES, size)))
    return jnp.concatenate([column] * (columns // LANES), axis=1)


def near_kernel(w, low, own, high, diag, image, token):
    token[...] = jnp.zeros_like(token)
    ops, rows, columns = image.shape
    size = w.shape[1] // ops
    blocks = rows // size
    for b in range(blocks):
        product = near_product(w.at[b], (low, own, high), b, blocks, size)
        here = slice(b * size, (b + 1) * size)
        ub = own[here, :].astype(F32)
        for o in range(ops):
            image[o, here, :] = (
                product[o * size:(o + 1) * size] + diagonal_of(diag, o, b, size, columns) * ub
            )


def image_kernel(own, near, left, right, cmsg, out0, out1, mout, image, coef):
    ops = image.shape[0]
    blocks, rank, size = right.shape
    rows, columns = own.shape
    take_coefs(cmsg, coef, ops * rank)
    inner = [None] * ops
    squares = None
    for b in range(blocks):
        here = slice(b * size, (b + 1) * size)
        ub = own[here, :].astype(F32)
        part = jnp.sum(ub * ub, axis=0, keepdims=True)
        squares = part if squares is None else squares + part
        for o in range(ops):
            far = dot(left[b], coef[b, o * rank:(o + 1) * rank, :], ((0,), (0,)))
            value = near[o, here, :] + far.astype(BF16).astype(F32)
            image[o, here, :] = value
            part = jnp.sum(ub * value, axis=0, keepdims=True)
            inner[o] = part if inner[o] is None else inner[o] + part
    stats = []
    spreads = []
    good = squares > 0
    for o in range(ops):
        shift = jnp.where(good, inner[o] / jnp.where(good, squares, 1.0), 0.0)
        pieces = split3(shift)
        stats += pieces
        shift = pieces[0].astype(F32) + pieces[1].astype(F32) + pieces[2].astype(F32)
        spread = None
        z = []
        for b in range(blocks):
            ub = own[b * size:(b + 1) * size, :].astype(F32)
            v = image[o, b * size:(b + 1) * size, :] - shift * ub
            part = jnp.sum(v * v, axis=0, keepdims=True)
            spread = part if spread is None else spread + part
            v = v.astype(BF16)
            (out0, out1)[o][b * size:(b + 1) * size, :] = v
            z.append(dot(right[b], v))
        for pair in range(SLICES // 2):
            first, second = halves(chunk(z[0], pair), chunk(z[1], pair))
            mout[2 * pair, o * rank:(o + 1) * rank, :] = first.astype(BF16)
            mout[2 * pair + 1, o * rank:(o + 1) * rank, :] = second.astype(BF16)
        spreads.append(spread)
    zero = jnp.zeros((1, columns), BF16)
    out0[rows:, :] = jnp.concatenate(stats + [zero] * (STATS - len(stats)), axis=0)
    stats += split3(squares)
    for spread in spreads:
        stats += split3(spread)
    stats = jnp.concatenate(stats + [zero] * (STATS - len(stats)), axis=0).astype(F32)
    for pair in range(SLICES // 2):
        part = chunk(stats, pair)
        first, second = halves(part, part)
        mout[2 * pair, ops * rank:ops * rank + STATS, :] = first.astype(BF16)
        mout[2 * pair + 1, ops * rank:ops * rank + STATS, :] = second.astype(BF16)


def second_couple(panels, ops, rank, far, cols, group, after_low, after_high, held, *refs):
    out, zs, st = refs[-3:]
    count = (len(refs) - 3) // 2
    z1, msgs = refs[:count], refs[count:2 * count]
    body = ops * rank
    step = SLICES * 2 * rank
    for m, msg in enumerate(msgs):
        at = group_at(group, m, count, SLICES)
        st[pl.ds(at, SLICES)] = msg[:, body:body + STATS, :].astype(F32)
    every = st[...]
    squares = join3(every, ops)
    scale_sq = jnp.sum(squares, axis=0, keepdims=True) / panels + EPSILON
    reverse = 1.0 / jnp.sqrt(scale_sq)
    heights, norms = [], []
    for o in range(ops):
        shift = join3(every, o)
        height = jnp.sum(shift * squares, axis=0, keepdims=True) / panels / scale_sq
        delta = shift - height
        spread = join3(every, ops + 1 + o) + delta * delta * squares
        norm = jnp.sqrt(jnp.sum(spread, axis=0, keepdims=True) / panels / scale_sq + EPSILON)
        heights.append(height)
        norms.append(norm)
    for m, msg in enumerate(msgs):
        at = group_at(group, m, count, step)
        mine = msg[:, body:body + STATS, :].astype(F32)
        base = z1[m][...].astype(F32)
        for o in range(ops):
            delta = join3(mine, o) - heights[o]
            z = msg[:, o * rank:(o + 1) * rank, :].astype(F32) + delta[:, None, :] * base
            z = z * (reverse / norms[o])[None]
            zs[o, pl.ds(at, step), :] = spread_rows(z, rank)
    rows = []
    for row in heights + norms + [reverse]:
        rows += split3(row)
    rows += [jnp.zeros_like(rows[0])] * (STATS - len(rows))
    rows = jnp.concatenate(rows, axis=0)
    for s in range(SLICES):
        c = [couple(cols, held, s, b, ops, rank, far, [zs.at[o] for o in range(ops)]) for b in range(2)]
        out[s, 0:body, :] = halves(c[0], c[1])[0].astype(BF16)
        out[s, body:body + STATS, :] = rows


def final_kernel(
    w,
    ulow,
    uown,
    uhigh,
    low0,
    own0,
    high0,
    low1,
    own1,
    high1,
    diag,
    left,
    cmsg,
    images,
    heights,
    norms,
    ext,
    coef,
    out,
    stat,
    sems,
):
    blocks, rank, size = left.shape
    rows, columns = uown.shape
    ops = w.shape[1] // size
    body = ops * rank
    for pair in range(SLICES // 2):
        stat[:, pair * LANES:(pair + 1) * LANES] = halves(
            cmsg[2 * pair, body:body + STATS, :].astype(F32),
            cmsg[2 * pair + 1, body:body + STATS, :].astype(F32),
        )[0]
    st = stat[...]
    take_coefs(cmsg, coef, body)
    reverse = row3(st, 2 * ops)
    copies = []
    for o in range(ops):
        height = row3(st, o)
        norm = row3(st, ops + o)
        heights[o:o + 1, :] = height
        norms[o:o + 1, :] = norm
        factor = reverse / norm
        triples = (ulow, low0, low1), (uown, own0, own1), (uhigh, high0, high1)
        for at, (u, v0, v1) in enumerate(triples):
            change = (row3(v0[rows:, :].astype(F32), o) - height) * factor
            v = (v0, v1)[o][0:rows, :].astype(F32)
            ext[o, at] = (v * factor + u[...].astype(F32) * change).astype(BF16)
        for b in range(blocks):
            parts = [ext.at[o, at] for at in range(3)]
            product = near_product(w.at[b, o * size:(o + 1) * size], parts, b, blocks, size)
            far = dot(left[b], coef[b, o * rank:(o + 1) * rank, :], ((0,), (0,)))
            here = slice(b * size, (b + 1) * size)
            out[o, here, :] = (
                product
                + diagonal_of(diag, o, b, size, columns) * ext[o, 1, here, :].astype(F32)
                + far.astype(BF16).astype(F32)
            )
            copy = pltpu.make_async_copy(out.at[o, here], images.at[o, here], sems.at[o, b])
            copy.start()
            copies.append(copy)
    for copy in copies:
        copy.wait()


def ring(block):
    count = lax.axis_size("store")
    forward = [(i, (i + 1) % count) for i in range(count)]
    backward = [(target, source) for source, target in forward]
    return lax.ppermute(block, "store", forward), lax.ppermute(block, "store", backward)


def shards(
    sources,
    self_terms,
    near_tiles,
    near_cols,
    near_count,
    far_cols,
    basis_left,
    basis_right,
    couplings,
):
    n = lax.axis_size("store")
    ops, blocks, near, size, _ = near_tiles.shape
    rank = basis_left.shape[2]
    far = far_cols.shape[1]
    rows, columns = sources.shape
    all_blocks = blocks * n
    count = n // SLICES
    groups = [[s * count + g for s in range(SLICES)] for g in range(count)]
    sds = jax.ShapeDtypeStruct
    body = ops * rank

    def exchange(x):
        return lax.all_to_all(x, "store", 0, 0, axis_index_groups=groups, tiled=True)

    def across(x):
        parts = [x]
        for m in range(1, count):
            pairs = [(i, i - i % count + (i + m) % count) for i in range(n)]
            parts.append(lax.ppermute(x, "store", pairs))
        return parts

    place = lax.axis_index("store").astype(jnp.int32)
    row0 = (place * blocks).reshape(1)
    group = lax.rem(place, jnp.int32(count)).reshape(1)
    left = jnp.transpose(basis_left, (0, 2, 1))
    right = jnp.transpose(basis_right, (0, 2, 1))

    shared = (blocks + 1) * body
    mine, own = call(
        functools.partial(coeff_kernel, count),
        [sds((SLICES, shared + STATS + rank, LANES), BF16), sds(sources.shape, BF16)],
        [SMEM] + [VMEM] * 3,
        megabytes=60,
    )(far_cols, sources, right, couplings)
    low, high = ring(own)
    held = exchange(mine)
    cols = held[:, shared, :blocks * far].astype(jnp.int32).reshape(-1)

    w = call(
        functools.partial(order_tiles, all_blocks),
        sds((blocks, ops * size, near * size), BF16),
        [SMEM, SMEM, SMEM, VMEM, ANY],
        megabytes=60,
    )(near_cols, near_count, row0, near_tiles, mine)
    image, token = call(
        near_kernel,
        [sds((ops, rows, columns), F32), sds((8, LANES), F32)],
        [VMEM] * 5,
        micros=10.0,
    )(w, low, sources, high, self_terms)
    z1 = across(call(take_kernel, sds((SLICES, rank, LANES), BF16), [VMEM, ANY])(held, token))

    c1 = call(
        functools.partial(first_couple, ops, rank, far),
        sds((SLICES, body, LANES), BF16),
        [SMEM, SMEM, ANY] + [VMEM] * (1 + count),
        [pltpu.VMEM((n * blocks * rank, LANES), BF16)],
    )(cols, group, image, held, *z1)
    c1 = exchange(c1)

    first, second, msg = call(
        image_kernel,
        [
            sds((rows + STATS, columns), BF16),
            sds((rows, columns), BF16),
            sds((SLICES, body + STATS, LANES), BF16),
        ],
        [VMEM] * 5,
        [
            pltpu.VMEM((ops, rows, columns), F32),
            pltpu.VMEM((blocks, body, columns), BF16),
        ],
        micros=2.0,
    )(sources, image, left, right, c1)
    low0, high0 = ring(first)
    low1, high1 = ring(second)
    msgs = across(exchange(msg))

    c2 = call(
        functools.partial(second_couple, all_blocks * size, ops, rank, far),
        sds((SLICES, body + STATS, LANES), BF16),
        [SMEM, SMEM, ANY, ANY] + [VMEM] * (1 + 2 * count),
        [
            pltpu.VMEM((ops, n * blocks * rank, LANES), BF16),
            pltpu.VMEM((n, STATS, LANES), F32),
        ],
        micros=30.0,
    )(cols, group, low0, high0, held, *z1, *msgs)
    c2 = exchange(c2)

    images, heights, norms = call(
        final_kernel,
        [sds((ops, rows, columns), F32), sds((ops, columns), F32), sds((ops, columns), F32)],
        [VMEM] * 13,
        [
            pltpu.VMEM((ops, 3, rows, columns), BF16),
            pltpu.VMEM((blocks, body, columns), BF16),
            pltpu.VMEM((ops, rows, columns), F32),
            pltpu.VMEM((STATS, columns), F32),
            pltpu.SemaphoreType.DMA((ops, blocks)),
        ],
        out_specs=[ANY, VMEM, VMEM],
    )(w, low, sources, high, low0, first, high0, low1, second, high1, self_terms, left, c2)
    return images, heights, norms


def solution(mesh):
    placed = (
        P(("groups", "store"), None),
        P(None, "store"),
        P(None, "store", None, None, None),
        P("store", None),
        P("store"),
        P("store", None),
        P("store", None, None),
        P("store", None, None),
        P(None, "store", None, None, None),
    )
    return jax.shard_map(
        shards,
        mesh=mesh,
        in_specs=placed,
        out_specs=(P(None, ("groups", "store"), None), P("groups", None), P("groups", None)),
        check_vma=False,
    )
```

```python
import functools

import jax
import jax.numpy as jnp
from jax import lax
from jax.experimental import pallas as pl
from jax.experimental.pallas import tpu as pltpu
from jax.sharding import PartitionSpec as P

REACH = 2
EPSILON = 1e-06
LANES = 128
HALF = 64
SLICES = 8
STATS = 16
FLOP_RATE = 1150000000
F32 = jnp.float32
BF16 = jnp.bfloat16

VMEM = pl.BlockSpec(memory_space=pltpu.VMEM)
SMEM = pl.BlockSpec(memory_space=pltpu.SMEM)
ANY = pl.BlockSpec(memory_space=pl.ANY)


def call(body, out_shape, in_specs, scratch=(), micros=0.0, megabytes=20, out_specs=None, alias=None):
    many = isinstance(out_shape, (list, tuple))
    if out_specs is None:
        out_specs = [VMEM] * len(out_shape) if many else VMEM
    return pl.pallas_call(
        body,
        out_shape=out_shape,
        in_specs=in_specs,
        out_specs=out_specs,
        input_output_aliases=alias or {},
        scratch_shapes=list(scratch),
        compiler_params=pltpu.CompilerParams(vmem_limit_bytes=megabytes * 1024 * 1024),
        cost_estimate=pl.CostEstimate(
            flops=int(micros * FLOP_RATE), bytes_accessed=0, transcendentals=0
        ),
    )


def dot(a, b, dims=((1,), (0,))):
    return lax.dot_general(a, b, (dims, ((), ())), preferred_element_type=F32)


def split3(row):
    high = row.astype(BF16)
    rest = row - high.astype(F32)
    middle = rest.astype(BF16)
    low = (rest - middle.astype(F32)).astype(BF16)
    return [high, middle, low]


def join3(rows, at):
    return rows[..., 3 * at, :] + rows[..., 3 * at + 1, :] + rows[..., 3 * at + 2, :]


def row3(values, at):
    return values[3 * at:3 * at + 1] + values[3 * at + 1:3 * at + 2] + values[3 * at + 2:3 * at + 3]


def halves(x, y):
    left = lax.broadcasted_iota(jnp.int32, x.shape, x.ndim - 1) < HALF
    first = jnp.where(left, x, pltpu.roll(y, HALF, x.ndim - 1))
    second = jnp.where(left, pltpu.roll(x, HALF, x.ndim - 1), y)
    return first, second


def chunk(x, pair):
    return x[:, pair * LANES:(pair + 1) * LANES]


def order_tiles(all_blocks, cols, count, row0, tiles, after, out):
    ops, blocks, near, size, _ = tiles.shape
    for b in range(blocks):
        for k in range(near):
            rel = lax.rem(cols[b, k] - (row0[0] + b) + REACH + all_blocks, all_blocks)
            rel = lax.rem(rel, all_blocks)
            at = pl.multiple_of(rel * size, size)
            live = k < count[b]
            for o in range(ops):
                tile = tiles[o, b, k]
                out[b, o * size:(o + 1) * size, pl.ds(at, size)] = jnp.where(
                    live, tile, jnp.zeros_like(tile)
                )


def coeff_kernel(count, far_cols, u, right, coup, out, u_out):
    ops, blocks, far, rank, _ = coup.shape
    size = right.shape[2]
    u_out[...] = u[...]
    z = [dot(right[b], u[b * size:(b + 1) * size, :]) for b in range(blocks)]
    at = 3 * ops * rank + STATS
    for pair in range(SLICES // 2):
        first, second = halves(chunk(z[0], pair), chunk(z[1], pair))
        out[2 * pair, at:at + rank, :] = first.astype(BF16)
        out[2 * pair + 1, at:at + rank, :] = second.astype(BF16)
    whole, rest = [], []
    for b in range(blocks):
        tiles = [
            jnp.concatenate([coup[o, b, f] for f in range(far)], axis=1) for o in range(ops)
        ]
        tiles = jnp.concatenate(tiles, axis=0)
        whole.append(tiles[:, :LANES])
        rest.append(tiles[:, LANES:])
    lane = lax.broadcasted_iota(jnp.int32, (STATS, LANES), 1)
    names = jnp.zeros((STATS, LANES), F32)
    for b in range(blocks):
        for f in range(far):
            col = far_cols[b, f]
            device = lax.div(col, blocks)
            slot = lax.rem(device, count) * SLICES + lax.div(device, count)
            name = (slot * blocks + lax.rem(col, blocks)).astype(F32)
            names = jnp.where(lane == b * far + f, name, names)
    whole = jnp.concatenate(
        whole + [jnp.concatenate(rest, axis=1), names.astype(BF16)], axis=0
    )
    for s in range(SLICES):
        out[s, 0:at, :] = whole


def take_kernel(held, after, out):
    out[...] = held[:, held.shape[1] - out.shape[1]:, :]


def coupling_rows(held, s, b, ops, rank):
    body = ops * rank
    first = held[s, b * body:(b + 1) * body, :]
    rest = held[s, 2 * body:3 * body, b * HALF:(b + 1) * HALF]
    return jnp.concatenate([first, rest], axis=1)


def couple(cols, held, s, b, ops, rank, far, z):
    at = (s * 2 + b) * far
    lhs = coupling_rows(held, s, b, ops, rank)
    starts = [pl.multiple_of(cols[at + f] * rank, rank) for f in range(far)]
    picked = [
        jnp.concatenate([x[pl.ds(start, rank), :] for start in starts], axis=0) for x in z
    ]
    if len(z) == 1:
        return dot(lhs, picked[0])
    return jnp.concatenate(
        [dot(lhs[o * rank:(o + 1) * rank], picked[o]) for o in range(ops)], axis=0
    )


def spread_rows(source, rank):
    count = source.shape[0]
    turned = pltpu.roll(source, HALF, 2)
    both = jnp.concatenate([source[:, None], turned[:, None]], axis=1)
    return both.reshape(count * 2 * rank, LANES).astype(BF16)


def group_at(group, m, groups, step):
    return pl.multiple_of(lax.rem(group[0] + (groups - m), groups) * step, step)


def first_couple(ops, rank, far, cols, group, after, held, *refs):
    parts, (out, zs) = refs[:-2], refs[-2:]
    step = SLICES * 2 * rank
    for m, part in enumerate(parts):
        at = group_at(group, m, len(parts), step)
        zs[pl.ds(at, step), :] = spread_rows(part[...].astype(F32), rank)
    for s in range(SLICES):
        c = [couple(cols, held, s, b, ops, rank, far, [zs]) for b in range(2)]
        out[s] = halves(c[0], c[1])[0].astype(BF16)


def take_coefs(cmsg, coef, rows):
    for pair in range(SLICES // 2):
        parts = halves(
            cmsg[2 * pair, 0:rows, :].astype(F32), cmsg[2 * pair + 1, 0:rows, :].astype(F32)
        )
        for b in range(2):
            coef[b, :, pair * LANES:(pair + 1) * LANES] = parts[b].astype(BF16)


def near_product(tiles, parts, b, blocks, size):
    total = None
    first = b - REACH
    at = 0
    for d, part in enumerate(parts):
        start = max((d - 1) * blocks, first)
        stop = min(d * blocks, first + 2 * REACH + 1)
        if stop <= start:
            continue
        begin = (start - (d - 1) * blocks) * size
        width = (stop - start) * size
        value = dot(tiles[:, at:at + width], part[begin:begin + width, :])
        total = value if total is None else total + value
        at += width
    return total


def diagonal_of(diag, o, b, size, columns):
    row = diag[o:o + 1, b * size:(b + 1) * size]
    column = jnp.transpose(jnp.broadcast_to(row, (LANES, size)))
    return jnp.concatenate([column] * (columns // LANES), axis=1)


def near_kernel(w, low, own, high, diag, image, token):
    token[...] = jnp.zeros_like(token)
    ops, rows, columns = image.shape
    size = w.shape[1] // ops
    blocks = rows // size
    for b in range(blocks):
        product = near_product(w.at[b], (low, own, high), b, blocks, size)
        here = slice(b * size, (b + 1) * size)
        ub = own[here, :].astype(F32)
        for o in range(ops):
            image[o, here, :] = (
                product[o * size:(o + 1) * size] + diagonal_of(diag, o, b, size, columns) * ub
            )


def image_kernel(own, near, left, right, cmsg, out0, out1, mout, image, coef):
    ops = image.shape[0]
    blocks, rank, size = right.shape
    rows, columns = own.shape
    take_coefs(cmsg, coef, ops * rank)
    inner = [None] * ops
    squares = None
    for b in range(blocks):
        here = slice(b * size, (b + 1) * size)
        ub = own[here, :].astype(F32)
        part = jnp.sum(ub * ub, axis=0, keepdims=True)
        squares = part if squares is None else squares + part
        for o in range(ops):
            far = dot(left[b], coef[b, o * rank:(o + 1) * rank, :], ((0,), (0,)))
            value = near[o, here, :] + far.astype(BF16).astype(F32)
            image[o, here, :] = value
            part = jnp.sum(ub * value, axis=0, keepdims=True)
            inner[o] = part if inner[o] is None else inner[o] + part
    stats = []
    spreads = []
    good = squares > 0
    for o in range(ops):
        shift = jnp.where(good, inner[o] / jnp.where(good, squares, 1.0), 0.0)
        pieces = split3(shift)
        stats += pieces
        shift = pieces[0].astype(F32) + pieces[1].astype(F32) + pieces[2].astype(F32)
        spread = None
        z = []
        for b in range(blocks):
            ub = own[b * size:(b + 1) * size, :].astype(F32)
            v = image[o, b * size:(b + 1) * size, :] - shift * ub
            part = jnp.sum(v * v, axis=0, keepdims=True)
            spread = part if spread is None else spread + part
            v = v.astype(BF16)
            (out0, out1)[o][b * size:(b + 1) * size, :] = v
            z.append(dot(right[b], v))
        for pair in range(SLICES // 2):
            first, second = halves(chunk(z[0], pair), chunk(z[1], pair))
            mout[2 * pair, o * rank:(o + 1) * rank, :] = first.astype(BF16)
            mout[2 * pair + 1, o * rank:(o + 1) * rank, :] = second.astype(BF16)
        spreads.append(spread)
    zero = jnp.zeros((1, columns), BF16)
    out0[rows:, :] = jnp.concatenate(stats + [zero] * (STATS - len(stats)), axis=0)
    stats += split3(squares)
    for spread in spreads:
        stats += split3(spread)
    stats = jnp.concatenate(stats + [zero] * (STATS - len(stats)), axis=0).astype(F32)
    for pair in range(SLICES // 2):
        part = chunk(stats, pair)
        first, second = halves(part, part)
        mout[2 * pair, ops * rank:ops * rank + STATS, :] = first.astype(BF16)
        mout[2 * pair + 1, ops * rank:ops * rank + STATS, :] = second.astype(BF16)


def second_couple(panels, ops, rank, far, cols, group, after_low, after_high, held, *refs):
    out, zs, st = refs[-3:]
    count = (len(refs) - 3) // 2
    z1, msgs = refs[:count], refs[count:2 * count]
    body = ops * rank
    step = SLICES * 2 * rank
    for m, msg in enumerate(msgs):
        at = group_at(group, m, count, SLICES)
        st[pl.ds(at, SLICES)] = msg[:, body:body + STATS, :].astype(F32)
    every = st[...]
    squares = join3(every, ops)
    scale_sq = jnp.sum(squares, axis=0, keepdims=True) / panels + EPSILON
    reverse = 1.0 / jnp.sqrt(scale_sq)
    heights, norms = [], []
    for o in range(ops):
        shift = join3(every, o)
        height = jnp.sum(shift * squares, axis=0, keepdims=True) / panels / scale_sq
        delta = shift - height
        spread = join3(every, ops + 1 + o) + delta * delta * squares
        norm = jnp.sqrt(jnp.sum(spread, axis=0, keepdims=True) / panels / scale_sq + EPSILON)
        heights.append(height)
        norms.append(norm)
    for m, msg in enumerate(msgs):
        at = group_at(group, m, count, step)
        mine = msg[:, body:body + STATS, :].astype(F32)
        base = z1[m][...].astype(F32)
        for o in range(ops):
            delta = join3(mine, o) - heights[o]
            z = msg[:, o * rank:(o + 1) * rank, :].astype(F32) + delta[:, None, :] * base
            z = z * (reverse / norms[o])[None]
            zs[o, pl.ds(at, step), :] = spread_rows(z, rank)
    rows = []
    for row in heights + norms + [reverse]:
        rows += split3(row)
    rows += [jnp.zeros_like(rows[0])] * (STATS - len(rows))
    rows = jnp.concatenate(rows, axis=0)
    for s in range(SLICES):
        c = [couple(cols, held, s, b, ops, rank, far, [zs.at[o] for o in range(ops)]) for b in range(2)]
        out[s, 0:body, :] = halves(c[0], c[1])[0].astype(BF16)
        out[s, body:body + STATS, :] = rows


def apply_second(o, factor, changes, u3, v3, w, diag, left, cmsg, images, ext, coef, out, sems):
    blocks, rank, size = left.shape
    rows, columns = u3[1].shape
    ops = w.shape[1] // size
    take_coefs(cmsg, coef, ops * rank)
    for at, (u, v) in enumerate(zip(u3, v3)):
        value = v[0:rows, :].astype(F32) * factor + u[...].astype(F32) * changes[at]
        ext[at] = value.astype(BF16)
    copies = []
    for b in range(blocks):
        parts = [ext.at[at] for at in range(3)]
        product = near_product(w.at[b, o * size:(o + 1) * size], parts, b, blocks, size)
        far = dot(left[b], coef[b, o * rank:(o + 1) * rank, :], ((0,), (0,)))
        here = slice(b * size, (b + 1) * size)
        out[here, :] = (
            product
            + diagonal_of(diag, o, b, size, columns) * ext[1, here, :].astype(F32)
            + far.astype(BF16).astype(F32)
        )
        copies.append(pltpu.make_async_copy(out.at[here], images.at[o, here], sems.at[b]))
        copies[-1].start()
    for copy in copies:
        copy.wait()


def final_first(
    w,
    ulow,
    uown,
    uhigh,
    vlow,
    vown,
    vhigh,
    diag,
    left,
    cmsg,
    images,
    heights,
    norms,
    aux,
    ext,
    coef,
    out,
    stat,
    sems,
):
    blocks, rank, size = left.shape
    rows, columns = uown.shape
    ops = w.shape[1] // size
    body = ops * rank
    for pair in range(SLICES // 2):
        stat[:, pair * LANES:(pair + 1) * LANES] = halves(
            cmsg[2 * pair, body:body + STATS, :].astype(F32),
            cmsg[2 * pair + 1, body:body + STATS, :].astype(F32),
        )[0]
    st = stat[...]
    reverse = row3(st, 2 * ops)
    scales = []
    for o in range(ops):
        height = row3(st, o)
        norm = row3(st, ops + o)
        heights[o:o + 1, :] = height
        norms[o:o + 1, :] = norm
        factor = reverse / norm
        changes = [
            (row3(v[rows:, :].astype(F32), o) - height) * factor for v in (vlow, vown, vhigh)
        ]
        scales.append((factor, changes))
    factor, changes = scales[1]
    aux[0:1, :] = factor
    for at in range(3):
        aux[1 + at:2 + at, :] = changes[at]
    factor, changes = scales[0]
    u3, v3 = (ulow, uown, uhigh), (vlow, vown, vhigh)
    apply_second(0, factor, changes, u3, v3, w, diag, left, cmsg, images, ext, coef, out, sems)


def final_second(
    begun,
    w,
    ulow,
    uown,
    uhigh,
    vlow,
    vown,
    vhigh,
    diag,
    left,
    cmsg,
    aux,
    images,
    ext,
    coef,
    out,
    sems,
):
    factor, changes = aux[0:1, :], [aux[1 + at:2 + at, :] for at in range(3)]
    u3, v3 = (ulow, uown, uhigh), (vlow, vown, vhigh)
    apply_second(1, factor, changes, u3, v3, w, diag, left, cmsg, images, ext, coef, out, sems)


def ring(block):
    count = lax.axis_size("store")
    forward = [(i, (i + 1) % count) for i in range(count)]
    backward = [(target, source) for source, target in forward]
    return lax.ppermute(block, "store", forward), lax.ppermute(block, "store", backward)


def shards(
    sources,
    self_terms,
    near_tiles,
    near_cols,
    near_count,
    far_cols,
    basis_left,
    basis_right,
    couplings,
):
    n = lax.axis_size("store")
    ops, blocks, near, size, _ = near_tiles.shape
    rank = basis_left.shape[2]
    far = far_cols.shape[1]
    rows, columns = sources.shape
    all_blocks = blocks * n
    count = n // SLICES
    groups = [[s * count + g for s in range(SLICES)] for g in range(count)]
    sds = jax.ShapeDtypeStruct
    body = ops * rank

    def exchange(x):
        return lax.all_to_all(x, "store", 0, 0, axis_index_groups=groups, tiled=True)

    def across(x):
        parts = [x]
        for m in range(1, count):
            pairs = [(i, i - i % count + (i + m) % count) for i in range(n)]
            parts.append(lax.ppermute(x, "store", pairs))
        return parts

    place = lax.axis_index("store").astype(jnp.int32)
    row0 = (place * blocks).reshape(1)
    group = lax.rem(place, jnp.int32(count)).reshape(1)
    left = jnp.transpose(basis_left, (0, 2, 1))
    right = jnp.transpose(basis_right, (0, 2, 1))

    shared = (blocks + 1) * body
    mine, own = call(
        functools.partial(coeff_kernel, count),
        [sds((SLICES, shared + STATS + rank, LANES), BF16), sds(sources.shape, BF16)],
        [SMEM] + [VMEM] * 3,
        megabytes=60,
    )(far_cols, sources, right, couplings)
    low, high = ring(own)
    held = exchange(mine)
    cols = held[:, shared, :blocks * far].astype(jnp.int32).reshape(-1)

    w = call(
        functools.partial(order_tiles, all_blocks),
        sds((blocks, ops * size, near * size), BF16),
        [SMEM, SMEM, SMEM, VMEM, ANY],
        megabytes=60,
    )(near_cols, near_count, row0, near_tiles, mine)
    image, token = call(
        near_kernel,
        [sds((ops, rows, columns), F32), sds((8, LANES), F32)],
        [VMEM] * 5,
        micros=10.0,
    )(w, low, sources, high, self_terms)
    z1 = across(call(take_kernel, sds((SLICES, rank, LANES), BF16), [VMEM, ANY])(held, token))

    c1 = call(
        functools.partial(first_couple, ops, rank, far),
        sds((SLICES, body, LANES), BF16),
        [SMEM, SMEM, ANY] + [VMEM] * (1 + count),
        [pltpu.VMEM((n * blocks * rank, LANES), BF16)],
    )(cols, group, image, held, *z1)
    c1 = exchange(c1)

    first, second, msg = call(
        image_kernel,
        [
            sds((rows + STATS, columns), BF16),
            sds((rows, columns), BF16),
            sds((SLICES, body + STATS, LANES), BF16),
        ],
        [VMEM] * 5,
        [
            pltpu.VMEM((ops, rows, columns), F32),
            pltpu.VMEM((blocks, body, columns), BF16),
        ],
        micros=2.0,
    )(sources, image, left, right, c1)
    low0, high0 = ring(first)
    low1, high1 = ring(second)
    msgs = across(exchange(msg))

    c2 = call(
        functools.partial(second_couple, all_blocks * size, ops, rank, far),
        sds((SLICES, body + STATS, LANES), BF16),
        [SMEM, SMEM, ANY, ANY] + [VMEM] * (1 + 2 * count),
        [
            pltpu.VMEM((ops, n * blocks * rank, LANES), BF16),
            pltpu.VMEM((n, STATS, LANES), F32),
        ],
        micros=30.0,
    )(cols, group, low0, high0, held, *z1, *msgs)
    c2 = exchange(c2)

    outs = sds((ops, rows, columns), F32)
    scratch = [
        pltpu.VMEM((3, rows, columns), BF16),
        pltpu.VMEM((blocks, body, columns), BF16),
        pltpu.VMEM((rows, columns), F32),
    ]
    images, heights, norms, aux = call(
        final_first,
        [outs, sds((ops, columns), F32), sds((ops, columns), F32), sds((8, columns), F32)],
        [VMEM] * 10,
        scratch + [pltpu.VMEM((STATS, columns), F32), pltpu.SemaphoreType.DMA((blocks,))],
        out_specs=[ANY, VMEM, VMEM, VMEM],
    )(w, low, sources, high, low0, first, high0, self_terms, left, c2)
    images = call(
        final_second,
        outs,
        [ANY] + [VMEM] * 11,
        scratch + [pltpu.SemaphoreType.DMA((blocks,))],
        out_specs=ANY,
        alias={0: 0},
    )(images, w, low, sources, high, low1, second, high1, self_terms, left, c2, aux)
    return images, heights, norms


def solution(mesh):
    placed = (
        P(("groups", "store"), None),
        P(None, "store"),
        P(None, "store", None, None, None),
        P("store", None),
        P("store"),
        P("store", None),
        P("store", None, None),
        P("store", None, None),
        P(None, "store", None, None, None),
    )
    return jax.shard_map(
        shards,
        mesh=mesh,
        in_specs=placed,
        out_specs=(P(None, ("groups", "store"), None), P("groups", None), P("groups", None)),
        check_vma=False,
    )
```

```python
import functools

import jax
import jax.numpy as jnp
from jax import lax
from jax.experimental import pallas as pl
from jax.experimental.pallas import tpu as pltpu
from jax.sharding import PartitionSpec as P

REACH = 2
EPSILON = 1e-06
LANES = 128
HALF = 64
SLICES = 8
STATS = 16
FLOP_RATE = 1150000000
F32 = jnp.float32
BF16 = jnp.bfloat16

VMEM = pl.BlockSpec(memory_space=pltpu.VMEM)
SMEM = pl.BlockSpec(memory_space=pltpu.SMEM)
ANY = pl.BlockSpec(memory_space=pl.ANY)


def call(body, out_shape, in_specs, scratch=(), micros=0.0, megabytes=20, out_specs=None, alias=None):
    many = isinstance(out_shape, (list, tuple))
    if out_specs is None:
        out_specs = [VMEM] * len(out_shape) if many else VMEM
    return pl.pallas_call(
        body,
        out_shape=out_shape,
        in_specs=in_specs,
        out_specs=out_specs,
        input_output_aliases=alias or {},
        scratch_shapes=list(scratch),
        compiler_params=pltpu.CompilerParams(vmem_limit_bytes=megabytes * 1024 * 1024),
        cost_estimate=pl.CostEstimate(
            flops=int(micros * FLOP_RATE), bytes_accessed=0, transcendentals=0
        ),
    )


def dot(a, b, dims=((1,), (0,))):
    return lax.dot_general(a, b, (dims, ((), ())), preferred_element_type=F32)


def split3(row):
    high = row.astype(BF16)
    rest = row - high.astype(F32)
    middle = rest.astype(BF16)
    low = (rest - middle.astype(F32)).astype(BF16)
    return [high, middle, low]


def join3(rows, at):
    return rows[..., 3 * at, :] + rows[..., 3 * at + 1, :] + rows[..., 3 * at + 2, :]


def row3(values, at):
    return values[3 * at:3 * at + 1] + values[3 * at + 1:3 * at + 2] + values[3 * at + 2:3 * at + 3]


def halves(x, y):
    left = lax.broadcasted_iota(jnp.int32, x.shape, x.ndim - 1) < HALF
    first = jnp.where(left, x, pltpu.roll(y, HALF, x.ndim - 1))
    second = jnp.where(left, pltpu.roll(x, HALF, x.ndim - 1), y)
    return first, second


def chunk(x, pair):
    return x[:, pair * LANES:(pair + 1) * LANES]


def order_tiles(all_blocks, cols, count, row0, tiles, after, out):
    ops, blocks, near, size, _ = tiles.shape
    for b in range(blocks):
        for k in range(near):
            rel = lax.rem(cols[b, k] - (row0[0] + b) + REACH + all_blocks, all_blocks)
            rel = lax.rem(rel, all_blocks)
            at = pl.multiple_of(rel * size, size)
            live = k < count[b]
            for o in range(ops):
                tile = tiles[o, b, k]
                out[b, o * size:(o + 1) * size, pl.ds(at, size)] = jnp.where(
                    live, tile, jnp.zeros_like(tile)
                )


def coeff_kernel(count, far_cols, u, right, coup, out, u_out):
    ops, blocks, far, rank, _ = coup.shape
    size = right.shape[2]
    u_out[...] = u[...]
    z = [dot(right[b], u[b * size:(b + 1) * size, :]) for b in range(blocks)]
    at = 3 * ops * rank + STATS
    for pair in range(SLICES // 2):
        first, second = halves(chunk(z[0], pair), chunk(z[1], pair))
        out[2 * pair, at:at + rank, :] = first.astype(BF16)
        out[2 * pair + 1, at:at + rank, :] = second.astype(BF16)
    whole, rest = [], []
    for b in range(blocks):
        tiles = [
            jnp.concatenate([coup[o, b, f] for f in range(far)], axis=1) for o in range(ops)
        ]
        tiles = jnp.concatenate(tiles, axis=0)
        whole.append(tiles[:, :LANES])
        rest.append(tiles[:, LANES:])
    lane = lax.broadcasted_iota(jnp.int32, (STATS, LANES), 1)
    names = jnp.zeros((STATS, LANES), F32)
    for b in range(blocks):
        for f in range(far):
            col = far_cols[b, f]
            device = lax.div(col, blocks)
            slot = lax.rem(device, count) * SLICES + lax.div(device, count)
            name = (slot * blocks + lax.rem(col, blocks)).astype(F32)
            names = jnp.where(lane == b * far + f, name, names)
    whole = jnp.concatenate(
        whole + [jnp.concatenate(rest, axis=1), names.astype(BF16)], axis=0
    )
    for s in range(SLICES):
        out[s, 0:at, :] = whole


def take_kernel(held, after, out):
    out[...] = held[:, held.shape[1] - out.shape[1]:, :]


def coupling_rows(held, s, b, ops, rank):
    body = ops * rank
    first = held[s, b * body:(b + 1) * body, :]
    rest = held[s, 2 * body:3 * body, b * HALF:(b + 1) * HALF]
    return jnp.concatenate([first, rest], axis=1)


def couple(cols, held, s, b, ops, rank, far, z):
    at = (s * 2 + b) * far
    lhs = coupling_rows(held, s, b, ops, rank)
    starts = [pl.multiple_of(cols[at + f] * rank, rank) for f in range(far)]
    picked = [
        jnp.concatenate([x[pl.ds(start, rank), :] for start in starts], axis=0) for x in z
    ]
    if len(z) == 1:
        return dot(lhs, picked[0])
    return jnp.concatenate(
        [dot(lhs[o * rank:(o + 1) * rank], picked[o]) for o in range(ops)], axis=0
    )


def spread_rows(source, rank):
    count = source.shape[0]
    turned = pltpu.roll(source, HALF, 2)
    both = jnp.concatenate([source[:, None], turned[:, None]], axis=1)
    return both.reshape(count * 2 * rank, LANES).astype(BF16)


def group_at(group, m, groups, step):
    return pl.multiple_of(lax.rem(group[0] + (groups - m), groups) * step, step)


def first_couple(ops, rank, far, cols, group, held, *refs):
    parts, (out, zs) = refs[:-2], refs[-2:]
    step = SLICES * 2 * rank
    for m, part in enumerate(parts):
        at = group_at(group, m, len(parts), step)
        zs[pl.ds(at, step), :] = spread_rows(part[...].astype(F32), rank)
    for s in range(SLICES):
        c = [couple(cols, held, s, b, ops, rank, far, [zs]) for b in range(2)]
        out[s] = halves(c[0], c[1])[0].astype(BF16)


def take_coefs(cmsg, coef, rows):
    for pair in range(SLICES // 2):
        parts = halves(
            cmsg[2 * pair, 0:rows, :].astype(F32), cmsg[2 * pair + 1, 0:rows, :].astype(F32)
        )
        for b in range(2):
            coef[b, :, pair * LANES:(pair + 1) * LANES] = parts[b].astype(BF16)


def near_product(tiles, parts, b, blocks, size):
    total = None
    first = b - REACH
    at = 0
    for d, part in enumerate(parts):
        start = max((d - 1) * blocks, first)
        stop = min(d * blocks, first + 2 * REACH + 1)
        if stop <= start:
            continue
        begin = (start - (d - 1) * blocks) * size
        width = (stop - start) * size
        value = dot(tiles[:, at:at + width], part[begin:begin + width, :])
        total = value if total is None else total + value
        at += width
    return total


def diagonal_of(diag, o, b, size, columns):
    row = diag[o:o + 1, b * size:(b + 1) * size]
    column = jnp.transpose(jnp.broadcast_to(row, (LANES, size)))
    return jnp.concatenate([column] * (columns // LANES), axis=1)


def ratio(inner, squares):
    good = squares > 0
    return jnp.where(good, inner / jnp.where(good, squares, 1.0), 0.0)


def near_kernel(w, low, own, high, diag, image, token, early):
    token[...] = jnp.zeros_like(token)
    ops, rows, columns = image.shape
    size = w.shape[1] // ops
    blocks = rows // size
    squares, inner = 0.0, 0.0
    for b in range(blocks):
        product = near_product(w.at[b], (low, own, high), b, blocks, size)
        here = slice(b * size, (b + 1) * size)
        ub = own[here, :].astype(F32)
        squares = squares + jnp.sum(ub * ub, axis=0, keepdims=True)
        for o in range(ops):
            value = product[o * size:(o + 1) * size] + diagonal_of(diag, o, b, size, columns) * ub
            image[o, here, :] = value
            if o == 0:
                inner = inner + jnp.sum(ub * value, axis=0, keepdims=True)
    pieces = split3(ratio(inner, squares))
    shift = sum(x.astype(F32) for x in pieces)
    early[0:rows, :] = (image[0] - shift * own[...].astype(F32)).astype(BF16)
    zero = jnp.zeros_like(pieces[0])
    early[rows:, :] = jnp.concatenate(pieces + [zero] * (STATS - len(pieces)), axis=0)


def image_kernel(
    own, near, left, right, cmsg, after_low, after_high, out0, half0, half1, mout, image, coef
):
    ops = image.shape[0]
    blocks, rank, size = right.shape
    rows, columns = own.shape
    take_coefs(cmsg, coef, ops * rank)
    inner = [None] * ops
    squares = None
    for b in range(blocks):
        here = slice(b * size, (b + 1) * size)
        ub = own[here, :].astype(F32)
        part = jnp.sum(ub * ub, axis=0, keepdims=True)
        squares = part if squares is None else squares + part
        for o in range(ops):
            far = dot(left[b], coef[b, o * rank:(o + 1) * rank, :], ((0,), (0,)))
            value = near[o, here, :] + far.astype(BF16).astype(F32)
            image[o, here, :] = value
            part = jnp.sum(ub * value, axis=0, keepdims=True)
            inner[o] = part if inner[o] is None else inner[o] + part
    stats = []
    spreads = []
    good = squares > 0
    for o in range(ops):
        shift = jnp.where(good, inner[o] / jnp.where(good, squares, 1.0), 0.0)
        pieces = split3(shift)
        stats += pieces
        shift = pieces[0].astype(F32) + pieces[1].astype(F32) + pieces[2].astype(F32)
        spread = None
        z = []
        for b in range(blocks):
            ub = own[b * size:(b + 1) * size, :].astype(F32)
            v = image[o, b * size:(b + 1) * size, :] - shift * ub
            part = jnp.sum(v * v, axis=0, keepdims=True)
            spread = part if spread is None else spread + part
            v = v.astype(BF16)
            if o == 0:
                out0[b * size:(b + 1) * size, :] = v
            else:
                (half0, half1)[b][0:size, :] = v
            z.append(dot(right[b], v))
        for pair in range(SLICES // 2):
            first, second = halves(chunk(z[0], pair), chunk(z[1], pair))
            mout[2 * pair, o * rank:(o + 1) * rank, :] = first.astype(BF16)
            mout[2 * pair + 1, o * rank:(o + 1) * rank, :] = second.astype(BF16)
        spreads.append(spread)
    zero = jnp.zeros((1, columns), BF16)
    edge = jnp.concatenate(stats + [zero] * (STATS - len(stats)), axis=0)
    out0[rows:, :] = edge
    half1[size:, :] = edge
    at = size + blocks * rank
    for b in range(blocks):
        half0[size + b * rank:size + (b + 1) * rank, :] = coef[b, 0:rank, :]
        half0[at:at + rank, b * size:(b + 1) * size] = left[b]
    stats += split3(squares)
    for spread in spreads:
        stats += split3(spread)
    stats = jnp.concatenate(stats + [zero] * (STATS - len(stats)), axis=0).astype(F32)
    for pair in range(SLICES // 2):
        part = chunk(stats, pair)
        first, second = halves(part, part)
        mout[2 * pair, ops * rank:ops * rank + STATS, :] = first.astype(BF16)
        mout[2 * pair + 1, ops * rank:ops * rank + STATS, :] = second.astype(BF16)


def second_couple(panels, ops, rank, far, cols, group, after_low, after_high, held, *refs):
    out, zs, st = refs[-3:]
    count = (len(refs) - 3) // 2
    z1, msgs = refs[:count], refs[count:2 * count]
    body = ops * rank
    step = SLICES * 2 * rank
    for m, msg in enumerate(msgs):
        at = group_at(group, m, count, SLICES)
        st[pl.ds(at, SLICES)] = msg[:, body:body + STATS, :].astype(F32)
    every = st[...]
    squares = join3(every, ops)
    scale_sq = jnp.sum(squares, axis=0, keepdims=True) / panels + EPSILON
    reverse = 1.0 / jnp.sqrt(scale_sq)
    heights, norms = [], []
    for o in range(ops):
        shift = join3(every, o)
        height = jnp.sum(shift * squares, axis=0, keepdims=True) / panels / scale_sq
        delta = shift - height
        spread = join3(every, ops + 1 + o) + delta * delta * squares
        norm = jnp.sqrt(jnp.sum(spread, axis=0, keepdims=True) / panels / scale_sq + EPSILON)
        heights.append(height)
        norms.append(norm)
    for m, msg in enumerate(msgs):
        at = group_at(group, m, count, step)
        mine = msg[:, body:body + STATS, :].astype(F32)
        base = z1[m][...].astype(F32)
        for o in range(ops):
            delta = join3(mine, o) - heights[o]
            z = msg[:, o * rank:(o + 1) * rank, :].astype(F32) + delta[:, None, :] * base
            z = z * (reverse / norms[o])[None]
            zs[o, pl.ds(at, step), :] = spread_rows(z, rank)
    rows = []
    for row in heights + norms + [reverse]:
        rows += split3(row)
    rows += [jnp.zeros_like(rows[0])] * (STATS - len(rows))
    rows = jnp.concatenate(rows, axis=0)
    for s in range(SLICES):
        c = [couple(cols, held, s, b, ops, rank, far, [zs.at[o] for o in range(ops)]) for b in range(2)]
        out[s, 0:body, :] = halves(c[0], c[1])[0].astype(BF16)
        out[s, body:body + STATS, :] = rows


def apply_second(o, factor, changes, u3, value_of, w, diag, left, cmsg, images, ext, coef, out, sems):
    blocks, rank, size = left.shape
    ops = w.shape[1] // size
    columns = u3[1].shape[1]
    take_coefs(cmsg, coef, ops * rank)
    for at, u in enumerate(u3):
        for b in range(blocks):
            here = slice(b * size, (b + 1) * size)
            value = value_of(at, b) * factor + u[here, :].astype(F32) * changes[at]
            ext[at, here, :] = value.astype(BF16)
    copies = []
    for b in range(blocks):
        parts = [ext.at[at] for at in range(3)]
        product = near_product(w.at[b, o * size:(o + 1) * size], parts, b, blocks, size)
        far = dot(left[b], coef[b, o * rank:(o + 1) * rank, :], ((0,), (0,)))
        here = slice(b * size, (b + 1) * size)
        out[here, :] = (
            product
            + diagonal_of(diag, o, b, size, columns) * ext[1, here, :].astype(F32)
            + far.astype(BF16).astype(F32)
        )
        copies.append(pltpu.make_async_copy(out.at[here], images.at[o, here], sems.at[b]))
        copies[-1].start()
    for copy in copies:
        copy.wait()


def final_first(
    w,
    ulow,
    uown,
    uhigh,
    elow,
    own0,
    ehigh,
    halflow,
    halfhigh,
    diag,
    left,
    cmsg,
    images,
    heights,
    norms,
    aux,
    ext,
    coef,
    out,
    stat,
    sems,
):
    blocks, rank, size = left.shape
    rows, columns = uown.shape
    ops = w.shape[1] // size
    body = ops * rank
    for pair in range(SLICES // 2):
        stat[:, pair * LANES:(pair + 1) * LANES] = halves(
            cmsg[2 * pair, body:body + STATS, :].astype(F32),
            cmsg[2 * pair + 1, body:body + STATS, :].astype(F32),
        )[0]
    st = stat[...]
    reverse = row3(st, 2 * ops)
    own_edge = own0[rows:, :].astype(F32)
    for o in range(ops):
        height = row3(st, o)
        norm = row3(st, ops + o)
        heights[o:o + 1, :] = height
        norms[o:o + 1, :] = norm
        if o == 1:
            aux[0:1, :] = reverse / norm
            aux[1:2, :] = height
            aux[2:3, :] = row3(own_edge, 1)
    height = row3(st, 0)
    factor = reverse / row3(st, ops)
    changes = [
        (row3(edge, 0) - height) * factor
        for edge in (elow[rows:, :].astype(F32), own_edge, ehigh[rows:, :].astype(F32))
    ]

    def value_of(at, b):
        here = slice(b * size, (b + 1) * size)
        if at == 1:
            return own0[here, :].astype(F32)
        v, half = (elow, halflow) if at == 0 else (ehigh, halfhigh)
        start = size + blocks * rank
        far = dot(
            half[start:start + rank, here],
            half[size + b * rank:size + (b + 1) * rank, :],
            ((0,), (0,)),
        )
        return v[here, :].astype(F32) + far.astype(BF16).astype(F32)

    u3 = (ulow, uown, uhigh)
    apply_second(
        0, factor, changes, u3, value_of, w, diag, left, cmsg, images, ext, coef, out, sems
    )


def final_second(
    begun,
    w,
    ulow,
    uown,
    uhigh,
    low0,
    own0,
    high0,
    low1,
    own1,
    high1,
    diag,
    left,
    cmsg,
    aux,
    images,
    ext,
    coef,
    out,
    sems,
):
    size = left.shape[2]
    factor, height = aux[0:1, :], aux[1:2, :]
    changes = [
        (edge - height) * factor
        for edge in (
            row3(low1[size:, :].astype(F32), 1),
            aux[2:3, :],
            row3(high1[size:, :].astype(F32), 1),
        )
    ]
    pieces = ((low0, low1), (own0, own1), (high0, high1))

    def value_of(at, b):
        return pieces[at][b][0:size, :].astype(F32)

    u3 = (ulow, uown, uhigh)
    apply_second(
        1, factor, changes, u3, value_of, w, diag, left, cmsg, images, ext, coef, out, sems
    )


def ring(block):
    count = lax.axis_size("store")
    forward = [(i, (i + 1) % count) for i in range(count)]
    backward = [(target, source) for source, target in forward]
    return lax.ppermute(block, "store", forward), lax.ppermute(block, "store", backward)


def shards(
    sources,
    self_terms,
    near_tiles,
    near_cols,
    near_count,
    far_cols,
    basis_left,
    basis_right,
    couplings,
):
    n = lax.axis_size("store")
    ops, blocks, near, size, _ = near_tiles.shape
    rank = basis_left.shape[2]
    far = far_cols.shape[1]
    rows, columns = sources.shape
    all_blocks = blocks * n
    count = n // SLICES
    groups = [[s * count + g for s in range(SLICES)] for g in range(count)]
    sds = jax.ShapeDtypeStruct
    body = ops * rank

    def exchange(x):
        return lax.all_to_all(x, "store", 0, 0, axis_index_groups=groups, tiled=True)

    def across(x):
        parts = [x]
        for m in range(1, count):
            pairs = [(i, i - i % count + (i + m) % count) for i in range(n)]
            parts.append(lax.ppermute(x, "store", pairs))
        return parts

    place = lax.axis_index("store").astype(jnp.int32)
    row0 = (place * blocks).reshape(1)
    group = lax.rem(place, jnp.int32(count)).reshape(1)
    left = jnp.transpose(basis_left, (0, 2, 1))
    right = jnp.transpose(basis_right, (0, 2, 1))

    shared = (blocks + 1) * body
    mine, own = call(
        functools.partial(coeff_kernel, count),
        [sds((SLICES, shared + STATS + rank, LANES), BF16), sds(sources.shape, BF16)],
        [SMEM] + [VMEM] * 3,
        megabytes=60,
    )(far_cols, sources, right, couplings)
    low, high = ring(own)
    held = exchange(mine)
    cols = held[:, shared, :blocks * far].astype(jnp.int32).reshape(-1)

    w = call(
        functools.partial(order_tiles, all_blocks),
        sds((blocks, ops * size, near * size), BF16),
        [SMEM, SMEM, SMEM, VMEM, ANY],
        megabytes=60,
    )(near_cols, near_count, row0, near_tiles, mine)
    image, token, early = call(
        near_kernel,
        [
            sds((ops, rows, columns), F32),
            sds((8, LANES), F32),
            sds((rows + STATS, columns), BF16),
        ],
        [VMEM] * 5,
        micros=10.0,
    )(w, low, sources, high, self_terms)
    elow, ehigh = ring(early)
    z1 = across(call(take_kernel, sds((SLICES, rank, LANES), BF16), [VMEM, ANY])(held, token))

    c1 = call(
        functools.partial(first_couple, ops, rank, far),
        sds((SLICES, body, LANES), BF16),
        [SMEM, SMEM] + [VMEM] * (1 + count),
        [pltpu.VMEM((n * blocks * rank, LANES), BF16)],
        micros=30.0,
    )(cols, group, held, *z1)
    c1 = exchange(c1)

    own0, half0, half1, msg = call(
        image_kernel,
        [
            sds((rows + STATS, columns), BF16),
            sds((size + (blocks + 1) * rank, columns), BF16),
            sds((size + STATS, columns), BF16),
            sds((SLICES, body + STATS, LANES), BF16),
        ],
        [VMEM] * 5 + [ANY] * 2,
        [
            pltpu.VMEM((ops, rows, columns), F32),
            pltpu.VMEM((blocks, body, columns), BF16),
        ],
        micros=2.0,
    )(sources, image, left, right, c1, elow, ehigh)
    low0, high0 = ring(half0)
    low1, high1 = ring(half1)
    msgs = across(exchange(msg))

    c2 = call(
        functools.partial(second_couple, all_blocks * size, ops, rank, far),
        sds((SLICES, body + STATS, LANES), BF16),
        [SMEM, SMEM, ANY, ANY] + [VMEM] * (1 + 2 * count),
        [
            pltpu.VMEM((ops, n * blocks * rank, LANES), BF16),
            pltpu.VMEM((n, STATS, LANES), F32),
        ],
        micros=30.0,
    )(cols, group, low0, high0, held, *z1, *msgs)
    c2 = exchange(c2)

    outs = sds((ops, rows, columns), F32)
    scratch = [
        pltpu.VMEM((3, rows, columns), BF16),
        pltpu.VMEM((blocks, body, columns), BF16),
        pltpu.VMEM((rows, columns), F32),
    ]
    images, heights, norms, aux = call(
        final_first,
        [outs, sds((ops, columns), F32), sds((ops, columns), F32), sds((8, columns), F32)],
        [VMEM] * 12,
        scratch + [pltpu.VMEM((STATS, columns), F32), pltpu.SemaphoreType.DMA((blocks,))],
        out_specs=[ANY, VMEM, VMEM, VMEM],
    )(w, low, sources, high, elow, own0, ehigh, low0, high0, self_terms, left, c2)
    images = call(
        final_second,
        outs,
        [ANY] + [VMEM] * 14,
        scratch + [pltpu.SemaphoreType.DMA((blocks,))],
        out_specs=ANY,
        alias={0: 0},
    )(
        images,
        w,
        low,
        sources,
        high,
        low0,
        half0,
        high0,
        low1,
        half1,
        high1,
        self_terms,
        left,
        c2,
        aux,
    )
    return images, heights, norms


def solution(mesh):
    placed = (
        P(("groups", "store"), None),
        P(None, "store"),
        P(None, "store", None, None, None),
        P("store", None),
        P("store"),
        P("store", None),
        P("store", None, None),
        P("store", None, None),
        P(None, "store", None, None, None),
    )
    return jax.shard_map(
        shards,
        mesh=mesh,
        in_specs=placed,
        out_specs=(P(None, ("groups", "store"), None), P("groups", None), P("groups", None)),
        check_vma=False,
    )
```

```python
import functools

import jax
import jax.numpy as jnp
from jax import lax
from jax.experimental import pallas as pl
from jax.experimental.pallas import tpu as pltpu
from jax.sharding import PartitionSpec as P

REACH = 2
EPSILON = 1e-06
LANES = 128
HALF = 64
SLICES = 8
STATS = 16
FLOP_RATE = 1150000000
F32 = jnp.float32
BF16 = jnp.bfloat16

VMEM = pl.BlockSpec(memory_space=pltpu.VMEM)
SMEM = pl.BlockSpec(memory_space=pltpu.SMEM)
ANY = pl.BlockSpec(memory_space=pl.ANY)


def call(body, out_shape, in_specs, scratch=(), micros=0.0, megabytes=20, out_specs=None, alias=None):
    many = isinstance(out_shape, (list, tuple))
    if out_specs is None:
        out_specs = [VMEM] * len(out_shape) if many else VMEM
    return pl.pallas_call(
        body,
        out_shape=out_shape,
        in_specs=in_specs,
        out_specs=out_specs,
        input_output_aliases=alias or {},
        scratch_shapes=list(scratch),
        compiler_params=pltpu.CompilerParams(vmem_limit_bytes=megabytes * 1024 * 1024),
        cost_estimate=pl.CostEstimate(
            flops=int(micros * FLOP_RATE), bytes_accessed=0, transcendentals=0
        ),
    )


def dot(a, b, dims=((1,), (0,))):
    return lax.dot_general(a, b, (dims, ((), ())), preferred_element_type=F32)


def split3(row):
    high = row.astype(BF16)
    rest = row - high.astype(F32)
    middle = rest.astype(BF16)
    low = (rest - middle.astype(F32)).astype(BF16)
    return [high, middle, low]


def join3(rows, at):
    return rows[..., 3 * at, :] + rows[..., 3 * at + 1, :] + rows[..., 3 * at + 2, :]


def row3(values, at):
    return values[3 * at:3 * at + 1] + values[3 * at + 1:3 * at + 2] + values[3 * at + 2:3 * at + 3]


def halves(x, y):
    left = lax.broadcasted_iota(jnp.int32, x.shape, x.ndim - 1) < HALF
    first = jnp.where(left, x, pltpu.roll(y, HALF, x.ndim - 1))
    second = jnp.where(left, pltpu.roll(x, HALF, x.ndim - 1), y)
    return first, second


def chunk(x, pair):
    return x[:, pair * LANES:(pair + 1) * LANES]


def order_tiles(all_blocks, cols, count, row0, tiles, after, out):
    ops, blocks, near, size, _ = tiles.shape
    for b in range(blocks):
        for k in range(near):
            rel = lax.rem(cols[b, k] - (row0[0] + b) + REACH + all_blocks, all_blocks)
            rel = lax.rem(rel, all_blocks)
            at = pl.multiple_of(rel * size, size)
            live = k < count[b]
            for o in range(ops):
                tile = tiles[o, b, k]
                out[b, o * size:(o + 1) * size, pl.ds(at, size)] = jnp.where(
                    live, tile, jnp.zeros_like(tile)
                )


def coeff_kernel(count, far_cols, u, right, coup, out):
    ops, blocks, far, rank, _ = coup.shape
    size = right.shape[2]
    z = [dot(right[b], u[b * size:(b + 1) * size, :]) for b in range(blocks)]
    at = 3 * ops * rank + STATS
    for pair in range(SLICES // 2):
        first, second = halves(chunk(z[0], pair), chunk(z[1], pair))
        out[2 * pair, at:at + rank, :] = first.astype(BF16)
        out[2 * pair + 1, at:at + rank, :] = second.astype(BF16)
    whole, rest = [], []
    for b in range(blocks):
        tiles = [
            jnp.concatenate([coup[o, b, f] for f in range(far)], axis=1) for o in range(ops)
        ]
        tiles = jnp.concatenate(tiles, axis=0)
        whole.append(tiles[:, :LANES])
        rest.append(tiles[:, LANES:])
    lane = lax.broadcasted_iota(jnp.int32, (STATS, LANES), 1)
    names = jnp.zeros((STATS, LANES), F32)
    for b in range(blocks):
        for f in range(far):
            col = far_cols[b, f]
            device = lax.div(col, blocks)
            slot = lax.rem(device, count) * SLICES + lax.div(device, count)
            name = (slot * blocks + lax.rem(col, blocks)).astype(F32)
            names = jnp.where(lane == b * far + f, name, names)
    whole = jnp.concatenate(
        whole + [jnp.concatenate(rest, axis=1), names.astype(BF16)], axis=0
    )
    for s in range(SLICES):
        out[s, 0:at, :] = whole


def take_kernel(held, after, out):
    out[...] = held[:, held.shape[1] - out.shape[1]:, :]


def coupling_rows(held, s, b, ops, rank):
    body = ops * rank
    first = held[s, b * body:(b + 1) * body, :]
    rest = held[s, 2 * body:3 * body, b * HALF:(b + 1) * HALF]
    return jnp.concatenate([first, rest], axis=1)


def couple(cols, held, s, b, ops, rank, far, z):
    at = (s * 2 + b) * far
    lhs = coupling_rows(held, s, b, ops, rank)
    starts = [pl.multiple_of(cols[at + f] * rank, rank) for f in range(far)]
    picked = [
        jnp.concatenate([x[pl.ds(start, rank), :] for start in starts], axis=0) for x in z
    ]
    if len(z) == 1:
        return dot(lhs, picked[0])
    return jnp.concatenate(
        [dot(lhs[o * rank:(o + 1) * rank], picked[o]) for o in range(ops)], axis=0
    )


def spread_rows(source, rank):
    count = source.shape[0]
    turned = pltpu.roll(source, HALF, 2)
    both = jnp.concatenate([source[:, None], turned[:, None]], axis=1)
    return both.reshape(count * 2 * rank, LANES).astype(BF16)


def group_at(group, m, groups, step):
    return pl.multiple_of(lax.rem(group[0] + (groups - m), groups) * step, step)


def first_couple(ops, rank, far, cols, group, held, *refs):
    parts, (out, zs) = refs[:-2], refs[-2:]
    step = SLICES * 2 * rank
    for m, part in enumerate(parts):
        at = group_at(group, m, len(parts), step)
        zs[pl.ds(at, step), :] = spread_rows(part[...].astype(F32), rank)
    for s in range(SLICES):
        c = [couple(cols, held, s, b, ops, rank, far, [zs]) for b in range(2)]
        out[s] = halves(c[0], c[1])[0].astype(BF16)


def take_coefs(cmsg, coef, rows):
    for pair in range(SLICES // 2):
        parts = halves(
            cmsg[2 * pair, 0:rows, :].astype(F32), cmsg[2 * pair + 1, 0:rows, :].astype(F32)
        )
        for b in range(2):
            coef[b, :, pair * LANES:(pair + 1) * LANES] = parts[b].astype(BF16)


def near_product(tiles, parts, b, blocks, size):
    total = None
    first = b - REACH
    at = 0
    for d, part in enumerate(parts):
        start = max((d - 1) * blocks, first)
        stop = min(d * blocks, first + 2 * REACH + 1)
        if stop <= start:
            continue
        begin = (start - (d - 1) * blocks) * size
        width = (stop - start) * size
        value = dot(tiles[:, at:at + width], part[begin:begin + width, :])
        total = value if total is None else total + value
        at += width
    return total


def diagonal_of(diag, o, b, size, columns):
    row = diag[o:o + 1, b * size:(b + 1) * size]
    column = jnp.transpose(jnp.broadcast_to(row, (LANES, size)))
    return jnp.concatenate([column] * (columns // LANES), axis=1)


def near_kernel(w, low, own, high, diag, image, token):
    token[...] = jnp.zeros_like(token)
    ops, rows, columns = image.shape
    size = w.shape[1] // ops
    blocks = rows // size
    for b in range(blocks):
        product = near_product(w.at[b], (low, own, high), b, blocks, size)
        here = slice(b * size, (b + 1) * size)
        ub = own[here, :].astype(F32)
        for o in range(ops):
            image[o, here, :] = (
                product[o * size:(o + 1) * size] + diagonal_of(diag, o, b, size, columns) * ub
            )


def image_kernel(own, near, left, right, cmsg, out0, out1, mout, image, coef):
    ops = image.shape[0]
    blocks, rank, size = right.shape
    rows, columns = own.shape
    take_coefs(cmsg, coef, ops * rank)
    inner = [None] * ops
    squares = None
    for b in range(blocks):
        here = slice(b * size, (b + 1) * size)
        ub = own[here, :].astype(F32)
        part = jnp.sum(ub * ub, axis=0, keepdims=True)
        squares = part if squares is None else squares + part
        for o in range(ops):
            far = dot(left[b], coef[b, o * rank:(o + 1) * rank, :], ((0,), (0,)))
            value = near[o, here, :] + far.astype(BF16).astype(F32)
            image[o, here, :] = value
            part = jnp.sum(ub * value, axis=0, keepdims=True)
            inner[o] = part if inner[o] is None else inner[o] + part
    stats = []
    spreads = []
    good = squares > 0
    for o in range(ops):
        shift = jnp.where(good, inner[o] / jnp.where(good, squares, 1.0), 0.0)
        pieces = split3(shift)
        stats += pieces
        shift = pieces[0].astype(F32) + pieces[1].astype(F32) + pieces[2].astype(F32)
        spread = None
        z = []
        for b in range(blocks):
            ub = own[b * size:(b + 1) * size, :].astype(F32)
            v = image[o, b * size:(b + 1) * size, :] - shift * ub
            part = jnp.sum(v * v, axis=0, keepdims=True)
            spread = part if spread is None else spread + part
            v = v.astype(BF16)
            (out0, out1)[o][b * size:(b + 1) * size, :] = v
            z.append(dot(right[b], v))
        for pair in range(SLICES // 2):
            first, second = halves(chunk(z[0], pair), chunk(z[1], pair))
            mout[2 * pair, o * rank:(o + 1) * rank, :] = first.astype(BF16)
            mout[2 * pair + 1, o * rank:(o + 1) * rank, :] = second.astype(BF16)
        spreads.append(spread)
    zero = jnp.zeros((1, columns), BF16)
    out0[rows:, :] = jnp.concatenate(stats + [zero] * (STATS - len(stats)), axis=0)
    stats += split3(squares)
    for spread in spreads:
        stats += split3(spread)
    stats = jnp.concatenate(stats + [zero] * (STATS - len(stats)), axis=0).astype(F32)
    for pair in range(SLICES // 2):
        part = chunk(stats, pair)
        first, second = halves(part, part)
        mout[2 * pair, ops * rank:ops * rank + STATS, :] = first.astype(BF16)
        mout[2 * pair + 1, ops * rank:ops * rank + STATS, :] = second.astype(BF16)


def second_couple(panels, ops, rank, far, cols, group, after_low, after_high, held, *refs):
    out, zs, st = refs[-3:]
    count = (len(refs) - 3) // 2
    z1, msgs = refs[:count], refs[count:2 * count]
    body = ops * rank
    step = SLICES * 2 * rank
    for m, msg in enumerate(msgs):
        at = group_at(group, m, count, SLICES)
        st[pl.ds(at, SLICES)] = msg[:, body:body + STATS, :].astype(F32)
    every = st[...]
    squares = join3(every, ops)
    scale_sq = jnp.sum(squares, axis=0, keepdims=True) / panels + EPSILON
    reverse = 1.0 / jnp.sqrt(scale_sq)
    heights, norms = [], []
    for o in range(ops):
        shift = join3(every, o)
        height = jnp.sum(shift * squares, axis=0, keepdims=True) / panels / scale_sq
        delta = shift - height
        spread = join3(every, ops + 1 + o) + delta * delta * squares
        norm = jnp.sqrt(jnp.sum(spread, axis=0, keepdims=True) / panels / scale_sq + EPSILON)
        heights.append(height)
        norms.append(norm)
    for m, msg in enumerate(msgs):
        at = group_at(group, m, count, step)
        mine = msg[:, body:body + STATS, :].astype(F32)
        base = z1[m][...].astype(F32)
        for o in range(ops):
            delta = join3(mine, o) - heights[o]
            z = msg[:, o * rank:(o + 1) * rank, :].astype(F32) + delta[:, None, :] * base
            z = z * (reverse / norms[o])[None]
            zs[o, pl.ds(at, step), :] = spread_rows(z, rank)
    rows = []
    for row in heights + norms + [reverse]:
        rows += split3(row)
    rows += [jnp.zeros_like(rows[0])] * (STATS - len(rows))
    rows = jnp.concatenate(rows, axis=0)
    for s in range(SLICES):
        c = [couple(cols, held, s, b, ops, rank, far, [zs.at[o] for o in range(ops)]) for b in range(2)]
        out[s, 0:body, :] = halves(c[0], c[1])[0].astype(BF16)
        out[s, body:body + STATS, :] = rows


def apply_second(o, factor, changes, u3, v3, w, diag, left, cmsg, images, ext, coef, out, sems):
    blocks, rank, size = left.shape
    rows, columns = u3[1].shape
    ops = w.shape[1] // size
    take_coefs(cmsg, coef, ops * rank)
    for at, (u, v) in enumerate(zip(u3, v3)):
        value = v[0:rows, :].astype(F32) * factor + u[...].astype(F32) * changes[at]
        ext[at] = value.astype(BF16)
    copies = []
    for b in range(blocks):
        parts = [ext.at[at] for at in range(3)]
        product = near_product(w.at[b, o * size:(o + 1) * size], parts, b, blocks, size)
        far = dot(left[b], coef[b, o * rank:(o + 1) * rank, :], ((0,), (0,)))
        here = slice(b * size, (b + 1) * size)
        out[here, :] = (
            product
            + diagonal_of(diag, o, b, size, columns) * ext[1, here, :].astype(F32)
            + far.astype(BF16).astype(F32)
        )
        copies.append(pltpu.make_async_copy(out.at[here], images.at[o, here], sems.at[b]))
        copies[-1].start()
    for copy in copies:
        copy.wait()


def final_first(
    w,
    ulow,
    uown,
    uhigh,
    vlow,
    vown,
    vhigh,
    diag,
    left,
    cmsg,
    images,
    heights,
    norms,
    aux,
    ext,
    coef,
    out,
    stat,
    sems,
):
    blocks, rank, size = left.shape
    rows, columns = uown.shape
    ops = w.shape[1] // size
    body = ops * rank
    for pair in range(SLICES // 2):
        stat[:, pair * LANES:(pair + 1) * LANES] = halves(
            cmsg[2 * pair, body:body + STATS, :].astype(F32),
            cmsg[2 * pair + 1, body:body + STATS, :].astype(F32),
        )[0]
    st = stat[...]
    reverse = row3(st, 2 * ops)
    scales = []
    for o in range(ops):
        height = row3(st, o)
        norm = row3(st, ops + o)
        heights[o:o + 1, :] = height
        norms[o:o + 1, :] = norm
        factor = reverse / norm
        changes = [
            (row3(v[rows:, :].astype(F32), o) - height) * factor for v in (vlow, vown, vhigh)
        ]
        scales.append((factor, changes))
    factor, changes = scales[1]
    aux[0:1, :] = factor
    for at in range(3):
        aux[1 + at:2 + at, :] = changes[at]
    factor, changes = scales[0]
    u3, v3 = (ulow, uown, uhigh), (vlow, vown, vhigh)
    apply_second(0, factor, changes, u3, v3, w, diag, left, cmsg, images, ext, coef, out, sems)


def final_second(
    begun,
    w,
    ulow,
    uown,
    uhigh,
    vlow,
    vown,
    vhigh,
    diag,
    left,
    cmsg,
    aux,
    images,
    ext,
    coef,
    out,
    sems,
):
    factor, changes = aux[0:1, :], [aux[1 + at:2 + at, :] for at in range(3)]
    u3, v3 = (ulow, uown, uhigh), (vlow, vown, vhigh)
    apply_second(1, factor, changes, u3, v3, w, diag, left, cmsg, images, ext, coef, out, sems)


def ring(block):
    count = lax.axis_size("store")
    forward = [(i, (i + 1) % count) for i in range(count)]
    backward = [(target, source) for source, target in forward]
    return lax.ppermute(block, "store", forward), lax.ppermute(block, "store", backward)


def shards(
    sources,
    self_terms,
    near_tiles,
    near_cols,
    near_count,
    far_cols,
    basis_left,
    basis_right,
    couplings,
):
    n = lax.axis_size("store")
    ops, blocks, near, size, _ = near_tiles.shape
    rank = basis_left.shape[2]
    far = far_cols.shape[1]
    rows, columns = sources.shape
    all_blocks = blocks * n
    count = n // SLICES
    groups = [[s * count + g for s in range(SLICES)] for g in range(count)]
    sds = jax.ShapeDtypeStruct
    body = ops * rank

    def exchange(x):
        return lax.all_to_all(x, "store", 0, 0, axis_index_groups=groups, tiled=True)

    def across(x):
        parts = [x]
        for m in range(1, count):
            pairs = [(i, i - i % count + (i + m) % count) for i in range(n)]
            parts.append(lax.ppermute(x, "store", pairs))
        return parts

    place = lax.axis_index("store").astype(jnp.int32)
    row0 = (place * blocks).reshape(1)
    group = lax.rem(place, jnp.int32(count)).reshape(1)
    left = jnp.transpose(basis_left, (0, 2, 1))
    right = jnp.transpose(basis_right, (0, 2, 1))

    shared = (blocks + 1) * body
    low, high = ring(sources)
    mine = call(
        functools.partial(coeff_kernel, count),
        sds((SLICES, shared + STATS + rank, LANES), BF16),
        [SMEM] + [VMEM] * 3,
        megabytes=60,
    )(far_cols, sources, right, couplings)
    held = exchange(mine)
    cols = held[:, shared, :blocks * far].astype(jnp.int32).reshape(-1)

    w = call(
        functools.partial(order_tiles, all_blocks),
        sds((blocks, ops * size, near * size), BF16),
        [SMEM, SMEM, SMEM, VMEM, ANY],
        megabytes=60,
    )(near_cols, near_count, row0, near_tiles, mine)
    image, token = call(
        near_kernel,
        [sds((ops, rows, columns), F32), sds((8, LANES), F32)],
        [VMEM] * 5,
        micros=10.0,
    )(w, low, sources, high, self_terms)
    z1 = across(call(take_kernel, sds((SLICES, rank, LANES), BF16), [VMEM, ANY])(held, token))

    c1 = call(
        functools.partial(first_couple, ops, rank, far),
        sds((SLICES, body, LANES), BF16),
        [SMEM, SMEM] + [VMEM] * (1 + count),
        [pltpu.VMEM((n * blocks * rank, LANES), BF16)],
    )(cols, group, held, *z1)
    c1 = exchange(c1)

    first, second, msg = call(
        image_kernel,
        [
            sds((rows + STATS, columns), BF16),
            sds((rows, columns), BF16),
            sds((SLICES, body + STATS, LANES), BF16),
        ],
        [VMEM] * 5,
        [
            pltpu.VMEM((ops, rows, columns), F32),
            pltpu.VMEM((blocks, body, columns), BF16),
        ],
        micros=2.0,
    )(sources, image, left, right, c1)
    low0, high0 = ring(first)
    low1, high1 = ring(second)
    msgs = across(exchange(msg))

    c2 = call(
        functools.partial(second_couple, all_blocks * size, ops, rank, far),
        sds((SLICES, body + STATS, LANES), BF16),
        [SMEM, SMEM, ANY, ANY] + [VMEM] * (1 + 2 * count),
        [
            pltpu.VMEM((ops, n * blocks * rank, LANES), BF16),
            pltpu.VMEM((n, STATS, LANES), F32),
        ],
        micros=30.0,
    )(cols, group, low0, high0, held, *z1, *msgs)
    c2 = exchange(c2)

    outs = sds((ops, rows, columns), F32)
    scratch = [
        pltpu.VMEM((3, rows, columns), BF16),
        pltpu.VMEM((blocks, body, columns), BF16),
        pltpu.VMEM((rows, columns), F32),
    ]
    images, heights, norms, aux = call(
        final_first,
        [outs, sds((ops, columns), F32), sds((ops, columns), F32), sds((8, columns), F32)],
        [VMEM] * 10,
        scratch + [pltpu.VMEM((STATS, columns), F32), pltpu.SemaphoreType.DMA((blocks,))],
        out_specs=[ANY, VMEM, VMEM, VMEM],
    )(w, low, sources, high, low0, first, high0, self_terms, left, c2)
    images = call(
        final_second,
        outs,
        [ANY] + [VMEM] * 11,
        scratch + [pltpu.SemaphoreType.DMA((blocks,))],
        out_specs=ANY,
        alias={0: 0},
    )(images, w, low, sources, high, low1, second, high1, self_terms, left, c2, aux)
    return images, heights, norms


def solution(mesh):
    placed = (
        P(("groups", "store"), None),
        P(None, "store"),
        P(None, "store", None, None, None),
        P("store", None),
        P("store"),
        P("store", None),
        P("store", None, None),
        P("store", None, None),
        P(None, "store", None, None, None),
    )
    return jax.shard_map(
        shards,
        mesh=mesh,
        in_specs=placed,
        out_specs=(P(None, ("groups", "store"), None), P("groups", None), P("groups", None)),
        check_vma=False,
    )
```

```python
import functools

import jax
import jax.numpy as jnp
from jax import lax
from jax.experimental import pallas as pl
from jax.experimental.pallas import tpu as pltpu
from jax.sharding import PartitionSpec as P

REACH = 2
EPSILON = 1e-06
LANES = 128
HALF = 64
SLICES = 8
STATS = 16
FLOP_RATE = 1150000000
F32 = jnp.float32
BF16 = jnp.bfloat16

VMEM = pl.BlockSpec(memory_space=pltpu.VMEM)
SMEM = pl.BlockSpec(memory_space=pltpu.SMEM)
ANY = pl.BlockSpec(memory_space=pl.ANY)


def call(body, out_shape, in_specs, scratch=(), micros=0.0, megabytes=20, out_specs=None, alias=None):
    many = isinstance(out_shape, (list, tuple))
    if out_specs is None:
        out_specs = [VMEM] * len(out_shape) if many else VMEM
    return pl.pallas_call(
        body,
        out_shape=out_shape,
        in_specs=in_specs,
        out_specs=out_specs,
        input_output_aliases=alias or {},
        scratch_shapes=list(scratch),
        compiler_params=pltpu.CompilerParams(vmem_limit_bytes=megabytes * 1024 * 1024),
        cost_estimate=pl.CostEstimate(
            flops=int(micros * FLOP_RATE), bytes_accessed=0, transcendentals=0
        ),
    )


def dot(a, b, dims=((1,), (0,))):
    return lax.dot_general(a, b, (dims, ((), ())), preferred_element_type=F32)


def split3(row):
    high = row.astype(BF16)
    rest = row - high.astype(F32)
    middle = rest.astype(BF16)
    low = (rest - middle.astype(F32)).astype(BF16)
    return [high, middle, low]


def join3(rows, at):
    return rows[..., 3 * at, :] + rows[..., 3 * at + 1, :] + rows[..., 3 * at + 2, :]


def row3(values, at):
    return values[3 * at:3 * at + 1] + values[3 * at + 1:3 * at + 2] + values[3 * at + 2:3 * at + 3]


def halves(x, y):
    left = lax.broadcasted_iota(jnp.int32, x.shape, x.ndim - 1) < HALF
    first = jnp.where(left, x, pltpu.roll(y, HALF, x.ndim - 1))
    second = jnp.where(left, pltpu.roll(x, HALF, x.ndim - 1), y)
    return first, second


def chunk(x, pair):
    return x[:, pair * LANES:(pair + 1) * LANES]


def order_tiles(all_blocks, cols, count, row0, tiles, after, out):
    ops, blocks, near, size, _ = tiles.shape
    for b in range(blocks):
        for k in range(near):
            rel = lax.rem(cols[b, k] - (row0[0] + b) + REACH + all_blocks, all_blocks)
            rel = lax.rem(rel, all_blocks)
            at = pl.multiple_of(rel * size, size)
            live = k < count[b]
            for o in range(ops):
                tile = tiles[o, b, k]
                out[b, o * size:(o + 1) * size, pl.ds(at, size)] = jnp.where(
                    live, tile, jnp.zeros_like(tile)
                )


def coeff_kernel(count, far_cols, u, right, coup, out):
    ops, blocks, far, rank, _ = coup.shape
    size = right.shape[2]
    z = [dot(right[b], u[b * size:(b + 1) * size, :]) for b in range(blocks)]
    at = 3 * ops * rank + STATS
    for pair in range(SLICES // 2):
        first, second = halves(chunk(z[0], pair), chunk(z[1], pair))
        out[2 * pair, at:at + rank, :] = first.astype(BF16)
        out[2 * pair + 1, at:at + rank, :] = second.astype(BF16)
    whole, rest = [], []
    for b in range(blocks):
        tiles = [
            jnp.concatenate([coup[o, b, f] for f in range(far)], axis=1) for o in range(ops)
        ]
        tiles = jnp.concatenate(tiles, axis=0)
        whole.append(tiles[:, :LANES])
        rest.append(tiles[:, LANES:])
    lane = lax.broadcasted_iota(jnp.int32, (STATS, LANES), 1)
    names = jnp.zeros((STATS, LANES), F32)
    for b in range(blocks):
        for f in range(far):
            col = far_cols[b, f]
            device = lax.div(col, blocks)
            slot = lax.rem(device, count) * SLICES + lax.div(device, count)
            name = (slot * blocks + lax.rem(col, blocks)).astype(F32)
            names = jnp.where(lane == b * far + f, name, names)
    whole = jnp.concatenate(
        whole + [jnp.concatenate(rest, axis=1), names.astype(BF16)], axis=0
    )
    for s in range(SLICES):
        out[s, 0:at, :] = whole


def take_kernel(held, after, out):
    out[...] = held[:, held.shape[1] - out.shape[1]:, :]


def coupling_rows(held, s, b, ops, rank):
    body = ops * rank
    first = held[s, b * body:(b + 1) * body, :]
    rest = held[s, 2 * body:3 * body, b * HALF:(b + 1) * HALF]
    return jnp.concatenate([first, rest], axis=1)


def couple(cols, held, s, b, ops, rank, far, z):
    at = (s * 2 + b) * far
    lhs = coupling_rows(held, s, b, ops, rank)
    starts = [pl.multiple_of(cols[at + f] * rank, rank) for f in range(far)]
    picked = [
        jnp.concatenate([x[pl.ds(start, rank), :] for start in starts], axis=0) for x in z
    ]
    if len(z) == 1:
        return dot(lhs, picked[0])
    return jnp.concatenate(
        [dot(lhs[o * rank:(o + 1) * rank], picked[o]) for o in range(ops)], axis=0
    )


def spread_rows(source, rank):
    count = source.shape[0]
    turned = pltpu.roll(source, HALF, 2)
    both = jnp.concatenate([source[:, None], turned[:, None]], axis=1)
    return both.reshape(count * 2 * rank, LANES).astype(BF16)


def group_at(group, m, groups, step):
    return pl.multiple_of(lax.rem(group[0] + (groups - m), groups) * step, step)


def first_couple(ops, rank, far, cols, group, held, *refs):
    parts, (out, zs) = refs[:-2], refs[-2:]
    step = SLICES * 2 * rank
    for m, part in enumerate(parts):
        at = group_at(group, m, len(parts), step)
        zs[pl.ds(at, step), :] = spread_rows(part[...].astype(F32), rank)
    for s in range(SLICES):
        c = [couple(cols, held, s, b, ops, rank, far, [zs]) for b in range(2)]
        out[s] = halves(c[0], c[1])[0].astype(BF16)


def take_coefs(cmsg, coef, rows):
    for pair in range(SLICES // 2):
        parts = halves(
            cmsg[2 * pair, 0:rows, :].astype(F32), cmsg[2 * pair + 1, 0:rows, :].astype(F32)
        )
        for b in range(2):
            coef[b, :, pair * LANES:(pair + 1) * LANES] = parts[b].astype(BF16)


def near_product(tiles, parts, b, blocks, size):
    total = None
    first = b - REACH
    at = 0
    for d, part in enumerate(parts):
        start = max((d - 1) * blocks, first)
        stop = min(d * blocks, first + 2 * REACH + 1)
        if stop <= start:
            continue
        begin = (start - (d - 1) * blocks) * size
        width = (stop - start) * size
        value = dot(tiles[:, at:at + width], part[begin:begin + width, :])
        total = value if total is None else total + value
        at += width
    return total


def diagonal_of(diag, o, b, size, columns):
    row = diag[o:o + 1, b * size:(b + 1) * size]
    column = jnp.transpose(jnp.broadcast_to(row, (LANES, size)))
    return jnp.concatenate([column] * (columns // LANES), axis=1)


def near_kernel(w, low, own, high, diag, image0, image1, token):
    token[...] = jnp.zeros_like(token)
    images = (image0, image1)
    ops = len(images)
    rows, columns = own.shape
    size = w.shape[1] // ops
    blocks = rows // size
    for b in range(blocks):
        product = near_product(w.at[b], (low, own, high), b, blocks, size)
        here = slice(b * size, (b + 1) * size)
        ub = own[here, :].astype(F32)
        for o in range(ops):
            images[o][here, :] = (
                product[o * size:(o + 1) * size] + diagonal_of(diag, o, b, size, columns) * ub
            )


def image_part(own, near, left, right, cmsg, out, z_out, image, coef, o):
    blocks, rank, size = right.shape
    rows, columns = own.shape
    take_coefs(cmsg, coef, cmsg.shape[1])
    squares, inner = 0.0, 0.0
    for b in range(blocks):
        here = slice(b * size, (b + 1) * size)
        ub = own[here, :].astype(F32)
        squares = squares + jnp.sum(ub * ub, axis=0, keepdims=True)
        far = dot(left[b], coef[b, o * rank:(o + 1) * rank, :], ((0,), (0,)))
        value = near[here, :] + far.astype(BF16).astype(F32)
        image[here, :] = value
        inner = inner + jnp.sum(ub * value, axis=0, keepdims=True)
    good = squares > 0
    pieces = split3(jnp.where(good, inner / jnp.where(good, squares, 1.0), 0.0))
    shift = pieces[0].astype(F32) + pieces[1].astype(F32) + pieces[2].astype(F32)
    spread = 0.0
    z = []
    for b in range(blocks):
        here = slice(b * size, (b + 1) * size)
        v = image[here, :] - shift * own[here, :].astype(F32)
        spread = spread + jnp.sum(v * v, axis=0, keepdims=True)
        v = v.astype(BF16)
        out[here, :] = v
        z.append(dot(right[b], v))
    for pair in range(SLICES // 2):
        first, second = halves(chunk(z[0], pair), chunk(z[1], pair))
        z_out[2 * pair, o * rank:(o + 1) * rank, :] = first.astype(BF16)
        z_out[2 * pair + 1, o * rank:(o + 1) * rank, :] = second.astype(BF16)
    zero = jnp.zeros((1, columns), BF16)
    out[rows:, :] = jnp.concatenate(pieces + [zero] * (STATS - len(pieces)), axis=0)
    return shift, squares, spread


def image_first(own, near, left, right, cmsg, out, z_out, keep, image, coef):
    shift, squares, spread = image_part(own, near, left, right, cmsg, out, z_out, image, coef, 0)
    keep[0:1, :] = shift
    keep[1:2, :] = spread


def image_second(own, near, left, right, cmsg, z_first, keep, out, mout, image, coef):
    shift, squares, spread = image_part(own, near, left, right, cmsg, out, mout, image, coef, 1)
    blocks, rank, size = right.shape
    columns = own.shape[1]
    body = 2 * rank
    mout[:, 0:rank, :] = z_first[...]
    stats = []
    for row in (keep[0:1, :], shift, squares, keep[1:2, :], spread):
        stats += split3(row)
    zero = jnp.zeros((1, columns), BF16)
    stats = jnp.concatenate(stats + [zero] * (STATS - len(stats)), axis=0).astype(F32)
    for pair in range(SLICES // 2):
        part = chunk(stats, pair)
        first, second = halves(part, part)
        mout[2 * pair, body:body + STATS, :] = first.astype(BF16)
        mout[2 * pair + 1, body:body + STATS, :] = second.astype(BF16)


def second_couple(panels, ops, rank, far, cols, group, after_low, after_high, held, *refs):
    out, zs, st = refs[-3:]
    count = (len(refs) - 3) // 2
    z1, msgs = refs[:count], refs[count:2 * count]
    body = ops * rank
    step = SLICES * 2 * rank
    for m, msg in enumerate(msgs):
        at = group_at(group, m, count, SLICES)
        st[pl.ds(at, SLICES)] = msg[:, body:body + STATS, :].astype(F32)
    every = st[...]
    squares = join3(every, ops)
    scale_sq = jnp.sum(squares, axis=0, keepdims=True) / panels + EPSILON
    reverse = 1.0 / jnp.sqrt(scale_sq)
    heights, norms = [], []
    for o in range(ops):
        shift = join3(every, o)
        height = jnp.sum(shift * squares, axis=0, keepdims=True) / panels / scale_sq
        delta = shift - height
        spread = join3(every, ops + 1 + o) + delta * delta * squares
        norm = jnp.sqrt(jnp.sum(spread, axis=0, keepdims=True) / panels / scale_sq + EPSILON)
        heights.append(height)
        norms.append(norm)
    for m, msg in enumerate(msgs):
        at = group_at(group, m, count, step)
        mine = msg[:, body:body + STATS, :].astype(F32)
        base = z1[m][...].astype(F32)
        for o in range(ops):
            delta = join3(mine, o) - heights[o]
            z = msg[:, o * rank:(o + 1) * rank, :].astype(F32) + delta[:, None, :] * base
            z = z * (reverse / norms[o])[None]
            zs[o, pl.ds(at, step), :] = spread_rows(z, rank)
    rows = []
    for row in heights + norms + [reverse]:
        rows += split3(row)
    rows += [jnp.zeros_like(rows[0])] * (STATS - len(rows))
    rows = jnp.concatenate(rows, axis=0)
    for s in range(SLICES):
        c = [couple(cols, held, s, b, ops, rank, far, [zs.at[o] for o in range(ops)]) for b in range(2)]
        out[s, 0:body, :] = halves(c[0], c[1])[0].astype(BF16)
        out[s, body:body + STATS, :] = rows


def shift_changes(parts, height, factor):
    return [
        (row3(v[v.shape[0] - STATS:, :].astype(F32), 0) - height) * factor for v in parts
    ]


def apply_second(o, factor, changes, u3, v3, w, diag, left, cmsg, images, ext, coef, out, sems):
    blocks, rank, size = left.shape
    rows, columns = u3[1].shape
    ops = w.shape[1] // size
    take_coefs(cmsg, coef, ops * rank)
    for at, (u, v) in enumerate(zip(u3, v3)):
        value = v[0:rows, :].astype(F32) * factor + u[...].astype(F32) * changes[at]
        ext[at] = value.astype(BF16)
    copies = []
    for b in range(blocks):
        parts = [ext.at[at] for at in range(3)]
        product = near_product(w.at[b, o * size:(o + 1) * size], parts, b, blocks, size)
        far = dot(left[b], coef[b, o * rank:(o + 1) * rank, :], ((0,), (0,)))
        here = slice(b * size, (b + 1) * size)
        out[here, :] = (
            product
            + diagonal_of(diag, o, b, size, columns) * ext[1, here, :].astype(F32)
            + far.astype(BF16).astype(F32)
        )
        copies.append(pltpu.make_async_copy(out.at[here], images.at[o, here], sems.at[b]))
        copies[-1].start()
    for copy in copies:
        copy.wait()


def final_first(
    w,
    ulow,
    uown,
    uhigh,
    vlow,
    vown,
    vhigh,
    diag,
    left,
    cmsg,
    images,
    heights,
    norms,
    aux,
    ext,
    coef,
    out,
    stat,
    sems,
):
    blocks, rank, size = left.shape
    rows, columns = uown.shape
    ops = w.shape[1] // size
    body = ops * rank
    for pair in range(SLICES // 2):
        stat[:, pair * LANES:(pair + 1) * LANES] = halves(
            cmsg[2 * pair, body:body + STATS, :].astype(F32),
            cmsg[2 * pair + 1, body:body + STATS, :].astype(F32),
        )[0]
    st = stat[...]
    reverse = row3(st, 2 * ops)
    for o in range(ops):
        heights[o:o + 1, :] = row3(st, o)
        norms[o:o + 1, :] = row3(st, ops + o)
    aux[0:1, :] = reverse / row3(st, ops + 1)
    aux[1:2, :] = row3(st, 1)
    factor = reverse / row3(st, ops)
    changes = shift_changes((vlow, vown, vhigh), row3(st, 0), factor)
    u3, v3 = (ulow, uown, uhigh), (vlow, vown, vhigh)
    apply_second(0, factor, changes, u3, v3, w, diag, left, cmsg, images, ext, coef, out, sems)


def final_second(
    begun,
    w,
    ulow,
    uown,
    uhigh,
    vlow,
    vown,
    vhigh,
    diag,
    left,
    cmsg,
    aux,
    images,
    ext,
    coef,
    out,
    sems,
):
    factor = aux[0:1, :]
    changes = shift_changes((vlow, vown, vhigh), aux[1:2, :], factor)
    u3, v3 = (ulow, uown, uhigh), (vlow, vown, vhigh)
    apply_second(1, factor, changes, u3, v3, w, diag, left, cmsg, images, ext, coef, out, sems)


def ring(block):
    count = lax.axis_size("store")
    forward = [(i, (i + 1) % count) for i in range(count)]
    backward = [(target, source) for source, target in forward]
    return lax.ppermute(block, "store", forward), lax.ppermute(block, "store", backward)


def shards(
    sources,
    self_terms,
    near_tiles,
    near_cols,
    near_count,
    far_cols,
    basis_left,
    basis_right,
    couplings,
):
    n = lax.axis_size("store")
    ops, blocks, near, size, _ = near_tiles.shape
    rank = basis_left.shape[2]
    far = far_cols.shape[1]
    rows, columns = sources.shape
    all_blocks = blocks * n
    count = n // SLICES
    groups = [[s * count + g for s in range(SLICES)] for g in range(count)]
    sds = jax.ShapeDtypeStruct
    body = ops * rank

    def exchange(x):
        return lax.all_to_all(x, "store", 0, 0, axis_index_groups=groups, tiled=True)

    def across(x):
        parts = [x]
        for m in range(1, count):
            pairs = [(i, i - i % count + (i + m) % count) for i in range(n)]
            parts.append(lax.ppermute(x, "store", pairs))
        return parts

    place = lax.axis_index("store").astype(jnp.int32)
    row0 = (place * blocks).reshape(1)
    group = lax.rem(place, jnp.int32(count)).reshape(1)
    left = jnp.transpose(basis_left, (0, 2, 1))
    right = jnp.transpose(basis_right, (0, 2, 1))

    shared = (blocks + 1) * body
    low, high = ring(sources)
    mine = call(
        functools.partial(coeff_kernel, count),
        sds((SLICES, shared + STATS + rank, LANES), BF16),
        [SMEM] + [VMEM] * 3,
        megabytes=60,
    )(far_cols, sources, right, couplings)
    held = exchange(mine)
    cols = held[:, shared, :blocks * far].astype(jnp.int32).reshape(-1)

    w = call(
        functools.partial(order_tiles, all_blocks),
        sds((blocks, ops * size, near * size), BF16),
        [SMEM, SMEM, SMEM, VMEM, ANY],
        megabytes=60,
    )(near_cols, near_count, row0, near_tiles, mine)
    image0, image1, token = call(
        near_kernel,
        [sds((rows, columns), F32), sds((rows, columns), F32), sds((8, LANES), F32)],
        [VMEM] * 5,
        micros=10.0,
    )(w, low, sources, high, self_terms)
    z1 = across(call(take_kernel, sds((SLICES, rank, LANES), BF16), [VMEM, ANY])(held, token))

    c1 = call(
        functools.partial(first_couple, ops, rank, far),
        sds((SLICES, body, LANES), BF16),
        [SMEM, SMEM] + [VMEM] * (1 + count),
        [pltpu.VMEM((n * blocks * rank, LANES), BF16)],
    )(cols, group, held, *z1)
    c1 = exchange(c1)

    piece = sds((rows + STATS, columns), BF16)
    scratch = [pltpu.VMEM((rows, columns), F32), pltpu.VMEM((blocks, body, columns), BF16)]
    first, z_first, keep = call(
        image_first,
        [piece, sds((SLICES, rank, LANES), BF16), sds((8, columns), F32)],
        [VMEM] * 5,
        scratch,
    )(sources, image0, left, right, c1)
    low0, high0 = ring(first)
    second, msg = call(
        image_second,
        [piece, sds((SLICES, body + STATS, LANES), BF16)],
        [VMEM] * 7,
        scratch,
    )(sources, image1, left, right, c1, z_first, keep)
    low1, high1 = ring(second)
    msgs = across(exchange(msg))

    c2 = call(
        functools.partial(second_couple, all_blocks * size, ops, rank, far),
        sds((SLICES, body + STATS, LANES), BF16),
        [SMEM, SMEM, ANY, ANY] + [VMEM] * (1 + 2 * count),
        [
            pltpu.VMEM((ops, n * blocks * rank, LANES), BF16),
            pltpu.VMEM((n, STATS, LANES), F32),
        ],
        micros=30.0,
    )(cols, group, low0, high0, held, *z1, *msgs)
    c2 = exchange(c2)

    outs = sds((ops, rows, columns), F32)
    scratch = [
        pltpu.VMEM((3, rows, columns), BF16),
        pltpu.VMEM((blocks, body, columns), BF16),
        pltpu.VMEM((rows, columns), F32),
    ]
    images, heights, norms, aux = call(
        final_first,
        [outs, sds((ops, columns), F32), sds((ops, columns), F32), sds((8, columns), F32)],
        [VMEM] * 10,
        scratch + [pltpu.VMEM((STATS, columns), F32), pltpu.SemaphoreType.DMA((blocks,))],
        out_specs=[ANY, VMEM, VMEM, VMEM],
    )(w, low, sources, high, low0, first, high0, self_terms, left, c2)
    images = call(
        final_second,
        outs,
        [ANY] + [VMEM] * 11,
        scratch + [pltpu.SemaphoreType.DMA((blocks,))],
        out_specs=ANY,
        alias={0: 0},
    )(images, w, low, sources, high, low1, second, high1, self_terms, left, c2, aux)
    return images, heights, norms


def solution(mesh):
    placed = (
        P(("groups", "store"), None),
        P(None, "store"),
        P(None, "store", None, None, None),
        P("store", None),
        P("store"),
        P("store", None),
        P("store", None, None),
        P("store", None, None),
        P(None, "store", None, None, None),
    )
    return jax.shard_map(
        shards,
        mesh=mesh,
        in_specs=placed,
        out_specs=(P(None, ("groups", "store"), None), P("groups", None), P("groups", None)),
        check_vma=False,
    )
```

```python
import functools

import jax
import jax.numpy as jnp
from jax import lax
from jax.experimental import pallas as pl
from jax.experimental.pallas import tpu as pltpu
from jax.sharding import PartitionSpec as P

REACH = 2
EPSILON = 1e-06
LANES = 128
HALF = 64
SLICES = 8
STATS = 16
FLOP_RATE = 1150000000
F32 = jnp.float32
BF16 = jnp.bfloat16

VMEM = pl.BlockSpec(memory_space=pltpu.VMEM)
SMEM = pl.BlockSpec(memory_space=pltpu.SMEM)
ANY = pl.BlockSpec(memory_space=pl.ANY)


def call(body, out_shape, in_specs, scratch=(), micros=0.0, megabytes=20, out_specs=None, alias=None):
    many = isinstance(out_shape, (list, tuple))
    if out_specs is None:
        out_specs = [VMEM] * len(out_shape) if many else VMEM
    return pl.pallas_call(
        body,
        out_shape=out_shape,
        in_specs=in_specs,
        out_specs=out_specs,
        input_output_aliases=alias or {},
        scratch_shapes=list(scratch),
        compiler_params=pltpu.CompilerParams(vmem_limit_bytes=megabytes * 1024 * 1024),
        cost_estimate=pl.CostEstimate(
            flops=int(micros * FLOP_RATE), bytes_accessed=0, transcendentals=0
        ),
    )


def dot(a, b, dims=((1,), (0,))):
    return lax.dot_general(a, b, (dims, ((), ())), preferred_element_type=F32)


def split3(row):
    high = row.astype(BF16)
    rest = row - high.astype(F32)
    middle = rest.astype(BF16)
    low = (rest - middle.astype(F32)).astype(BF16)
    return [high, middle, low]


def join3(rows, at):
    return rows[..., 3 * at, :] + rows[..., 3 * at + 1, :] + rows[..., 3 * at + 2, :]


def row3(values, at):
    return values[3 * at:3 * at + 1] + values[3 * at + 1:3 * at + 2] + values[3 * at + 2:3 * at + 3]


def halves(x, y):
    left = lax.broadcasted_iota(jnp.int32, x.shape, x.ndim - 1) < HALF
    first = jnp.where(left, x, pltpu.roll(y, HALF, x.ndim - 1))
    second = jnp.where(left, pltpu.roll(x, HALF, x.ndim - 1), y)
    return first, second


def chunk(x, pair):
    return x[:, pair * LANES:(pair + 1) * LANES]


def order_tiles(all_blocks, cols, count, row0, tiles, after, out):
    ops, blocks, near, size, _ = tiles.shape
    for b in range(blocks):
        for k in range(near):
            rel = lax.rem(cols[b, k] - (row0[0] + b) + REACH + all_blocks, all_blocks)
            rel = lax.rem(rel, all_blocks)
            at = pl.multiple_of(rel * size, size)
            live = k < count[b]
            for o in range(ops):
                tile = tiles[o, b, k]
                out[b, o * size:(o + 1) * size, pl.ds(at, size)] = jnp.where(
                    live, tile, jnp.zeros_like(tile)
                )


def coeff_kernel(count, far_cols, u, right, coup, out):
    ops, blocks, far, rank, _ = coup.shape
    size = right.shape[2]
    z = [dot(right[b], u[b * size:(b + 1) * size, :]) for b in range(blocks)]
    at = 3 * ops * rank + STATS
    for pair in range(SLICES // 2):
        first, second = halves(chunk(z[0], pair), chunk(z[1], pair))
        out[2 * pair, at:at + rank, :] = first.astype(BF16)
        out[2 * pair + 1, at:at + rank, :] = second.astype(BF16)
    whole, rest = [], []
    for b in range(blocks):
        tiles = [
            jnp.concatenate([coup[o, b, f] for f in range(far)], axis=1) for o in range(ops)
        ]
        tiles = jnp.concatenate(tiles, axis=0)
        whole.append(tiles[:, :LANES])
        rest.append(tiles[:, LANES:])
    lane = lax.broadcasted_iota(jnp.int32, (STATS, LANES), 1)
    names = jnp.zeros((STATS, LANES), F32)
    for b in range(blocks):
        for f in range(far):
            col = far_cols[b, f]
            device = lax.div(col, blocks)
            slot = lax.rem(device, count) * SLICES + lax.div(device, count)
            name = (slot * blocks + lax.rem(col, blocks)).astype(F32)
            names = jnp.where(lane == b * far + f, name, names)
    whole = jnp.concatenate(
        whole + [jnp.concatenate(rest, axis=1), names.astype(BF16)], axis=0
    )
    for s in range(SLICES):
        out[s, 0:at, :] = whole


def take_kernel(held, after, out):
    out[...] = held[:, held.shape[1] - out.shape[1]:, :]


def coupling_rows(held, s, b, ops, rank):
    body = ops * rank
    first = held[s, b * body:(b + 1) * body, :]
    rest = held[s, 2 * body:3 * body, b * HALF:(b + 1) * HALF]
    return jnp.concatenate([first, rest], axis=1)


def couple(cols, held, s, b, ops, rank, far, z):
    at = (s * 2 + b) * far
    lhs = coupling_rows(held, s, b, ops, rank)
    starts = [pl.multiple_of(cols[at + f] * rank, rank) for f in range(far)]
    picked = [
        jnp.concatenate([x[pl.ds(start, rank), :] for start in starts], axis=0) for x in z
    ]
    if len(z) == 1:
        return dot(lhs, picked[0])
    return jnp.concatenate(
        [dot(lhs[o * rank:(o + 1) * rank], picked[o]) for o in range(ops)], axis=0
    )


def spread_rows(source, rank):
    count = source.shape[0]
    turned = pltpu.roll(source, HALF, 2)
    both = jnp.concatenate([source[:, None], turned[:, None]], axis=1)
    return both.reshape(count * 2 * rank, LANES).astype(BF16)


def group_at(group, m, groups, step):
    return pl.multiple_of(lax.rem(group[0] + (groups - m), groups) * step, step)


def first_couple(ops, rank, far, cols, group, held, *refs):
    parts, (out, zs) = refs[:-2], refs[-2:]
    step = SLICES * 2 * rank
    for m, part in enumerate(parts):
        at = group_at(group, m, len(parts), step)
        zs[pl.ds(at, step), :] = spread_rows(part[...].astype(F32), rank)
    for s in range(SLICES):
        c = [couple(cols, held, s, b, ops, rank, far, [zs]) for b in range(2)]
        out[s] = halves(c[0], c[1])[0].astype(BF16)


def take_coefs(cmsg, coef, rows):
    for pair in range(SLICES // 2):
        parts = halves(
            cmsg[2 * pair, 0:rows, :].astype(F32), cmsg[2 * pair + 1, 0:rows, :].astype(F32)
        )
        for b in range(2):
            coef[b, :, pair * LANES:(pair + 1) * LANES] = parts[b].astype(BF16)


def near_product(tiles, parts, b, blocks, size):
    total = None
    first = b - REACH
    at = 0
    for d, part in enumerate(parts):
        start = max((d - 1) * blocks, first)
        stop = min(d * blocks, first + 2 * REACH + 1)
        if stop <= start:
            continue
        begin = (start - (d - 1) * blocks) * size
        width = (stop - start) * size
        value = dot(tiles[:, at:at + width], part[begin:begin + width, :])
        total = value if total is None else total + value
        at += width
    return total


def diagonal_of(diag, o, b, size, columns):
    row = diag[o:o + 1, b * size:(b + 1) * size]
    column = jnp.transpose(jnp.broadcast_to(row, (LANES, size)))
    return jnp.concatenate([column] * (columns // LANES), axis=1)


def near_kernel(w, low, own, high, diag, image0, image1, token):
    token[...] = jnp.zeros_like(token)
    images = (image0, image1)
    ops = len(images)
    rows, columns = own.shape
    size = w.shape[1] // ops
    blocks = rows // size
    for b in range(blocks):
        product = near_product(w.at[b], (low, own, high), b, blocks, size)
        here = slice(b * size, (b + 1) * size)
        ub = own[here, :].astype(F32)
        for o in range(ops):
            images[o][here, :] = (
                product[o * size:(o + 1) * size] + diagonal_of(diag, o, b, size, columns) * ub
            )


def image_part(own, near, left, right, cmsg, out, z_out, image, coef, o):
    blocks, rank, size = right.shape
    rows, columns = own.shape
    take_coefs(cmsg, coef, cmsg.shape[1])
    squares, inner = 0.0, 0.0
    for b in range(blocks):
        here = slice(b * size, (b + 1) * size)
        ub = own[here, :].astype(F32)
        squares = squares + jnp.sum(ub * ub, axis=0, keepdims=True)
        far = dot(left[b], coef[b, o * rank:(o + 1) * rank, :], ((0,), (0,)))
        value = near[here, :] + far.astype(BF16).astype(F32)
        image[here, :] = value
        inner = inner + jnp.sum(ub * value, axis=0, keepdims=True)
    good = squares > 0
    pieces = split3(jnp.where(good, inner / jnp.where(good, squares, 1.0), 0.0))
    shift = pieces[0].astype(F32) + pieces[1].astype(F32) + pieces[2].astype(F32)
    spread = 0.0
    z = []
    for b in range(blocks):
        here = slice(b * size, (b + 1) * size)
        v = image[here, :] - shift * own[here, :].astype(F32)
        spread = spread + jnp.sum(v * v, axis=0, keepdims=True)
        v = v.astype(BF16)
        out[here, :] = v
        z.append(dot(right[b], v))
    for pair in range(SLICES // 2):
        first, second = halves(chunk(z[0], pair), chunk(z[1], pair))
        z_out[2 * pair, o * rank:(o + 1) * rank, :] = first.astype(BF16)
        z_out[2 * pair + 1, o * rank:(o + 1) * rank, :] = second.astype(BF16)
    zero = jnp.zeros((1, columns), BF16)
    out[rows:, :] = jnp.concatenate(pieces + [zero] * (STATS - len(pieces)), axis=0)
    return shift, squares, spread


def image_first(own, near, left, right, cmsg, out, z_out, keep, image, coef):
    shift, squares, spread = image_part(own, near, left, right, cmsg, out, z_out, image, coef, 0)
    keep[0:1, :] = shift
    keep[1:2, :] = spread


def image_second(own, near, left, right, cmsg, z_first, keep, out, mout, image, coef):
    shift, squares, spread = image_part(own, near, left, right, cmsg, out, mout, image, coef, 1)
    blocks, rank, size = right.shape
    columns = own.shape[1]
    body = 2 * rank
    mout[:, 0:rank, :] = z_first[...]
    stats = []
    for row in (keep[0:1, :], shift, squares, keep[1:2, :], spread):
        stats += split3(row)
    zero = jnp.zeros((1, columns), BF16)
    stats = jnp.concatenate(stats + [zero] * (STATS - len(stats)), axis=0).astype(F32)
    for pair in range(SLICES // 2):
        part = chunk(stats, pair)
        first, second = halves(part, part)
        mout[2 * pair, body:body + STATS, :] = first.astype(BF16)
        mout[2 * pair + 1, body:body + STATS, :] = second.astype(BF16)


def second_couple(panels, ops, rank, far, cols, group, after_low, after_high, held, *refs):
    out, zs, st = refs[-3:]
    count = (len(refs) - 3) // 2
    z1, msgs = refs[:count], refs[count:2 * count]
    body = ops * rank
    step = SLICES * 2 * rank
    for m, msg in enumerate(msgs):
        at = group_at(group, m, count, SLICES)
        st[pl.ds(at, SLICES)] = msg[:, body:body + STATS, :].astype(F32)
    every = st[...]
    squares = join3(every, ops)
    scale_sq = jnp.sum(squares, axis=0, keepdims=True) / panels + EPSILON
    reverse = 1.0 / jnp.sqrt(scale_sq)
    heights, norms = [], []
    for o in range(ops):
        shift = join3(every, o)
        height = jnp.sum(shift * squares, axis=0, keepdims=True) / panels / scale_sq
        delta = shift - height
        spread = join3(every, ops + 1 + o) + delta * (delta * squares)
        norm = jnp.sqrt(jnp.sum(spread, axis=0, keepdims=True) / panels / scale_sq + EPSILON)
        heights.append(height)
        norms.append(norm)
    for m, msg in enumerate(msgs):
        at = group_at(group, m, count, step)
        mine = msg[:, body:body + STATS, :].astype(F32)
        base = z1[m][...].astype(F32)
        for o in range(ops):
            delta = join3(mine, o) - heights[o]
            z = msg[:, o * rank:(o + 1) * rank, :].astype(F32) + delta[:, None, :] * base
            z = z * (reverse / norms[o])[None]
            zs[o, pl.ds(at, step), :] = spread_rows(z, rank)
    rows = []
    for row in heights + norms + [reverse]:
        rows += split3(row)
    rows += [jnp.zeros_like(rows[0])] * (STATS - len(rows))
    rows = jnp.concatenate(rows, axis=0)
    for s in range(SLICES):
        c = [couple(cols, held, s, b, ops, rank, far, [zs.at[o] for o in range(ops)]) for b in range(2)]
        out[s, 0:body, :] = halves(c[0], c[1])[0].astype(BF16)
        out[s, body:body + STATS, :] = rows


def shift_changes(parts, height, factor):
    return [
        (row3(v[v.shape[0] - STATS:, :].astype(F32), 0) - height) * factor for v in parts
    ]


def apply_second(o, factor, changes, u3, v3, w, diag, left, cmsg, images, ext, coef, out, sems):
    blocks, rank, size = left.shape
    rows, columns = u3[1].shape
    ops = w.shape[1] // size
    take_coefs(cmsg, coef, ops * rank)
    for at, (u, v) in enumerate(zip(u3, v3)):
        value = v[0:rows, :].astype(F32) * factor + u[...].astype(F32) * changes[at]
        ext[at] = value.astype(BF16)
    copies = []
    for b in range(blocks):
        parts = [ext.at[at] for at in range(3)]
        product = near_product(w.at[b, o * size:(o + 1) * size], parts, b, blocks, size)
        far = dot(left[b], coef[b, o * rank:(o + 1) * rank, :], ((0,), (0,)))
        here = slice(b * size, (b + 1) * size)
        out[here, :] = (
            product
            + diagonal_of(diag, o, b, size, columns) * ext[1, here, :].astype(F32)
            + far.astype(BF16).astype(F32)
        )
        copies.append(pltpu.make_async_copy(out.at[here], images.at[o, here], sems.at[b]))
        copies[-1].start()
    for copy in copies:
        copy.wait()


def final_first(
    w,
    ulow,
    uown,
    uhigh,
    vlow,
    vown,
    vhigh,
    diag,
    left,
    cmsg,
    images,
    heights,
    norms,
    aux,
    ext,
    coef,
    out,
    stat,
    sems,
):
    blocks, rank, size = left.shape
    rows, columns = uown.shape
    ops = w.shape[1] // size
    body = ops * rank
    for pair in range(SLICES // 2):
        stat[:, pair * LANES:(pair + 1) * LANES] = halves(
            cmsg[2 * pair, body:body + STATS, :].astype(F32),
            cmsg[2 * pair + 1, body:body + STATS, :].astype(F32),
        )[0]
    st = stat[...]
    reverse = row3(st, 2 * ops)
    for o in range(ops):
        heights[o:o + 1, :] = row3(st, o)
        norms[o:o + 1, :] = row3(st, ops + o)
    aux[0:1, :] = reverse / row3(st, ops + 1)
    aux[1:2, :] = row3(st, 1)
    factor = reverse / row3(st, ops)
    changes = shift_changes((vlow, vown, vhigh), row3(st, 0), factor)
    u3, v3 = (ulow, uown, uhigh), (vlow, vown, vhigh)
    apply_second(0, factor, changes, u3, v3, w, diag, left, cmsg, images, ext, coef, out, sems)


def final_second(
    begun,
    w,
    ulow,
    uown,
    uhigh,
    vlow,
    vown,
    vhigh,
    diag,
    left,
    cmsg,
    aux,
    images,
    ext,
    coef,
    out,
    sems,
):
    factor = aux[0:1, :]
    changes = shift_changes((vlow, vown, vhigh), aux[1:2, :], factor)
    u3, v3 = (ulow, uown, uhigh), (vlow, vown, vhigh)
    apply_second(1, factor, changes, u3, v3, w, diag, left, cmsg, images, ext, coef, out, sems)


def ring(block):
    count = lax.axis_size("store")
    forward = [(i, (i + 1) % count) for i in range(count)]
    backward = [(target, source) for source, target in forward]
    return lax.ppermute(block, "store", forward), lax.ppermute(block, "store", backward)


def shards(
    sources,
    self_terms,
    near_tiles,
    near_cols,
    near_count,
    far_cols,
    basis_left,
    basis_right,
    couplings,
):
    n = lax.axis_size("store")
    ops, blocks, near, size, _ = near_tiles.shape
    rank = basis_left.shape[2]
    far = far_cols.shape[1]
    rows, columns = sources.shape
    all_blocks = blocks * n
    count = n // SLICES
    groups = [[s * count + g for s in range(SLICES)] for g in range(count)]
    sds = jax.ShapeDtypeStruct
    body = ops * rank

    def exchange(x):
        return lax.all_to_all(x, "store", 0, 0, axis_index_groups=groups, tiled=True)

    def across(x):
        parts = [x]
        for m in range(1, count):
            pairs = [(i, i - i % count + (i + m) % count) for i in range(n)]
            parts.append(lax.ppermute(x, "store", pairs))
        return parts

    place = lax.axis_index("store").astype(jnp.int32)
    row0 = (place * blocks).reshape(1)
    group = lax.rem(place, jnp.int32(count)).reshape(1)
    left = jnp.transpose(basis_left, (0, 2, 1))
    right = jnp.transpose(basis_right, (0, 2, 1))

    shared = (blocks + 1) * body
    low, high = ring(sources)
    mine = call(
        functools.partial(coeff_kernel, count),
        sds((SLICES, shared + STATS + rank, LANES), BF16),
        [SMEM] + [VMEM] * 3,
        megabytes=60,
    )(far_cols, sources, right, couplings)
    held = exchange(mine)
    cols = held[:, shared, :blocks * far].astype(jnp.int32).reshape(-1)

    w = call(
        functools.partial(order_tiles, all_blocks),
        sds((blocks, ops * size, near * size), BF16),
        [SMEM, SMEM, SMEM, VMEM, ANY],
        megabytes=60,
    )(near_cols, near_count, row0, near_tiles, mine)
    image0, image1, token = call(
        near_kernel,
        [sds((rows, columns), F32), sds((rows, columns), F32), sds((8, LANES), F32)],
        [VMEM] * 5,
        micros=10.0,
    )(w, low, sources, high, self_terms)
    z1 = across(call(take_kernel, sds((SLICES, rank, LANES), BF16), [VMEM, ANY])(held, token))

    c1 = call(
        functools.partial(first_couple, ops, rank, far),
        sds((SLICES, body, LANES), BF16),
        [SMEM, SMEM] + [VMEM] * (1 + count),
        [pltpu.VMEM((n * blocks * rank, LANES), BF16)],
    )(cols, group, held, *z1)
    c1 = exchange(c1)

    piece = sds((rows + STATS, columns), BF16)
    scratch = [pltpu.VMEM((rows, columns), F32), pltpu.VMEM((blocks, body, columns), BF16)]
    first, z_first, keep = call(
        image_first,
        [piece, sds((SLICES, rank, LANES), BF16), sds((8, columns), F32)],
        [VMEM] * 5,
        scratch,
    )(sources, image0, left, right, c1)
    low0, high0 = ring(first)
    second, msg = call(
        image_second,
        [piece, sds((SLICES, body + STATS, LANES), BF16)],
        [VMEM] * 7,
        scratch,
    )(sources, image1, left, right, c1, z_first, keep)
    low1, high1 = ring(second)
    msgs = across(exchange(msg))

    c2 = call(
        functools.partial(second_couple, all_blocks * size, ops, rank, far),
        sds((SLICES, body + STATS, LANES), BF16),
        [SMEM, SMEM, ANY, ANY] + [VMEM] * (1 + 2 * count),
        [
            pltpu.VMEM((ops, n * blocks * rank, LANES), BF16),
            pltpu.VMEM((n, STATS, LANES), F32),
        ],
        micros=30.0,
    )(cols, group, low0, high0, held, *z1, *msgs)
    c2 = exchange(c2)

    outs = sds((ops, rows, columns), F32)
    scratch = [
        pltpu.VMEM((3, rows, columns), BF16),
        pltpu.VMEM((blocks, body, columns), BF16),
        pltpu.VMEM((rows, columns), F32),
    ]
    images, heights, norms, aux = call(
        final_first,
        [outs, sds((ops, columns), F32), sds((ops, columns), F32), sds((8, columns), F32)],
        [VMEM] * 10,
        scratch + [pltpu.VMEM((STATS, columns), F32), pltpu.SemaphoreType.DMA((blocks,))],
        out_specs=[ANY, VMEM, VMEM, VMEM],
    )(w, low, sources, high, low0, first, high0, self_terms, left, c2)
    images = call(
        final_second,
        outs,
        [ANY] + [VMEM] * 11,
        scratch + [pltpu.SemaphoreType.DMA((blocks,))],
        out_specs=ANY,
        alias={0: 0},
    )(images, w, low, sources, high, low1, second, high1, self_terms, left, c2, aux)
    return images, heights, norms


def solution(mesh):
    placed = (
        P(("groups", "store"), None),
        P(None, "store"),
        P(None, "store", None, None, None),
        P("store", None),
        P("store"),
        P("store", None),
        P("store", None, None),
        P("store", None, None),
        P(None, "store", None, None, None),
    )
    return jax.shard_map(
        shards,
        mesh=mesh,
        in_specs=placed,
        out_specs=(P(None, ("groups", "store"), None), P("groups", None), P("groups", None)),
        check_vma=False,
    )
```

```python
import functools

import jax
import jax.numpy as jnp
from jax import lax
from jax.experimental import pallas as pl
from jax.experimental.pallas import tpu as pltpu
from jax.sharding import PartitionSpec as P

REACH = 2
EPSILON = 1e-06
LANES = 128
HALF = 64
SLICES = 8
STATS = 16
FLOP_RATE = 1150000000
F32 = jnp.float32
BF16 = jnp.bfloat16

VMEM = pl.BlockSpec(memory_space=pltpu.VMEM)
SMEM = pl.BlockSpec(memory_space=pltpu.SMEM)
ANY = pl.BlockSpec(memory_space=pl.ANY)


def call(body, out_shape, in_specs, scratch=(), micros=0.0, megabytes=20, out_specs=None, alias=None):
    many = isinstance(out_shape, (list, tuple))
    if out_specs is None:
        out_specs = [VMEM] * len(out_shape) if many else VMEM
    return pl.pallas_call(
        body,
        out_shape=out_shape,
        in_specs=in_specs,
        out_specs=out_specs,
        input_output_aliases=alias or {},
        scratch_shapes=list(scratch),
        compiler_params=pltpu.CompilerParams(vmem_limit_bytes=megabytes * 1024 * 1024),
        cost_estimate=pl.CostEstimate(
            flops=int(micros * FLOP_RATE), bytes_accessed=0, transcendentals=0
        ),
    )


def dot(a, b, dims=((1,), (0,))):
    return lax.dot_general(a, b, (dims, ((), ())), preferred_element_type=F32)


def split3(row):
    high = row.astype(BF16)
    rest = row - high.astype(F32)
    middle = rest.astype(BF16)
    low = (rest - middle.astype(F32)).astype(BF16)
    return [high, middle, low]


def join3(rows, at):
    return rows[..., 3 * at, :] + rows[..., 3 * at + 1, :] + rows[..., 3 * at + 2, :]


def row3(values, at):
    return values[3 * at:3 * at + 1] + values[3 * at + 1:3 * at + 2] + values[3 * at + 2:3 * at + 3]


def halves(x, y):
    left = lax.broadcasted_iota(jnp.int32, x.shape, x.ndim - 1) < HALF
    first = jnp.where(left, x, pltpu.roll(y, HALF, x.ndim - 1))
    second = jnp.where(left, pltpu.roll(x, HALF, x.ndim - 1), y)
    return first, second


def chunk(x, pair):
    return x[:, pair * LANES:(pair + 1) * LANES]


def order_tiles(all_blocks, cols, count, row0, tiles, after, out):
    ops, blocks, near, size, _ = tiles.shape
    for b in range(blocks):
        for k in range(near):
            rel = lax.rem(cols[b, k] - (row0[0] + b) + REACH + all_blocks, all_blocks)
            rel = lax.rem(rel, all_blocks)
            at = pl.multiple_of(rel * size, size)
            live = k < count[b]
            for o in range(ops):
                tile = tiles[o, b, k]
                out[b, o * size:(o + 1) * size, pl.ds(at, size)] = jnp.where(
                    live, tile, jnp.zeros_like(tile)
                )


def coeff_kernel(count, far_cols, u, right, coup, out):
    ops, blocks, far, rank, _ = coup.shape
    size = right.shape[2]
    z = [dot(right[b], u[b * size:(b + 1) * size, :]) for b in range(blocks)]
    at = 3 * ops * rank + STATS
    for pair in range(SLICES // 2):
        first, second = halves(chunk(z[0], pair), chunk(z[1], pair))
        out[2 * pair, at:at + rank, :] = first.astype(BF16)
        out[2 * pair + 1, at:at + rank, :] = second.astype(BF16)
    whole, rest = [], []
    for b in range(blocks):
        tiles = [
            jnp.concatenate([coup[o, b, f] for f in range(far)], axis=1) for o in range(ops)
        ]
        tiles = jnp.concatenate(tiles, axis=0)
        whole.append(tiles[:, :LANES])
        rest.append(tiles[:, LANES:])
    lane = lax.broadcasted_iota(jnp.int32, (STATS, LANES), 1)
    names = jnp.zeros((STATS, LANES), F32)
    for b in range(blocks):
        for f in range(far):
            col = far_cols[b, f]
            device = lax.div(col, blocks)
            slot = lax.rem(device, count) * SLICES + lax.div(device, count)
            name = (slot * blocks + lax.rem(col, blocks)).astype(F32)
            names = jnp.where(lane == b * far + f, name, names)
    whole = jnp.concatenate(
        whole + [jnp.concatenate(rest, axis=1), names.astype(BF16)], axis=0
    )
    for s in range(SLICES):
        out[s, 0:at, :] = whole


def take_kernel(held, after, out):
    out[...] = held[:, held.shape[1] - out.shape[1]:, :]


def coupling_rows(held, s, b, ops, rank):
    body = ops * rank
    first = held[s, b * body:(b + 1) * body, :]
    rest = held[s, 2 * body:3 * body, b * HALF:(b + 1) * HALF]
    return jnp.concatenate([first, rest], axis=1)


def couple(cols, held, s, b, ops, rank, far, z):
    at = (s * 2 + b) * far
    lhs = coupling_rows(held, s, b, ops, rank)
    starts = [pl.multiple_of(cols[at + f] * rank, rank) for f in range(far)]
    picked = [
        jnp.concatenate([x[pl.ds(start, rank), :] for start in starts], axis=0) for x in z
    ]
    if len(z) == 1:
        return dot(lhs, picked[0])
    return jnp.concatenate(
        [dot(lhs[o * rank:(o + 1) * rank], picked[o]) for o in range(ops)], axis=0
    )


def spread_rows(source, rank):
    count = source.shape[0]
    turned = pltpu.roll(source, HALF, 2)
    both = jnp.concatenate([source[:, None], turned[:, None]], axis=1)
    return both.reshape(count * 2 * rank, LANES).astype(BF16)


def group_at(group, m, groups, step):
    return pl.multiple_of(lax.rem(group[0] + (groups - m), groups) * step, step)


def first_couple(ops, rank, far, cols, group, held, *refs):
    parts, (out, zs) = refs[:-2], refs[-2:]
    step = SLICES * 2 * rank
    for m, part in enumerate(parts):
        at = group_at(group, m, len(parts), step)
        zs[pl.ds(at, step), :] = spread_rows(part[...].astype(F32), rank)
    for s in range(SLICES):
        c = [couple(cols, held, s, b, ops, rank, far, [zs]) for b in range(2)]
        out[s] = halves(c[0], c[1])[0].astype(BF16)


def take_coefs(cmsg, coef, o, rank):
    rows = slice(o * rank, (o + 1) * rank)
    for pair in range(SLICES // 2):
        parts = halves(
            cmsg[2 * pair, rows, :].astype(F32), cmsg[2 * pair + 1, rows, :].astype(F32)
        )
        for b in range(2):
            coef[b, rows, pair * LANES:(pair + 1) * LANES] = parts[b].astype(BF16)


def near_product(tiles, parts, b, blocks, size):
    total = None
    first = b - REACH
    at = 0
    for d, part in enumerate(parts):
        start = max((d - 1) * blocks, first)
        stop = min(d * blocks, first + 2 * REACH + 1)
        if stop <= start:
            continue
        begin = (start - (d - 1) * blocks) * size
        width = (stop - start) * size
        value = dot(tiles[:, at:at + width], part[begin:begin + width, :])
        total = value if total is None else total + value
        at += width
    return total


def diagonal_of(diag, o, b, size, columns):
    row = diag[o:o + 1, b * size:(b + 1) * size]
    column = jnp.transpose(jnp.broadcast_to(row, (LANES, size)))
    return jnp.concatenate([column] * (columns // LANES), axis=1)


def near_kernel(w, low, own, high, diag, image0, image1, token):
    token[...] = jnp.zeros_like(token)
    images = (image0, image1)
    ops = len(images)
    rows, columns = own.shape
    size = w.shape[1] // ops
    blocks = rows // size
    for b in range(blocks):
        product = near_product(w.at[b], (low, own, high), b, blocks, size)
        here = slice(b * size, (b + 1) * size)
        ub = own[here, :].astype(F32)
        for o in range(ops):
            images[o][here, :] = (
                product[o * size:(o + 1) * size] + diagonal_of(diag, o, b, size, columns) * ub
            )


def image_part(own, near, left, right, cmsg, out, z_out, image, coef, o):
    blocks, rank, size = right.shape
    rows, columns = own.shape
    take_coefs(cmsg, coef, o, rank)
    squares, inner = 0.0, 0.0
    for b in range(blocks):
        here = slice(b * size, (b + 1) * size)
        ub = own[here, :].astype(F32)
        squares = squares + jnp.sum(ub * ub, axis=0, keepdims=True)
        far = dot(left[b], coef[b, o * rank:(o + 1) * rank, :], ((0,), (0,)))
        value = near[here, :] + far.astype(BF16).astype(F32)
        image[here, :] = value
        inner = inner + jnp.sum(ub * value, axis=0, keepdims=True)
    good = squares > 0
    pieces = split3(jnp.where(good, inner / jnp.where(good, squares, 1.0), 0.0))
    shift = pieces[0].astype(F32) + pieces[1].astype(F32) + pieces[2].astype(F32)
    spread = 0.0
    z = []
    for b in range(blocks):
        here = slice(b * size, (b + 1) * size)
        v = image[here, :] - shift * own[here, :].astype(F32)
        spread = spread + jnp.sum(v * v, axis=0, keepdims=True)
        v = v.astype(BF16)
        out[here, :] = v
        z.append(dot(right[b], v))
    for pair in range(SLICES // 2):
        first, second = halves(chunk(z[0], pair), chunk(z[1], pair))
        z_out[2 * pair, o * rank:(o + 1) * rank, :] = first.astype(BF16)
        z_out[2 * pair + 1, o * rank:(o + 1) * rank, :] = second.astype(BF16)
    zero = jnp.zeros((1, columns), BF16)
    out[rows:, :] = jnp.concatenate(pieces + [zero] * (STATS - len(pieces)), axis=0)
    return shift, squares, spread


def image_first(own, near, left, right, cmsg, out, z_out, keep, image, coef):
    shift, squares, spread = image_part(own, near, left, right, cmsg, out, z_out, image, coef, 0)
    keep[0:1, :] = shift
    keep[1:2, :] = spread


def image_second(own, near, left, right, cmsg, z_first, keep, out, mout, image, coef):
    shift, squares, spread = image_part(own, near, left, right, cmsg, out, mout, image, coef, 1)
    blocks, rank, size = right.shape
    columns = own.shape[1]
    body = 2 * rank
    mout[:, 0:rank, :] = z_first[...]
    stats = []
    for row in (keep[0:1, :], shift, squares, keep[1:2, :], spread):
        stats += split3(row)
    zero = jnp.zeros((1, columns), BF16)
    stats = jnp.concatenate(stats + [zero] * (STATS - len(stats)), axis=0).astype(F32)
    for pair in range(SLICES // 2):
        part = chunk(stats, pair)
        first, second = halves(part, part)
        mout[2 * pair, body:body + STATS, :] = first.astype(BF16)
        mout[2 * pair + 1, body:body + STATS, :] = second.astype(BF16)


def second_couple(panels, ops, rank, far, cols, group, after_low, after_high, held, *refs):
    out, zs, st = refs[-3:]
    count = (len(refs) - 3) // 2
    z1, msgs = refs[:count], refs[count:2 * count]
    body = ops * rank
    step = SLICES * 2 * rank
    for m, msg in enumerate(msgs):
        at = group_at(group, m, count, SLICES)
        st[pl.ds(at, SLICES)] = msg[:, body:body + STATS, :].astype(F32)
    every = st[...]
    squares = join3(every, ops)
    scale_sq = jnp.sum(squares, axis=0, keepdims=True) / panels + EPSILON
    reverse = 1.0 / jnp.sqrt(scale_sq)
    heights, norms = [], []
    for o in range(ops):
        shift = join3(every, o)
        height = jnp.sum(shift * squares, axis=0, keepdims=True) / panels / scale_sq
        delta = shift - height
        spread = join3(every, ops + 1 + o) + delta * (delta * squares)
        norm = jnp.sqrt(jnp.sum(spread, axis=0, keepdims=True) / panels / scale_sq + EPSILON)
        heights.append(height)
        norms.append(norm)
    for m, msg in enumerate(msgs):
        at = group_at(group, m, count, step)
        mine = msg[:, body:body + STATS, :].astype(F32)
        base = z1[m][...].astype(F32)
        for o in range(ops):
            delta = join3(mine, o) - heights[o]
            z = msg[:, o * rank:(o + 1) * rank, :].astype(F32) + delta[:, None, :] * base
            z = z * (reverse / norms[o])[None]
            zs[o, pl.ds(at, step), :] = spread_rows(z, rank)
    rows = []
    for row in heights + norms + [reverse]:
        rows += split3(row)
    rows += [jnp.zeros_like(rows[0])] * (STATS - len(rows))
    rows = jnp.concatenate(rows, axis=0)
    for s in range(SLICES):
        c = [couple(cols, held, s, b, ops, rank, far, [zs.at[o] for o in range(ops)]) for b in range(2)]
        out[s, 0:body, :] = halves(c[0], c[1])[0].astype(BF16)
        out[s, body:body + STATS, :] = rows


def shift_changes(parts, height, factor):
    return [
        (row3(v[v.shape[0] - STATS:, :].astype(F32), 0) - height) * factor for v in parts
    ]


def apply_second(o, factor, changes, u3, v3, w, diag, left, cmsg, images, ext, coef, out, sems):
    blocks, rank, size = left.shape
    rows, columns = u3[1].shape
    ops = w.shape[1] // size
    take_coefs(cmsg, coef, o, rank)
    for at, (u, v) in enumerate(zip(u3, v3)):
        value = v[0:rows, :].astype(F32) * factor + u[...].astype(F32) * changes[at]
        ext[at] = value.astype(BF16)
    copies = []
    for b in range(blocks):
        parts = [ext.at[at] for at in range(3)]
        product = near_product(w.at[b, o * size:(o + 1) * size], parts, b, blocks, size)
        far = dot(left[b], coef[b, o * rank:(o + 1) * rank, :], ((0,), (0,)))
        here = slice(b * size, (b + 1) * size)
        out[here, :] = (
            product
            + diagonal_of(diag, o, b, size, columns) * ext[1, here, :].astype(F32)
            + far.astype(BF16).astype(F32)
        )
        copies.append(pltpu.make_async_copy(out.at[here], images.at[o, here], sems.at[b]))
        copies[-1].start()
    for copy in copies:
        copy.wait()


def final_first(
    w,
    ulow,
    uown,
    uhigh,
    vlow,
    vown,
    vhigh,
    diag,
    left,
    cmsg,
    images,
    heights,
    norms,
    aux,
    ext,
    coef,
    out,
    stat,
    sems,
):
    blocks, rank, size = left.shape
    rows, columns = uown.shape
    ops = w.shape[1] // size
    body = ops * rank
    for pair in range(SLICES // 2):
        stat[:, pair * LANES:(pair + 1) * LANES] = halves(
            cmsg[2 * pair, body:body + STATS, :].astype(F32),
            cmsg[2 * pair + 1, body:body + STATS, :].astype(F32),
        )[0]
    st = stat[...]
    reverse = row3(st, 2 * ops)
    for o in range(ops):
        heights[o:o + 1, :] = row3(st, o)
        norms[o:o + 1, :] = row3(st, ops + o)
    aux[0:1, :] = reverse / row3(st, ops + 1)
    aux[1:2, :] = row3(st, 1)
    factor = reverse / row3(st, ops)
    changes = shift_changes((vlow, vown, vhigh), row3(st, 0), factor)
    u3, v3 = (ulow, uown, uhigh), (vlow, vown, vhigh)
    apply_second(0, factor, changes, u3, v3, w, diag, left, cmsg, images, ext, coef, out, sems)


def final_second(
    begun,
    w,
    ulow,
    uown,
    uhigh,
    vlow,
    vown,
    vhigh,
    diag,
    left,
    cmsg,
    aux,
    images,
    ext,
    coef,
    out,
    sems,
):
    factor = aux[0:1, :]
    changes = shift_changes((vlow, vown, vhigh), aux[1:2, :], factor)
    u3, v3 = (ulow, uown, uhigh), (vlow, vown, vhigh)
    apply_second(1, factor, changes, u3, v3, w, diag, left, cmsg, images, ext, coef, out, sems)


def ring(block):
    count = lax.axis_size("store")
    forward = [(i, (i + 1) % count) for i in range(count)]
    backward = [(target, source) for source, target in forward]
    return lax.ppermute(block, "store", forward), lax.ppermute(block, "store", backward)


def shards(
    sources,
    self_terms,
    near_tiles,
    near_cols,
    near_count,
    far_cols,
    basis_left,
    basis_right,
    couplings,
):
    n = lax.axis_size("store")
    ops, blocks, near, size, _ = near_tiles.shape
    rank = basis_left.shape[2]
    far = far_cols.shape[1]
    rows, columns = sources.shape
    all_blocks = blocks * n
    count = n // SLICES
    groups = [[s * count + g for s in range(SLICES)] for g in range(count)]
    sds = jax.ShapeDtypeStruct
    body = ops * rank

    def exchange(x):
        return lax.all_to_all(x, "store", 0, 0, axis_index_groups=groups, tiled=True)

    def across(x):
        parts = [x]
        for m in range(1, count):
            pairs = [(i, i - i % count + (i + m) % count) for i in range(n)]
            parts.append(lax.ppermute(x, "store", pairs))
        return parts

    place = lax.axis_index("store").astype(jnp.int32)
    row0 = (place * blocks).reshape(1)
    group = lax.rem(place, jnp.int32(count)).reshape(1)
    left = jnp.transpose(basis_left, (0, 2, 1))
    right = jnp.transpose(basis_right, (0, 2, 1))

    shared = (blocks + 1) * body
    low, high = ring(sources)
    mine = call(
        functools.partial(coeff_kernel, count),
        sds((SLICES, shared + STATS + rank, LANES), BF16),
        [SMEM] + [VMEM] * 3,
        megabytes=60,
    )(far_cols, sources, right, couplings)
    held = exchange(mine)
    cols = held[:, shared, :blocks * far].astype(jnp.int32).reshape(-1)

    w = call(
        functools.partial(order_tiles, all_blocks),
        sds((blocks, ops * size, near * size), BF16),
        [SMEM, SMEM, SMEM, VMEM, ANY],
        megabytes=60,
    )(near_cols, near_count, row0, near_tiles, mine)
    image0, image1, token = call(
        near_kernel,
        [sds((rows, columns), F32), sds((rows, columns), F32), sds((8, LANES), F32)],
        [VMEM] * 5,
        micros=10.0,
    )(w, low, sources, high, self_terms)
    z1 = across(call(take_kernel, sds((SLICES, rank, LANES), BF16), [VMEM, ANY])(held, token))

    c1 = call(
        functools.partial(first_couple, ops, rank, far),
        sds((SLICES, body, LANES), BF16),
        [SMEM, SMEM] + [VMEM] * (1 + count),
        [pltpu.VMEM((n * blocks * rank, LANES), BF16)],
    )(cols, group, held, *z1)
    c1 = exchange(c1)

    piece = sds((rows + STATS, columns), BF16)
    scratch = [pltpu.VMEM((rows, columns), F32), pltpu.VMEM((blocks, body, columns), BF16)]
    first, z_first, keep = call(
        image_first,
        [piece, sds((SLICES, rank, LANES), BF16), sds((8, columns), F32)],
        [VMEM] * 5,
        scratch,
    )(sources, image0, left, right, c1)
    low0, high0 = ring(first)
    second, msg = call(
        image_second,
        [piece, sds((SLICES, body + STATS, LANES), BF16)],
        [VMEM] * 7,
        scratch,
    )(sources, image1, left, right, c1, z_first, keep)
    low1, high1 = ring(second)
    msgs = across(exchange(msg))

    c2 = call(
        functools.partial(second_couple, all_blocks * size, ops, rank, far),
        sds((SLICES, body + STATS, LANES), BF16),
        [SMEM, SMEM, ANY, ANY] + [VMEM] * (1 + 2 * count),
        [
            pltpu.VMEM((ops, n * blocks * rank, LANES), BF16),
            pltpu.VMEM((n, STATS, LANES), F32),
        ],
        micros=30.0,
    )(cols, group, low0, high0, held, *z1, *msgs)
    c2 = exchange(c2)

    outs = sds((ops, rows, columns), F32)
    scratch = [
        pltpu.VMEM((3, rows, columns), BF16),
        pltpu.VMEM((blocks, body, columns), BF16),
        pltpu.VMEM((rows, columns), F32),
    ]
    images, heights, norms, aux = call(
        final_first,
        [outs, sds((ops, columns), F32), sds((ops, columns), F32), sds((8, columns), F32)],
        [VMEM] * 10,
        scratch + [pltpu.VMEM((STATS, columns), F32), pltpu.SemaphoreType.DMA((blocks,))],
        out_specs=[ANY, VMEM, VMEM, VMEM],
    )(w, low, sources, high, low0, first, high0, self_terms, left, c2)
    images = call(
        final_second,
        outs,
        [ANY] + [VMEM] * 11,
        scratch + [pltpu.SemaphoreType.DMA((blocks,))],
        out_specs=ANY,
        alias={0: 0},
    )(images, w, low, sources, high, low1, second, high1, self_terms, left, c2, aux)
    return images, heights, norms


def solution(mesh):
    placed = (
        P(("groups", "store"), None),
        P(None, "store"),
        P(None, "store", None, None, None),
        P("store", None),
        P("store"),
        P("store", None),
        P("store", None, None),
        P("store", None, None),
        P(None, "store", None, None, None),
    )
    return jax.shard_map(
        shards,
        mesh=mesh,
        in_specs=placed,
        out_specs=(P(None, ("groups", "store"), None), P("groups", None), P("groups", None)),
        check_vma=False,
    )
```
